32 devices in a mesh: fsdp: 8 (over y, x, core), seq: 4 (over z).
Axes of the slice: x: 2, y: 2, z: 4, core: 2. Of those that a mesh axis runs over, the one named last changes fastest.
Arguments:
- layer_input_rows: bfloat16 [8, 1536, 1792], P('fsdp', 'seq'), may hold values from -6 to 6
- segments: int32 [8, 1536], P('fsdp', 'seq'), may hold values from 0 to 2, as said below
- sequence_adapter_index: int32 [8, 1], P('fsdp'), may hold values from 0 to 7
- output_gradient: bfloat16 [8, 1536, 1792], P('fsdp', 'seq'), may hold values from -6 to 6
- mixer_norm_gain: float32 [1792], replicated, may hold values from 0.1 to 1.9
- feedforward_norm_gain: float32 [1792], replicated, may hold values from 0.1 to 1.9
- convolution_taps: float32 [3, 1792], replicated, may hold values from -3.5 to 3.5
- mixer_input_weight: bfloat16 [1792, 4096], P('fsdp'), may hold values from -0.125 to 0.125
- mixer_output_weight: bfloat16 [1792, 1792], P('fsdp'), may hold values from -1.5 to 1.5
- gate_up_weight: bfloat16 [1792, 9728], P('fsdp'), may hold values from -0.125 to 0.125
- down_weight: bfloat16 [4864, 1792], P('fsdp'), may hold values from -0.078125 to 0.078125
- adapter_input_down: bfloat16 [8, 1792, 64], replicated, may hold values from -0.125 to 0.125
- adapter_querykey_up: bfloat16 [8, 2, 16, 256], replicated, may hold values from -0.5 to 0.5
- adapter_valuegate_up: bfloat16 [8, 2, 16, 1792], replicated, may hold values from -0.5 to 0.5
- adapter_output_down: bfloat16 [8, 1792, 16], replicated, may hold values from -1.5 to 1.5
- adapter_output_up: bfloat16 [8, 16, 1792], replicated, may hold values from -0.5 to 0.5
- adapter_gateup_down: bfloat16 [8, 1792, 32], replicated, may hold values from -0.125 to 0.125
- adapter_gateup_up: bfloat16 [8, 2, 16, 4864], replicated, may hold values from -0.5 to 0.5
- adapter_feedforward_down: bfloat16 [8, 4864, 16], replicated, may hold values from -0.078125 to 0.078125
- adapter_feedforward_up: bfloat16 [8, 16, 1792], replicated, may hold values from -0.5 to 0.5
Outputs:
- output: bfloat16 [8, 1536, 1792], P('fsdp', 'seq')
- grad_input: float32 [8, 1536, 1792], P('fsdp', 'seq')
- grad_in_down: float32 [8, 1792, 64], replicated
- grad_qk_up: float32 [8, 2, 16, 256], replicated
- grad_vg_up: float32 [8, 2, 16, 1792], replicated
- grad_out_down: float32 [8, 1792, 16], replicated
- grad_out_up: float32 [8, 16, 1792], replicated
- grad_mlp_down: float32 [8, 1792, 32], replicated
- grad_mlp_up: float32 [8, 2, 16, 4864], replicated
- grad_ffd_down: float32 [8, 4864, 16], replicated
- grad_ffd_up: float32 [8, 16, 1792], replicated
The draws below stay inside these ranges and needn't reach their ends.
Inputs may be any that keep to these rules, and one draw needn't show every extreme that they name: `segments`: each sequence holds three documents in order, numbered 0, 1 and 2; the first and the last have 1536 // 8 to 383 tokens each, the middle one the rest. `sequence_adapter_index`: every adapter is chosen by at least one sequence.
All inputs are finite; a program needn't handle non-finite values.
Results may differ from the reference program's by a relative error of at most 0.015.
Values may be sent and summed in bfloat16 or wider, within the bound.
A program may use at most 320 MiB of HBM per device.

```python
import jax
import jax.numpy as jnp
from jax import lax

MODEL_WIDTH = 1792
HEAD_COUNT = 16
FEATURE_SIZE = 16
DV = 112
HIDDEN_UNITS = 4864
ADAPTER_RANK = 16
ADAPTER_COUNT = 8
LEN = 1536
SEQS = 8


def draw_segments(key, part):
    key = jax.random.fold_in(key, 7)
    key_first, key_last = jax.random.split(key)
    first_len = jax.random.randint(key_first, (SEQS, 1), LEN // 8, LEN // 4)
    last_len = jax.random.randint(key_last, (SEQS, 1), LEN // 8, LEN // 4)
    position = jnp.arange(LEN, dtype=jnp.int32)[None, :]
    return (position >= first_len).astype(jnp.int32) + (position >= LEN - last_len).astype(jnp.int32)


def levels(stream_key, shape, cuts, least, high):
    level = 1.0
    for axis_at, blocks in cuts:
        heights = jax.random.uniform(jax.random.fold_in(jax.random.fold_in(stream_key, 6), axis_at), (blocks,), jnp.float32, least / len(cuts), high / len(cuts))
        level = level * jnp.repeat(jnp.exp(heights), shape[axis_at] // blocks).reshape((-1,) + (1,) * (len(shape) - 1 - axis_at))
    return level


def picks_of(own_key, rows, count, top, lift):
    order = jax.random.permutation(jax.random.fold_in(own_key, 1), count)
    favour = order
    for power in range(3):
        favour = favour * favour // count
    favour = favour * lift // count
    chance = jax.random.randint(jax.random.fold_in(own_key, 2), (rows, count), 0, 4096) + favour
    sure = jax.random.permutation(jax.random.fold_in(own_key, 3), rows)[jnp.arange(count) % rows]
    chance = jnp.where(jnp.arange(rows)[:, None] == sure[None, :], 1 << 14, chance)
    merit = chance * count + jnp.arange(count)
    return lax.top_k(merit.astype(jnp.int32), top)[1].astype(jnp.int32)


def noise(own_key, dims, width, reach, pieces=(), held_as=jnp.bfloat16):
    result = jax.random.normal(own_key, dims, jnp.float32) * width
    if len(pieces) > 0:
        result = levels(own_key, dims, pieces, -0.22, 0.18) * result
    return jnp.clip(result, min=-reach, max=reach).astype(held_as)


def setup_inputs(seed: int = 0) -> dict:
    splits = jax.random.split(jax.random.key(seed), 21)
    layer_input_rows = noise(splits[0], (SEQS, LEN, MODEL_WIDTH), 1.0, 6.0, ((0, 8), (1, 4)))
    segments = draw_segments(jax.random.fold_in(splits[20], 71), 0)
    sequence_adapter_index = picks_of(splits[2], SEQS, ADAPTER_COUNT, 1, 0)
    output_gradient = noise(splits[3], (SEQS, LEN, MODEL_WIDTH), 1.0, 6.0, ((0, 8), (1, 4)))
    mixer_norm_gain = jnp.clip(1.0 + 0.18 * jax.random.normal(splits[4], (MODEL_WIDTH,), jnp.float32), 0.1, 1.9)
    feedforward_norm_gain = jnp.clip(1.0 + 0.18 * jax.random.normal(splits[5], (MODEL_WIDTH,), jnp.float32), 0.1, 1.9)
    convolution_taps = noise(splits[6], (3, MODEL_WIDTH), 3 ** -0.5, 3.5, (), jnp.float32)
    mixer_input_weight = noise(splits[7], (MODEL_WIDTH, 2 * HEAD_COUNT * FEATURE_SIZE + 2 * MODEL_WIDTH), MODEL_WIDTH ** -0.5, 0.125, ((0, 8),))
    mixer_output_weight = noise(splits[8], (MODEL_WIDTH, MODEL_WIDTH), (max(MODEL_WIDTH // 128, 1)) ** -0.5, 1.5, ((0, 8),))
    gate_up_weight = noise(splits[9], (MODEL_WIDTH, 2 * HIDDEN_UNITS), MODEL_WIDTH ** -0.5, 0.125, ((0, 8),))
    down_weight = noise(splits[10], (HIDDEN_UNITS, MODEL_WIDTH), HIDDEN_UNITS ** -0.5, 0.078125, ((0, 8),))
    adapter_input_down = noise(splits[11], (ADAPTER_COUNT, MODEL_WIDTH, 4 * ADAPTER_RANK), MODEL_WIDTH ** -0.5, 0.125)
    adapter_querykey_up = noise(splits[12], (ADAPTER_COUNT, 2, ADAPTER_RANK, HEAD_COUNT * FEATURE_SIZE), (10 * ADAPTER_RANK) ** -0.5, 0.5)
    adapter_valuegate_up = noise(splits[13], (ADAPTER_COUNT, 2, ADAPTER_RANK, MODEL_WIDTH), (10 * ADAPTER_RANK) ** -0.5, 0.5)
    adapter_output_down = noise(splits[14], (ADAPTER_COUNT, MODEL_WIDTH, ADAPTER_RANK), (max(MODEL_WIDTH // 128, 1)) ** -0.5, 1.5)
    adapter_output_up = noise(splits[15], (ADAPTER_COUNT, ADAPTER_RANK, MODEL_WIDTH), (10 * ADAPTER_RANK) ** -0.5, 0.5)
    adapter_gateup_down = noise(splits[16], (ADAPTER_COUNT, MODEL_WIDTH, 2 * ADAPTER_RANK), MODEL_WIDTH ** -0.5, 0.125)
    adapter_gateup_up = noise(splits[17], (ADAPTER_COUNT, 2, ADAPTER_RANK, HIDDEN_UNITS), (10 * ADAPTER_RANK) ** -0.5, 0.5)
    adapter_feedforward_down = noise(splits[18], (ADAPTER_COUNT, HIDDEN_UNITS, ADAPTER_RANK), HIDDEN_UNITS ** -0.5, 0.078125)
    adapter_feedforward_up = noise(splits[19], (ADAPTER_COUNT, ADAPTER_RANK, MODEL_WIDTH), (10 * ADAPTER_RANK) ** -0.5, 0.5)
    return {"layer_input_rows": layer_input_rows, "segments": segments, "sequence_adapter_index": sequence_adapter_index, "output_gradient": output_gradient, "mixer_norm_gain": mixer_norm_gain, "feedforward_norm_gain": feedforward_norm_gain, "convolution_taps": convolution_taps, "mixer_input_weight": mixer_input_weight, "mixer_output_weight": mixer_output_weight, "gate_up_weight": gate_up_weight, "down_weight": down_weight, "adapter_input_down": adapter_input_down, "adapter_querykey_up": adapter_querykey_up, "adapter_valuegate_up": adapter_valuegate_up, "adapter_output_down": adapter_output_down, "adapter_output_up": adapter_output_up, "adapter_gateup_down": adapter_gateup_down, "adapter_gateup_up": adapter_gateup_up, "adapter_feedforward_down": adapter_feedforward_down, "adapter_feedforward_up": adapter_feedforward_up}


@jax.custom_vjp
def low(v):
    return lax.optimization_barrier(v.astype(jnp.bfloat16)).astype(jnp.float32)

@jax.custom_vjp
def low_back(v):
    return v

def low_keep(v):
    return (low(v), None)

def low_pass(kept, grad):
    return (grad,)

def back_keep(v):
    return (v, None)

def back_low(kept, grad):
    return (low(grad),)
low.defvjp(low_keep, low_pass)
low_back.defvjp(back_keep, back_low)

def multiplier(spec, left, right):
    return jnp.einsum(spec, left, right, precision=lax.Precision.HIGHEST)

def rms_norm(value, gain):
    return value * lax.rsqrt(lax.optimization_barrier(jnp.mean(value * value, -1, keepdims=True)) + 1e-05) * gain

def short_conv(signal, kernel, document_labels):
    length = signal.shape[0]
    summed = kernel[0] * signal
    for offset in (1, 2):
        shifted = jnp.concatenate([jnp.zeros((offset, signal.shape[1]), signal.dtype), signal[:length - offset]], 0)
        same_doc = jnp.concatenate([jnp.zeros((offset,), bool), document_labels[offset:] == document_labels[:length - offset]], 0)
        summed = summed + kernel[offset] * shifted * same_doc[:, None].astype(signal.dtype)
    return summed

def attend(queries, every_key, values, document_labels):
    length = queries.shape[0]
    block_rows = min(512, length)
    count_blocks = length // block_rows
    score_scale = FEATURE_SIZE ** (-0.5)
    key_pos = jnp.arange(length, dtype=jnp.int32)

    def one_block(start):
        query_block = lax.dynamic_slice_in_dim(queries, start, block_rows, 0)
        unmasked_scores = multiplier('cmn,imn->mci', query_block, every_key) * score_scale
        scores = low_back(unmasked_scores)
        query_pos = start + jnp.arange(block_rows, dtype=jnp.int32)
        doc_query = lax.dynamic_slice_in_dim(document_labels, start, block_rows, 0)
        visible = (key_pos[None, :] <= query_pos[:, None]) & (doc_query[:, None] == document_labels[None, :])
        kernel_weights = jnp.where(visible[None], 1.0 + scores + 0.5 * scores * scores, 0.0)
        denominator = lax.optimization_barrier(jnp.sum(kernel_weights, -1, keepdims=True))
        attn_probs = low(kernel_weights / denominator)
        return multiplier('hqk,khd->qhd', attn_probs, values)
    starts = jnp.arange(count_blocks, dtype=jnp.int32) * block_rows
    blocks_out = lax.map(jax.checkpoint(one_block), starts)
    return blocks_out.reshape(length, HEAD_COUNT * DV)

def forward_apply(input_arrays, adapter_tuple, document_labels, selection_index, frozen_params, mixer_norm_gain, feedforward_norm_gain, convolution_taps):
    mixer_in, mixer_out, gate_up, down_w = frozen_params
    selected_adapters = [lax.dynamic_index_in_dim(adapter_table, selection_index, 0, keepdims=False) for adapter_table in adapter_tuple]
    input_down_maps, querykey_up_maps, valuegate_up_maps, output_down_maps, output_up_maps, gateup_down_maps, gateup_up_maps, feedforward_down_maps, feedforward_up_maps = selected_adapters
    length = input_arrays.shape[0]
    hidden1 = low(rms_norm(input_arrays, mixer_norm_gain))
    rank_in = low_back(low(multiplier('td,dr->tr', hidden1, input_down_maps)))
    extra_rank = jnp.concatenate([multiplier('tr,re->te', rank_in[:, 0:ADAPTER_RANK], querykey_up_maps[0]).reshape(length, HEAD_COUNT, FEATURE_SIZE), multiplier('tr,re->te', rank_in[:, ADAPTER_RANK:2 * ADAPTER_RANK], querykey_up_maps[1]).reshape(length, HEAD_COUNT, FEATURE_SIZE), multiplier('tr,re->te', rank_in[:, 2 * ADAPTER_RANK:3 * ADAPTER_RANK], valuegate_up_maps[0]).reshape(length, HEAD_COUNT, DV), multiplier('tr,re->te', rank_in[:, 3 * ADAPTER_RANK:], valuegate_up_maps[1]).reshape(length, HEAD_COUNT, DV)], axis=-1)
    projected = multiplier('td,de->te', hidden1, mixer_in).reshape(length, HEAD_COUNT, 2 * FEATURE_SIZE + 2 * DV) + extra_rank
    projected = low_back(low(projected))
    queries = projected[..., 0:FEATURE_SIZE]
    every_key = projected[..., FEATURE_SIZE:2 * FEATURE_SIZE]
    conv_in = projected[..., 2 * FEATURE_SIZE:2 * FEATURE_SIZE + DV].reshape(length, MODEL_WIDTH)
    gate_in = projected[..., 2 * FEATURE_SIZE + DV:].reshape(length, MODEL_WIDTH)
    conv_out = short_conv(conv_in, convolution_taps, document_labels)
    values = low(jax.nn.silu(gate_in) * conv_out).reshape(length, HEAD_COUNT, DV)
    attended = low_back(low(attend(queries, every_key, values, document_labels)))
    rank_out = low_back(low(multiplier('td,dr->tr', attended, output_down_maps)))
    branch = low_back(multiplier('td,de->te', attended, mixer_out) + multiplier('tr,re->te', rank_out, output_up_maps))
    resid = input_arrays + branch
    hidden2 = low(rms_norm(resid, feedforward_norm_gain))
    rank_mlp = low_back(low(multiplier('td,dr->tr', hidden2, gateup_down_maps)))
    both_pre = multiplier('td,de->te', hidden2, gate_up)
    gate_pre = low_back(both_pre[:, 0:HIDDEN_UNITS] + multiplier('tr,re->te', rank_mlp[:, 0:ADAPTER_RANK], gateup_up_maps[0]))
    up_pre = low_back(both_pre[:, HIDDEN_UNITS:] + multiplier('tr,re->te', rank_mlp[:, ADAPTER_RANK:], gateup_up_maps[1]))
    inner_act = low(jax.nn.silu(gate_pre) * up_pre)
    rank_ffd = low_back(low(multiplier('tf,fr->tr', inner_act, feedforward_down_maps)))
    return resid + low_back(multiplier('tf,fe->te', inner_act, down_w) + multiplier('tr,re->te', rank_ffd, feedforward_up_maps))

def reference(layer_input_rows, segments, sequence_adapter_index, output_gradient, mixer_norm_gain, feedforward_norm_gain, convolution_taps, mixer_input_weight, mixer_output_weight, gate_up_weight, down_weight, adapter_input_down, adapter_querykey_up, adapter_valuegate_up, adapter_output_down, adapter_output_up, adapter_gateup_down, adapter_gateup_up, adapter_feedforward_down, adapter_feedforward_up):
    frozen_params = (mixer_input_weight.astype(jnp.float32), mixer_output_weight.astype(jnp.float32), gate_up_weight.astype(jnp.float32), down_weight.astype(jnp.float32))
    adapter_bundle = (adapter_input_down.astype(jnp.float32), adapter_querykey_up.astype(jnp.float32), adapter_valuegate_up.astype(jnp.float32), adapter_output_down.astype(jnp.float32), adapter_output_up.astype(jnp.float32), adapter_gateup_down.astype(jnp.float32), adapter_gateup_up.astype(jnp.float32), adapter_feedforward_down.astype(jnp.float32), adapter_feedforward_up.astype(jnp.float32))

    def one_sequence(running_totals, sequence_items):
        input_arrays, document_labels, selection_index, output_cotangent = sequence_items

        def layer_function(layer_entry, adapter_tuple):
            return forward_apply(layer_entry, adapter_tuple, document_labels, selection_index, frozen_params, mixer_norm_gain, feedforward_norm_gain, convolution_taps)
        output_arrays, pullback_function = jax.vjp(layer_function, input_arrays.astype(jnp.float32), adapter_bundle)
        input_gradient, adapter_gradient_list = pullback_function(output_cotangent.astype(jnp.float32))
        running_totals = tuple((left_partial_sum + right_partial_sum for left_partial_sum, right_partial_sum in zip(running_totals, adapter_gradient_list)))
        return (running_totals, (output_arrays.astype(jnp.bfloat16), input_gradient))
    empty_totals = tuple((jnp.zeros_like(adapter_table) for adapter_table in adapter_bundle))
    running_totals, (output_arrays, grads) = lax.scan(one_sequence, empty_totals, (layer_input_rows, segments, sequence_adapter_index[:, 0], output_gradient))
    return (output_arrays, grads, running_totals[0], running_totals[1], running_totals[2], running_totals[3], running_totals[4], running_totals[5], running_totals[6], running_totals[7], running_totals[8])
```

```python
import functools

import jax
import jax.numpy as jnp
from jax import lax
from jax.experimental import pallas as pl
from jax.experimental.pallas import tpu as pltpu
from jax.sharding import PartitionSpec as P

HEAD_COUNT = 16
FEATURE_SIZE = 16
DV = 112
ADAPTER_RANK = 16
ADAPTER_COUNT = 8
PER_HEAD = 2 * FEATURE_SIZE + 2 * DV
TBLOCK = 128

epsilon = 1e-05


FEATS = 176
VROWS = 128


def dot_nn(a, b):
    return lax.dot_general(a, b, (((1,), (0,)), ((), ())), preferred_element_type=jnp.float32)


def dot_nt(a, b):
    return lax.dot_general(a, b, (((1,), (1,)), ((), ())), preferred_element_type=jnp.float32)


def dot_tn(a, b):
    return lax.dot_general(a, b, (((0,), (0,)), ((), ())), preferred_element_type=jnp.float32)


def group_scale(shift):
    return 1.0 / 32.0 if shift in (0, 8) else 1.0 / 16.0


def cycle(rows, shift):
    if shift == 0:
        return rows
    return jnp.concatenate([rows[shift:], rows[:shift]], axis=0)


def features(rows, keep, scaled):
    length = rows.shape[1]
    rows_kept = rows * keep
    parts = []
    for shift in range(9):
        item = rows_kept * cycle(rows, shift)
        parts.append(item * group_scale(shift) if scaled else item)
    parts.append(rows_kept * 0.25 if scaled else rows_kept)
    first_row = lax.broadcasted_iota(jnp.int32, (16, length), 0) == 0
    parts.append(jnp.where(first_row, jnp.broadcast_to(keep, (16, length)), 0.0))
    return jnp.concatenate(parts, axis=0).astype(jnp.bfloat16)


def features_back(rows, grad, scaled):
    total = grad[144:160] * 0.25 if scaled else grad[144:160]
    for shift in range(9):
        item = grad[16 * shift : 16 * shift + 16]
        if scaled:
            item = item * group_scale(shift)
        total = total + item * cycle(rows, shift) + cycle(item * rows, (16 - shift) % 16)
    return total


def later_by(rows, offset, before):
    lane = lax.broadcasted_iota(jnp.int32, rows.shape, 1)
    moved = pltpu.roll(rows, offset, 1)
    if offset == 1:
        return jnp.where(lane == 0, before[:, 1:2], moved)
    return jnp.where(lane == 0, before[:, 0:1], jnp.where(lane == 1, before[:, 1:2], moved))


def sooner_by(rows, offset, after):
    length = rows.shape[1]
    lane = lax.broadcasted_iota(jnp.int32, rows.shape, 1)
    moved = pltpu.roll(rows, length - offset, 1)
    if offset == 1:
        return jnp.where(lane == length - 1, after[:, 0:1], moved)
    return jnp.where(
        lane == length - 2,
        after[:, 0:1],
        jnp.where(lane == length - 1, after[:, 1:2], moved),
    )


def conv_forward(signal, before, taps, same):
    total = taps[:, 0:1] * signal
    for offset in (1, 2):
        total = total + taps[:, offset : offset + 1] * later_by(signal, offset, before) * same[offset - 1]
    return total


def conv_backward(grad, after, taps, same):
    total = taps[:, 0:1] * grad
    for offset in (1, 2):
        total = total + taps[:, offset : offset + 1] * sooner_by(grad, offset, after) * same[offset - 1]
    return total


def add_ones(values):
    length = values.shape[1]
    row = lax.broadcasted_iota(jnp.int32, (VROWS - DV, length), 0)
    return jnp.concatenate(
        [values, jnp.where(row == 0, 1.0, 0.0).astype(jnp.bfloat16)], axis=0
    )


def weights_of(keys, queries, mask):
    shifted = dot_tn(keys, queries) + 1.0
    return shifted, (0.5 * shifted * shifted + 0.5) * mask


def mix_forward(tokens, before_tokens, taps, doc_row, prev_docs, mask_ref):
    length = tokens.shape[0]
    block = tokens.astype(jnp.float32).T.astype(jnp.bfloat16)
    before = before_tokens.astype(jnp.float32).T[2 * FEATURE_SIZE : 2 * FEATURE_SIZE + DV, 14:16]
    values, _, _, _ = values_of(block, before, taps, doc_row, prev_docs)
    marked = add_ones(values)
    keep_last = (doc_row == doc_row[:, length - 1 : length]).astype(jnp.float32)
    key_feats = features(block[16:32].astype(jnp.float32), keep_last, False)
    state = dot_nt(key_feats, marked)
    scaled_q = (block[0:16].astype(jnp.float32) * 0.25).astype(jnp.bfloat16)
    sums = []
    for start in range(0, length, TBLOCK):
        stop = start + TBLOCK
        _, weights = weights_of(
            block[16:32, :stop], scaled_q[:, start:stop], mask_ref[:stop, start:stop]
        )
        sums.append(dot_nn(marked[:, :stop], weights.astype(jnp.bfloat16)))
    return block, marked, jnp.concatenate(sums, axis=1), state


def values_of(block, before, taps, doc_row, prev_docs):
    length = block.shape[1]
    doc8 = jnp.broadcast_to(doc_row, (8, length))
    prev8 = jnp.broadcast_to(prev_docs, (8, 2))
    same = [
        (doc8 == later_by(doc8, offset, prev8)).astype(jnp.float32)[0:1] for offset in (1, 2)
    ]
    conv_in = block[32 : 32 + DV].astype(jnp.float32)
    gate_in = block[32 + DV :].astype(jnp.float32)
    conv_out = conv_forward(conv_in, before, taps, same)
    sigmoid = 1.0 / (1.0 + jnp.exp(-gate_in))
    values = (gate_in * sigmoid * conv_out).astype(jnp.bfloat16)
    return values, conv_out, gate_in, sigmoid


def fill_mask(mask_ref, doc_row, doc_col):
    shape = mask_ref.shape
    causal = lax.broadcasted_iota(jnp.int32, shape, 0) <= lax.broadcasted_iota(jnp.int32, shape, 1)
    mask_ref[...] = jnp.where(causal & (doc_col == doc_row), 1.0, 0.0)


def f1_kernel(p_ref, halo_ref, taps_ref, row_ref, col_ref, prev_ref, pt_ref, v_ref, o_ref, l_ref, mask_ref):
    @pl.when(pl.program_id(0) == 0)
    def _():
        fill_mask(mask_ref, row_ref[...], col_ref[...])

    block, marked, sums, state = mix_forward(
        p_ref[...], halo_ref[...], taps_ref[0], row_ref[...], prev_ref[:, 0:2], mask_ref
    )
    pt_ref[...] = block
    v_ref[...] = marked
    o_ref[...] = sums
    l_ref[...] = state.astype(jnp.bfloat16)


def mix_finish(block, sums, carry, doc_row):
    keep_first = (doc_row == doc_row[:, 0:1]).astype(jnp.float32)
    query_feats = features(block[0:16].astype(jnp.float32), keep_first, True)
    total = sums + dot_tn(carry, query_feats)
    denominator = total[DV : DV + 1]
    return (total[:DV] / denominator).astype(jnp.bfloat16), denominator


def f2_kernel(pt_ref, o_ref, s_ref, row_ref, att_ref, den_ref):
    attended, denominator = mix_finish(pt_ref[...], o_ref[...], s_ref[...], row_ref[...])
    att_ref[...] = attended
    den_ref[...] = jnp.broadcast_to(denominator, den_ref.shape)


def sum_grads(grad, attended, denominator):
    length = grad.shape[1]
    inverse = 1.0 / denominator
    grad_f = grad.astype(jnp.float32)
    dot_term = jnp.sum(grad_f * attended.astype(jnp.float32), axis=0, keepdims=True)
    row = lax.broadcasted_iota(jnp.int32, (VROWS - DV, length), 0)
    tail = jnp.where(row == 0, jnp.broadcast_to(-dot_term * inverse, row.shape), 0.0)
    return jnp.concatenate([grad_f * inverse, tail], axis=0).astype(jnp.bfloat16)


def mix_back_local(block, marked, sums_grad, carry, doc_row, mask_ref):
    length = block.shape[1]
    keys = block[16:32]
    queries = block[0:16].astype(jnp.float32)
    scaled_q = (queries * 0.25).astype(jnp.bfloat16)
    keep_first = (doc_row == doc_row[:, 0:1]).astype(jnp.float32)
    query_grad = features_back(queries, dot_nn(carry, sums_grad) * keep_first, True)
    key_grad = jnp.zeros((16, length), jnp.float32)
    value_grad = jnp.zeros((VROWS, length), jnp.float32)
    parts = []
    for start in range(0, length, TBLOCK):
        stop = start + TBLOCK
        mask = mask_ref[:stop, start:stop]
        shifted, weights = weights_of(keys[:, :stop], scaled_q[:, start:stop], mask)
        grad_block = sums_grad[:, start:stop]
        weight_grad = dot_tn(marked[:, :stop], grad_block)
        score_grad = (weight_grad * shifted * mask).astype(jnp.bfloat16)
        parts.append(dot_nn(keys[:, :stop], score_grad) * 0.25)
        key_part = dot_nt(scaled_q[:, start:stop], score_grad)
        value_part = dot_nt(grad_block, weights.astype(jnp.bfloat16))
        if stop < length:
            key_part = jnp.concatenate(
                [key_part, jnp.zeros((16, length - stop), jnp.float32)], axis=1
            )
            value_part = jnp.concatenate(
                [value_part, jnp.zeros((VROWS, length - stop), jnp.float32)], axis=1
            )
        key_grad = key_grad + key_part
        value_grad = value_grad + value_part
    query_grad = query_grad + jnp.concatenate(parts, axis=1)
    return query_grad, key_grad, value_grad


def b1_kernel(pt_ref, v_ref, g_ref, att_ref, den_ref, s_ref, row_ref, col_ref, d_ref, dq_ref, dk_ref, dv_ref, mask_ref):
    @pl.when(pl.program_id(0) == 0)
    def _():
        fill_mask(mask_ref, row_ref[...], col_ref[...])

    doc_row = row_ref[...]
    block = pt_ref[...]
    sums_grad = sum_grads(g_ref[...], att_ref[...], den_ref[0:1])
    keep_first = (doc_row == doc_row[:, 0:1]).astype(jnp.float32)
    query_feats = features(block[0:16].astype(jnp.float32), keep_first, True)
    d_ref[...] = dot_nt(query_feats, sums_grad).astype(jnp.bfloat16)
    dq, dk, dv = mix_back_local(block, v_ref[...], sums_grad, s_ref[...], doc_row, mask_ref)
    dq_ref[...] = dq
    dk_ref[...] = dk
    dv_ref[...] = dv


def mix_back_finish(block, marked, later_state, key_grad, value_grad, doc_row, before, taps, prev_docs):
    length = block.shape[1]
    keep_last = (doc_row == doc_row[:, length - 1 : length]).astype(jnp.float32)
    keys = block[16:32].astype(jnp.float32)
    key_feats = features(keys, keep_last, False)
    key_grad = key_grad + features_back(keys, dot_nn(later_state, marked) * keep_last, False)
    value_grad = (value_grad + dot_tn(later_state, key_feats))[:DV]
    _, conv_out, gate_in, sigmoid = values_of(block, before, taps, doc_row, prev_docs)
    gate_grad = value_grad * conv_out * sigmoid * (1.0 + gate_in * (1.0 - sigmoid))
    conv_grad = value_grad * gate_in * sigmoid
    return key_grad, gate_grad, conv_grad


def b2_kernel(pt_ref, v_ref, g_ref, dq_ref, dk_ref, dv_ref, halo_ref, taps_ref, row_ref, prev_ref, dp_ref, first_ref, tail_ref):
    doc_row = row_ref[...]
    length = doc_row.shape[1]
    taps = taps_ref[0]
    before = halo_ref[...].astype(jnp.float32).T[2 * FEATURE_SIZE : 2 * FEATURE_SIZE + DV, 14:16]
    key_grad, gate_grad, conv_grad = mix_back_finish(
        pt_ref[...], v_ref[...], g_ref[...], dk_ref[...], dv_ref[...], doc_row, before, taps, prev_ref[:, 0:2]
    )
    doc8 = jnp.broadcast_to(doc_row, (8, length))
    none = jnp.full((8, 2), -1.0, jnp.float32)
    same = [(doc8 == sooner_by(doc8, offset, none)).astype(jnp.float32)[0:1] for offset in (1, 2)]
    conv_in_grad = conv_backward(conv_grad, jnp.zeros((DV, 2), jnp.float32), taps, same)
    whole = jnp.concatenate([dq_ref[...], key_grad, conv_in_grad, gate_grad], axis=0).T
    dp_ref[...] = whole.astype(jnp.bfloat16)
    tail_ref[...] = whole[length - 16 :]
    pad = jnp.zeros((16, length), jnp.float32)
    conv_tokens = jnp.concatenate([jnp.zeros((32, length), jnp.float32), conv_grad, jnp.zeros((DV, length), jnp.float32)], axis=0).T
    first_ref[...] = conv_tokens[0:16]


def call_heads(kernel, length, ins, outs, scratch=()):
    def spec(shape, how):
        if how == "rows":
            return pl.BlockSpec((shape[0] // HEAD_COUNT,) + shape[1:], lambda h: (h,) + (0,) * (len(shape) - 1))
        if how == "cols":
            return pl.BlockSpec((shape[0], shape[1] // HEAD_COUNT), lambda h: (0, h))
        return pl.BlockSpec(shape, lambda h: (0,) * len(shape))

    return pl.pallas_call(
        kernel,
        grid=(HEAD_COUNT,),
        in_specs=[spec(a.shape, how) for a, how in ins],
        out_specs=[spec(s.shape, how) for s, how in outs],
        out_shape=[s for s, _ in outs],
        scratch_shapes=list(scratch),
        compiler_params=pltpu.CompilerParams(vmem_limit_bytes=48 * 1024 * 1024),
    )(*[a for a, _ in ins])


def shift_pairs(count, step):
    return [(i, i + step) for i in range(count) if 0 <= i + step < count]


def chain(own, whole, link, step):
    count = lax.axis_size("seq")
    pairs = shift_pairs(count, step)
    message = own
    for _ in range(count - 2):
        got = lax.ppermute(message, "seq", pairs)
        message = (own.astype(jnp.float32) + (whole * link) * got.astype(jnp.float32)).astype(jnp.bfloat16)
    got = lax.ppermute(message, "seq", pairs)
    return (got.astype(jnp.float32) * link).astype(jnp.bfloat16)


def product(spec, left, right):
    return jnp.einsum(spec, left, right, preferred_element_type=jnp.float32)


def rms_forward(value, gain):
    inv_root = lax.rsqrt(jnp.mean(value * value, -1, keepdims=True) + epsilon)
    normed = value * inv_root
    return (normed, inv_root, (normed * gain).astype(jnp.bfloat16))


def rms_backward(grad_hidden, normed, inv_root, gain):
    scaled = grad_hidden * gain
    return inv_root * (scaled - normed * jnp.mean(scaled * normed, -1, keepdims=True))


def up_by_head(querykey, valuegate):
    parts = [
        (querykey[0], 0, FEATURE_SIZE),
        (querykey[1], FEATURE_SIZE, FEATURE_SIZE),
        (valuegate[0], 2 * FEATURE_SIZE, DV),
        (valuegate[1], 2 * FEATURE_SIZE + DV, DV),
    ]
    rows = [
        jnp.pad(
            part.reshape(ADAPTER_RANK, HEAD_COUNT, size),
            ((0, 0), (0, 0), (at, PER_HEAD - at - size)),
        )
        for part, at, size in parts
    ]
    return jnp.concatenate(rows, axis=0).reshape(4 * ADAPTER_RANK, HEAD_COUNT * PER_HEAD)


def per_device(
    layer_input_rows,
    segments,
    sequence_adapter_index,
    output_gradient,
    mixer_norm_gain,
    feedforward_norm_gain,
    convolution_taps,
    mixer_input_weight,
    mixer_output_weight,
    gate_up_weight,
    down_weight,
    adapter_input_down,
    adapter_querykey_up,
    adapter_valuegate_up,
    adapter_output_down,
    adapter_output_up,
    adapter_gateup_down,
    adapter_gateup_up,
    adapter_feedforward_down,
    adapter_feedforward_up,
):
    batch, length, width = layer_input_rows.shape
    assert batch == 1
    seq_count = lax.axis_size("seq")
    ff = gate_up_weight.shape[1] // 2
    bf16, f32 = jnp.bfloat16, jnp.float32
    chosen = sequence_adapter_index[0, 0]

    def select(table):
        return lax.dynamic_index_in_dim(table, chosen, 0, keepdims=False)

    in_down = select(adapter_input_down.swapaxes(1, 2))
    up_maps = up_by_head(select(adapter_querykey_up), select(adapter_valuegate_up))
    out_down = select(adapter_output_down.swapaxes(1, 2))
    out_up = select(adapter_output_up)
    gu_down = select(adapter_gateup_down.swapaxes(1, 2))
    gu_up = select(adapter_gateup_up)
    ffd_down = select(adapter_feedforward_down.swapaxes(1, 2))
    ffd_up = select(adapter_feedforward_up)
    mixer_in, mixer_out, gate_up, down_w = (
        lax.all_gather(mixer_input_weight, "fsdp", axis=0, tiled=True),
        lax.all_gather(mixer_output_weight, "fsdp", axis=0, tiled=True),
        lax.all_gather(gate_up_weight, "fsdp", axis=0, tiled=True),
        lax.all_gather(down_weight, "fsdp", axis=0, tiled=True),
    )
    docs = segments.astype(f32)
    place = lax.axis_index("seq")
    edge = jnp.concatenate([docs[:, :1], docs[:, length - 2 :], jnp.zeros((1, 125), f32)], axis=1)
    before_edge = lax.ppermute(edge, "seq", shift_pairs(seq_count, 1))
    after_edge = lax.ppermute(edge, "seq", shift_pairs(seq_count, -1))
    prev_docs = jnp.where(place == 0, -1.0, before_edge[:, 1:3])
    next_doc = jnp.where(place == seq_count - 1, -1.0, after_edge[:, 0])
    link_before = (prev_docs[0, 1] == docs[0, 0]).astype(f32)
    link_after = (next_doc[0] == docs[0, length - 1]).astype(f32)
    whole = (docs[0, 0] == docs[0, length - 1]).astype(f32)
    prev_pad = jnp.pad(prev_docs, ((0, 0), (0, 126)))
    doc_col = docs.reshape(length, 1)
    taps = jnp.pad(convolution_taps.T.reshape(HEAD_COUNT, DV, 3), ((0, 0), (0, 0), (0, 5)))

    inputs_f = layer_input_rows[0].astype(f32)
    grad_out = output_gradient[0]
    normed1, root1, hidden1 = rms_forward(inputs_f, mixer_norm_gain)
    rank_in = product("td,rd->tr", hidden1, in_down).astype(bf16)
    projected = (
        product("td,de->te", hidden1, mixer_in) + product("tr,re->te", rank_in, up_maps)
    ).astype(bf16)
    halo = lax.ppermute(projected[length - 16 :], "seq", shift_pairs(seq_count, 1))
    mask = pltpu.VMEM((length, length), f32)
    heads = HEAD_COUNT
    blocks, values, sums, state = call_heads(
        f1_kernel,
        length,
        [(projected, "cols"), (halo, "cols"), (taps, "rows"), (docs, None), (doc_col, None), (prev_pad, None)],
        [
            (jax.ShapeDtypeStruct((heads * PER_HEAD, length), bf16), "rows"),
            (jax.ShapeDtypeStruct((heads * VROWS, length), bf16), "rows"),
            (jax.ShapeDtypeStruct((heads * VROWS, length), f32), "rows"),
            (jax.ShapeDtypeStruct((heads * FEATS, VROWS), bf16), "rows"),
        ],
        [mask],
    )
    carry = chain(state, whole, link_before, 1)
    attended_t, denominator = call_heads(
        f2_kernel,
        length,
        [(blocks, "rows"), (sums, "rows"), (carry, "rows"), (docs, None)],
        [
            (jax.ShapeDtypeStruct((heads * DV, length), bf16), "rows"),
            (jax.ShapeDtypeStruct((heads * 8, length), f32), "rows"),
        ],
    )
    attended = attended_t.T
    rank_out = product("td,rd->tr", attended, out_down).astype(bf16)
    resid = (
        inputs_f
        + product("td,de->te", attended, mixer_out)
        + product("tr,re->te", rank_out, out_up)
    )
    normed2, root2, hidden2 = rms_forward(resid, feedforward_norm_gain)
    rank_mlp = product("td,rd->tr", hidden2, gu_down).astype(bf16)
    rank_ffd_grad = product("te,re->tr", grad_out, ffd_up).astype(bf16)
    inner_grad = product("te,fe->tf", grad_out, down_w) + product("tr,rf->tf", rank_ffd_grad, ffd_down)
    gate_pre = product("td,de->te", hidden2, gate_up[:, :ff]) + product(
        "tr,re->te", rank_mlp[:, :ADAPTER_RANK], gu_up[0]
    )
    up_pre = product("td,de->te", hidden2, gate_up[:, ff:]) + product(
        "tr,re->te", rank_mlp[:, ADAPTER_RANK:], gu_up[1]
    )
    sigmoid = jax.nn.sigmoid(gate_pre)
    gate_val = gate_pre * sigmoid
    inner_act = (gate_val * up_pre).astype(bf16)
    gate_grad = (inner_grad * up_pre * (sigmoid * (1.0 + gate_pre * (1.0 - sigmoid)))).astype(bf16)
    up_grad = (inner_grad * gate_val).astype(bf16)
    rank_ffd = product("tf,rf->tr", inner_act, ffd_down).astype(bf16)
    output = (
        resid + product("tf,fe->te", inner_act, down_w) + product("tr,re->te", rank_ffd, ffd_up)
    ).astype(bf16)
    rank_mlp_grad = jnp.concatenate(
        [product("tf,rf->tr", gate_grad, gu_up[0]), product("tf,rf->tr", up_grad, gu_up[1])], -1
    ).astype(bf16)
    hidden2_grad = (
        product("tf,df->td", gate_grad, gate_up[:, :ff])
        + product("tf,df->td", up_grad, gate_up[:, ff:])
        + product("tr,rd->td", rank_mlp_grad, gu_down)
    )
    resid_grad = grad_out.astype(f32) + rms_backward(hidden2_grad, normed2, root2, feedforward_norm_gain)
    branch_grad = resid_grad.astype(bf16)
    rank_out_grad = product("te,re->tr", branch_grad, out_up).astype(bf16)
    attended_grad = (
        product("te,de->td", branch_grad, mixer_out) + product("tr,rd->td", rank_out_grad, out_down)
    ).astype(bf16)
    grad_t = attended_grad.T
    later, query_grad, key_grad, value_grad = call_heads(
        b1_kernel,
        length,
        [(blocks, "rows"), (values, "rows"), (grad_t, "rows"), (attended_t, "rows"), (denominator, "rows"), (carry, "rows"), (docs, None), (doc_col, None)],
        [
            (jax.ShapeDtypeStruct((heads * FEATS, VROWS), bf16), "rows"),
            (jax.ShapeDtypeStruct((heads * 16, length), f32), "rows"),
            (jax.ShapeDtypeStruct((heads * 16, length), f32), "rows"),
            (jax.ShapeDtypeStruct((heads * VROWS, length), f32), "rows"),
        ],
        [mask],
    )
    later = chain(later, whole, link_after, -1)
    projected_grad, first_conv, tail_grad = call_heads(
        b2_kernel,
        length,
        [(blocks, "rows"), (values, "rows"), (later, "rows"), (query_grad, "rows"), (key_grad, "rows"), (value_grad, "rows"), (halo, "cols"), (taps, "rows"), (docs, None), (prev_pad, None)],
        [
            (jax.ShapeDtypeStruct((length, heads * PER_HEAD), bf16), "cols"),
            (jax.ShapeDtypeStruct((16, heads * PER_HEAD), f32), "cols"),
            (jax.ShapeDtypeStruct((16, heads * PER_HEAD), f32), "cols"),
        ],
    )
    next_conv = lax.ppermute(first_conv[:2], "seq", shift_pairs(seq_count, -1))
    taps_row = jnp.pad(
        convolution_taps.reshape(3, heads, DV),
        ((0, 0), (0, 0), (2 * FEATURE_SIZE, PER_HEAD - 2 * FEATURE_SIZE - DV)),
    ).reshape(3, heads * PER_HEAD)
    after_docs = jnp.where(place == seq_count - 1, -1.0, after_edge[0, 0])
    link_1 = (after_docs == docs[0, length - 1]).astype(f32)
    link_2 = (after_docs == docs[0, length - 2]).astype(f32)
    second = (docs[0, 1] == docs[0, 0]).astype(f32)
    second_next = lax.ppermute(second, "seq", shift_pairs(seq_count, -1))
    extra_last = taps_row[1] * next_conv[0] * link_1 + taps_row[2] * next_conv[1] * link_1 * second_next
    extra_before = taps_row[2] * next_conv[0] * link_2
    extra = jnp.concatenate(
        [jnp.zeros((14, heads * PER_HEAD), f32), extra_before[None], extra_last[None]], axis=0
    )
    projected_grad = lax.dynamic_update_slice(
        projected_grad, (tail_grad + extra).astype(bf16), (length - 16, 0)
    )
    rank_in_grad = product("te,re->tr", projected_grad, up_maps).astype(bf16)
    hidden1_grad = product("te,de->td", projected_grad, mixer_in) + product(
        "tr,rd->td", rank_in_grad, in_down
    )
    input_grad = resid_grad + rms_backward(hidden1_grad, normed1, root1, mixer_norm_gain)

    wide = product("tr,te->re", rank_in, projected_grad).reshape(4, ADAPTER_RANK, heads, PER_HEAD)
    term_qk = jnp.stack(
        [wide[0, :, :, 0:16].reshape(ADAPTER_RANK, -1), wide[1, :, :, 16:32].reshape(ADAPTER_RANK, -1)]
    )
    term_vg = jnp.concatenate(
        [
            wide[2, :, :, 32 : 32 + DV].reshape(ADAPTER_RANK, -1),
            wide[3, :, :, 32 + DV :].reshape(ADAPTER_RANK, -1),
        ]
    )
    by_width = jnp.concatenate(
        [
            product("tr,td->rd", rank_in_grad, hidden1),
            term_vg,
            product("tr,td->rd", rank_out_grad, attended),
            product("tr,td->rd", rank_out, branch_grad),
            product("tr,td->rd", rank_mlp_grad, hidden2),
            product("tr,td->rd", rank_ffd, grad_out),
        ]
    )
    by_ff = jnp.concatenate(
        [
            product("tr,tf->rf", rank_mlp[:, :ADAPTER_RANK], gate_grad),
            product("tr,tf->rf", rank_mlp[:, ADAPTER_RANK:], up_grad),
            product("tr,tf->rf", rank_ffd_grad, inner_act),
        ]
    )
    by_rank = jnp.concatenate([term_qk.reshape(32, -1), jnp.full((16, 256), chosen.astype(f32) / seq_count)])
    by_width, by_ff, by_rank = spread(by_width, by_ff, by_rank)
    sequences = by_rank.shape[0]
    onehot = (by_rank[:, 32, 0][None, :] == jnp.arange(ADAPTER_COUNT, dtype=bf16)[:, None])

    if sequences == ADAPTER_COUNT:
        where = jnp.argmax(onehot, axis=1)

        def arrange(rows):
            return jnp.take(rows, where, axis=0).astype(f32)
    else:

        def arrange(rows):
            return jnp.einsum("as,s...->a...", onehot.astype(f32), rows.astype(f32), precision="highest")

    sizes = [64, 32, 16, 16, 32, 16]
    cut = [sum(sizes[:n]) for n in range(len(sizes) + 1)]
    widths = [arrange(by_width[:, cut[n] : cut[n + 1]]) for n in range(len(sizes))]
    return (
        output[None],
        input_grad[None],
        widths[0].swapaxes(1, 2),
        arrange(by_rank[:, :32]).reshape(ADAPTER_COUNT, 2, ADAPTER_RANK, -1),
        widths[1].reshape(ADAPTER_COUNT, 2, ADAPTER_RANK, width),
        widths[2].swapaxes(1, 2),
        widths[3],
        widths[4].swapaxes(1, 2),
        arrange(by_ff[:, :32]).reshape(ADAPTER_COUNT, 2, ADAPTER_RANK, ff),
        arrange(by_ff[:, 32:]).swapaxes(1, 2),
        widths[5],
    )


def spread(*terms):
    summed = lax.psum(terms, "seq")
    return [lax.all_gather(term.astype(jnp.bfloat16), "fsdp") for term in summed]


def solution(mesh):
    return jax.shard_map(
        per_device,
        mesh=mesh,
        in_specs=(
            P("fsdp", "seq", None),
            P("fsdp", "seq"),
            P("fsdp", None),
            P("fsdp", "seq", None),
            P(),
            P(),
            P(),
            P("fsdp", None),
            P("fsdp", None),
            P("fsdp", None),
            P("fsdp", None),
        )
        + (P(),) * 9,
        out_specs=(P("fsdp", "seq", None), P("fsdp", "seq", None)) + (P(),) * 9,
        check_vma=False,
    )
```

```python
import functools

import jax
import jax.numpy as jnp
from jax import lax
from jax.experimental import pallas as pl
from jax.experimental.pallas import tpu as pltpu
from jax.sharding import PartitionSpec as P

HEAD_COUNT = 16
FEATURE_SIZE = 16
DV = 112
ADAPTER_RANK = 16
ADAPTER_COUNT = 8
PER_HEAD = 2 * FEATURE_SIZE + 2 * DV
TBLOCK = 128

epsilon = 1e-05


FEATS = 176
VROWS = 128


def dot_nn(a, b):
    return lax.dot_general(a, b, (((1,), (0,)), ((), ())), preferred_element_type=jnp.float32)


def dot_nt(a, b):
    return lax.dot_general(a, b, (((1,), (1,)), ((), ())), preferred_element_type=jnp.float32)


def dot_tn(a, b):
    return lax.dot_general(a, b, (((0,), (0,)), ((), ())), preferred_element_type=jnp.float32)


def group_scale(shift):
    return 1.0 / 32.0 if shift in (0, 8) else 1.0 / 16.0


def cycle(rows, shift):
    if shift == 0:
        return rows
    return jnp.concatenate([rows[shift:], rows[:shift]], axis=0)


def features(rows, keep, scaled):
    length = rows.shape[1]
    rows_kept = rows * keep
    parts = []
    for shift in range(9):
        item = rows_kept * cycle(rows, shift)
        parts.append(item * group_scale(shift) if scaled else item)
    parts.append(rows_kept * 0.25 if scaled else rows_kept)
    first_row = lax.broadcasted_iota(jnp.int32, (16, length), 0) == 0
    parts.append(jnp.where(first_row, jnp.broadcast_to(keep, (16, length)), 0.0))
    return jnp.concatenate(parts, axis=0).astype(jnp.bfloat16)


def features_back(rows, grad, scaled):
    total = grad[144:160] * 0.25 if scaled else grad[144:160]
    for shift in range(9):
        item = grad[16 * shift : 16 * shift + 16]
        if scaled:
            item = item * group_scale(shift)
        total = total + item * cycle(rows, shift) + cycle(item * rows, (16 - shift) % 16)
    return total


def later_by(rows, offset, before):
    lane = lax.broadcasted_iota(jnp.int32, rows.shape, 1)
    moved = pltpu.roll(rows, offset, 1)
    if offset == 1:
        return jnp.where(lane == 0, before[:, 1:2], moved)
    return jnp.where(lane == 0, before[:, 0:1], jnp.where(lane == 1, before[:, 1:2], moved))


def sooner_by(rows, offset, after):
    length = rows.shape[1]
    lane = lax.broadcasted_iota(jnp.int32, rows.shape, 1)
    moved = pltpu.roll(rows, length - offset, 1)
    if offset == 1:
        return jnp.where(lane == length - 1, after[:, 0:1], moved)
    return jnp.where(
        lane == length - 2,
        after[:, 0:1],
        jnp.where(lane == length - 1, after[:, 1:2], moved),
    )


def conv_forward(signal, before, taps, same):
    total = taps[:, 0:1] * signal
    for offset in (1, 2):
        total = total + taps[:, offset : offset + 1] * later_by(signal, offset, before) * same[offset - 1]
    return total


def conv_backward(grad, after, taps, same):
    total = taps[:, 0:1] * grad
    for offset in (1, 2):
        total = total + taps[:, offset : offset + 1] * sooner_by(grad, offset, after) * same[offset - 1]
    return total


def add_ones(values):
    length = values.shape[1]
    row = lax.broadcasted_iota(jnp.int32, (VROWS - DV, length), 0)
    return jnp.concatenate(
        [values, jnp.where(row == 0, 1.0, 0.0).astype(jnp.bfloat16)], axis=0
    )


def weights_of(keys, queries, mask):
    shifted = dot_tn(keys, queries) + 1.0
    return shifted, (0.5 * shifted * shifted + 0.5) * mask


def mix_forward(tokens, before_tokens, taps, doc_row, prev_docs, mask_ref):
    length = tokens.shape[0]
    block = tokens.astype(jnp.float32).T.astype(jnp.bfloat16)
    before = before_tokens.astype(jnp.float32).T[2 * FEATURE_SIZE : 2 * FEATURE_SIZE + DV, 14:16]
    values, _, _, _ = values_of(block, before, taps, doc_row, prev_docs)
    marked = add_ones(values)
    keep_last = (doc_row == doc_row[:, length - 1 : length]).astype(jnp.float32)
    key_feats = features(block[16:32].astype(jnp.float32), keep_last, False)
    state = dot_nt(key_feats, marked)
    scaled_q = (block[0:16].astype(jnp.float32) * 0.25).astype(jnp.bfloat16)
    sums = []
    for start in range(0, length, TBLOCK):
        stop = start + TBLOCK
        _, weights = weights_of(
            block[16:32, :stop], scaled_q[:, start:stop], mask_ref[:stop, start:stop]
        )
        sums.append(dot_nn(marked[:, :stop], weights.astype(jnp.bfloat16)))
    return block, marked, jnp.concatenate(sums, axis=1), state


def values_of(block, before, taps, doc_row, prev_docs):
    length = block.shape[1]
    doc8 = jnp.broadcast_to(doc_row, (8, length))
    prev8 = jnp.broadcast_to(prev_docs, (8, 2))
    same = [
        (doc8 == later_by(doc8, offset, prev8)).astype(jnp.float32)[0:1] for offset in (1, 2)
    ]
    conv_in = block[32 : 32 + DV].astype(jnp.float32)
    gate_in = block[32 + DV :].astype(jnp.float32)
    conv_out = conv_forward(conv_in, before, taps, same)
    sigmoid = 1.0 / (1.0 + jnp.exp(-gate_in))
    values = (gate_in * sigmoid * conv_out).astype(jnp.bfloat16)
    return values, conv_out, gate_in, sigmoid


def fill_mask(mask_ref, doc_row, doc_col):
    shape = mask_ref.shape
    causal = lax.broadcasted_iota(jnp.int32, shape, 0) <= lax.broadcasted_iota(jnp.int32, shape, 1)
    mask_ref[...] = jnp.where(causal & (doc_col == doc_row), 1.0, 0.0)


def f1_kernel(p_ref, halo_ref, taps_ref, row_ref, col_ref, prev_ref, pt_ref, v_ref, o_ref, l_ref, mask_ref):
    @pl.when(pl.program_id(0) == 0)
    def _():
        fill_mask(mask_ref, row_ref[...], col_ref[...])

    block, marked, sums, state = mix_forward(
        p_ref[...], halo_ref[...], taps_ref[0], row_ref[...], prev_ref[:, 0:2], mask_ref
    )
    pt_ref[...] = block
    v_ref[...] = marked
    o_ref[...] = sums
    l_ref[...] = state.astype(jnp.bfloat16)


def mix_finish(block, sums, carry, doc_row):
    keep_first = (doc_row == doc_row[:, 0:1]).astype(jnp.float32)
    query_feats = features(block[0:16].astype(jnp.float32), keep_first, True)
    total = sums + dot_tn(carry, query_feats)
    denominator = total[DV : DV + 1]
    return (total[:DV] / denominator).astype(jnp.bfloat16), denominator


def f2_kernel(pt_ref, o_ref, s_ref, row_ref, att_ref, den_ref):
    attended, denominator = mix_finish(pt_ref[...], o_ref[...], s_ref[...], row_ref[...])
    att_ref[...] = attended
    den_ref[...] = jnp.broadcast_to(denominator, den_ref.shape)


def sum_grads(grad, attended, denominator):
    length = grad.shape[1]
    inverse = 1.0 / denominator
    grad_f = grad.astype(jnp.float32)
    dot_term = jnp.sum(grad_f * attended.astype(jnp.float32), axis=0, keepdims=True)
    row = lax.broadcasted_iota(jnp.int32, (VROWS - DV, length), 0)
    tail = jnp.where(row == 0, jnp.broadcast_to(-dot_term * inverse, row.shape), 0.0)
    return jnp.concatenate([grad_f * inverse, tail], axis=0).astype(jnp.bfloat16)


def mix_back_local(block, marked, sums_grad, carry, doc_row, mask_ref):
    length = block.shape[1]
    keys = block[16:32]
    queries = block[0:16].astype(jnp.float32)
    scaled_q = (queries * 0.25).astype(jnp.bfloat16)
    keep_first = (doc_row == doc_row[:, 0:1]).astype(jnp.float32)
    query_grad = features_back(queries, dot_nn(carry, sums_grad) * keep_first, True)
    key_grad = jnp.zeros((16, length), jnp.float32)
    value_grad = jnp.zeros((VROWS, length), jnp.float32)
    parts = []
    for start in range(0, length, TBLOCK):
        stop = start + TBLOCK
        mask = mask_ref[:stop, start:stop]
        shifted, weights = weights_of(keys[:, :stop], scaled_q[:, start:stop], mask)
        grad_block = sums_grad[:, start:stop]
        weight_grad = dot_tn(marked[:, :stop], grad_block)
        score_grad = (weight_grad * shifted * mask).astype(jnp.bfloat16)
        parts.append(dot_nn(keys[:, :stop], score_grad) * 0.25)
        key_part = dot_nt(scaled_q[:, start:stop], score_grad)
        value_part = dot_nt(grad_block, weights.astype(jnp.bfloat16))
        if stop < length:
            key_part = jnp.concatenate(
                [key_part, jnp.zeros((16, length - stop), jnp.float32)], axis=1
            )
            value_part = jnp.concatenate(
                [value_part, jnp.zeros((VROWS, length - stop), jnp.float32)], axis=1
            )
        key_grad = key_grad + key_part
        value_grad = value_grad + value_part
    query_grad = query_grad + jnp.concatenate(parts, axis=1)
    return query_grad, key_grad, value_grad


def b1_kernel(pt_ref, v_ref, g_ref, att_ref, den_ref, s_ref, row_ref, col_ref, d_ref, dq_ref, dk_ref, dv_ref, mask_ref):
    @pl.when(pl.program_id(0) == 0)
    def _():
        fill_mask(mask_ref, row_ref[...], col_ref[...])

    doc_row = row_ref[...]
    block = pt_ref[...]
    sums_grad = sum_grads(g_ref[...], att_ref[...], den_ref[0:1])
    keep_first = (doc_row == doc_row[:, 0:1]).astype(jnp.float32)
    query_feats = features(block[0:16].astype(jnp.float32), keep_first, True)
    d_ref[...] = dot_nt(query_feats, sums_grad).astype(jnp.bfloat16)
    dq, dk, dv = mix_back_local(block, v_ref[...], sums_grad, s_ref[...], doc_row, mask_ref)
    dq_ref[...] = dq
    dk_ref[...] = dk
    dv_ref[...] = dv


def mix_back_finish(block, marked, later_state, key_grad, value_grad, doc_row, before, taps, prev_docs):
    length = block.shape[1]
    keep_last = (doc_row == doc_row[:, length - 1 : length]).astype(jnp.float32)
    keys = block[16:32].astype(jnp.float32)
    key_feats = features(keys, keep_last, False)
    key_grad = key_grad + features_back(keys, dot_nn(later_state, marked) * keep_last, False)
    value_grad = (value_grad + dot_tn(later_state, key_feats))[:DV]
    _, conv_out, gate_in, sigmoid = values_of(block, before, taps, doc_row, prev_docs)
    gate_grad = value_grad * conv_out * sigmoid * (1.0 + gate_in * (1.0 - sigmoid))
    conv_grad = value_grad * gate_in * sigmoid
    return key_grad, gate_grad, conv_grad


def b2_kernel(pt_ref, v_ref, g_ref, dq_ref, dk_ref, dv_ref, halo_ref, taps_ref, row_ref, prev_ref, dp_ref, first_ref, tail_ref):
    doc_row = row_ref[...]
    length = doc_row.shape[1]
    taps = taps_ref[0]
    before = halo_ref[...].astype(jnp.float32).T[2 * FEATURE_SIZE : 2 * FEATURE_SIZE + DV, 14:16]
    key_grad, gate_grad, conv_grad = mix_back_finish(
        pt_ref[...], v_ref[...], g_ref[...], dk_ref[...], dv_ref[...], doc_row, before, taps, prev_ref[:, 0:2]
    )
    doc8 = jnp.broadcast_to(doc_row, (8, length))
    none = jnp.full((8, 2), -1.0, jnp.float32)
    same = [(doc8 == sooner_by(doc8, offset, none)).astype(jnp.float32)[0:1] for offset in (1, 2)]
    conv_in_grad = conv_backward(conv_grad, jnp.zeros((DV, 2), jnp.float32), taps, same)
    whole = jnp.concatenate([dq_ref[...], key_grad, conv_in_grad, gate_grad], axis=0).T
    dp_ref[...] = whole.astype(jnp.bfloat16)
    tail_ref[...] = whole[length - 16 :]
    pad = jnp.zeros((16, length), jnp.float32)
    conv_tokens = jnp.concatenate([jnp.zeros((32, length), jnp.float32), conv_grad, jnp.zeros((DV, length), jnp.float32)], axis=0).T
    first_ref[...] = conv_tokens[0:16]


MESH = pl.DeviceIdType.MESH
TILE = 256
GROUPS = 4


class Gather:
    kinds = 8

    def __init__(self, shards, wholes, sends, lands):
        self.shards, self.wholes = shards, wholes
        self.sends, self.lands = sends, lands
        i = lax.axis_index("fsdp")
        z = lax.axis_index("seq")
        odd = z % 2
        self.odd = odd
        by_y = 4 - 8 * (i // 4)
        by_x = 2 - 4 * ((i // 2) % 2)
        by_core = 1 - 2 * (i % 2)
        self.slot = [i, i + by_y, i + by_x + odd * by_y, i + by_x + (1 - odd) * by_y, i + by_core]
        self.near = [
            {"fsdp": i + by_y, "seq": z},
            {"fsdp": i + by_x, "seq": z},
            {"fsdp": i, "seq": z + 1 - 2 * odd},
            {"fsdp": i + by_core, "seq": z},
        ]

    def part(self, piece, slot):
        _, which, start, size = piece
        rows = self.shards[which].shape[0]
        return self.wholes[which].at[
            pl.ds(pl.multiple_of(slot * rows, 32), rows), pl.ds(start, size)
        ]

    def own_part(self, piece):
        _, which, start, size = piece
        return self.shards[which].at[:, pl.ds(start, size)]

    def copy(self, kind, piece, relay=False):
        source = [0, 0, 2, 0, 1, 2, 3, 4][kind]
        if relay:
            source = 1
        slot = self.slot[source]
        return pltpu.make_async_remote_copy(
            src_ref=self.own_part(piece) if source == 0 else self.part(piece, slot),
            dst_ref=self.part(piece, slot),
            send_sem=self.sends.at[kind, piece[0]],
            recv_sem=self.lands.at[kind, piece[0]],
            device_id=self.near[min(kind, 3)],
            device_id_type=MESH,
        )

    def first(self, piece):
        self.copy(0, piece).start()

        @pl.when(self.odd == 0)
        def _():
            self.copy(1, piece).start()

        self.copy(3, piece).start()

    def from_y(self, piece):
        self.copy(0, piece).wait_recv()

        @pl.when(self.odd == 1)
        def _():
            self.copy(1, piece, relay=True).start()

        self.copy(4, piece).start()
        self.copy(3, piece).wait_recv()
        self.copy(7, piece).start()

    def from_x(self, piece):
        self.copy(1, piece).wait_recv()
        self.copy(2, piece).start()
        self.copy(5, piece).start()

    def from_z(self, piece):
        self.copy(2, piece).wait_recv()
        self.copy(6, piece).start()

    def ready(self, piece):
        for kind in (4, 5, 6, 7):
            self.copy(kind, piece).wait_recv()

    def finish(self, piece):
        for kind in range(self.kinds):
            self.copy(kind, piece).wait_send()


def cuts(which, width, size):
    return [(which, at, min(size, width - at)) for at in range(0, width, size)]


def by_rows(length, body, rows=64):
    def step(n, _):
        body(pl.ds(pl.multiple_of(n * rows, rows), rows))
        return 0

    lax.fori_loop(0, length // rows, step, 0)


def row_root(value):
    return lax.rsqrt(jnp.mean(value * value, -1, keepdims=True) + epsilon)


def m_kernel(
    x, g, gain1, gain2, taps, doc_row_ref, doc_col_ref, in_down, up_maps, out_down, out_up, gu_down, gu_up, ffd_down, ffd_up,
    a_in, b_in, c_in, d_in,
    a_all, b_all, c_all, d_all,
    out, blocks, marked, att_t, dens, carry, attended, resid_grad, hidden1, rank_in, rank_out, halo, term_ff, term_w,
    halo_send, mask, sums, state, message, resid, hidden2, out_acc, grad_acc, a_tile, b_tile, g_tile, u_tile, d_tile, rank_acc,
    sends, lands, halo_sems, chain_sems, load_sems,
):
    length, width = x.shape
    ff = d_all.shape[0]
    tiles = ff // TILE
    f32, bf16 = jnp.float32, jnp.bfloat16
    place = lax.axis_index("seq")
    planes = lax.axis_size("seq")
    me = lax.axis_index("fsdp")
    job = Gather([a_in, b_in, c_in, d_in], [a_all, b_all, c_all, d_all], sends, lands)

    early = cuts(0, a_in.shape[1], 512) + cuts(1, b_in.shape[1], 896) + cuts(3, d_in.shape[1], 256)
    early = [(number,) + piece for number, piece in enumerate(early)]
    base = len(early)
    mix_pieces = [p for p in early if p[1] == 0]
    out_pieces = [p for p in early if p[1] == 1]
    down_pieces = [p for p in early if p[1] == 3]
    total = base + 2 * tiles

    def late(number):
        at = number - base
        start = (at // 2) * TILE + (at % 2) * ff
        return (number, 2, pl.multiple_of(start, TILE), TILE)

    def piece_at(number):
        return early[number] if number < base else late(number)

    def pump(number):
        job.from_y(piece_at(number))
        if number >= 1:
            job.from_x(piece_at(number - 1))
        if number >= 2:
            job.from_z(piece_at(number - 2))

    barrier = pltpu.get_barrier_semaphore()
    for device in (job.near[0], job.near[1], job.near[3]):
        pl.semaphore_signal(barrier, inc=1, device_id=device, device_id_type=MESH)
    before = {"fsdp": me, "seq": (place + planes - 1) % planes}
    after = {"fsdp": me, "seq": (place + 1) % planes}

    @pl.when(place > 0)
    def _():
        pl.semaphore_signal(barrier, inc=1, device_id=before, device_id_type=MESH)

    @pl.when(place < planes - 1)
    def _():
        pl.semaphore_signal(barrier, inc=1, device_id=after, device_id_type=MESH)

    inner = (place > 0) & (place < planes - 1)

    @pl.when(inner)
    def _():
        pl.semaphore_wait(barrier, 5)

    @pl.when(jnp.logical_not(inner))
    def _():
        pl.semaphore_wait(barrier, 4)

    for piece in early:
        job.first(piece)

    def first_late(number, _):
        job.first(late(number))
        return 0

    lax.fori_loop(base, total, first_late, 0)

    def norm1(rows):
        value = x[rows, :].astype(f32)
        hidden1[rows, :] = (value * row_root(value) * gain1[...]).astype(bf16)

    by_rows(length, norm1)
    rank_in[...] = dot_nt(hidden1[...], in_down[...]).astype(bf16)
    doc_row = doc_row_ref[...]
    fill_mask(mask, doc_row, doc_col_ref[...])
    cond_whole = (doc_row[:, 0:1] == doc_row[:, length - 1 : length]).astype(f32)

    pump(0)
    pump(1)
    for number, piece in enumerate(mix_pieces):
        if number + 2 < len(mix_pieces):
            pump(number + 2)
        elif number + 1 < len(mix_pieces):
            job.from_x(mix_pieces[number + 1])
            job.from_z(mix_pieces[number])
        else:
            job.from_z(mix_pieces[number])
        job.ready(piece)
        _, _, start, size = piece
        load = pltpu.make_async_copy(a_all.at[:, pl.ds(start, size)], a_tile, load_sems.at[0])
        load.start()
        load.wait()
        projected = dot_nn(hidden1[...], a_tile[...]) + dot_nn(rank_in[...], up_maps[:, start : start + size])
        halo_send[:, start : start + size] = projected[length - 16 :].astype(bf16)
        for at in range(0, size, PER_HEAD):
            blocks[start + at : start + at + PER_HEAD, :] = projected[:, at : at + PER_HEAD].T.astype(bf16)
    columns = HEAD_COUNT * PER_HEAD
    halo_send[:, columns:] = jnp.broadcast_to(
        doc_col_ref[length - 16 :, :], (16, 128)
    ).astype(bf16)
    to_next = pltpu.make_async_remote_copy(
        src_ref=halo_send, dst_ref=halo, send_sem=halo_sems.at[0], recv_sem=halo_sems.at[1], device_id=after, device_id_type=MESH
    )

    @pl.when(place < planes - 1)
    def _():
        to_next.start()

    @pl.when(place == 0)
    def _():
        halo[:, :columns] = jnp.zeros((16, columns), bf16)
        halo[:, columns:] = jnp.full((16, 128), -1.0, bf16)

    def pump_rest(number):
        job.from_y(piece_at(number))
        if number - 1 >= len(mix_pieces):
            job.from_x(piece_at(number - 1))
        if number - 2 >= len(mix_pieces):
            job.from_z(piece_at(number - 2))

    next_piece = len(mix_pieces)
    pump_rest(next_piece)
    next_piece += 1

    @pl.when(place > 0)
    def _():
        to_next.wait_recv()

    prev_docs = halo[:, columns:].astype(f32).T[0:1, 14:16]
    cond_before = (prev_docs[:, 1:2] == doc_row[:, 0:1]).astype(f32)
    keep_last = (doc_row == doc_row[:, length - 1 : length]).astype(f32)

    def head_state(h, _):
        at = pl.multiple_of(h * PER_HEAD, PER_HEAD)
        block = blocks[pl.ds(at, PER_HEAD), :]
        prior = halo[:, pl.ds(at, PER_HEAD)].astype(f32).T[32 : 32 + DV, 14:16]
        values, _, _, _ = values_of(block, prior, taps[h], doc_row, prev_docs)
        ones = add_ones(values)
        marked[pl.ds(pl.multiple_of(h * VROWS, VROWS), VROWS), :] = ones
        key_feats = features(block[16:32].astype(f32), keep_last, False)
        state[pl.ds(pl.multiple_of(h * FEATS, 16), FEATS), :] = dot_nt(key_feats, ones).astype(bf16)
        return 0

    lax.fori_loop(0, HEAD_COUNT, head_state, 0)
    group = HEAD_COUNT // GROUPS
    span = group * FEATS

    def hand_on(number):
        part = pl.ds(number * span, span)
        return pltpu.make_async_remote_copy(
            src_ref=message.at[part], dst_ref=carry.at[part],
            send_sem=chain_sems.at[0, number], recv_sem=chain_sems.at[1, number], device_id=after, device_id_type=MESH,
        )

    @pl.when(place == 0)
    def _():
        carry[...] = jnp.zeros(carry.shape, bf16)

    def head_local(h, _):
        at = pl.multiple_of(h * PER_HEAD, PER_HEAD)
        keys = blocks[pl.ds(at + 16, 16), :]
        scaled_q = (blocks[pl.ds(at, 16), :].astype(f32) * 0.25).astype(bf16)
        rows = pl.multiple_of(h * VROWS, VROWS)
        ones = marked[pl.ds(rows, VROWS), :]
        for start in range(0, length, TBLOCK):
            stop = start + TBLOCK
            _, weights = weights_of(keys[:, :stop], scaled_q[:, start:stop], mask[:stop, start:stop])
            sums[pl.ds(rows, VROWS), start:stop] = dot_nn(ones[:, :stop], weights.astype(bf16))
        return 0

    for number in range(GROUPS):
        part = pl.ds(number * span, span)

        @pl.when(place > 0)
        def _():
            hand_on(number).wait_recv()

        message[part, :] = (
            state[part, :].astype(f32) + (cond_whole * cond_before) * carry[part, :].astype(f32)
        ).astype(bf16)

        @pl.when(place < planes - 1)
        def _():
            hand_on(number).start()

        lax.fori_loop(number * group, (number + 1) * group, head_local, 0)
        pump_rest(next_piece)
        next_piece += 1

    keep_first = (doc_row == doc_row[:, 0:1]).astype(f32) * cond_before

    def head_finish(h, _):
        at = pl.multiple_of(h * PER_HEAD, PER_HEAD)
        rows = pl.multiple_of(h * VROWS, VROWS)
        query_feats = features(blocks[pl.ds(at, 16), :].astype(f32), keep_first, True)
        both = sums[pl.ds(rows, VROWS), :] + dot_tn(carry[pl.ds(pl.multiple_of(h * FEATS, 16), FEATS), :], query_feats)
        denominator = both[DV : DV + 1]
        att_t[pl.ds(pl.multiple_of(h * DV, 16), DV), :] = (both[:DV] / denominator).astype(bf16)
        dens[pl.ds(pl.multiple_of(h * 8, 8), 8), :] = jnp.broadcast_to(denominator, (8, length))
        return 0

    lax.fori_loop(0, HEAD_COUNT, head_finish, 0)

    def turn(n, _):
        rows = pl.ds(pl.multiple_of(n * 128, 128), 128)
        attended[:, rows] = att_t[rows, :].astype(f32).T.astype(bf16)
        return 0

    lax.fori_loop(0, width // 128, turn, 0)
    pump_rest(next_piece)
    next_piece += 1

    rank_out[...] = dot_nt(attended[...], out_down[...]).astype(bf16)
    for piece in out_pieces:
        job.ready(piece)
        _, _, start, size = piece
        load = pltpu.make_async_copy(b_all.at[:, pl.ds(start, size)], b_tile, load_sems.at[0])
        load.start()
        load.wait()
        resid[:, start : start + size] = (
            x[:, start : start + size].astype(f32)
            + dot_nn(attended[...], b_tile[...])
            + dot_nn(rank_out[...], out_up[:, start : start + size])
        )
    pump_rest(next_piece)
    next_piece += 1

    def norm2(rows):
        value = resid[rows, :]
        hidden2[rows, :] = (value * row_root(value) * gain2[...]).astype(bf16)
        out_acc[rows, :] = value
        grad_acc[rows, :] = jnp.zeros(value.shape, f32)

    by_rows(length, norm2)
    rank_gate = dot_nt(hidden2[...], gu_down[0:16, :]).astype(bf16)
    rank_up = dot_nt(hidden2[...], gu_down[16:32, :]).astype(bf16)
    rank_ffd_grad = dot_nt(g[...], ffd_up[...]).astype(bf16)
    rank_gate_t = rank_gate.astype(f32).T.astype(bf16)
    rank_up_t = rank_up.astype(f32).T.astype(bf16)
    rank_ffd_grad_t = rank_ffd_grad.astype(f32).T.astype(bf16)
    rank_acc[...] = jnp.zeros(rank_acc.shape, f32)
    while next_piece < base + 4:
        pump_rest(next_piece)
        next_piece += 1
    for piece in down_pieces:
        job.ready(piece)

    def loads(tile):
        slot = tile % 2
        start = pl.multiple_of(tile * TILE, TILE)
        return [
            pltpu.make_async_copy(c_all.at[:, pl.ds(start, TILE)], g_tile.at[slot], load_sems.at[2 * 0 + slot]),
            pltpu.make_async_copy(c_all.at[:, pl.ds(pl.multiple_of(ff + start, TILE), TILE)], u_tile.at[slot], load_sems.at[2 + slot]),
            pltpu.make_async_copy(d_all.at[pl.ds(start, TILE), :], d_tile.at[slot], load_sems.at[4 + slot]),
        ]

    def hidden_tile(tile):
        slot = tile % 2
        cols = pl.ds(pl.multiple_of(tile * TILE, TILE), TILE)
        gate_w, up_w, down_w = g_tile[slot], u_tile[slot], d_tile[slot]
        gate_map, up_map, down_map = gu_up[0:16, cols], gu_up[16:32, cols], ffd_down[:, cols]
        gate_pre = dot_nn(hidden2[...], gate_w) + dot_nn(rank_gate, gate_map)
        up_pre = dot_nn(hidden2[...], up_w) + dot_nn(rank_up, up_map)
        inner_grad = dot_nt(g[...], down_w) + dot_nn(rank_ffd_grad, down_map)
        sigmoid = 1.0 / (1.0 + jnp.exp(-gate_pre))
        gate_val = gate_pre * sigmoid
        inner = (gate_val * up_pre).astype(bf16)
        gate_grad = (inner_grad * up_pre * (sigmoid * (1.0 + gate_pre * (1.0 - sigmoid)))).astype(bf16)
        up_grad = (inner_grad * gate_val).astype(bf16)
        out_acc[...] += dot_nn(inner, down_w)
        grad_acc[...] += dot_nt(gate_grad, gate_w) + dot_nt(up_grad, up_w)
        rank_acc[0] += dot_nt(inner, down_map)
        rank_acc[1] += dot_nt(gate_grad, gate_map)
        rank_acc[2] += dot_nt(up_grad, up_map)
        term_ff[0:16, cols] = dot_nn(rank_gate_t, gate_grad)
        term_ff[16:32, cols] = dot_nn(rank_up_t, up_grad)
        term_ff[32:48, cols] = dot_nn(rank_ffd_grad_t, inner)

    def ff_step(tile, _):
        for extra in (4, 5):
            number = base + 2 * tile + extra

            @pl.when(number < total)
            def _():
                job.from_y(late(number))

            @pl.when(number - 1 < total)
            def _():
                job.from_x(late(number - 1))

            @pl.when(number - 2 < total)
            def _():
                job.from_z(late(number - 2))

        @pl.when(tile < tiles)
        def _():
            job.ready(late(base + 2 * tile))
            job.ready(late(base + 2 * tile + 1))
            for load in loads(tile):
                load.start()

        @pl.when(tile >= 1)
        def _():
            for load in loads(tile - 1):
                load.wait()
            hidden_tile(tile - 1)

        return 0

    lax.fori_loop(0, tiles + 1, ff_step, 0)

    rank_ffd = rank_acc[0].astype(bf16)
    rank_gate_grad = rank_acc[1].astype(bf16)
    rank_up_grad = rank_acc[2].astype(bf16)
    out_acc[...] += dot_nn(rank_ffd, ffd_up[...])
    grad_acc[...] += dot_nn(rank_gate_grad, gu_down[0:16, :]) + dot_nn(rank_up_grad, gu_down[16:32, :])
    term_w[0:16, :] = dot_tn(rank_gate_grad, hidden2[...])
    term_w[16:32, :] = dot_tn(rank_up_grad, hidden2[...])
    term_w[32:48, :] = dot_tn(rank_ffd, g[...])

    def finish_rows(rows):
        out[rows, :] = out_acc[rows, :].astype(bf16)
        value = resid[rows, :]
        root = row_root(value)
        normed = value * root
        scaled = grad_acc[rows, :] * gain2[...]
        resid_grad[rows, :] = g[rows, :].astype(f32) + root * (
            scaled - normed * jnp.mean(scaled * normed, -1, keepdims=True)
        )

    by_rows(length, finish_rows)

    for piece in early:
        job.finish(piece)

    def finish_late(number, _):
        job.finish(late(number))
        return 0

    lax.fori_loop(base, total, finish_late, 0)

    @pl.when(place < planes - 1)
    def _():
        to_next.wait_send()
        for number in range(GROUPS):
            hand_on(number).wait_send()


def call_m(x, g, gain1, gain2, taps, doc_row, doc_col, maps, shards):
    length, width = x.shape
    f32, bf16 = jnp.float32, jnp.bfloat16
    count = lax.axis_size("fsdp")
    a, b, c, d = shards
    ff = d.shape[0] * count
    columns = a.shape[1]
    tiles = ff // TILE
    pieces = len(cuts(0, columns, 512) + cuts(1, width, 896) + cuts(3, width, 256)) + 2 * tiles
    whole = pl.BlockSpec(memory_space=pltpu.VMEM)
    anyplace = pl.BlockSpec(memory_space=pl.ANY)
    vmem_out = [
        ((length, width), bf16),
        ((columns, length), bf16),
        ((HEAD_COUNT * VROWS, length), bf16),
        ((width, length), bf16),
        ((HEAD_COUNT * 8, length), f32),
        ((HEAD_COUNT * FEATS, VROWS), bf16),
        ((length, width), bf16),
        ((length, width), f32),
        ((length, width), bf16),
        ((length, 64), bf16),
        ((length, 16), bf16),
        ((16, columns + 128), bf16),
        ((48, ff), f32),
        ((48, width), f32),
    ]
    args = (x, g, gain1, gain2, taps, doc_row, doc_col) + tuple(maps)
    return pl.pallas_call(
        m_kernel,
        in_specs=[whole] * len(args) + [anyplace] * 4,
        out_specs=[anyplace] * 4 + [whole] * len(vmem_out),
        out_shape=[jax.ShapeDtypeStruct((t.shape[0] * count, t.shape[1]), t.dtype) for t in shards]
        + [jax.ShapeDtypeStruct(s, t) for s, t in vmem_out],
        scratch_shapes=[
            pltpu.VMEM((16, columns + 128), bf16),
            pltpu.VMEM((length, length), f32),
            pltpu.VMEM((HEAD_COUNT * VROWS, length), f32),
            pltpu.VMEM((HEAD_COUNT * FEATS, VROWS), bf16),
            pltpu.VMEM((HEAD_COUNT * FEATS, VROWS), bf16),
            pltpu.VMEM((length, width), f32),
            pltpu.VMEM((length, width), bf16),
            pltpu.VMEM((length, width), f32),
            pltpu.VMEM((length, width), f32),
            pltpu.VMEM((width, 512), bf16),
            pltpu.VMEM((width, 896), bf16),
            pltpu.VMEM((2, width, TILE), bf16),
            pltpu.VMEM((2, width, TILE), bf16),
            pltpu.VMEM((2, TILE, width), bf16),
            pltpu.VMEM((3, length, 16), f32),
            pltpu.SemaphoreType.DMA((8, pieces)),
            pltpu.SemaphoreType.DMA((8, pieces)),
            pltpu.SemaphoreType.DMA((2,)),
            pltpu.SemaphoreType.DMA((2, GROUPS)),
            pltpu.SemaphoreType.DMA((6,)),
        ],
        compiler_params=pltpu.CompilerParams(
            collective_id=1, has_side_effects=True, vmem_limit_bytes=62 * 1024 * 1024
        ),
    )(*args, *shards)


def call_heads(kernel, length, ins, outs, scratch=()):
    def spec(shape, how):
        if how == "rows":
            return pl.BlockSpec((shape[0] // HEAD_COUNT,) + shape[1:], lambda h: (h,) + (0,) * (len(shape) - 1))
        if how == "cols":
            return pl.BlockSpec((shape[0], shape[1] // HEAD_COUNT), lambda h: (0, h))
        return pl.BlockSpec(shape, lambda h: (0,) * len(shape))

    return pl.pallas_call(
        kernel,
        grid=(HEAD_COUNT,),
        in_specs=[spec(a.shape, how) for a, how in ins],
        out_specs=[spec(s.shape, how) for s, how in outs],
        out_shape=[s for s, _ in outs],
        scratch_shapes=list(scratch),
        compiler_params=pltpu.CompilerParams(vmem_limit_bytes=48 * 1024 * 1024),
    )(*[a for a, _ in ins])


def shift_pairs(count, step):
    return [(i, i + step) for i in range(count) if 0 <= i + step < count]


def chain(own, whole, link, step):
    count = lax.axis_size("seq")
    pairs = shift_pairs(count, step)
    message = own
    for _ in range(count - 2):
        got = lax.ppermute(message, "seq", pairs)
        message = (own.astype(jnp.float32) + (whole * link) * got.astype(jnp.float32)).astype(jnp.bfloat16)
    got = lax.ppermute(message, "seq", pairs)
    return (got.astype(jnp.float32) * link).astype(jnp.bfloat16)


def product(spec, left, right):
    return jnp.einsum(spec, left, right, preferred_element_type=jnp.float32)


def rms_forward(value, gain):
    inv_root = lax.rsqrt(jnp.mean(value * value, -1, keepdims=True) + epsilon)
    normed = value * inv_root
    return (normed, inv_root, (normed * gain).astype(jnp.bfloat16))


def rms_backward(grad_hidden, normed, inv_root, gain):
    scaled = grad_hidden * gain
    return inv_root * (scaled - normed * jnp.mean(scaled * normed, -1, keepdims=True))


def up_by_head(querykey, valuegate):
    parts = [
        (querykey[0], 0, FEATURE_SIZE),
        (querykey[1], FEATURE_SIZE, FEATURE_SIZE),
        (valuegate[0], 2 * FEATURE_SIZE, DV),
        (valuegate[1], 2 * FEATURE_SIZE + DV, DV),
    ]
    rows = [
        jnp.pad(
            part.reshape(ADAPTER_RANK, HEAD_COUNT, size),
            ((0, 0), (0, 0), (at, PER_HEAD - at - size)),
        )
        for part, at, size in parts
    ]
    return jnp.concatenate(rows, axis=0).reshape(4 * ADAPTER_RANK, HEAD_COUNT * PER_HEAD)


def front_by_collectives(x, grad_out, gain1, gain2, taps, docs, doc_col, prev_pad, link_before, whole, maps, shards):
    bf16, f32 = jnp.bfloat16, jnp.float32
    in_down, up_maps, out_down, out_up, gu_down, gu_up, ffd_down, ffd_up = maps
    seq_count = lax.axis_size("seq")
    length = x.shape[0]
    mixer_in, mixer_out, gate_up, down_w = [
        lax.all_gather(shard, "fsdp", axis=0, tiled=True) for shard in shards
    ]
    ff = down_w.shape[0]
    inputs_f = x.astype(f32)
    normed1, root1, hidden1 = rms_forward(inputs_f, gain1)
    rank_in = product("td,rd->tr", hidden1, in_down).astype(bf16)
    projected = (
        product("td,de->te", hidden1, mixer_in) + product("tr,re->te", rank_in, up_maps)
    ).astype(bf16)
    halo = lax.ppermute(projected[length - 16 :], "seq", shift_pairs(seq_count, 1))
    mask = pltpu.VMEM((length, length), f32)
    heads = HEAD_COUNT
    blocks, values, sums, state = call_heads(
        f1_kernel,
        length,
        [(projected, "cols"), (halo, "cols"), (taps, "rows"), (docs, None), (doc_col, None), (prev_pad, None)],
        [
            (jax.ShapeDtypeStruct((heads * PER_HEAD, length), bf16), "rows"),
            (jax.ShapeDtypeStruct((heads * VROWS, length), bf16), "rows"),
            (jax.ShapeDtypeStruct((heads * VROWS, length), f32), "rows"),
            (jax.ShapeDtypeStruct((heads * FEATS, VROWS), bf16), "rows"),
        ],
        [mask],
    )
    carry = chain(state, whole, link_before, 1)
    attended_t, denominator = call_heads(
        f2_kernel,
        length,
        [(blocks, "rows"), (sums, "rows"), (carry, "rows"), (docs, None)],
        [
            (jax.ShapeDtypeStruct((heads * DV, length), bf16), "rows"),
            (jax.ShapeDtypeStruct((heads * 8, length), f32), "rows"),
        ],
    )
    attended = attended_t.T
    rank_out = product("td,rd->tr", attended, out_down).astype(bf16)
    resid = (
        inputs_f
        + product("td,de->te", attended, mixer_out)
        + product("tr,re->te", rank_out, out_up)
    )
    normed2, root2, hidden2 = rms_forward(resid, gain2)
    rank_mlp = product("td,rd->tr", hidden2, gu_down).astype(bf16)
    rank_ffd_grad = product("te,re->tr", grad_out, ffd_up).astype(bf16)
    inner_grad = product("te,fe->tf", grad_out, down_w) + product("tr,rf->tf", rank_ffd_grad, ffd_down)
    gate_pre = product("td,de->te", hidden2, gate_up[:, :ff]) + product(
        "tr,re->te", rank_mlp[:, :ADAPTER_RANK], gu_up[:ADAPTER_RANK]
    )
    up_pre = product("td,de->te", hidden2, gate_up[:, ff:]) + product(
        "tr,re->te", rank_mlp[:, ADAPTER_RANK:], gu_up[ADAPTER_RANK:]
    )
    sigmoid = jax.nn.sigmoid(gate_pre)
    gate_val = gate_pre * sigmoid
    inner_act = (gate_val * up_pre).astype(bf16)
    gate_grad = (inner_grad * up_pre * (sigmoid * (1.0 + gate_pre * (1.0 - sigmoid)))).astype(bf16)
    up_grad = (inner_grad * gate_val).astype(bf16)
    rank_ffd = product("tf,rf->tr", inner_act, ffd_down).astype(bf16)
    output = (
        resid + product("tf,fe->te", inner_act, down_w) + product("tr,re->te", rank_ffd, ffd_up)
    ).astype(bf16)
    rank_mlp_grad = jnp.concatenate(
        [product("tf,rf->tr", gate_grad, gu_up[:ADAPTER_RANK]), product("tf,rf->tr", up_grad, gu_up[ADAPTER_RANK:])], -1
    ).astype(bf16)
    hidden2_grad = (
        product("tf,df->td", gate_grad, gate_up[:, :ff])
        + product("tf,df->td", up_grad, gate_up[:, ff:])
        + product("tr,rd->td", rank_mlp_grad, gu_down)
    )
    resid_grad = grad_out.astype(f32) + rms_backward(hidden2_grad, normed2, root2, gain2)
    term_ff = jnp.concatenate(
        [
            product("tr,tf->rf", rank_mlp[:, :ADAPTER_RANK], gate_grad),
            product("tr,tf->rf", rank_mlp[:, ADAPTER_RANK:], up_grad),
            product("tr,tf->rf", rank_ffd_grad, inner_act),
        ]
    )
    term_w = jnp.concatenate(
        [product("tr,td->rd", rank_mlp_grad, hidden2), product("tr,td->rd", rank_ffd, grad_out)]
    )
    return (mixer_in, mixer_out, output, blocks, values, attended_t, denominator, carry, attended, resid_grad,
            hidden1, rank_in, rank_out, halo, term_ff, term_w)


def per_device(
    layer_input_rows,
    segments,
    sequence_adapter_index,
    output_gradient,
    mixer_norm_gain,
    feedforward_norm_gain,
    convolution_taps,
    mixer_input_weight,
    mixer_output_weight,
    gate_up_weight,
    down_weight,
    adapter_input_down,
    adapter_querykey_up,
    adapter_valuegate_up,
    adapter_output_down,
    adapter_output_up,
    adapter_gateup_down,
    adapter_gateup_up,
    adapter_feedforward_down,
    adapter_feedforward_up,
):
    batch, length, width = layer_input_rows.shape
    assert batch == 1
    seq_count = lax.axis_size("seq")
    ff = gate_up_weight.shape[1] // 2
    bf16, f32 = jnp.bfloat16, jnp.float32
    chosen = sequence_adapter_index[0, 0]

    def select(table):
        return lax.dynamic_index_in_dim(table, chosen, 0, keepdims=False)

    in_down = select(adapter_input_down.swapaxes(1, 2))
    up_maps = up_by_head(select(adapter_querykey_up), select(adapter_valuegate_up))
    out_down = select(adapter_output_down.swapaxes(1, 2))
    out_up = select(adapter_output_up)
    gu_down = select(adapter_gateup_down.swapaxes(1, 2))
    gu_up = select(adapter_gateup_up)
    ffd_down = select(adapter_feedforward_down.swapaxes(1, 2))
    ffd_up = select(adapter_feedforward_up)
    docs = segments.astype(f32)
    place = lax.axis_index("seq")
    edge = jnp.concatenate([docs[:, :1], docs[:, length - 2 :], jnp.zeros((1, 125), f32)], axis=1)
    before_edge = lax.ppermute(edge, "seq", shift_pairs(seq_count, 1))
    after_edge = lax.ppermute(edge, "seq", shift_pairs(seq_count, -1))
    prev_docs = jnp.where(place == 0, -1.0, before_edge[:, 1:3])
    next_doc = jnp.where(place == seq_count - 1, -1.0, after_edge[:, 0])
    link_before = (prev_docs[0, 1] == docs[0, 0]).astype(f32)
    link_after = (next_doc[0] == docs[0, length - 1]).astype(f32)
    whole = (docs[0, 0] == docs[0, length - 1]).astype(f32)
    prev_pad = jnp.pad(prev_docs, ((0, 0), (0, 126)))
    doc_col = docs.reshape(length, 1)
    taps = jnp.pad(convolution_taps.T.reshape(HEAD_COUNT, DV, 3), ((0, 0), (0, 0), (0, 5)))

    inputs_f = layer_input_rows[0].astype(f32)
    grad_out = output_gradient[0]
    heads = HEAD_COUNT
    mask = pltpu.VMEM((length, length), f32)
    maps = (in_down, up_maps, out_down, out_up, gu_down, gu_up.reshape(32, ff), ffd_down, ffd_up)
    shards = (mixer_input_weight, mixer_output_weight, gate_up_weight, down_weight)
    grid = (lax.axis_size("fsdp"), seq_count)
    if grid == (8, 4):
        found = call_m(
            layer_input_rows[0], grad_out, mixer_norm_gain[None], feedforward_norm_gain[None], taps, docs, doc_col, maps, shards
        )
        found = found[:2] + found[4:]
    else:
        found = front_by_collectives(
            layer_input_rows[0], grad_out, mixer_norm_gain, feedforward_norm_gain, taps, docs, doc_col, prev_pad, link_before, whole, maps, shards
        )
    (mixer_in, mixer_out, output, blocks, values, attended_t, denominator, carry, attended, resid_grad,
     hidden1, rank_in, rank_out, halo, term_ff, term_w) = found
    halo = halo[:, : heads * PER_HEAD]
    carry = carry * link_before.astype(bf16)
    root1 = lax.rsqrt(jnp.mean(inputs_f * inputs_f, -1, keepdims=True) + epsilon)
    normed1 = inputs_f * root1
    branch_grad = resid_grad.astype(bf16)
    rank_out_grad = product("te,re->tr", branch_grad, out_up).astype(bf16)
    attended_grad = (
        product("te,de->td", branch_grad, mixer_out) + product("tr,rd->td", rank_out_grad, out_down)
    ).astype(bf16)
    grad_t = attended_grad.T
    later, query_grad, key_grad, value_grad = call_heads(
        b1_kernel,
        length,
        [(blocks, "rows"), (values, "rows"), (grad_t, "rows"), (attended_t, "rows"), (denominator, "rows"), (carry, "rows"), (docs, None), (doc_col, None)],
        [
            (jax.ShapeDtypeStruct((heads * FEATS, VROWS), bf16), "rows"),
            (jax.ShapeDtypeStruct((heads * 16, length), f32), "rows"),
            (jax.ShapeDtypeStruct((heads * 16, length), f32), "rows"),
            (jax.ShapeDtypeStruct((heads * VROWS, length), f32), "rows"),
        ],
        [mask],
    )
    later = chain(later, whole, link_after, -1)
    projected_grad, first_conv, tail_grad = call_heads(
        b2_kernel,
        length,
        [(blocks, "rows"), (values, "rows"), (later, "rows"), (query_grad, "rows"), (key_grad, "rows"), (value_grad, "rows"), (halo, "cols"), (taps, "rows"), (docs, None), (prev_pad, None)],
        [
            (jax.ShapeDtypeStruct((length, heads * PER_HEAD), bf16), "cols"),
            (jax.ShapeDtypeStruct((16, heads * PER_HEAD), f32), "cols"),
            (jax.ShapeDtypeStruct((16, heads * PER_HEAD), f32), "cols"),
        ],
    )
    next_conv = lax.ppermute(first_conv[:2], "seq", shift_pairs(seq_count, -1))
    taps_row = jnp.pad(
        convolution_taps.reshape(3, heads, DV),
        ((0, 0), (0, 0), (2 * FEATURE_SIZE, PER_HEAD - 2 * FEATURE_SIZE - DV)),
    ).reshape(3, heads * PER_HEAD)
    after_docs = jnp.where(place == seq_count - 1, -1.0, after_edge[0, 0])
    link_1 = (after_docs == docs[0, length - 1]).astype(f32)
    link_2 = (after_docs == docs[0, length - 2]).astype(f32)
    second = (docs[0, 1] == docs[0, 0]).astype(f32)
    second_next = lax.ppermute(second, "seq", shift_pairs(seq_count, -1))
    extra_last = taps_row[1] * next_conv[0] * link_1 + taps_row[2] * next_conv[1] * link_1 * second_next
    extra_before = taps_row[2] * next_conv[0] * link_2
    extra = jnp.concatenate(
        [jnp.zeros((14, heads * PER_HEAD), f32), extra_before[None], extra_last[None]], axis=0
    )
    projected_grad = lax.dynamic_update_slice(
        projected_grad, (tail_grad + extra).astype(bf16), (length - 16, 0)
    )
    rank_in_grad = product("te,re->tr", projected_grad, up_maps).astype(bf16)
    hidden1_grad = product("te,de->td", projected_grad, mixer_in) + product(
        "tr,rd->td", rank_in_grad, in_down
    )
    input_grad = resid_grad + rms_backward(hidden1_grad, normed1, root1, mixer_norm_gain)

    wide = product("tr,te->re", rank_in, projected_grad).reshape(4, ADAPTER_RANK, heads, PER_HEAD)
    term_qk = jnp.stack(
        [wide[0, :, :, 0:16].reshape(ADAPTER_RANK, -1), wide[1, :, :, 16:32].reshape(ADAPTER_RANK, -1)]
    )
    term_vg = jnp.concatenate(
        [
            wide[2, :, :, 32 : 32 + DV].reshape(ADAPTER_RANK, -1),
            wide[3, :, :, 32 + DV :].reshape(ADAPTER_RANK, -1),
        ]
    )
    by_width = jnp.concatenate(
        [
            product("tr,td->rd", rank_in_grad, hidden1),
            term_vg,
            product("tr,td->rd", rank_out_grad, attended),
            product("tr,td->rd", rank_out, branch_grad),
            term_w,
        ]
    )
    by_ff = term_ff
    by_rank = jnp.concatenate([term_qk.reshape(32, -1), jnp.full((16, 256), chosen.astype(f32) / seq_count)])
    by_width, by_ff, by_rank = spread(by_width, by_ff, by_rank)
    sequences = by_rank.shape[0]
    onehot = (by_rank[:, 32, 0][None, :] == jnp.arange(ADAPTER_COUNT, dtype=bf16)[:, None])

    if sequences == ADAPTER_COUNT:
        where = jnp.argmax(onehot, axis=1)

        def arrange(rows):
            return jnp.take(rows, where, axis=0).astype(f32)
    else:

        def arrange(rows):
            return jnp.einsum("as,s...->a...", onehot.astype(f32), rows.astype(f32), precision="highest")

    sizes = [64, 32, 16, 16, 32, 16]
    cut = [sum(sizes[:n]) for n in range(len(sizes) + 1)]
    widths = [arrange(by_width[:, cut[n] : cut[n + 1]]) for n in range(len(sizes))]
    return (
        output[None],
        input_grad[None],
        widths[0].swapaxes(1, 2),
        arrange(by_rank[:, :32]).reshape(ADAPTER_COUNT, 2, ADAPTER_RANK, -1),
        widths[1].reshape(ADAPTER_COUNT, 2, ADAPTER_RANK, width),
        widths[2].swapaxes(1, 2),
        widths[3],
        widths[4].swapaxes(1, 2),
        arrange(by_ff[:, :32]).reshape(ADAPTER_COUNT, 2, ADAPTER_RANK, ff),
        arrange(by_ff[:, 32:]).swapaxes(1, 2),
        widths[5],
    )


def spread(*terms):
    summed = lax.psum(terms, "seq")
    return [lax.all_gather(term.astype(jnp.bfloat16), "fsdp") for term in summed]


def solution(mesh):
    return jax.shard_map(
        per_device,
        mesh=mesh,
        in_specs=(
            P("fsdp", "seq", None),
            P("fsdp", "seq"),
            P("fsdp", None),
            P("fsdp", "seq", None),
            P(),
            P(),
            P(),
            P("fsdp", None),
            P("fsdp", None),
            P("fsdp", None),
            P("fsdp", None),
        )
        + (P(),) * 9,
        out_specs=(P("fsdp", "seq", None), P("fsdp", "seq", None)) + (P(),) * 9,
        check_vma=False,
    )
```

```python
import functools

import jax
import jax.numpy as jnp
from jax import lax
from jax.experimental import pallas as pl
from jax.experimental.pallas import tpu as pltpu
from jax.sharding import PartitionSpec as P

HEAD_COUNT = 16
FEATURE_SIZE = 16
DV = 112
ADAPTER_RANK = 16
ADAPTER_COUNT = 8
PER_HEAD = 2 * FEATURE_SIZE + 2 * DV
TBLOCK = 128

epsilon = 1e-05


FEATS = 176
VROWS = 128


def dot_nn(a, b):
    return lax.dot_general(a, b, (((1,), (0,)), ((), ())), preferred_element_type=jnp.float32)


def dot_nt(a, b):
    return lax.dot_general(a, b, (((1,), (1,)), ((), ())), preferred_element_type=jnp.float32)


def dot_tn(a, b):
    return lax.dot_general(a, b, (((0,), (0,)), ((), ())), preferred_element_type=jnp.float32)


def group_scale(shift):
    return 1.0 / 32.0 if shift in (0, 8) else 1.0 / 16.0


def cycle(rows, shift):
    if shift == 0:
        return rows
    return jnp.concatenate([rows[shift:], rows[:shift]], axis=0)


def features(rows, keep, scaled):
    length = rows.shape[1]
    rows_kept = rows * keep
    parts = []
    for shift in range(9):
        item = rows_kept * cycle(rows, shift)
        parts.append(item * group_scale(shift) if scaled else item)
    parts.append(rows_kept * 0.25 if scaled else rows_kept)
    first_row = lax.broadcasted_iota(jnp.int32, (16, length), 0) == 0
    parts.append(jnp.where(first_row, jnp.broadcast_to(keep, (16, length)), 0.0))
    return jnp.concatenate(parts, axis=0).astype(jnp.bfloat16)


def features_back(rows, grad, scaled):
    total = grad[144:160] * 0.25 if scaled else grad[144:160]
    for shift in range(9):
        item = grad[16 * shift : 16 * shift + 16]
        if scaled:
            item = item * group_scale(shift)
        total = total + item * cycle(rows, shift) + cycle(item * rows, (16 - shift) % 16)
    return total


def later_by(rows, offset, before):
    lane = lax.broadcasted_iota(jnp.int32, rows.shape, 1)
    moved = pltpu.roll(rows, offset, 1)
    if offset == 1:
        return jnp.where(lane == 0, before[:, 1:2], moved)
    return jnp.where(lane == 0, before[:, 0:1], jnp.where(lane == 1, before[:, 1:2], moved))


def sooner_by(rows, offset, after):
    length = rows.shape[1]
    lane = lax.broadcasted_iota(jnp.int32, rows.shape, 1)
    moved = pltpu.roll(rows, length - offset, 1)
    if offset == 1:
        return jnp.where(lane == length - 1, after[:, 0:1], moved)
    return jnp.where(
        lane == length - 2,
        after[:, 0:1],
        jnp.where(lane == length - 1, after[:, 1:2], moved),
    )


def conv_forward(signal, before, taps, same):
    total = taps[:, 0:1] * signal
    for offset in (1, 2):
        total = total + taps[:, offset : offset + 1] * later_by(signal, offset, before) * same[offset - 1]
    return total


def conv_backward(grad, after, taps, same):
    total = taps[:, 0:1] * grad
    for offset in (1, 2):
        total = total + taps[:, offset : offset + 1] * sooner_by(grad, offset, after) * same[offset - 1]
    return total


def add_ones(values):
    length = values.shape[1]
    row = lax.broadcasted_iota(jnp.int32, (VROWS - DV, length), 0)
    return jnp.concatenate(
        [values, jnp.where(row == 0, 1.0, 0.0).astype(jnp.bfloat16)], axis=0
    )


def weights_of(keys, queries, mask):
    shifted = dot_tn(keys, queries) + 1.0
    return shifted, (0.5 * shifted * shifted + 0.5) * mask


def mix_forward(tokens, before_tokens, taps, doc_row, prev_docs, mask_ref):
    length = tokens.shape[0]
    block = tokens.astype(jnp.float32).T.astype(jnp.bfloat16)
    before = before_tokens.astype(jnp.float32).T[2 * FEATURE_SIZE : 2 * FEATURE_SIZE + DV, 14:16]
    values, _, _, _ = values_of(block, before, taps, doc_row, prev_docs)
    marked = add_ones(values)
    keep_last = (doc_row == doc_row[:, length - 1 : length]).astype(jnp.float32)
    key_feats = features(block[16:32].astype(jnp.float32), keep_last, False)
    state = dot_nt(key_feats, marked)
    scaled_q = (block[0:16].astype(jnp.float32) * 0.25).astype(jnp.bfloat16)
    sums = []
    for start in range(0, length, TBLOCK):
        stop = start + TBLOCK
        _, weights = weights_of(
            block[16:32, :stop], scaled_q[:, start:stop], mask_ref[:stop, start:stop]
        )
        sums.append(dot_nn(marked[:, :stop], weights.astype(jnp.bfloat16)))
    return block, marked, jnp.concatenate(sums, axis=1), state


def values_of(block, before, taps, doc_row, prev_docs):
    length = block.shape[1]
    doc8 = jnp.broadcast_to(doc_row, (8, length))
    prev8 = jnp.broadcast_to(prev_docs, (8, 2))
    same = [
        (doc8 == later_by(doc8, offset, prev8)).astype(jnp.float32)[0:1] for offset in (1, 2)
    ]
    conv_in = block[32 : 32 + DV].astype(jnp.float32)
    gate_in = block[32 + DV :].astype(jnp.float32)
    conv_out = conv_forward(conv_in, before, taps, same)
    sigmoid = 1.0 / (1.0 + jnp.exp(-gate_in))
    values = (gate_in * sigmoid * conv_out).astype(jnp.bfloat16)
    return values, conv_out, gate_in, sigmoid


def fill_mask(mask_ref, doc_row, doc_col):
    shape = mask_ref.shape
    causal = lax.broadcasted_iota(jnp.int32, shape, 0) <= lax.broadcasted_iota(jnp.int32, shape, 1)
    mask_ref[...] = jnp.where(causal & (doc_col == doc_row), 1.0, 0.0)


def f1_kernel(p_ref, halo_ref, taps_ref, row_ref, col_ref, prev_ref, pt_ref, v_ref, o_ref, l_ref, mask_ref):
    @pl.when(pl.program_id(0) == 0)
    def _():
        fill_mask(mask_ref, row_ref[...], col_ref[...])

    block, marked, sums, state = mix_forward(
        p_ref[...], halo_ref[...], taps_ref[0], row_ref[...], prev_ref[:, 0:2], mask_ref
    )
    pt_ref[...] = block
    v_ref[...] = marked
    o_ref[...] = sums
    l_ref[...] = state.astype(jnp.bfloat16)


def mix_finish(block, sums, carry, doc_row):
    keep_first = (doc_row == doc_row[:, 0:1]).astype(jnp.float32)
    query_feats = features(block[0:16].astype(jnp.float32), keep_first, True)
    total = sums + dot_tn(carry, query_feats)
    denominator = total[DV : DV + 1]
    return (total[:DV] / denominator).astype(jnp.bfloat16), denominator


def f2_kernel(pt_ref, o_ref, s_ref, row_ref, att_ref, den_ref):
    attended, denominator = mix_finish(pt_ref[...], o_ref[...], s_ref[...], row_ref[...])
    att_ref[...] = attended
    den_ref[...] = jnp.broadcast_to(denominator, den_ref.shape)


def sum_grads(grad, attended, denominator):
    length = grad.shape[1]
    inverse = 1.0 / denominator
    grad_f = grad.astype(jnp.float32)
    dot_term = jnp.sum(grad_f * attended.astype(jnp.float32), axis=0, keepdims=True)
    row = lax.broadcasted_iota(jnp.int32, (VROWS - DV, length), 0)
    tail = jnp.where(row == 0, jnp.broadcast_to(-dot_term * inverse, row.shape), 0.0)
    return jnp.concatenate([grad_f * inverse, tail], axis=0).astype(jnp.bfloat16)


def mix_back_local(block, marked, sums_grad, carry, doc_row, mask_ref):
    length = block.shape[1]
    keys = block[16:32]
    queries = block[0:16].astype(jnp.float32)
    scaled_q = (queries * 0.25).astype(jnp.bfloat16)
    keep_first = (doc_row == doc_row[:, 0:1]).astype(jnp.float32)
    query_grad = features_back(queries, dot_nn(carry, sums_grad) * keep_first, True)
    key_grad = jnp.zeros((16, length), jnp.float32)
    value_grad = jnp.zeros((VROWS, length), jnp.float32)
    parts = []
    for start in range(0, length, TBLOCK):
        stop = start + TBLOCK
        mask = mask_ref[:stop, start:stop]
        shifted, weights = weights_of(keys[:, :stop], scaled_q[:, start:stop], mask)
        grad_block = sums_grad[:, start:stop]
        weight_grad = dot_tn(marked[:, :stop], grad_block)
        score_grad = (weight_grad * shifted * mask).astype(jnp.bfloat16)
        parts.append(dot_nn(keys[:, :stop], score_grad) * 0.25)
        key_part = dot_nt(scaled_q[:, start:stop], score_grad)
        value_part = dot_nt(grad_block, weights.astype(jnp.bfloat16))
        if stop < length:
            key_part = jnp.concatenate(
                [key_part, jnp.zeros((16, length - stop), jnp.float32)], axis=1
            )
            value_part = jnp.concatenate(
                [value_part, jnp.zeros((VROWS, length - stop), jnp.float32)], axis=1
            )
        key_grad = key_grad + key_part
        value_grad = value_grad + value_part
    query_grad = query_grad + jnp.concatenate(parts, axis=1)
    return query_grad, key_grad, value_grad


def b1_kernel(pt_ref, v_ref, g_ref, att_ref, den_ref, s_ref, row_ref, col_ref, d_ref, dq_ref, dk_ref, dv_ref, mask_ref):
    @pl.when(pl.program_id(0) == 0)
    def _():
        fill_mask(mask_ref, row_ref[...], col_ref[...])

    doc_row = row_ref[...]
    block = pt_ref[...]
    sums_grad = sum_grads(g_ref[...], att_ref[...], den_ref[0:1])
    keep_first = (doc_row == doc_row[:, 0:1]).astype(jnp.float32)
    query_feats = features(block[0:16].astype(jnp.float32), keep_first, True)
    d_ref[...] = dot_nt(query_feats, sums_grad).astype(jnp.bfloat16)
    dq, dk, dv = mix_back_local(block, v_ref[...], sums_grad, s_ref[...], doc_row, mask_ref)
    dq_ref[...] = dq
    dk_ref[...] = dk
    dv_ref[...] = dv


def mix_back_finish(block, marked, later_state, key_grad, value_grad, doc_row, before, taps, prev_docs):
    length = block.shape[1]
    keep_last = (doc_row == doc_row[:, length - 1 : length]).astype(jnp.float32)
    keys = block[16:32].astype(jnp.float32)
    key_feats = features(keys, keep_last, False)
    key_grad = key_grad + features_back(keys, dot_nn(later_state, marked) * keep_last, False)
    value_grad = (value_grad + dot_tn(later_state, key_feats))[:DV]
    _, conv_out, gate_in, sigmoid = values_of(block, before, taps, doc_row, prev_docs)
    gate_grad = value_grad * conv_out * sigmoid * (1.0 + gate_in * (1.0 - sigmoid))
    conv_grad = value_grad * gate_in * sigmoid
    return key_grad, gate_grad, conv_grad


def b2_kernel(pt_ref, v_ref, g_ref, dq_ref, dk_ref, dv_ref, halo_ref, taps_ref, row_ref, prev_ref, dp_ref, first_ref, tail_ref):
    doc_row = row_ref[...]
    length = doc_row.shape[1]
    taps = taps_ref[0]
    before = halo_ref[...].astype(jnp.float32).T[2 * FEATURE_SIZE : 2 * FEATURE_SIZE + DV, 14:16]
    key_grad, gate_grad, conv_grad = mix_back_finish(
        pt_ref[...], v_ref[...], g_ref[...], dk_ref[...], dv_ref[...], doc_row, before, taps, prev_ref[:, 0:2]
    )
    doc8 = jnp.broadcast_to(doc_row, (8, length))
    none = jnp.full((8, 2), -1.0, jnp.float32)
    same = [(doc8 == sooner_by(doc8, offset, none)).astype(jnp.float32)[0:1] for offset in (1, 2)]
    conv_in_grad = conv_backward(conv_grad, jnp.zeros((DV, 2), jnp.float32), taps, same)
    whole = jnp.concatenate([dq_ref[...], key_grad, conv_in_grad, gate_grad], axis=0).T
    dp_ref[...] = whole.astype(jnp.bfloat16)
    tail_ref[...] = whole[length - 16 :]
    pad = jnp.zeros((16, length), jnp.float32)
    conv_tokens = jnp.concatenate([jnp.zeros((32, length), jnp.float32), conv_grad, jnp.zeros((DV, length), jnp.float32)], axis=0).T
    first_ref[...] = conv_tokens[0:16]


MESH = pl.DeviceIdType.MESH
LAG = 2
AHEAD = 4
UNIT = 512
TILE = 256
GROUPS = 4


class Gather:
    kinds = 8

    def __init__(self, shards, wholes, sends, lands):
        self.shards, self.wholes = shards, wholes
        self.sends, self.lands = sends, lands
        i = lax.axis_index("fsdp")
        z = lax.axis_index("seq")
        odd = z % 2
        self.odd = odd
        by_y = 4 - 8 * (i // 4)
        by_x = 2 - 4 * ((i // 2) % 2)
        by_core = 1 - 2 * (i % 2)
        self.slot = [i, i + by_y, i + by_x + odd * by_y, i + by_x + (1 - odd) * by_y, i + by_core]
        self.near = [
            {"fsdp": i + by_y, "seq": z},
            {"fsdp": i + by_x, "seq": z},
            {"fsdp": i, "seq": z + 1 - 2 * odd},
            {"fsdp": i + by_core, "seq": z},
        ]

    def part(self, piece, slot):
        _, which, start, size = piece
        rows = self.shards[which].shape[0]
        return self.wholes[which].at[
            pl.ds(pl.multiple_of(slot * rows, 32), rows), pl.ds(start, size)
        ]

    def own_part(self, piece):
        _, which, start, size = piece
        return self.shards[which].at[:, pl.ds(start, size)]

    def copy(self, kind, piece, relay=False):
        source = [0, 0, 2, 0, 1, 2, 3, 4][kind]
        if relay:
            source = 1
        slot = self.slot[source]
        return pltpu.make_async_remote_copy(
            src_ref=self.own_part(piece) if source == 0 else self.part(piece, slot),
            dst_ref=self.part(piece, slot),
            send_sem=self.sends.at[kind, piece[0]],
            recv_sem=self.lands.at[kind, piece[0]],
            device_id=self.near[min(kind, 3)],
            device_id_type=MESH,
        )

    def first(self, piece):
        self.copy(0, piece).start()

        @pl.when(self.odd == 0)
        def _():
            self.copy(1, piece).start()

        self.copy(3, piece).start()

    def from_y(self, piece):
        self.copy(0, piece).wait_recv()

        @pl.when(self.odd == 1)
        def _():
            self.copy(1, piece, relay=True).start()

        self.copy(4, piece).start()
        self.copy(3, piece).wait_recv()
        self.copy(7, piece).start()

    def from_x(self, piece):
        self.copy(1, piece).wait_recv()
        self.copy(2, piece).start()
        self.copy(5, piece).start()

    def from_z(self, piece):
        self.copy(2, piece).wait_recv()
        self.copy(6, piece).start()

    def ready(self, piece):
        for kind in (4, 5, 6, 7):
            self.copy(kind, piece).wait_recv()

    def finish(self, piece):
        for kind in range(self.kinds):
            self.copy(kind, piece).wait_send()


def cuts(which, width, size):
    return [(which, at, min(size, width - at)) for at in range(0, width, size)]


def early_cuts(columns, width):
    return cuts(0, columns, 512) + cuts(1, width, 512) + cuts(3, width, 256)


def by_rows(length, body, rows=64):
    def step(n, _):
        body(pl.ds(pl.multiple_of(n * rows, rows), rows))
        return 0

    lax.fori_loop(0, length // rows, step, 0)


def row_root(value):
    return lax.rsqrt(jnp.mean(value * value, -1, keepdims=True) + epsilon)


def m_kernel(
    x, g, gain1, gain2, taps, doc_row_ref, doc_col_ref, in_down, up_maps, out_down, out_up, gu_down, gu_up, ffd_down, ffd_up,
    a_in, b_in, c_in, d_in,
    a_all, b_all, c_all, d_all,
    out, blocks, marked, att_t, dens, carry, attended, resid_grad, hidden1, rank_in, rank_out, halo, term_ff, term_w, next_docs,
    first_docs,    halo_send, mask, sums, state, message, resid, hidden2, out_acc, grad_acc, a_tile, b_tile, g_tile, u_tile, d_tile, rank_acc,
    sends, lands, halo_sems, chain_sems, load_sems,
):
    length, width = x.shape
    ff = d_all.shape[0]
    units = -(-ff // UNIT)
    last_size = ff - (units - 1) * UNIT
    f32, bf16 = jnp.float32, jnp.bfloat16
    place = lax.axis_index("seq")
    planes = lax.axis_size("seq")
    me = lax.axis_index("fsdp")
    job = Gather([a_in, b_in, c_in, d_in], [a_all, b_all, c_all, d_all], sends, lands)

    early = early_cuts(a_in.shape[1], b_in.shape[1])
    early = [(number,) + piece for number, piece in enumerate(early)]
    base = len(early)
    mix_pieces = [p for p in early if p[1] == 0]
    out_pieces = [p for p in early if p[1] == 1]
    down_pieces = [p for p in early if p[1] == 3]
    total = base + 2 * units

    def late(number, size=UNIT):
        at = number - base
        start = (at // 2) * UNIT + (at % 2) * ff
        if not isinstance(start, int):
            start = pl.multiple_of(start, TILE)
        return (number, 2, start, size)

    def piece_at(number):
        if number < base:
            return early[number]
        return late(number, UNIT if number < total - 2 else last_size)

    def each_late(number, action):
        @pl.when(number < total - 2)
        def _():
            action(late(number))

        for end in (total - 2, total - 1):

            @pl.when(number == end)
            def _():
                action(piece_at(end))

    def pump(number):
        job.from_y(piece_at(number))
        if number + AHEAD < total:
            job.first(piece_at(number + AHEAD))
        if number >= LAG:
            job.from_x(piece_at(number - LAG))
        if number >= 2 * LAG:
            job.from_z(piece_at(number - 2 * LAG))

    barrier = pltpu.get_barrier_semaphore()
    for device in (job.near[0], job.near[1], job.near[3]):
        pl.semaphore_signal(barrier, inc=1, device_id=device, device_id_type=MESH)
    before = {"fsdp": me, "seq": (place + planes - 1) % planes}
    after = {"fsdp": me, "seq": (place + 1) % planes}

    @pl.when(place > 0)
    def _():
        pl.semaphore_signal(barrier, inc=1, device_id=before, device_id_type=MESH)

    @pl.when(place < planes - 1)
    def _():
        pl.semaphore_signal(barrier, inc=1, device_id=after, device_id_type=MESH)

    inner = (place > 0) & (place < planes - 1)

    @pl.when(inner)
    def _():
        pl.semaphore_wait(barrier, 5)

    @pl.when(jnp.logical_not(inner))
    def _():
        pl.semaphore_wait(barrier, 4)

    for piece in early[:AHEAD]:
        job.first(piece)
    first_docs[...] = jnp.broadcast_to(doc_col_ref[0:8, :], (8, 128))
    docs_back = pltpu.make_async_remote_copy(
        src_ref=first_docs, dst_ref=next_docs, send_sem=halo_sems.at[2], recv_sem=halo_sems.at[3], device_id=before, device_id_type=MESH
    )

    @pl.when(place > 0)
    def _():
        docs_back.start()

    @pl.when(place == planes - 1)
    def _():
        next_docs[...] = jnp.full(next_docs.shape, -1.0, f32)

    def norm1(rows):
        value = x[rows, :].astype(f32)
        hidden1[rows, :] = (value * row_root(value) * gain1[...]).astype(bf16)

    by_rows(length, norm1)
    rank_in[...] = dot_nt(hidden1[...], in_down[...]).astype(bf16)
    doc_row = doc_row_ref[...]
    fill_mask(mask, doc_row, doc_col_ref[...])
    cond_whole = (doc_row[:, 0:1] == doc_row[:, length - 1 : length]).astype(f32)

    for number in range(2 * LAG):
        pump(number)
    for number, piece in enumerate(mix_pieces):
        pump(number + 2 * LAG)
        job.ready(piece)
        _, _, start, size = piece
        load = pltpu.make_async_copy(a_all.at[:, pl.ds(start, size)], a_tile, load_sems.at[0])
        load.start()
        load.wait()
        projected = dot_nn(hidden1[...], a_tile[...]) + dot_nn(rank_in[...], up_maps[:, start : start + size])
        halo_send[:, start : start + size] = projected[length - 16 :].astype(bf16)
        for at in range(0, size, PER_HEAD):
            blocks[start + at : start + at + PER_HEAD, :] = projected[:, at : at + PER_HEAD].T.astype(bf16)
    columns = HEAD_COUNT * PER_HEAD
    halo_send[:, columns:] = jnp.broadcast_to(
        doc_col_ref[length - 16 :, :], (16, 128)
    ).astype(bf16)
    to_next = pltpu.make_async_remote_copy(
        src_ref=halo_send, dst_ref=halo, send_sem=halo_sems.at[0], recv_sem=halo_sems.at[1], device_id=after, device_id_type=MESH
    )

    @pl.when(place < planes - 1)
    def _():
        to_next.start()

    @pl.when(place == 0)
    def _():
        halo[:, :columns] = jnp.zeros((16, columns), bf16)
        halo[:, columns:] = jnp.full((16, 128), -1.0, bf16)

    next_piece = len(mix_pieces) + 2 * LAG

    def pump_next():
        nonlocal next_piece
        pump(next_piece)
        next_piece += 1

    pump_next()

    @pl.when(place > 0)
    def _():
        to_next.wait_recv()

    prev_docs = halo[:, columns:].astype(f32).T[0:1, 14:16]
    cond_before = (prev_docs[:, 1:2] == doc_row[:, 0:1]).astype(f32)
    keep_last = (doc_row == doc_row[:, length - 1 : length]).astype(f32)

    def head_state(h, _):
        at = pl.multiple_of(h * PER_HEAD, PER_HEAD)
        block = blocks[pl.ds(at, PER_HEAD), :]
        prior = halo[:, pl.ds(at, PER_HEAD)].astype(f32).T[32 : 32 + DV, 14:16]
        values, _, _, _ = values_of(block, prior, taps[h], doc_row, prev_docs)
        ones = add_ones(values)
        marked[pl.ds(pl.multiple_of(h * VROWS, VROWS), VROWS), :] = ones
        key_feats = features(block[16:32].astype(f32), keep_last, False)
        state[pl.ds(pl.multiple_of(h * FEATS, 16), FEATS), :] = dot_nt(key_feats, ones).astype(bf16)
        return 0

    group = HEAD_COUNT // GROUPS
    half = HEAD_COUNT // 2
    lax.fori_loop(0, half, head_state, 0)
    pump_next()
    lax.fori_loop(half, HEAD_COUNT, head_state, 0)
    pump_next()
    span = group * FEATS

    def hand_on(number):
        part = pl.ds(number * span, span)
        return pltpu.make_async_remote_copy(
            src_ref=message.at[part], dst_ref=carry.at[part],
            send_sem=chain_sems.at[0, number], recv_sem=chain_sems.at[1, number], device_id=after, device_id_type=MESH,
        )

    @pl.when(place == 0)
    def _():
        carry[...] = jnp.zeros(carry.shape, bf16)

    def head_local(h, _):
        at = pl.multiple_of(h * PER_HEAD, PER_HEAD)
        keys = blocks[pl.ds(at + 16, 16), :]
        scaled_q = (blocks[pl.ds(at, 16), :].astype(f32) * 0.25).astype(bf16)
        rows = pl.multiple_of(h * VROWS, VROWS)
        ones = marked[pl.ds(rows, VROWS), :]
        for start in range(0, length, TBLOCK):
            stop = start + TBLOCK
            _, weights = weights_of(keys[:, :stop], scaled_q[:, start:stop], mask[:stop, start:stop])
            sums[pl.ds(rows, VROWS), start:stop] = dot_nn(ones[:, :stop], weights.astype(bf16))
        return 0

    for number in range(GROUPS):
        part = pl.ds(number * span, span)

        @pl.when(place > 0)
        def _():
            hand_on(number).wait_recv()

        message[part, :] = (
            state[part, :].astype(f32) + (cond_whole * cond_before) * carry[part, :].astype(f32)
        ).astype(bf16)

        @pl.when(place < planes - 1)
        def _():
            hand_on(number).start()

        lax.fori_loop(number * group, (number + 1) * group, head_local, 0)
        pump_next()

    keep_first = (doc_row == doc_row[:, 0:1]).astype(f32) * cond_before

    def head_finish(h, _):
        at = pl.multiple_of(h * PER_HEAD, PER_HEAD)
        rows = pl.multiple_of(h * VROWS, VROWS)
        query_feats = features(blocks[pl.ds(at, 16), :].astype(f32), keep_first, True)
        both = sums[pl.ds(rows, VROWS), :] + dot_tn(carry[pl.ds(pl.multiple_of(h * FEATS, 16), FEATS), :], query_feats)
        denominator = both[DV : DV + 1]
        att_t[pl.ds(pl.multiple_of(h * DV, 16), DV), :] = (both[:DV] / denominator).astype(bf16)
        dens[pl.ds(pl.multiple_of(h * 8, 8), 8), :] = jnp.broadcast_to(denominator, (8, length))
        return 0

    lax.fori_loop(0, half, head_finish, 0)
    pump_next()
    lax.fori_loop(half, HEAD_COUNT, head_finish, 0)

    def turn(n, _):
        rows = pl.ds(pl.multiple_of(n * 128, 128), 128)
        attended[:, rows] = att_t[rows, :].astype(f32).T.astype(bf16)
        return 0

    lax.fori_loop(0, width // 128, turn, 0)
    pump_next()

    rank_out[...] = dot_nt(attended[...], out_down[...]).astype(bf16)
    for piece in out_pieces:
        job.ready(piece)
        _, _, start, size = piece
        load = pltpu.make_async_copy(b_all.at[:, pl.ds(start, size)], b_tile.at[:, :size], load_sems.at[0])
        load.start()
        load.wait()
        resid[:, start : start + size] = (
            x[:, start : start + size].astype(f32)
            + dot_nn(attended[...], b_tile[:, :size])
            + dot_nn(rank_out[...], out_up[:, start : start + size])
        )
    pump_next()

    def norm2(rows):
        value = resid[rows, :]
        hidden2[rows, :] = (value * row_root(value) * gain2[...]).astype(bf16)
        out_acc[rows, :] = value
        grad_acc[rows, :] = jnp.zeros(value.shape, f32)

    by_rows(length, norm2)
    rank_gate = dot_nt(hidden2[...], gu_down[0:16, :]).astype(bf16)
    rank_up = dot_nt(hidden2[...], gu_down[16:32, :]).astype(bf16)
    rank_ffd_grad = dot_nt(g[...], ffd_up[...]).astype(bf16)
    rank_gate_t = rank_gate.astype(f32).T.astype(bf16)
    rank_up_t = rank_up.astype(f32).T.astype(bf16)
    rank_ffd_grad_t = rank_ffd_grad.astype(f32).T.astype(bf16)
    rank_acc[...] = jnp.zeros(rank_acc.shape, f32)
    while next_piece < base + 2 * LAG:
        pump_next()
    for piece in down_pieces:
        job.ready(piece)

    def loads(unit, slot, size):
        start = unit * UNIT
        if not isinstance(start, int):
            start = pl.multiple_of(start, TILE)
        return [
            pltpu.make_async_copy(c_all.at[:, pl.ds(start, size)], g_tile.at[slot, :, :size], load_sems.at[slot]),
            pltpu.make_async_copy(c_all.at[:, pl.ds(ff + start, size)], u_tile.at[slot, :, :size], load_sems.at[2 + slot]),
            pltpu.make_async_copy(d_all.at[pl.ds(start, size), :], d_tile.at[slot, :size, :], load_sems.at[4 + slot]),
        ]

    def hidden_tile(unit, slot, part):
        inside = slice(part * TILE, (part + 1) * TILE)
        start = unit * UNIT + part * TILE
        cols = pl.ds(start if isinstance(start, int) else pl.multiple_of(start, TILE), TILE)
        gate_w, up_w, down_w = g_tile[slot, :, inside], u_tile[slot, :, inside], d_tile[slot, inside, :]
        gate_map, up_map, down_map = gu_up[0:16, cols], gu_up[16:32, cols], ffd_down[:, cols]
        gate_pre = dot_nn(hidden2[...], gate_w) + dot_nn(rank_gate, gate_map)
        up_pre = dot_nn(hidden2[...], up_w) + dot_nn(rank_up, up_map)
        inner_grad = dot_nt(g[...], down_w) + dot_nn(rank_ffd_grad, down_map)
        sigmoid = 1.0 / (1.0 + jnp.exp(-gate_pre))
        gate_val = gate_pre * sigmoid
        inner = (gate_val * up_pre).astype(bf16)
        gate_grad = (inner_grad * up_pre * (sigmoid * (1.0 + gate_pre * (1.0 - sigmoid)))).astype(bf16)
        up_grad = (inner_grad * gate_val).astype(bf16)
        out_acc[...] += dot_nn(inner, down_w)
        grad_acc[...] += dot_nt(gate_grad, gate_w) + dot_nt(up_grad, up_w)
        rank_acc[0] += dot_nt(inner, down_map)
        rank_acc[1] += dot_nt(gate_grad, gate_map)
        rank_acc[2] += dot_nt(up_grad, up_map)
        term_ff[0:16, cols] = dot_nn(rank_gate_t, gate_grad)
        term_ff[16:32, cols] = dot_nn(rank_up_t, up_grad)
        term_ff[32:48, cols] = dot_nn(rank_ffd_grad_t, inner)

    def ff_pump(number):
        each_late(number, job.from_y)
        each_late(number + AHEAD, job.first)
        each_late(number - LAG, job.from_x)
        each_late(number - 2 * LAG, job.from_z)

    def ff_ready(unit, slot, size, pieces):
        for piece in pieces:
            job.ready(piece)
        for load in loads(unit, slot, size):
            load.start()

    def ff_load_wait(unit, slot, size):
        for load in loads(unit, slot, size):
            load.wait()

    def ff_step(unit, _):
        slot = unit % 2
        ahead = base + 2 * unit + 2 * LAG
        ff_pump(ahead)

        @pl.when(unit >= 1)
        def _():
            ff_load_wait(unit - 1, 1 - slot, UNIT)
            hidden_tile(unit - 1, 1 - slot, 0)

        ff_pump(ahead + 1)
        ff_ready(unit, slot, UNIT, [late(base + 2 * unit), late(base + 2 * unit + 1)])

        @pl.when(unit >= 1)
        def _():
            hidden_tile(unit - 1, 1 - slot, 1)

        return 0

    lax.fori_loop(0, units - 1, ff_step, 0)
    final = units - 1
    job.from_z(piece_at(total - 2))
    job.from_z(piece_at(total - 1))
    ff_load_wait(final - 1, (final - 1) % 2, UNIT)
    hidden_tile(final - 1, (final - 1) % 2, 0)
    ff_ready(final, final % 2, last_size, [piece_at(total - 2), piece_at(total - 1)])
    hidden_tile(final - 1, (final - 1) % 2, 1)
    ff_load_wait(final, final % 2, last_size)
    for part in range(last_size // TILE):
        hidden_tile(final, final % 2, part)

    rank_ffd = rank_acc[0].astype(bf16)
    rank_gate_grad = rank_acc[1].astype(bf16)
    rank_up_grad = rank_acc[2].astype(bf16)
    out_acc[...] += dot_nn(rank_ffd, ffd_up[...])
    grad_acc[...] += dot_nn(rank_gate_grad, gu_down[0:16, :]) + dot_nn(rank_up_grad, gu_down[16:32, :])
    term_w[0:16, :] = dot_tn(rank_gate_grad, hidden2[...])
    term_w[16:32, :] = dot_tn(rank_up_grad, hidden2[...])
    term_w[32:48, :] = dot_tn(rank_ffd, g[...])

    def finish_rows(rows):
        out[rows, :] = out_acc[rows, :].astype(bf16)
        value = resid[rows, :]
        root = row_root(value)
        normed = value * root
        scaled = grad_acc[rows, :] * gain2[...]
        resid_grad[rows, :] = g[rows, :].astype(f32) + root * (
            scaled - normed * jnp.mean(scaled * normed, -1, keepdims=True)
        )

    by_rows(length, finish_rows)

    for piece in early:
        job.finish(piece)

    def finish_late(number, _):
        job.finish(late(number))
        return 0

    lax.fori_loop(base, total - 2, finish_late, 0)
    job.finish(piece_at(total - 2))
    job.finish(piece_at(total - 1))

    @pl.when(place > 0)
    def _():
        docs_back.wait_send()

    @pl.when(place < planes - 1)
    def _():
        docs_back.wait_recv()
        to_next.wait_send()
        for number in range(GROUPS):
            hand_on(number).wait_send()


def call_m(x, g, gain1, gain2, taps, doc_row, doc_col, maps, shards):
    length, width = x.shape
    f32, bf16 = jnp.float32, jnp.bfloat16
    count = lax.axis_size("fsdp")
    a, b, c, d = shards
    ff = d.shape[0] * count
    columns = a.shape[1]
    pieces = len(early_cuts(columns, width)) + 2 * -(-ff // UNIT)
    whole = pl.BlockSpec(memory_space=pltpu.VMEM)
    anyplace = pl.BlockSpec(memory_space=pl.ANY)
    vmem_out = [
        ((length, width), bf16),
        ((columns, length), bf16),
        ((HEAD_COUNT * VROWS, length), bf16),
        ((width, length), bf16),
        ((HEAD_COUNT * 8, length), f32),
        ((HEAD_COUNT * FEATS, VROWS), bf16),
        ((length, width), bf16),
        ((length, width), f32),
        ((length, width), bf16),
        ((length, 64), bf16),
        ((length, 16), bf16),
        ((16, columns + 128), bf16),
        ((48, ff), f32),
        ((48, width), f32),
        ((8, 128), f32),
    ]
    args = (x, g, gain1, gain2, taps, doc_row, doc_col) + tuple(maps)
    return pl.pallas_call(
        m_kernel,
        in_specs=[whole] * len(args) + [anyplace] * 4,
        out_specs=[anyplace] * 4 + [whole] * len(vmem_out),
        out_shape=[jax.ShapeDtypeStruct((t.shape[0] * count, t.shape[1]), t.dtype) for t in shards]
        + [jax.ShapeDtypeStruct(s, t) for s, t in vmem_out],
        scratch_shapes=[
            pltpu.VMEM((8, 128), f32),
            pltpu.VMEM((16, columns + 128), bf16),
            pltpu.VMEM((length, length), f32),
            pltpu.VMEM((HEAD_COUNT * VROWS, length), f32),
            pltpu.VMEM((HEAD_COUNT * FEATS, VROWS), bf16),
            pltpu.VMEM((HEAD_COUNT * FEATS, VROWS), bf16),
            pltpu.VMEM((length, width), f32),
            pltpu.VMEM((length, width), bf16),
            pltpu.VMEM((length, width), f32),
            pltpu.VMEM((length, width), f32),
            pltpu.VMEM((width, 512), bf16),
            pltpu.VMEM((width, 512), bf16),
            pltpu.VMEM((2, width, UNIT), bf16),
            pltpu.VMEM((2, width, UNIT), bf16),
            pltpu.VMEM((2, UNIT, width), bf16),
            pltpu.VMEM((3, length, 16), f32),
            pltpu.SemaphoreType.DMA((8, pieces)),
            pltpu.SemaphoreType.DMA((8, pieces)),
            pltpu.SemaphoreType.DMA((4,)),
            pltpu.SemaphoreType.DMA((2, GROUPS)),
            pltpu.SemaphoreType.DMA((6,)),
        ],
        compiler_params=pltpu.CompilerParams(
            collective_id=1, has_side_effects=True, vmem_limit_bytes=62 * 1024 * 1024
        ),
    )(*args, *shards)


FF_ROWS, WIDE_ROWS, LATE_ROWS = 48, 80, 112
HALVES = (32, 48, 64)


class Share:
    def __init__(self, number, own, slots, total, everyone, z_sends, z_lands, sends, lands, local):
        self.number, self.own, self.slots, self.total, self.everyone = number, own, slots, total, everyone
        self.z_sends, self.z_lands, self.sends, self.lands, self.local = z_sends, z_lands, sends, lands, local
        i = lax.axis_index("fsdp")
        self.place = lax.axis_index("seq")
        self.planes = lax.axis_size("seq")
        by_y = 4 - 8 * (i // 4)
        by_x = 2 - 4 * ((i // 2) % 2)
        by_core = 1 - 2 * (i % 2)
        self.slot = [i, i + by_y, i + by_x, i + by_x + by_y]
        self.near = [
            {"fsdp": i + by_y, "seq": self.place},
            {"fsdp": i + by_x, "seq": self.place},
            {"fsdp": i + by_core, "seq": self.place},
        ]
        self.me = i

    def z_copy(self, distance):
        return pltpu.make_async_remote_copy(
            src_ref=self.own,
            dst_ref=self.slots.at[self.place],
            send_sem=self.z_sends.at[self.number, distance - 1],
            recv_sem=self.z_lands.at[self.number, distance - 1],
            device_id={"fsdp": self.me, "seq": (self.place + distance) % self.planes},
            device_id_type=MESH,
        )

    def z_start(self):
        self.slots[self.place] = self.own[...]
        for distance in range(1, self.planes):
            self.z_copy(distance).start()

    def copy(self, kind):
        half = HALVES[self.number]
        rows = self.own.shape[0]
        first, second, every = pl.ds(0, half), pl.ds(half, rows - half), pl.ds(0, rows)
        where, slot, part = [
            (0, 0, every), (1, 0, every), (2, 0, every),
            (1, 1, first), (0, 2, second),
            (2, 1, every), (2, 2, every), (2, 3, every),
        ][kind]
        there = self.everyone.at[self.slot[slot], part]
        return pltpu.make_async_remote_copy(
            src_ref=self.total if slot == 0 else there,
            dst_ref=there,
            send_sem=self.sends.at[self.number, kind],
            recv_sem=self.lands.at[self.number, kind],
            device_id=self.near[where],
            device_id_type=MESH,
        )

    def keep(self):
        return pltpu.make_async_copy(self.total, self.everyone.at[self.slot[0]], self.local.at[self.number])

    def gather_start(self):
        for distance in range(1, self.planes):
            self.z_copy(distance).wait_recv()
        total = self.slots[0].astype(jnp.float32)
        for plane in range(1, self.planes):
            total = total + self.slots[plane].astype(jnp.float32)
        self.total[...] = total.astype(jnp.bfloat16)
        for kind in (0, 1, 2):
            self.copy(kind).start()
        self.keep().start()

    def relay(self):
        self.copy(0).wait_recv()
        self.copy(3).start()
        self.copy(5).start()
        self.copy(1).wait_recv()
        self.copy(4).start()
        self.copy(6).start()

    def relay_last(self):
        self.copy(3).wait_recv()
        self.copy(4).wait_recv()
        self.copy(7).start()

    def finish(self):
        for kind in (2, 5, 6, 7):
            self.copy(kind).wait_recv()
        self.keep().wait()
        for kind in range(8):
            self.copy(kind).wait_send()
        for distance in range(1, self.planes):
            self.z_copy(distance).wait_send()


def t_kernel(
    x, gain1, taps, doc_row_ref, doc_col_ref, next_docs_ref, chosen, in_down, up_maps, out_down, out_up,
    blocks, marked, att_t, dens, carry, attended, resid_grad, hidden1, rank_in, rank_out, halo, term_ff, term_w,
    w_in, w_out,
    input_grad, all_ff, all_wide, all_late,
    out_tile, in_tile, branch_t, grad_t, sums_grad, state, message, later, query_grad, key_grad, value_grad, proj_grad,
    conv_last, halo_send, halo_next, vg_terms, qk_terms, mask,
    ff_own, ff_slots, ff_total, wide_own, wide_slots, wide_total, late_own, late_slots, late_total,
    chain_sems, halo_sems, load_sems, z_sends, z_lands, sends, lands, local,
):
    length, width = x.shape
    f32, bf16 = jnp.float32, jnp.bfloat16
    columns = HEAD_COUNT * PER_HEAD
    place = lax.axis_index("seq")
    planes = lax.axis_size("seq")
    me = lax.axis_index("fsdp")
    sems = (z_sends, z_lands, sends, lands, local)
    ff_share = Share(0, ff_own, ff_slots, ff_total, all_ff, *sems)
    wide_share = Share(1, wide_own, wide_slots, wide_total, all_wide, *sems)
    late_share = Share(2, late_own, late_slots, late_total, all_late, *sems)

    barrier = pltpu.get_barrier_semaphore()
    others = [{"fsdp": me, "seq": (place + distance) % planes} for distance in range(1, planes)]
    for device in ff_share.near + others:
        pl.semaphore_signal(barrier, inc=1, device_id=device, device_id_type=MESH)
    pl.semaphore_wait(barrier, 3 + planes - 1)

    load_out = pltpu.make_async_copy(w_out, out_tile, load_sems.at[0])
    load_out.start()
    step = in_tile.shape[1]
    blocks_in = width // step

    def load_in(number):
        return pltpu.make_async_copy(
            w_in.at[pl.ds(number * step, step), :], in_tile.at[number % 2], load_sems.at[1 + number % 2]
        )

    load_in(0).start()
    load_in(1).start()
    ff_own[...] = term_ff[...].astype(bf16)
    ff_share.z_start()
    wide_own[0:48, :] = term_w[...].astype(bf16)

    doc_row = doc_row_ref[...]
    fill_mask(mask, doc_row, doc_col_ref[...])
    prev_docs = halo[:, columns:].astype(f32).T[0:1, 14:16]
    next_docs = next_docs_ref[...].T[0:1, 0:2]
    cond_before = (prev_docs[:, 1:2] == doc_row[:, 0:1]).astype(f32)
    cond_after = (next_docs[:, 0:1] == doc_row[:, length - 1 : length]).astype(f32)
    cond_whole = (doc_row[:, 0:1] == doc_row[:, length - 1 : length]).astype(f32)
    keep_first = (doc_row == doc_row[:, 0:1]).astype(f32)
    keep_first_link = keep_first * cond_before
    keep_last = (doc_row == doc_row[:, length - 1 : length]).astype(f32) * cond_after

    for start in range(0, width, 128):
        branch_t[start : start + 128, :] = resid_grad[:, start : start + 128].T.astype(bf16)
    rank_grad_t = dot_nn(out_up[...], branch_t[...]).astype(bf16)
    load_out.wait()
    for start in range(0, width, 256):
        grad_t[start : start + 256, :] = (
            dot_nn(out_tile[start : start + 256, :], branch_t[...])
            + dot_tn(out_down[:, start : start + 256], rank_grad_t)
        ).astype(bf16)
    group = HEAD_COUNT // GROUPS
    span = group * FEATS

    def head_state(h, _):
        at = pl.multiple_of(h * PER_HEAD, PER_HEAD)
        rows = pl.ds(pl.multiple_of(h * VROWS, VROWS), VROWS)
        own = pl.ds(pl.multiple_of(h * DV, 16), DV)
        grads = sum_grads(grad_t[own, :], att_t[own, :], dens[pl.ds(pl.multiple_of(h * 8, 8), 8), :][0:1])
        sums_grad[rows, :] = grads
        query_feats = features(blocks[pl.ds(at, 16), :].astype(f32), keep_first, True)
        state[pl.ds(pl.multiple_of(h * FEATS, 16), FEATS), :] = dot_nt(query_feats, grads).astype(bf16)
        return 0

    def hand_on(number):
        part = pl.ds(number * span, span)
        return pltpu.make_async_remote_copy(
            src_ref=message.at[part], dst_ref=later.at[part],
            send_sem=chain_sems.at[0, number], recv_sem=chain_sems.at[1, number],
            device_id={"fsdp": me, "seq": (place + planes - 1) % planes}, device_id_type=MESH,
        )

    @pl.when(place == planes - 1)
    def _():
        later[...] = jnp.zeros(later.shape, bf16)

    for number in range(GROUPS):
        part = pl.ds(number * span, span)
        lax.fori_loop(number * group, (number + 1) * group, head_state, 0)

        @pl.when(place == planes - 1)
        def _():
            message[part, :] = state[part, :]
            hand_on(number).start()

    def head_local(h, _):
        at = pl.multiple_of(h * PER_HEAD, PER_HEAD)
        rows = pl.ds(pl.multiple_of(h * VROWS, VROWS), VROWS)
        keys = blocks[pl.ds(at + 16, 16), :]
        queries = blocks[pl.ds(at, 16), :].astype(f32)
        scaled_q = (queries * 0.25).astype(bf16)
        ones = marked[rows, :]
        grads = sums_grad[rows, :]
        from_carry = dot_nn(carry[pl.ds(pl.multiple_of(h * FEATS, 16), FEATS), :], grads) * keep_first_link
        query_total = features_back(queries, from_carry, True)
        small = pl.multiple_of(h * 16, 16)
        for start in range(0, length, TBLOCK):
            stop = start + TBLOCK
            seen = mask[:stop, start:stop]
            shifted, weights = weights_of(keys[:, :stop], scaled_q[:, start:stop], seen)
            grad_block = grads[:, start:stop]
            score_grad = (dot_tn(ones[:, :stop], grad_block) * shifted * seen).astype(bf16)
            query_grad[pl.ds(small, 16), start:stop] = (
                query_total[:, start:stop] + dot_nn(keys[:, :stop], score_grad) * 0.25
            )
            key_part = dot_nt(scaled_q[:, start:stop], score_grad)
            value_part = dot_nt(grad_block, weights.astype(bf16))
            if start > 0:
                key_grad[pl.ds(small, 16), :start] += key_part[:, :start]
                value_grad[rows, :start] += value_part[:, :start]
            key_grad[pl.ds(small, 16), start:stop] = key_part[:, start:]
            value_grad[rows, start:stop] = value_part[:, start:]
        return 0

    for number in range(GROUPS):
        part = pl.ds(number * span, span)

        @pl.when(place < planes - 1)
        def _():
            hand_on(number).wait_recv()

        @pl.when((place > 0) & (place < planes - 1))
        def _():
            message[part, :] = (
                state[part, :].astype(f32) + (cond_whole * cond_after) * later[part, :].astype(f32)
            ).astype(bf16)
            hand_on(number).start()

        lax.fori_loop(number * group, (number + 1) * group, head_local, 0)
        if number == 1:
            ff_share.gather_start()
    wide_own[48:64, :] = dot_nn(rank_grad_t, attended[...]).astype(bf16)
    wide_own[64:80, :] = dot_tn(rank_out[...], resid_grad[...].astype(bf16)).astype(bf16)
    wide_share.z_start()
    ff_share.relay()

    doc8 = jnp.broadcast_to(doc_row, (8, length))
    next8 = jnp.broadcast_to(next_docs, (8, 2))
    same_after = [(doc8 == sooner_by(doc8, offset, next8)).astype(f32)[0:1] for offset in (1, 2)]

    def head_finish(h, _):
        at = pl.multiple_of(h * PER_HEAD, PER_HEAD)
        rows = pl.ds(pl.multiple_of(h * VROWS, VROWS), VROWS)
        small = pl.ds(pl.multiple_of(h * 16, 16), 16)
        block = blocks[pl.ds(at, PER_HEAD), :]
        prior = halo[:, pl.ds(at, PER_HEAD)].astype(f32).T[32 : 32 + DV, 14:16]
        came = later[pl.ds(pl.multiple_of(h * FEATS, 16), FEATS), :]
        tap = taps[h]
        keys = block[16:32].astype(f32)
        key_feats = features(keys, keep_last, False)
        key_total = key_grad[small, :] + features_back(keys, dot_nn(came, marked[rows, :]) * keep_last, False)
        values = (value_grad[rows, :] + dot_tn(came, key_feats))[:DV]
        _, conv_out, gate_in, sigmoid = values_of(block, prior, tap, doc_row, prev_docs)
        conv_grad = values * gate_in * sigmoid
        proj_grad[pl.ds(at, 16), :] = query_grad[small, :].astype(bf16)
        proj_grad[pl.ds(at + 16, 16), :] = key_total.astype(bf16)
        proj_grad[pl.ds(at + 32, DV), :] = conv_backward(
            conv_grad, jnp.zeros((DV, 2), f32), tap, same_after
        ).astype(bf16)
        proj_grad[pl.ds(at + 32 + DV, DV), :] = (
            values * conv_out * sigmoid * (1.0 + gate_in * (1.0 - sigmoid))
        ).astype(bf16)
        conv_last[pl.ds(pl.multiple_of(h * DV, 16), DV), :] = conv_grad[:, length - 128 :]
        early = jnp.concatenate([conv_grad[:, :128], jnp.zeros((16, 128), f32)], axis=0).T
        halo_send[:, pl.ds(pl.multiple_of(h * 128, 128), 128)] = early[0:8]
        return 0

    for number in range(GROUPS):
        lax.fori_loop(number * group, (number + 1) * group, head_finish, 0)
        if number == 1:
            ff_share.relay_last()
    to_before = pltpu.make_async_remote_copy(
        src_ref=halo_send, dst_ref=halo_next, send_sem=halo_sems.at[0], recv_sem=halo_sems.at[1],
        device_id={"fsdp": me, "seq": (place + planes - 1) % planes}, device_id_type=MESH,
    )

    @pl.when(place > 0)
    def _():
        to_before.start()

    @pl.when(place == planes - 1)
    def _():
        halo_next[...] = jnp.zeros(halo_next.shape, f32)

    wide_share.gather_start()
    rank_in_t = rank_in[...].astype(f32).T.astype(bf16)

    @pl.when(place < planes - 1)
    def _():
        to_before.wait_recv()

    def head_end(h, total):
        at = pl.multiple_of(h * PER_HEAD, PER_HEAD)
        after = halo_next[:, pl.ds(pl.multiple_of(h * 128, 128), 128)].T[:DV, 0:2]
        last = conv_backward(
            conv_last[pl.ds(pl.multiple_of(h * DV, 16), DV), :], after, taps[h], [s[:, length - 128 :] for s in same_after]
        )
        proj_grad[pl.ds(at + 32, DV), length - 128 :] = last.astype(bf16)
        vg_terms[h, 0:16, 0:DV] = dot_nt(rank_in_t[32:48], proj_grad[pl.ds(at + 32, DV), :])
        vg_terms[h, 16:32, 0:DV] = dot_nt(rank_in_t[48:64], proj_grad[pl.ds(at + 32 + DV, DV), :])
        qk_terms[h, 0:16, 0:16] = dot_nt(rank_in_t[0:16], proj_grad[pl.ds(at, 16), :])
        qk_terms[h, 16:32, 0:16] = dot_nt(rank_in_t[16:32], proj_grad[pl.ds(at + 16, 16), :])
        return total + dot_nn(up_maps[:, pl.ds(at, PER_HEAD)], proj_grad[pl.ds(at, PER_HEAD), :])

    rank_in_grad_t = lax.fori_loop(0, HEAD_COUNT, head_end, jnp.zeros((64, length), f32)).astype(bf16)
    late_own[0:64, :] = dot_nn(rank_in_grad_t, hidden1[...]).astype(bf16)
    late_own[64:96, :] = jnp.concatenate([vg_terms[h, :, 0:DV] for h in range(HEAD_COUNT)], axis=1).astype(bf16)
    qk_rows = jnp.concatenate(
        [qk_terms[h, 0:16, 0:16] for h in range(HEAD_COUNT)]
        + [qk_terms[h, 16:32, 0:16] for h in range(HEAD_COUNT)]
        + [chosen[...] * (1.0 / planes), jnp.zeros((16, width - 512 - 128), f32)],
        axis=1,
    )
    late_own[96:112, :] = qk_rows.astype(bf16)
    late_share.z_start()
    wide_share.relay()

    for number in range(blocks_in):
        load_in(number).wait()
        rows = slice(number * step, (number + 1) * step)
        part = dot_nn(in_tile[number % 2], proj_grad[...]) + dot_tn(in_down[:, rows], rank_in_grad_t)
        input_grad[:, rows] = part.T
        if number + 2 < blocks_in:
            load_in(number + 2).start()
    wide_share.relay_last()
    late_share.gather_start()

    def finish_rows(rows):
        value = x[rows, :].astype(f32)
        root = row_root(value)
        normed = value * root
        scaled = input_grad[rows, :] * gain1[...]
        input_grad[rows, :] = resid_grad[rows, :] + root * (
            scaled - normed * jnp.mean(scaled * normed, -1, keepdims=True)
        )

    by_rows(length, finish_rows)
    late_share.relay()
    ff_share.finish()
    wide_share.finish()
    late_share.relay_last()
    late_share.finish()

    @pl.when(place > 0)
    def _():
        to_before.wait_send()
        for number in range(GROUPS):
            hand_on(number).wait_send()


def call_t(args, weights):
    f32, bf16 = jnp.float32, jnp.bfloat16
    length, width = args[0].shape
    count, planes = lax.axis_size("fsdp"), lax.axis_size("seq")
    columns = weights[0].shape[1]
    ff = args[-2].shape[1]
    whole = pl.BlockSpec(memory_space=pltpu.VMEM)
    anyplace = pl.BlockSpec(memory_space=pl.ANY)
    shapes = [(FF_ROWS, ff), (WIDE_ROWS, width), (LATE_ROWS, width)]
    shares = []
    for shape in shapes:
        shares += [pltpu.VMEM(shape, bf16), pltpu.VMEM((planes,) + shape, bf16), pltpu.VMEM(shape, bf16)]
    return pl.pallas_call(
        t_kernel,
        in_specs=[whole] * len(args) + [anyplace] * 2,
        out_specs=[whole] + [anyplace] * 3,
        out_shape=[jax.ShapeDtypeStruct((length, width), f32)]
        + [jax.ShapeDtypeStruct((count,) + shape, bf16) for shape in shapes],
        scratch_shapes=[
            pltpu.VMEM((width, width), bf16),
            pltpu.VMEM((2, 256, columns), bf16),
            pltpu.VMEM((width, length), bf16),
            pltpu.VMEM((width, length), bf16),
            pltpu.VMEM((HEAD_COUNT * VROWS, length), bf16),
            pltpu.VMEM((HEAD_COUNT * FEATS, VROWS), bf16),
            pltpu.VMEM((HEAD_COUNT * FEATS, VROWS), bf16),
            pltpu.VMEM((HEAD_COUNT * FEATS, VROWS), bf16),
            pltpu.VMEM((HEAD_COUNT * 16, length), f32),
            pltpu.VMEM((HEAD_COUNT * 16, length), f32),
            pltpu.VMEM((HEAD_COUNT * VROWS, length), f32),
            pltpu.VMEM((columns, length), bf16),
            pltpu.VMEM((width, 128), f32),
            pltpu.VMEM((8, HEAD_COUNT * 128), f32),
            pltpu.VMEM((8, HEAD_COUNT * 128), f32),
            pltpu.VMEM((HEAD_COUNT, 32, 128), f32),
            pltpu.VMEM((HEAD_COUNT, 32, 128), f32),
            pltpu.VMEM((length, length), f32),
        ]
        + shares
        + [
            pltpu.SemaphoreType.DMA((2, GROUPS)),
            pltpu.SemaphoreType.DMA((2,)),
            pltpu.SemaphoreType.DMA((3,)),
            pltpu.SemaphoreType.DMA((3, planes - 1)),
            pltpu.SemaphoreType.DMA((3, planes - 1)),
            pltpu.SemaphoreType.DMA((3, 8)),
            pltpu.SemaphoreType.DMA((3, 8)),
            pltpu.SemaphoreType.DMA((3,)),
        ],
        compiler_params=pltpu.CompilerParams(
            collective_id=2, has_side_effects=True, vmem_limit_bytes=62 * 1024 * 1024
        ),
    )(*args, *weights)


def place_kernel(where, ff, wide, late, in_down, qk_up, vg_up, out_down, out_up, gu_down, gu_up, ffd_down, ffd_up):
    f32 = jnp.float32
    gu_up[0] = ff[0, 0:32].astype(f32)
    ffd_down[0] = ff[0, 32:48].astype(f32)
    gu_down[0] = wide[0, 0:32].astype(f32)
    ffd_up[0] = wide[0, 32:48].astype(f32)
    out_down[0] = wide[0, 48:64].astype(f32)
    out_up[0] = wide[0, 64:80].astype(f32)
    in_down[0] = late[0, 0:64].astype(f32)
    vg_up[0] = late[0, 64:96].astype(f32)
    qk_up[0, 0:16] = late[0, 96:112, 0:256].astype(f32)
    qk_up[0, 16:32] = late[0, 96:112, 256:512].astype(f32)


def call_place(where, ff, wide, late):
    rows_ff, rows_w = ff.shape[2], wide.shape[2]
    outs = [(64, rows_w), (32, 256), (32, rows_w), (16, rows_w), (16, rows_w), (32, rows_w), (32, rows_ff), (16, rows_ff), (16, rows_w)]

    def block(shape):
        return pl.BlockSpec((1,) + shape, lambda a, where: (a, 0, 0))

    def picked(array):
        return pl.BlockSpec((1,) + array.shape[1:], lambda a, where: (where[a], 0, 0))

    return pl.pallas_call(
        place_kernel,
        grid_spec=pltpu.PrefetchScalarGridSpec(
            num_scalar_prefetch=1,
            grid=(ADAPTER_COUNT,),
            in_specs=[picked(ff), picked(wide), picked(late)],
            out_specs=[block(shape) for shape in outs],
        ),
        out_shape=[jax.ShapeDtypeStruct((ADAPTER_COUNT,) + shape, jnp.float32) for shape in outs],
        compiler_params=pltpu.CompilerParams(vmem_limit_bytes=62 * 1024 * 1024),
    )(where, ff, wide, late)


def pick_kernel(
    chosen, in_down_all, qk_all, vg_all, out_down_all, out_up_all, gu_down_all, gu_up_all, ffd_down_all, ffd_up_all,
    taps_all, docs, gain1, gain2,
    in_down, up_maps, out_down, out_up, gu_down, gu_up, ffd_down, ffd_up, taps, doc_row, doc_col, gain1_row, gain2_row, id_block,
):
    f32, bf16 = jnp.float32, jnp.bfloat16
    in_down[...] = in_down_all[0]
    out_down[...] = out_down_all[0]
    out_up[...] = out_up_all[0]
    gu_down[...] = gu_down_all[0]
    gu_up[0:16] = gu_up_all[0, 0]
    gu_up[16:32] = gu_up_all[0, 1]
    ffd_down[...] = ffd_down_all[0]
    ffd_up[...] = ffd_up_all[0]
    up_maps[...] = jnp.zeros(up_maps.shape, bf16)
    three = jnp.concatenate([taps_all[...], jnp.zeros((5, taps_all.shape[1]), f32)], axis=0)
    for h in range(HEAD_COUNT):
        at = h * PER_HEAD
        for n in range(2):
            up_maps[16 * n : 16 * n + 16, at + 16 * n : at + 16 * n + 16] = qk_all[0, n, :, 16 * h : 16 * h + 16]
            start = at + 32 + n * DV
            up_maps[32 + 16 * n : 48 + 16 * n, start : start + DV] = vg_all[0, n, :, DV * h : DV * h + DV]
        taps[h] = three[:, DV * h : DV * h + DV].T
    row = docs[...].astype(f32)
    doc_row[...] = row
    doc_col[...] = jnp.broadcast_to(row, (8, row.shape[1])).T[:, 0:1]
    gain1_row[...] = gain1[...].reshape(1, -1)
    gain2_row[...] = gain2[...].reshape(1, -1)
    id_block[...] = jnp.full(id_block.shape, chosen[0], jnp.int32).astype(f32)


def call_pick(chosen, tables, taps, docs, gain1, gain2):
    f32, bf16 = jnp.float32, jnp.bfloat16
    in_down, qk, vg, out_down, out_up, gu_down, gu_up, ffd_down, ffd_up = tables
    length = docs.shape[1]
    width, ff = out_up.shape[2], ffd_down.shape[2]

    def picked(table):
        zeros = (0,) * (table.ndim - 1)
        return pl.BlockSpec((1,) + table.shape[1:], lambda n, chosen: (chosen[0],) + zeros)

    def whole(shape):
        return pl.BlockSpec(shape, lambda n, chosen: (0,) * len(shape))

    outs = [
        ((64, width), bf16), ((64, HEAD_COUNT * PER_HEAD), bf16), ((16, width), bf16), ((16, width), bf16), ((32, width), bf16),
        ((32, ff), bf16), ((16, ff), bf16), ((16, width), bf16), ((HEAD_COUNT, DV, 8), f32), ((1, length), f32), ((length, 1), f32),
        ((1, width), f32), ((1, width), f32), ((16, 128), f32),
    ]
    rest = (taps, docs, gain1, gain2)
    return pl.pallas_call(
        pick_kernel,
        grid_spec=pltpu.PrefetchScalarGridSpec(
            num_scalar_prefetch=1,
            grid=(1,),
            in_specs=[picked(table) for table in tables] + [whole(array.shape) for array in rest],
            out_specs=[whole(shape) for shape, _ in outs],
        ),
        out_shape=[jax.ShapeDtypeStruct(shape, kind) for shape, kind in outs],
        compiler_params=pltpu.CompilerParams(vmem_limit_bytes=62 * 1024 * 1024),
    )(chosen, *tables, *rest)


def call_heads(kernel, length, ins, outs, scratch=()):
    def spec(shape, how):
        if how == "rows":
            return pl.BlockSpec((shape[0] // HEAD_COUNT,) + shape[1:], lambda h: (h,) + (0,) * (len(shape) - 1))
        if how == "cols":
            return pl.BlockSpec((shape[0], shape[1] // HEAD_COUNT), lambda h: (0, h))
        return pl.BlockSpec(shape, lambda h: (0,) * len(shape))

    return pl.pallas_call(
        kernel,
        grid=(HEAD_COUNT,),
        in_specs=[spec(a.shape, how) for a, how in ins],
        out_specs=[spec(s.shape, how) for s, how in outs],
        out_shape=[s for s, _ in outs],
        scratch_shapes=list(scratch),
        compiler_params=pltpu.CompilerParams(vmem_limit_bytes=48 * 1024 * 1024),
    )(*[a for a, _ in ins])


def shift_pairs(count, step):
    return [(i, i + step) for i in range(count) if 0 <= i + step < count]


def chain(own, whole, link, step):
    count = lax.axis_size("seq")
    pairs = shift_pairs(count, step)
    message = own
    for _ in range(count - 2):
        got = lax.ppermute(message, "seq", pairs)
        message = (own.astype(jnp.float32) + (whole * link) * got.astype(jnp.float32)).astype(jnp.bfloat16)
    got = lax.ppermute(message, "seq", pairs)
    return (got.astype(jnp.float32) * link).astype(jnp.bfloat16)


def product(spec, left, right):
    return jnp.einsum(spec, left, right, preferred_element_type=jnp.float32)


def rms_forward(value, gain):
    inv_root = lax.rsqrt(jnp.mean(value * value, -1, keepdims=True) + epsilon)
    normed = value * inv_root
    return (normed, inv_root, (normed * gain).astype(jnp.bfloat16))


def rms_backward(grad_hidden, normed, inv_root, gain):
    scaled = grad_hidden * gain
    return inv_root * (scaled - normed * jnp.mean(scaled * normed, -1, keepdims=True))


def up_by_head(querykey, valuegate):
    parts = [
        (querykey[0], 0, FEATURE_SIZE),
        (querykey[1], FEATURE_SIZE, FEATURE_SIZE),
        (valuegate[0], 2 * FEATURE_SIZE, DV),
        (valuegate[1], 2 * FEATURE_SIZE + DV, DV),
    ]
    rows = [
        jnp.pad(
            part.reshape(ADAPTER_RANK, HEAD_COUNT, size),
            ((0, 0), (0, 0), (at, PER_HEAD - at - size)),
        )
        for part, at, size in parts
    ]
    return jnp.concatenate(rows, axis=0).reshape(4 * ADAPTER_RANK, HEAD_COUNT * PER_HEAD)


def by_collectives(
    layer_input_rows,
    segments,
    sequence_adapter_index,
    output_gradient,
    mixer_norm_gain,
    feedforward_norm_gain,
    convolution_taps,
    mixer_input_weight,
    mixer_output_weight,
    gate_up_weight,
    down_weight,
    adapter_input_down,
    adapter_querykey_up,
    adapter_valuegate_up,
    adapter_output_down,
    adapter_output_up,
    adapter_gateup_down,
    adapter_gateup_up,
    adapter_feedforward_down,
    adapter_feedforward_up,
):
    batch, length, width = layer_input_rows.shape
    assert batch == 1
    seq_count = lax.axis_size("seq")
    ff = gate_up_weight.shape[1] // 2
    bf16, f32 = jnp.bfloat16, jnp.float32
    chosen = sequence_adapter_index[0, 0]

    def select(table):
        return lax.dynamic_index_in_dim(table, chosen, 0, keepdims=False)

    in_down = select(adapter_input_down.swapaxes(1, 2))
    up_maps = up_by_head(select(adapter_querykey_up), select(adapter_valuegate_up))
    out_down = select(adapter_output_down.swapaxes(1, 2))
    out_up = select(adapter_output_up)
    gu_down = select(adapter_gateup_down.swapaxes(1, 2))
    gu_up = select(adapter_gateup_up)
    ffd_down = select(adapter_feedforward_down.swapaxes(1, 2))
    ffd_up = select(adapter_feedforward_up)
    mixer_in, mixer_out, gate_up, down_w = (
        lax.all_gather(mixer_input_weight, "fsdp", axis=0, tiled=True),
        lax.all_gather(mixer_output_weight, "fsdp", axis=0, tiled=True),
        lax.all_gather(gate_up_weight, "fsdp", axis=0, tiled=True),
        lax.all_gather(down_weight, "fsdp", axis=0, tiled=True),
    )
    docs = segments.astype(f32)
    place = lax.axis_index("seq")
    edge = jnp.concatenate([docs[:, :1], docs[:, length - 2 :], jnp.zeros((1, 125), f32)], axis=1)
    before_edge = lax.ppermute(edge, "seq", shift_pairs(seq_count, 1))
    after_edge = lax.ppermute(edge, "seq", shift_pairs(seq_count, -1))
    prev_docs = jnp.where(place == 0, -1.0, before_edge[:, 1:3])
    next_doc = jnp.where(place == seq_count - 1, -1.0, after_edge[:, 0])
    link_before = (prev_docs[0, 1] == docs[0, 0]).astype(f32)
    link_after = (next_doc[0] == docs[0, length - 1]).astype(f32)
    whole = (docs[0, 0] == docs[0, length - 1]).astype(f32)
    prev_pad = jnp.pad(prev_docs, ((0, 0), (0, 126)))
    doc_col = docs.reshape(length, 1)
    taps = jnp.pad(convolution_taps.T.reshape(HEAD_COUNT, DV, 3), ((0, 0), (0, 0), (0, 5)))

    inputs_f = layer_input_rows[0].astype(f32)
    grad_out = output_gradient[0]
    normed1, root1, hidden1 = rms_forward(inputs_f, mixer_norm_gain)
    rank_in = product("td,rd->tr", hidden1, in_down).astype(bf16)
    projected = (
        product("td,de->te", hidden1, mixer_in) + product("tr,re->te", rank_in, up_maps)
    ).astype(bf16)
    halo = lax.ppermute(projected[length - 16 :], "seq", shift_pairs(seq_count, 1))
    mask = pltpu.VMEM((length, length), f32)
    heads = HEAD_COUNT
    blocks, values, sums, state = call_heads(
        f1_kernel,
        length,
        [(projected, "cols"), (halo, "cols"), (taps, "rows"), (docs, None), (doc_col, None), (prev_pad, None)],
        [
            (jax.ShapeDtypeStruct((heads * PER_HEAD, length), bf16), "rows"),
            (jax.ShapeDtypeStruct((heads * VROWS, length), bf16), "rows"),
            (jax.ShapeDtypeStruct((heads * VROWS, length), f32), "rows"),
            (jax.ShapeDtypeStruct((heads * FEATS, VROWS), bf16), "rows"),
        ],
        [mask],
    )
    carry = chain(state, whole, link_before, 1)
    attended_t, denominator = call_heads(
        f2_kernel,
        length,
        [(blocks, "rows"), (sums, "rows"), (carry, "rows"), (docs, None)],
        [
            (jax.ShapeDtypeStruct((heads * DV, length), bf16), "rows"),
            (jax.ShapeDtypeStruct((heads * 8, length), f32), "rows"),
        ],
    )
    attended = attended_t.T
    rank_out = product("td,rd->tr", attended, out_down).astype(bf16)
    resid = (
        inputs_f
        + product("td,de->te", attended, mixer_out)
        + product("tr,re->te", rank_out, out_up)
    )
    normed2, root2, hidden2 = rms_forward(resid, feedforward_norm_gain)
    rank_mlp = product("td,rd->tr", hidden2, gu_down).astype(bf16)
    rank_ffd_grad = product("te,re->tr", grad_out, ffd_up).astype(bf16)
    inner_grad = product("te,fe->tf", grad_out, down_w) + product("tr,rf->tf", rank_ffd_grad, ffd_down)
    gate_pre = product("td,de->te", hidden2, gate_up[:, :ff]) + product(
        "tr,re->te", rank_mlp[:, :ADAPTER_RANK], gu_up[0]
    )
    up_pre = product("td,de->te", hidden2, gate_up[:, ff:]) + product(
        "tr,re->te", rank_mlp[:, ADAPTER_RANK:], gu_up[1]
    )
    sigmoid = jax.nn.sigmoid(gate_pre)
    gate_val = gate_pre * sigmoid
    inner_act = (gate_val * up_pre).astype(bf16)
    gate_grad = (inner_grad * up_pre * (sigmoid * (1.0 + gate_pre * (1.0 - sigmoid)))).astype(bf16)
    up_grad = (inner_grad * gate_val).astype(bf16)
    rank_ffd = product("tf,rf->tr", inner_act, ffd_down).astype(bf16)
    output = (
        resid + product("tf,fe->te", inner_act, down_w) + product("tr,re->te", rank_ffd, ffd_up)
    ).astype(bf16)
    rank_mlp_grad = jnp.concatenate(
        [product("tf,rf->tr", gate_grad, gu_up[0]), product("tf,rf->tr", up_grad, gu_up[1])], -1
    ).astype(bf16)
    hidden2_grad = (
        product("tf,df->td", gate_grad, gate_up[:, :ff])
        + product("tf,df->td", up_grad, gate_up[:, ff:])
        + product("tr,rd->td", rank_mlp_grad, gu_down)
    )
    resid_grad = grad_out.astype(f32) + rms_backward(hidden2_grad, normed2, root2, feedforward_norm_gain)
    branch_grad = resid_grad.astype(bf16)
    rank_out_grad = product("te,re->tr", branch_grad, out_up).astype(bf16)
    attended_grad = (
        product("te,de->td", branch_grad, mixer_out) + product("tr,rd->td", rank_out_grad, out_down)
    ).astype(bf16)
    grad_t = attended_grad.T
    later, query_grad, key_grad, value_grad = call_heads(
        b1_kernel,
        length,
        [(blocks, "rows"), (values, "rows"), (grad_t, "rows"), (attended_t, "rows"), (denominator, "rows"), (carry, "rows"), (docs, None), (doc_col, None)],
        [
            (jax.ShapeDtypeStruct((heads * FEATS, VROWS), bf16), "rows"),
            (jax.ShapeDtypeStruct((heads * 16, length), f32), "rows"),
            (jax.ShapeDtypeStruct((heads * 16, length), f32), "rows"),
            (jax.ShapeDtypeStruct((heads * VROWS, length), f32), "rows"),
        ],
        [mask],
    )
    later = chain(later, whole, link_after, -1)
    projected_grad, first_conv, tail_grad = call_heads(
        b2_kernel,
        length,
        [(blocks, "rows"), (values, "rows"), (later, "rows"), (query_grad, "rows"), (key_grad, "rows"), (value_grad, "rows"), (halo, "cols"), (taps, "rows"), (docs, None), (prev_pad, None)],
        [
            (jax.ShapeDtypeStruct((length, heads * PER_HEAD), bf16), "cols"),
            (jax.ShapeDtypeStruct((16, heads * PER_HEAD), f32), "cols"),
            (jax.ShapeDtypeStruct((16, heads * PER_HEAD), f32), "cols"),
        ],
    )
    next_conv = lax.ppermute(first_conv[:2], "seq", shift_pairs(seq_count, -1))
    taps_row = jnp.pad(
        convolution_taps.reshape(3, heads, DV),
        ((0, 0), (0, 0), (2 * FEATURE_SIZE, PER_HEAD - 2 * FEATURE_SIZE - DV)),
    ).reshape(3, heads * PER_HEAD)
    after_docs = jnp.where(place == seq_count - 1, -1.0, after_edge[0, 0])
    link_1 = (after_docs == docs[0, length - 1]).astype(f32)
    link_2 = (after_docs == docs[0, length - 2]).astype(f32)
    second = (docs[0, 1] == docs[0, 0]).astype(f32)
    second_next = lax.ppermute(second, "seq", shift_pairs(seq_count, -1))
    extra_last = taps_row[1] * next_conv[0] * link_1 + taps_row[2] * next_conv[1] * link_1 * second_next
    extra_before = taps_row[2] * next_conv[0] * link_2
    extra = jnp.concatenate(
        [jnp.zeros((14, heads * PER_HEAD), f32), extra_before[None], extra_last[None]], axis=0
    )
    projected_grad = lax.dynamic_update_slice(
        projected_grad, (tail_grad + extra).astype(bf16), (length - 16, 0)
    )
    rank_in_grad = product("te,re->tr", projected_grad, up_maps).astype(bf16)
    hidden1_grad = product("te,de->td", projected_grad, mixer_in) + product(
        "tr,rd->td", rank_in_grad, in_down
    )
    input_grad = resid_grad + rms_backward(hidden1_grad, normed1, root1, mixer_norm_gain)

    wide = product("tr,te->re", rank_in, projected_grad).reshape(4, ADAPTER_RANK, heads, PER_HEAD)
    term_qk = jnp.stack(
        [wide[0, :, :, 0:16].reshape(ADAPTER_RANK, -1), wide[1, :, :, 16:32].reshape(ADAPTER_RANK, -1)]
    )
    term_vg = jnp.concatenate(
        [
            wide[2, :, :, 32 : 32 + DV].reshape(ADAPTER_RANK, -1),
            wide[3, :, :, 32 + DV :].reshape(ADAPTER_RANK, -1),
        ]
    )
    by_width = jnp.concatenate(
        [
            product("tr,td->rd", rank_in_grad, hidden1),
            term_vg,
            product("tr,td->rd", rank_out_grad, attended),
            product("tr,td->rd", rank_out, branch_grad),
            product("tr,td->rd", rank_mlp_grad, hidden2),
            product("tr,td->rd", rank_ffd, grad_out),
        ]
    )
    by_ff = jnp.concatenate(
        [
            product("tr,tf->rf", rank_mlp[:, :ADAPTER_RANK], gate_grad),
            product("tr,tf->rf", rank_mlp[:, ADAPTER_RANK:], up_grad),
            product("tr,tf->rf", rank_ffd_grad, inner_act),
        ]
    )
    by_rank = jnp.concatenate([term_qk.reshape(32, -1), jnp.full((16, 256), chosen.astype(f32) / seq_count)])
    by_width, by_ff, by_rank = spread(by_width, by_ff, by_rank)
    sequences = by_rank.shape[0]
    onehot = (by_rank[:, 32, 0][None, :] == jnp.arange(ADAPTER_COUNT, dtype=bf16)[:, None])

    if sequences == ADAPTER_COUNT:
        where = jnp.argmax(onehot, axis=1)

        def arrange(rows):
            return jnp.take(rows, where, axis=0).astype(f32)
    else:

        def arrange(rows):
            return jnp.einsum("as,s...->a...", onehot.astype(f32), rows.astype(f32), precision="highest")

    sizes = [64, 32, 16, 16, 32, 16]
    cut = [sum(sizes[:n]) for n in range(len(sizes) + 1)]
    widths = [arrange(by_width[:, cut[n] : cut[n + 1]]) for n in range(len(sizes))]
    return (
        output[None],
        input_grad[None],
        widths[0].swapaxes(1, 2),
        arrange(by_rank[:, :32]).reshape(ADAPTER_COUNT, 2, ADAPTER_RANK, -1),
        widths[1].reshape(ADAPTER_COUNT, 2, ADAPTER_RANK, width),
        widths[2].swapaxes(1, 2),
        widths[3],
        widths[4].swapaxes(1, 2),
        arrange(by_ff[:, :32]).reshape(ADAPTER_COUNT, 2, ADAPTER_RANK, ff),
        arrange(by_ff[:, 32:]).swapaxes(1, 2),
        widths[5],
    )


def by_kernels(
    layer_input_rows,
    segments,
    sequence_adapter_index,
    output_gradient,
    mixer_norm_gain,
    feedforward_norm_gain,
    convolution_taps,
    mixer_input_weight,
    mixer_output_weight,
    gate_up_weight,
    down_weight,
    adapter_input_down,
    adapter_querykey_up,
    adapter_valuegate_up,
    adapter_output_down,
    adapter_output_up,
    adapter_gateup_down,
    adapter_gateup_up,
    adapter_feedforward_down,
    adapter_feedforward_up,
):
    x, grad_out = layer_input_rows[0], output_gradient[0]
    width, ff = x.shape[1], adapter_gateup_up.shape[-1]
    tables = (
        adapter_input_down.swapaxes(1, 2), adapter_querykey_up, adapter_valuegate_up, adapter_output_down.swapaxes(1, 2),
        adapter_output_up, adapter_gateup_down.swapaxes(1, 2), adapter_gateup_up, adapter_feedforward_down.swapaxes(1, 2),
        adapter_feedforward_up,
    )
    *maps, taps, doc_row, doc_col, gain1, gain2, id_block = call_pick(
        sequence_adapter_index[0], tables, convolution_taps, segments, mixer_norm_gain, feedforward_norm_gain
    )
    in_down, up_maps, out_down, out_up = maps[:4]
    shards = (mixer_input_weight, mixer_output_weight, gate_up_weight, down_weight)
    mixer_in, mixer_out, _, _, output, *kept = call_m(x, grad_out, gain1, gain2, taps, doc_row, doc_col, maps, shards)
    *kept, next_docs = kept
    input_grad, all_ff, all_wide, all_late = call_t(
        (x, gain1, taps, doc_row, doc_col, next_docs, id_block, in_down, up_maps, out_down, out_up, *kept),
        (mixer_in, mixer_out),
    )
    chosen = all_late[:, 96, 512]
    where = jnp.argmax(chosen[None, :] == jnp.arange(ADAPTER_COUNT, dtype=jnp.bfloat16)[:, None], axis=1).astype(jnp.int32)
    in_down, qk_up, vg_up, out_down, out_up, gu_down, gu_up, ffd_down, ffd_up = call_place(where, all_ff, all_wide, all_late)
    return (
        output[None],
        input_grad[None],
        in_down.swapaxes(1, 2),
        qk_up.reshape(ADAPTER_COUNT, 2, ADAPTER_RANK, -1),
        vg_up.reshape(ADAPTER_COUNT, 2, ADAPTER_RANK, width),
        out_down.swapaxes(1, 2),
        out_up,
        gu_down.swapaxes(1, 2),
        gu_up.reshape(ADAPTER_COUNT, 2, ADAPTER_RANK, ff),
        ffd_down.swapaxes(1, 2),
        ffd_up,
    )


def spread(*terms):
    summed = lax.psum(terms, "seq")
    return [lax.all_gather(term.astype(jnp.bfloat16), "fsdp") for term in summed]


def solution(mesh):
    kernels = mesh.shape["fsdp"] == ADAPTER_COUNT and mesh.shape["seq"] == 4
    return jax.shard_map(
        by_kernels if kernels else by_collectives,
        mesh=mesh,
        in_specs=(
            P("fsdp", "seq", None),
            P("fsdp", "seq"),
            P("fsdp", None),
            P("fsdp", "seq", None),
            P(),
            P(),
            P(),
            P("fsdp", None),
            P("fsdp", None),
            P("fsdp", None),
            P("fsdp", None),
        )
        + (P(),) * 9,
        out_specs=(P("fsdp", "seq", None), P("fsdp", "seq", None)) + (P(),) * 9,
        check_vma=False,
    )
```

```python
import functools

import jax
import jax.numpy as jnp
from jax import lax
from jax.experimental import pallas as pl
from jax.experimental.pallas import tpu as pltpu
from jax.sharding import PartitionSpec as P

HEAD_COUNT = 16
FEATURE_SIZE = 16
DV = 112
ADAPTER_RANK = 16
ADAPTER_COUNT = 8
PER_HEAD = 2 * FEATURE_SIZE + 2 * DV
TBLOCK = 128

epsilon = 1e-05


FEATS = 176
VROWS = 128


def dot_nn(a, b):
    return lax.dot_general(a, b, (((1,), (0,)), ((), ())), preferred_element_type=jnp.float32)


def dot_nt(a, b):
    return lax.dot_general(a, b, (((1,), (1,)), ((), ())), preferred_element_type=jnp.float32)


def dot_tn(a, b):
    return lax.dot_general(a, b, (((0,), (0,)), ((), ())), preferred_element_type=jnp.float32)


def group_scale(shift):
    return 1.0 / 32.0 if shift in (0, 8) else 1.0 / 16.0


def cycle(rows, shift):
    if shift == 0:
        return rows
    return jnp.concatenate([rows[shift:], rows[:shift]], axis=0)


def features(rows, keep, scaled):
    length = rows.shape[1]
    rows_kept = rows * keep
    parts = []
    for shift in range(9):
        item = rows_kept * cycle(rows, shift)
        parts.append(item * group_scale(shift) if scaled else item)
    parts.append(rows_kept * 0.25 if scaled else rows_kept)
    first_row = lax.broadcasted_iota(jnp.int32, (16, length), 0) == 0
    parts.append(jnp.where(first_row, jnp.broadcast_to(keep, (16, length)), 0.0))
    return jnp.concatenate(parts, axis=0).astype(jnp.bfloat16)


def features_back(rows, grad, scaled):
    total = grad[144:160] * 0.25 if scaled else grad[144:160]
    for shift in range(9):
        item = grad[16 * shift : 16 * shift + 16]
        if scaled:
            item = item * group_scale(shift)
        total = total + item * cycle(rows, shift) + cycle(item * rows, (16 - shift) % 16)
    return total


def later_by(rows, offset, before):
    lane = lax.broadcasted_iota(jnp.int32, rows.shape, 1)
    moved = pltpu.roll(rows, offset, 1)
    if offset == 1:
        return jnp.where(lane == 0, before[:, 1:2], moved)
    return jnp.where(lane == 0, before[:, 0:1], jnp.where(lane == 1, before[:, 1:2], moved))


def sooner_by(rows, offset, after):
    length = rows.shape[1]
    lane = lax.broadcasted_iota(jnp.int32, rows.shape, 1)
    moved = pltpu.roll(rows, length - offset, 1)
    if offset == 1:
        return jnp.where(lane == length - 1, after[:, 0:1], moved)
    return jnp.where(
        lane == length - 2,
        after[:, 0:1],
        jnp.where(lane == length - 1, after[:, 1:2], moved),
    )


def conv_forward(signal, before, taps, same):
    total = taps[:, 0:1] * signal
    for offset in (1, 2):
        total = total + taps[:, offset : offset + 1] * later_by(signal, offset, before) * same[offset - 1]
    return total


def conv_backward(grad, after, taps, same):
    total = taps[:, 0:1] * grad
    for offset in (1, 2):
        total = total + taps[:, offset : offset + 1] * sooner_by(grad, offset, after) * same[offset - 1]
    return total


def add_ones(values):
    length = values.shape[1]
    row = lax.broadcasted_iota(jnp.int32, (VROWS - DV, length), 0)
    return jnp.concatenate(
        [values, jnp.where(row == 0, 1.0, 0.0).astype(jnp.bfloat16)], axis=0
    )


def weights_of(keys, queries, mask):
    shifted = dot_tn(keys, queries) + 1.0
    return shifted, (0.5 * shifted * shifted + 0.5) * mask


def mix_forward(tokens, before_tokens, taps, doc_row, prev_docs, mask_ref):
    length = tokens.shape[0]
    block = tokens.astype(jnp.float32).T.astype(jnp.bfloat16)
    before = before_tokens.astype(jnp.float32).T[2 * FEATURE_SIZE : 2 * FEATURE_SIZE + DV, 14:16]
    values, _, _, _ = values_of(block, before, taps, doc_row, prev_docs)
    marked = add_ones(values)
    keep_last = (doc_row == doc_row[:, length - 1 : length]).astype(jnp.float32)
    key_feats = features(block[16:32].astype(jnp.float32), keep_last, False)
    state = dot_nt(key_feats, marked)
    scaled_q = (block[0:16].astype(jnp.float32) * 0.25).astype(jnp.bfloat16)
    sums = []
    for start in range(0, length, TBLOCK):
        stop = start + TBLOCK
        _, weights = weights_of(
            block[16:32, :stop], scaled_q[:, start:stop], mask_ref[:stop, start:stop]
        )
        sums.append(dot_nn(marked[:, :stop], weights.astype(jnp.bfloat16)))
    return block, marked, jnp.concatenate(sums, axis=1), state


def values_of(block, before, taps, doc_row, prev_docs):
    length = block.shape[1]
    doc8 = jnp.broadcast_to(doc_row, (8, length))
    prev8 = jnp.broadcast_to(prev_docs, (8, 2))
    same = [
        (doc8 == later_by(doc8, offset, prev8)).astype(jnp.float32)[0:1] for offset in (1, 2)
    ]
    conv_in = block[32 : 32 + DV].astype(jnp.float32)
    gate_in = block[32 + DV :].astype(jnp.float32)
    conv_out = conv_forward(conv_in, before, taps, same)
    sigmoid = 1.0 / (1.0 + jnp.exp(-gate_in))
    values = (gate_in * sigmoid * conv_out).astype(jnp.bfloat16)
    return values, conv_out, gate_in, sigmoid


def fill_mask(mask_ref, doc_row, doc_col):
    shape = mask_ref.shape
    causal = lax.broadcasted_iota(jnp.int32, shape, 0) <= lax.broadcasted_iota(jnp.int32, shape, 1)
    mask_ref[...] = jnp.where(causal & (doc_col == doc_row), 1.0, 0.0)


def f1_kernel(p_ref, halo_ref, taps_ref, row_ref, col_ref, prev_ref, pt_ref, v_ref, o_ref, l_ref, mask_ref):
    @pl.when(pl.program_id(0) == 0)
    def _():
        fill_mask(mask_ref, row_ref[...], col_ref[...])

    block, marked, sums, state = mix_forward(
        p_ref[...], halo_ref[...], taps_ref[0], row_ref[...], prev_ref[:, 0:2], mask_ref
    )
    pt_ref[...] = block
    v_ref[...] = marked
    o_ref[...] = sums
    l_ref[...] = state.astype(jnp.bfloat16)


def mix_finish(block, sums, carry, doc_row):
    keep_first = (doc_row == doc_row[:, 0:1]).astype(jnp.float32)
    query_feats = features(block[0:16].astype(jnp.float32), keep_first, True)
    total = sums + dot_tn(carry, query_feats)
    denominator = total[DV : DV + 1]
    return (total[:DV] / denominator).astype(jnp.bfloat16), denominator


def f2_kernel(pt_ref, o_ref, s_ref, row_ref, att_ref, den_ref):
    attended, denominator = mix_finish(pt_ref[...], o_ref[...], s_ref[...], row_ref[...])
    att_ref[...] = attended
    den_ref[...] = jnp.broadcast_to(denominator, den_ref.shape)


def sum_grads(grad, attended, denominator):
    length = grad.shape[1]
    inverse = 1.0 / denominator
    grad_f = grad.astype(jnp.float32)
    dot_term = jnp.sum(grad_f * attended.astype(jnp.float32), axis=0, keepdims=True)
    row = lax.broadcasted_iota(jnp.int32, (VROWS - DV, length), 0)
    tail = jnp.where(row == 0, jnp.broadcast_to(-dot_term * inverse, row.shape), 0.0)
    return jnp.concatenate([grad_f * inverse, tail], axis=0).astype(jnp.bfloat16)


def mix_back_local(block, marked, sums_grad, carry, doc_row, mask_ref):
    length = block.shape[1]
    keys = block[16:32]
    queries = block[0:16].astype(jnp.float32)
    scaled_q = (queries * 0.25).astype(jnp.bfloat16)
    keep_first = (doc_row == doc_row[:, 0:1]).astype(jnp.float32)
    query_grad = features_back(queries, dot_nn(carry, sums_grad) * keep_first, True)
    key_grad = jnp.zeros((16, length), jnp.float32)
    value_grad = jnp.zeros((VROWS, length), jnp.float32)
    parts = []
    for start in range(0, length, TBLOCK):
        stop = start + TBLOCK
        mask = mask_ref[:stop, start:stop]
        shifted, weights = weights_of(keys[:, :stop], scaled_q[:, start:stop], mask)
        grad_block = sums_grad[:, start:stop]
        weight_grad = dot_tn(marked[:, :stop], grad_block)
        score_grad = (weight_grad * shifted * mask).astype(jnp.bfloat16)
        parts.append(dot_nn(keys[:, :stop], score_grad) * 0.25)
        key_part = dot_nt(scaled_q[:, start:stop], score_grad)
        value_part = dot_nt(grad_block, weights.astype(jnp.bfloat16))
        if stop < length:
            key_part = jnp.concatenate(
                [key_part, jnp.zeros((16, length - stop), jnp.float32)], axis=1
            )
            value_part = jnp.concatenate(
                [value_part, jnp.zeros((VROWS, length - stop), jnp.float32)], axis=1
            )
        key_grad = key_grad + key_part
        value_grad = value_grad + value_part
    query_grad = query_grad + jnp.concatenate(parts, axis=1)
    return query_grad, key_grad, value_grad


def b1_kernel(pt_ref, v_ref, g_ref, att_ref, den_ref, s_ref, row_ref, col_ref, d_ref, dq_ref, dk_ref, dv_ref, mask_ref):
    @pl.when(pl.program_id(0) == 0)
    def _():
        fill_mask(mask_ref, row_ref[...], col_ref[...])

    doc_row = row_ref[...]
    block = pt_ref[...]
    sums_grad = sum_grads(g_ref[...], att_ref[...], den_ref[0:1])
    keep_first = (doc_row == doc_row[:, 0:1]).astype(jnp.float32)
    query_feats = features(block[0:16].astype(jnp.float32), keep_first, True)
    d_ref[...] = dot_nt(query_feats, sums_grad).astype(jnp.bfloat16)
    dq, dk, dv = mix_back_local(block, v_ref[...], sums_grad, s_ref[...], doc_row, mask_ref)
    dq_ref[...] = dq
    dk_ref[...] = dk
    dv_ref[...] = dv


def mix_back_finish(block, marked, later_state, key_grad, value_grad, doc_row, before, taps, prev_docs):
    length = block.shape[1]
    keep_last = (doc_row == doc_row[:, length - 1 : length]).astype(jnp.float32)
    keys = block[16:32].astype(jnp.float32)
    key_feats = features(keys, keep_last, False)
    key_grad = key_grad + features_back(keys, dot_nn(later_state, marked) * keep_last, False)
    value_grad = (value_grad + dot_tn(later_state, key_feats))[:DV]
    _, conv_out, gate_in, sigmoid = values_of(block, before, taps, doc_row, prev_docs)
    gate_grad = value_grad * conv_out * sigmoid * (1.0 + gate_in * (1.0 - sigmoid))
    conv_grad = value_grad * gate_in * sigmoid
    return key_grad, gate_grad, conv_grad


def b2_kernel(pt_ref, v_ref, g_ref, dq_ref, dk_ref, dv_ref, halo_ref, taps_ref, row_ref, prev_ref, dp_ref, first_ref, tail_ref):
    doc_row = row_ref[...]
    length = doc_row.shape[1]
    taps = taps_ref[0]
    before = halo_ref[...].astype(jnp.float32).T[2 * FEATURE_SIZE : 2 * FEATURE_SIZE + DV, 14:16]
    key_grad, gate_grad, conv_grad = mix_back_finish(
        pt_ref[...], v_ref[...], g_ref[...], dk_ref[...], dv_ref[...], doc_row, before, taps, prev_ref[:, 0:2]
    )
    doc8 = jnp.broadcast_to(doc_row, (8, length))
    none = jnp.full((8, 2), -1.0, jnp.float32)
    same = [(doc8 == sooner_by(doc8, offset, none)).astype(jnp.float32)[0:1] for offset in (1, 2)]
    conv_in_grad = conv_backward(conv_grad, jnp.zeros((DV, 2), jnp.float32), taps, same)
    whole = jnp.concatenate([dq_ref[...], key_grad, conv_in_grad, gate_grad], axis=0).T
    dp_ref[...] = whole.astype(jnp.bfloat16)
    tail_ref[...] = whole[length - 16 :]
    pad = jnp.zeros((16, length), jnp.float32)
    conv_tokens = jnp.concatenate([jnp.zeros((32, length), jnp.float32), conv_grad, jnp.zeros((DV, length), jnp.float32)], axis=0).T
    first_ref[...] = conv_tokens[0:16]


MESH = pl.DeviceIdType.MESH
LAG = 2
FLAT = (7,9,11,13,15,17,37,38)
AHEAD = 4
UNIT = 512
TILE = 256
KEPT = (1, 2, 3, 5, 6, 8)
GROUPS = 4


class Gather:
    kinds = 9
    flat = FLAT

    def __init__(self, shards, wholes, sends, lands):
        self.shards, self.wholes = shards, wholes
        self.sends, self.lands = sends, lands
        i = lax.axis_index("fsdp")
        z = lax.axis_index("seq")
        odd = z % 2
        self.odd = odd
        by_y = 4 - 8 * (i // 4)
        by_x = 2 - 4 * ((i // 2) % 2)
        by_core = 1 - 2 * (i % 2)
        self.slot = [i, i + by_y, i + by_x + odd * by_y, i + by_x + (1 - odd) * by_y, i + by_core]
        self.flat_slot = [i, i + by_y, i + by_x, i + by_x + by_y, i + by_core]
        self.near = [
            {"fsdp": i + by_y, "seq": z},
            {"fsdp": i + by_x, "seq": z},
            {"fsdp": i, "seq": z + 1 - 2 * odd},
            {"fsdp": i + by_core, "seq": z},
        ]

    def is_flat(self, piece):
        return isinstance(piece[0], int) and piece[0] in self.flat

    def part(self, piece, slot, half=None):
        _, which, start, size = piece
        rows = self.shards[which].shape[0]
        first, count = (0, rows) if half is None else (half * (rows // 2), rows // 2)
        return self.wholes[which].at[
            pl.ds(pl.multiple_of(slot * rows + first, 16), count), pl.ds(start, size)
        ]

    def own_part(self, piece):
        _, which, start, size = piece
        return self.shards[which].at[:, pl.ds(start, size)]

    def copy(self, kind, piece, relay=False):
        source = [0, 0, 2, 0, 1, 2, 3, 4][kind] if kind < 8 else 2
        half = None
        link = min(kind, 3)
        slots = self.slot
        if self.is_flat(piece):
            slots = self.flat_slot
            if kind == 2:
                source, half, link = 1, 0, 1
            if kind == 8:
                source, half, link = 2, 1, 0
        if relay:
            source = 1
        slot = slots[source]
        return pltpu.make_async_remote_copy(
            src_ref=self.own_part(piece) if source == 0 else self.part(piece, slot, half),
            dst_ref=self.part(piece, slot, half),
            send_sem=self.sends.at[kind, piece[0]],
            recv_sem=self.lands.at[kind, piece[0]],
            device_id=self.near[link],
            device_id_type=MESH,
        )

    def first(self, piece):
        self.copy(0, piece).start()
        if self.is_flat(piece):
            self.copy(1, piece).start()
        else:

            @pl.when(self.odd == 0)
            def _():
                self.copy(1, piece).start()

        self.copy(3, piece).start()

    def from_y(self, piece):
        self.copy(0, piece).wait_recv()

        if not self.is_flat(piece):

            @pl.when(self.odd == 1)
            def _():
                self.copy(1, piece, relay=True).start()

        self.copy(4, piece).start()
        self.copy(3, piece).wait_recv()
        self.copy(7, piece).start()

    def from_x(self, piece):
        self.copy(1, piece).wait_recv()
        self.copy(2, piece).start()
        if self.is_flat(piece):
            self.copy(8, piece).start()
        self.copy(5, piece).start()

    def from_z(self, piece):
        self.copy(2, piece).wait_recv()
        if self.is_flat(piece):
            self.copy(8, piece).wait_recv()
        self.copy(6, piece).start()

    def ready(self, piece):
        for kind in (4, 5, 6, 7):
            self.copy(kind, piece).wait_recv()

    def finish(self, piece):
        for kind in range(self.kinds if self.is_flat(piece) else 8):
            self.copy(kind, piece).wait_send()


def cuts(which, width, size):
    return [(which, at, min(size, width - at)) for at in range(0, width, size)]


def early_cuts(columns, width):
    return cuts(0, columns, 512) + cuts(1, width, 512) + cuts(3, width, 256)


def by_rows(length, body, rows=64):
    def step(n, _):
        body(pl.ds(pl.multiple_of(n * rows, rows), rows))
        return 0

    lax.fori_loop(0, length // rows, step, 0)


def row_root(value):
    return lax.rsqrt(jnp.mean(value * value, -1, keepdims=True) + epsilon)


def m_kernel(
    x, g, gain1, gain2, taps, doc_row_ref, doc_col_ref, in_down, up_maps, out_down, out_up, gu_down, gu_up, ffd_down, ffd_up,
    a_in, b_in, c_in, d_in,
    a_all, b_all, c_all, d_all,
    out, blocks_out, marked_out, att_t_out, dens, carry_out, attended_out, resid_grad, hidden1_out, rank_in, rank_out, halo, term_ff, term_w, next_docs,
    blocks, marked, att_t, carry, attended, hidden1, keep_sems, first_docs,    halo_send, mask, sums, state, message, resid, hidden2, out_acc, grad_acc, a_tile, b_tile, g_tile, u_tile, d_tile, rank_acc,
    sends, lands, halo_sems, chain_sems, load_sems,
):
    length, width = x.shape
    ff = d_all.shape[0]
    units = -(-ff // UNIT)
    last_size = ff - (units - 1) * UNIT
    f32, bf16 = jnp.float32, jnp.bfloat16
    place = lax.axis_index("seq")
    planes = lax.axis_size("seq")
    me = lax.axis_index("fsdp")
    job = Gather([a_in, b_in, c_in, d_in], [a_all, b_all, c_all, d_all], sends, lands)

    early = early_cuts(a_in.shape[1], b_in.shape[1])
    early = [(number,) + piece for number, piece in enumerate(early)]
    base = len(early)
    mix_pieces = [p for p in early if p[1] == 0]
    out_pieces = [p for p in early if p[1] == 1]
    down_pieces = [p for p in early if p[1] == 3]
    total = base + 2 * units

    def late(number, size=UNIT):
        at = number - base
        start = (at // 2) * UNIT + (at % 2) * ff
        if not isinstance(start, int):
            start = pl.multiple_of(start, TILE)
        return (number, 2, start, size)

    def piece_at(number):
        if number < base:
            return early[number]
        return late(number, UNIT if number < total - 2 else last_size)

    def each_late(number, action):
        @pl.when(number < total - 2)
        def _():
            action(late(number))

        for end in (total - 2, total - 1):

            @pl.when(number == end)
            def _():
                action(piece_at(end))

    def pump(number):
        job.from_y(piece_at(number))
        if number + AHEAD < total:
            job.first(piece_at(number + AHEAD))
        if number >= LAG:
            job.from_x(piece_at(number - LAG))
        if number >= 2 * LAG:
            job.from_z(piece_at(number - 2 * LAG))

    barrier = pltpu.get_barrier_semaphore()
    for device in (job.near[0], job.near[1], job.near[3]):
        pl.semaphore_signal(barrier, inc=1, device_id=device, device_id_type=MESH)
    before = {"fsdp": me, "seq": (place + planes - 1) % planes}
    after = {"fsdp": me, "seq": (place + 1) % planes}

    @pl.when(place > 0)
    def _():
        pl.semaphore_signal(barrier, inc=1, device_id=before, device_id_type=MESH)

    @pl.when(place < planes - 1)
    def _():
        pl.semaphore_signal(barrier, inc=1, device_id=after, device_id_type=MESH)

    inner = (place > 0) & (place < planes - 1)

    @pl.when(inner)
    def _():
        pl.semaphore_wait(barrier, 5)

    @pl.when(jnp.logical_not(inner))
    def _():
        pl.semaphore_wait(barrier, 4)

    for piece in early[:AHEAD]:
        job.first(piece)
    first_docs[...] = jnp.broadcast_to(doc_col_ref[0:8, :], (8, 128))
    docs_back = pltpu.make_async_remote_copy(
        src_ref=first_docs, dst_ref=next_docs, send_sem=halo_sems.at[2], recv_sem=halo_sems.at[3], device_id=before, device_id_type=MESH
    )

    @pl.when(place > 0)
    def _():
        docs_back.start()

    @pl.when(place == planes - 1)
    def _():
        next_docs[...] = jnp.full(next_docs.shape, -1.0, f32)

    def norm1(rows):
        value = x[rows, :].astype(f32)
        hidden1[rows, :] = (value * row_root(value) * gain1[...]).astype(bf16)

    by_rows(length, norm1)
    rank_in[...] = dot_nt(hidden1[...], in_down[...]).astype(bf16)
    doc_row = doc_row_ref[...]
    fill_mask(mask, doc_row, doc_col_ref[...])
    cond_whole = (doc_row[:, 0:1] == doc_row[:, length - 1 : length]).astype(f32)

    def load_mix(number):
        _, _, start, size = mix_pieces[number]
        return pltpu.make_async_copy(
            a_all.at[:, pl.ds(start, size)], a_tile.at[number % 2], load_sems.at[number % 2]
        )

    def project(number):
        _, _, start, size = mix_pieces[number]
        load_mix(number).wait()
        projected = dot_nn(hidden1[...], a_tile[number % 2]) + dot_nn(rank_in[...], up_maps[:, start : start + size])
        halo_send[:, start : start + size] = projected[length - 16 :].astype(bf16)
        for at in range(0, size, PER_HEAD):
            blocks[start + at : start + at + PER_HEAD, :] = projected[:, at : at + PER_HEAD].T.astype(bf16)

    for number in range(2 * LAG):
        pump(number)
    for number, piece in enumerate(mix_pieces):
        pump(number + 2 * LAG)
        job.ready(piece)
        load_mix(number).start()
        if number > 0:
            project(number - 1)
    project(len(mix_pieces) - 1)
    columns = HEAD_COUNT * PER_HEAD
    halo_send[:, columns:] = jnp.broadcast_to(
        doc_col_ref[length - 16 :, :], (16, 128)
    ).astype(bf16)
    to_next = pltpu.make_async_remote_copy(
        src_ref=halo_send, dst_ref=halo, send_sem=halo_sems.at[0], recv_sem=halo_sems.at[1], device_id=after, device_id_type=MESH
    )

    @pl.when(place < planes - 1)
    def _():
        to_next.start()

    @pl.when(place == 0)
    def _():
        halo[:, :columns] = jnp.zeros((16, columns), bf16)
        halo[:, columns:] = jnp.full((16, 128), -1.0, bf16)

    next_piece = len(mix_pieces) + 2 * LAG

    def pump_next():
        nonlocal next_piece
        pump(next_piece)
        next_piece += 1

    pump_next()

    @pl.when(place > 0)
    def _():
        to_next.wait_recv()

    prev_docs = halo[:, columns:].astype(f32).T[0:1, 14:16]
    cond_before = (prev_docs[:, 1:2] == doc_row[:, 0:1]).astype(f32)
    keep_last = (doc_row == doc_row[:, length - 1 : length]).astype(f32)

    def head_state(h, _):
        at = pl.multiple_of(h * PER_HEAD, PER_HEAD)
        block = blocks[pl.ds(at, PER_HEAD), :]
        prior = halo[:, pl.ds(at, PER_HEAD)].astype(f32).T[32 : 32 + DV, 14:16]
        values, _, _, _ = values_of(block, prior, taps[h], doc_row, prev_docs)
        ones = add_ones(values)
        marked[pl.ds(pl.multiple_of(h * VROWS, VROWS), VROWS), :] = ones
        key_feats = features(block[16:32].astype(f32), keep_last, False)
        state[pl.ds(pl.multiple_of(h * FEATS, 16), FEATS), :] = dot_nt(key_feats, ones).astype(bf16)
        return 0

    group = HEAD_COUNT // GROUPS
    half = HEAD_COUNT // 2
    lax.fori_loop(0, half, head_state, 0)
    pump_next()
    lax.fori_loop(half, HEAD_COUNT, head_state, 0)
    pump_next()
    span = group * FEATS

    def hand_on(number):
        part = pl.ds(number * span, span)
        return pltpu.make_async_remote_copy(
            src_ref=message.at[part], dst_ref=carry.at[part],
            send_sem=chain_sems.at[0, number], recv_sem=chain_sems.at[1, number], device_id=after, device_id_type=MESH,
        )

    @pl.when(place == 0)
    def _():
        carry[...] = jnp.zeros(carry.shape, bf16)
        message[...] = state[...]
        for number in range(GROUPS):
            hand_on(number).start()

    def chain_slot(slot):
        for plane in range(1, 4):
            number = slot - plane + 1
            if 0 <= number < GROUPS:

                @pl.when(place == plane)
                def _():
                    part = pl.ds(number * span, span)
                    hand_on(number).wait_recv()
                    if plane < 3:
                        message[part, :] = (
                            state[part, :].astype(f32) + (cond_whole * cond_before) * carry[part, :].astype(f32)
                        ).astype(bf16)
                        hand_on(number).start()

    def head_local(h, _):
        at = pl.multiple_of(h * PER_HEAD, PER_HEAD)
        keys = blocks[pl.ds(at + 16, 16), :]
        scaled_q = (blocks[pl.ds(at, 16), :].astype(f32) * 0.25).astype(bf16)
        rows = pl.multiple_of(h * VROWS, VROWS)
        ones = marked[pl.ds(rows, VROWS), :]
        for start in range(0, length, TBLOCK):
            stop = start + TBLOCK
            _, weights = weights_of(keys[:, :stop], scaled_q[:, start:stop], mask[:stop, start:stop])
            sums[pl.ds(rows, VROWS), start:stop] = dot_nn(ones[:, :stop], weights.astype(bf16))
        return 0

    for number in range(GROUPS):
        lax.fori_loop(number * group, (number + 1) * group, head_local, 0)
        chain_slot(number)
        pump_next()

    keep_first = (doc_row == doc_row[:, 0:1]).astype(f32) * cond_before

    def head_finish(h, _):
        at = pl.multiple_of(h * PER_HEAD, PER_HEAD)
        rows = pl.multiple_of(h * VROWS, VROWS)
        query_feats = features(blocks[pl.ds(at, 16), :].astype(f32), keep_first, True)
        both = sums[pl.ds(rows, VROWS), :] + dot_tn(carry[pl.ds(pl.multiple_of(h * FEATS, 16), FEATS), :], query_feats)
        denominator = both[DV : DV + 1]
        att_t[pl.ds(pl.multiple_of(h * DV, 16), DV), :] = (both[:DV] / denominator).astype(bf16)
        dens[pl.ds(pl.multiple_of(h * 8, 8), 8), :] = jnp.broadcast_to(denominator, (8, length))
        return 0

    chain_slot(GROUPS)
    lax.fori_loop(0, half, head_finish, 0)
    pump_next()
    chain_slot(GROUPS + 1)
    lax.fori_loop(half, HEAD_COUNT, head_finish, 0)

    def turn(n, _):
        rows = pl.ds(pl.multiple_of(n * 128, 128), 128)
        attended[:, rows] = att_t[rows, :].astype(f32).T.astype(bf16)
        return 0

    lax.fori_loop(0, width // 128, turn, 0)
    keeps = [
        pltpu.make_async_copy(have, kept, keep_sems.at[n])
        for n, (have, kept) in enumerate(
            [
                (blocks, blocks_out), (marked, marked_out), (att_t, att_t_out),
                (carry, carry_out), (attended, attended_out), (hidden1, hidden1_out),
            ]
        )
    ]
    for keep in keeps:
        keep.start()
    pump_next()

    rank_out[...] = dot_nt(attended[...], out_down[...]).astype(bf16)
    for piece in out_pieces:
        job.ready(piece)
        _, _, start, size = piece
        load = pltpu.make_async_copy(b_all.at[:, pl.ds(start, size)], b_tile.at[:, :size], load_sems.at[0])
        load.start()
        load.wait()
        resid[:, start : start + size] = (
            x[:, start : start + size].astype(f32)
            + dot_nn(attended[...], b_tile[:, :size])
            + dot_nn(rank_out[...], out_up[:, start : start + size])
        )
    pump_next()

    def norm2(rows):
        value = resid[rows, :]
        hidden2[rows, :] = (value * row_root(value) * gain2[...]).astype(bf16)
        out_acc[rows, :] = value
        grad_acc[rows, :] = jnp.zeros(value.shape, f32)

    by_rows(length, norm2)
    rank_gate = dot_nt(hidden2[...], gu_down[0:16, :]).astype(bf16)
    rank_up = dot_nt(hidden2[...], gu_down[16:32, :]).astype(bf16)
    rank_ffd_grad = dot_nt(g[...], ffd_up[...]).astype(bf16)
    rank_gate_t = rank_gate.astype(f32).T.astype(bf16)
    rank_up_t = rank_up.astype(f32).T.astype(bf16)
    rank_ffd_grad_t = rank_ffd_grad.astype(f32).T.astype(bf16)
    rank_acc[...] = jnp.zeros(rank_acc.shape, f32)
    while next_piece < base + 2 * LAG:
        pump_next()
    for piece in down_pieces:
        job.ready(piece)

    def loads(unit, slot, size):
        start = unit * UNIT
        if not isinstance(start, int):
            start = pl.multiple_of(start, TILE)
        return [
            pltpu.make_async_copy(c_all.at[:, pl.ds(start, size)], g_tile.at[slot, :, :size], load_sems.at[slot]),
            pltpu.make_async_copy(c_all.at[:, pl.ds(ff + start, size)], u_tile.at[slot, :, :size], load_sems.at[2 + slot]),
            pltpu.make_async_copy(d_all.at[pl.ds(start, size), :], d_tile.at[slot, :size, :], load_sems.at[4 + slot]),
        ]

    def hidden_tile(unit, slot, part):
        inside = slice(part * TILE, (part + 1) * TILE)
        start = unit * UNIT + part * TILE
        cols = pl.ds(start if isinstance(start, int) else pl.multiple_of(start, TILE), TILE)
        gate_w, up_w, down_w = g_tile[slot, :, inside], u_tile[slot, :, inside], d_tile[slot, inside, :]
        gate_map, up_map, down_map = gu_up[0:16, cols], gu_up[16:32, cols], ffd_down[:, cols]
        gate_pre = dot_nn(hidden2[...], gate_w) + dot_nn(rank_gate, gate_map)
        up_pre = dot_nn(hidden2[...], up_w) + dot_nn(rank_up, up_map)
        inner_grad = dot_nt(g[...], down_w) + dot_nn(rank_ffd_grad, down_map)
        sigmoid = 1.0 / (1.0 + jnp.exp(-gate_pre))
        gate_val = gate_pre * sigmoid
        inner = (gate_val * up_pre).astype(bf16)
        gate_grad = (inner_grad * up_pre * (sigmoid * (1.0 + gate_pre * (1.0 - sigmoid)))).astype(bf16)
        up_grad = (inner_grad * gate_val).astype(bf16)
        out_acc[...] += dot_nn(inner, down_w)
        grad_acc[...] += dot_nt(gate_grad, gate_w) + dot_nt(up_grad, up_w)
        rank_acc[0] += dot_nt(inner, down_map)
        rank_acc[1] += dot_nt(gate_grad, gate_map)
        rank_acc[2] += dot_nt(up_grad, up_map)
        term_ff[0:16, cols] = dot_nn(rank_gate_t, gate_grad)
        term_ff[16:32, cols] = dot_nn(rank_up_t, up_grad)
        term_ff[32:48, cols] = dot_nn(rank_ffd_grad_t, inner)

    def ff_pump(number):
        each_late(number, job.from_y)
        each_late(number + AHEAD, job.first)
        each_late(number - LAG, job.from_x)
        each_late(number - 2 * LAG, job.from_z)

    def ff_ready(unit, slot, size, pieces):
        for piece in pieces:
            job.ready(piece)
        for load in loads(unit, slot, size):
            load.start()

    def ff_load_wait(unit, slot, size):
        for load in loads(unit, slot, size):
            load.wait()

    def ff_step(unit, _):
        slot = unit % 2
        ahead = base + 2 * unit + 2 * LAG
        ff_pump(ahead)

        @pl.when(unit >= 1)
        def _():
            ff_load_wait(unit - 1, 1 - slot, UNIT)
            hidden_tile(unit - 1, 1 - slot, 0)

        ff_pump(ahead + 1)
        ff_ready(unit, slot, UNIT, [late(base + 2 * unit), late(base + 2 * unit + 1)])

        @pl.when(unit >= 1)
        def _():
            hidden_tile(unit - 1, 1 - slot, 1)

        return 0

    lax.fori_loop(0, units - 1, ff_step, 0)
    final = units - 1
    job.from_z(piece_at(total - 2))
    job.from_z(piece_at(total - 1))
    ff_load_wait(final - 1, (final - 1) % 2, UNIT)
    hidden_tile(final - 1, (final - 1) % 2, 0)
    ff_ready(final, final % 2, last_size, [piece_at(total - 2), piece_at(total - 1)])
    hidden_tile(final - 1, (final - 1) % 2, 1)
    ff_load_wait(final, final % 2, last_size)
    for part in range(last_size // TILE):
        hidden_tile(final, final % 2, part)

    rank_ffd = rank_acc[0].astype(bf16)
    rank_gate_grad = rank_acc[1].astype(bf16)
    rank_up_grad = rank_acc[2].astype(bf16)
    out_acc[...] += dot_nn(rank_ffd, ffd_up[...])
    grad_acc[...] += dot_nn(rank_gate_grad, gu_down[0:16, :]) + dot_nn(rank_up_grad, gu_down[16:32, :])
    term_w[0:16, :] = dot_tn(rank_gate_grad, hidden2[...])
    term_w[16:32, :] = dot_tn(rank_up_grad, hidden2[...])
    term_w[32:48, :] = dot_tn(rank_ffd, g[...])

    def finish_rows(rows):
        out[rows, :] = out_acc[rows, :].astype(bf16)
        value = resid[rows, :]
        root = row_root(value)
        normed = value * root
        scaled = grad_acc[rows, :] * gain2[...]
        resid_grad[rows, :] = g[rows, :].astype(f32) + root * (
            scaled - normed * jnp.mean(scaled * normed, -1, keepdims=True)
        )

    by_rows(length, finish_rows)

    for keep in keeps:
        keep.wait()
    for piece in early:
        job.finish(piece)

    def finish_late(number, _):
        job.finish(late(number))
        return 0

    lax.fori_loop(base, total - 2, finish_late, 0)
    job.finish(piece_at(total - 2))
    job.finish(piece_at(total - 1))

    @pl.when(place > 0)
    def _():
        docs_back.wait_send()

    @pl.when(place < planes - 1)
    def _():
        docs_back.wait_recv()
        to_next.wait_send()
        for number in range(GROUPS):
            hand_on(number).wait_send()


def call_m(x, g, gain1, gain2, taps, doc_row, doc_col, maps, shards):
    length, width = x.shape
    f32, bf16 = jnp.float32, jnp.bfloat16
    count = lax.axis_size("fsdp")
    a, b, c, d = shards
    ff = d.shape[0] * count
    columns = a.shape[1]
    pieces = len(early_cuts(columns, width)) + 2 * -(-ff // UNIT)
    whole = pl.BlockSpec(memory_space=pltpu.VMEM)
    anyplace = pl.BlockSpec(memory_space=pl.ANY)
    vmem_out = [
        ((length, width), bf16),
        ((columns, length), bf16),
        ((HEAD_COUNT * VROWS, length), bf16),
        ((width, length), bf16),
        ((HEAD_COUNT * 8, length), f32),
        ((HEAD_COUNT * FEATS, VROWS), bf16),
        ((length, width), bf16),
        ((length, width), f32),
        ((length, width), bf16),
        ((length, 64), bf16),
        ((length, 16), bf16),
        ((16, columns + 128), bf16),
        ((48, ff), f32),
        ((48, width), f32),
        ((8, 128), f32),
    ]
    args = (x, g, gain1, gain2, taps, doc_row, doc_col) + tuple(maps)
    return pl.pallas_call(
        m_kernel,
        in_specs=[whole] * len(args) + [anyplace] * 4,
        out_specs=[anyplace] * 4 + [anyplace if n in KEPT else whole for n in range(len(vmem_out))],
        out_shape=[jax.ShapeDtypeStruct((t.shape[0] * count, t.shape[1]), t.dtype) for t in shards]
        + [jax.ShapeDtypeStruct(s, t) for s, t in vmem_out],
        scratch_shapes=[pltpu.VMEM(*vmem_out[n]) for n in KEPT]
        + [
            pltpu.SemaphoreType.DMA((len(KEPT),)),
            pltpu.VMEM((8, 128), f32),
            pltpu.VMEM((16, columns + 128), bf16),
            pltpu.VMEM((length, length), f32),
            pltpu.VMEM((HEAD_COUNT * VROWS, length), f32),
            pltpu.VMEM((HEAD_COUNT * FEATS, VROWS), bf16),
            pltpu.VMEM((HEAD_COUNT * FEATS, VROWS), bf16),
            pltpu.VMEM((length, width), f32),
            pltpu.VMEM((length, width), bf16),
            pltpu.VMEM((length, width), f32),
            pltpu.VMEM((length, width), f32),
            pltpu.VMEM((2, width, 512), bf16),
            pltpu.VMEM((width, 512), bf16),
            pltpu.VMEM((2, width, UNIT), bf16),
            pltpu.VMEM((2, width, UNIT), bf16),
            pltpu.VMEM((2, UNIT, width), bf16),
            pltpu.VMEM((3, length, 16), f32),
            pltpu.SemaphoreType.DMA((9, pieces)),
            pltpu.SemaphoreType.DMA((9, pieces)),
            pltpu.SemaphoreType.DMA((4,)),
            pltpu.SemaphoreType.DMA((2, GROUPS)),
            pltpu.SemaphoreType.DMA((6,)),
        ],
        compiler_params=pltpu.CompilerParams(
            collective_id=1, has_side_effects=True, vmem_limit_bytes=62 * 1024 * 1024
        ),
    )(*args, *shards)


def stripe_width(columns):
    return -(-columns // (4 * 128)) * 128


FETCHED = (0, 11, 12, 13, 15, 16, 18)


def to_stripes(own, rows, value):
    size = own.shape[2]
    columns = value.shape[1]
    for n in range(own.shape[0]):
        piece = value[:, n * size : min((n + 1) * size, columns)]
        if piece.shape[1] < size:
            piece = jnp.concatenate(
                [piece, jnp.zeros((piece.shape[0], size - piece.shape[1]), piece.dtype)], axis=1
            )
        own[n, rows, :] = piece


class Share:
    def __init__(self, number, own, slots, total, everyone, z_sends, z_lands, sends, lands, local):
        self.number, self.own, self.slots, self.total, self.everyone = number, own, slots, total, everyone
        self.z_sends, self.z_lands, self.sends, self.lands, self.local = z_sends, z_lands, sends, lands, local
        i = lax.axis_index("fsdp")
        self.place = lax.axis_index("seq")
        self.planes = lax.axis_size("seq")
        by_y = 4 - 8 * (i // 4)
        by_x = 2 - 4 * ((i // 2) % 2)
        by_core = 1 - 2 * (i % 2)
        self.slot = [i, i + by_y, i + by_x, i + by_x + by_y]
        self.near = [
            {"fsdp": i + by_y, "seq": self.place},
            {"fsdp": i + by_x, "seq": self.place},
            {"fsdp": i + by_core, "seq": self.place},
        ]
        self.me = i

    def z_copy(self, distance, summed):
        plane = (self.place + distance) % self.planes
        kind = 3 * summed + distance - 1
        return pltpu.make_async_remote_copy(
            src_ref=self.total.at[self.place] if summed else self.own.at[plane],
            dst_ref=(self.total if summed else self.slots).at[self.place],
            send_sem=self.z_sends.at[self.number, kind],
            recv_sem=self.z_lands.at[self.number, kind],
            device_id={"fsdp": self.me, "seq": plane},
            device_id_type=MESH,
        )

    def z_start(self):
        for distance in range(1, self.planes):
            self.z_copy(distance, 0).start()
        self.slots[self.place] = self.own[self.place]

    def z_sum(self):
        for distance in range(1, self.planes):
            self.z_copy(distance, 0).wait_recv()
        total = self.slots[0].astype(jnp.float32)
        for plane in range(1, self.planes):
            total = total + self.slots[plane].astype(jnp.float32)
        self.total[self.place] = total.astype(jnp.bfloat16)
        for distance in range(1, self.planes):
            self.z_copy(distance, 1).start()

    def copy(self, kind):
        half = self.planes // 2
        first, second, every = pl.ds(0, half), pl.ds(half, half), pl.ds(0, self.planes)
        where, slot, part = [
            (0, 0, every), (1, 0, every), (2, 0, every),
            (1, 1, first), (0, 2, second),
            (2, 1, every), (2, 2, every), (2, 3, every),
        ][kind]
        there = self.everyone.at[self.slot[slot], part]
        return pltpu.make_async_remote_copy(
            src_ref=self.total if slot == 0 else there,
            dst_ref=there,
            send_sem=self.sends.at[self.number, kind],
            recv_sem=self.lands.at[self.number, kind],
            device_id=self.near[where],
            device_id_type=MESH,
        )

    def keep(self):
        return pltpu.make_async_copy(self.total, self.everyone.at[self.slot[0]], self.local.at[self.number])

    def gather_start(self):
        for distance in range(1, self.planes):
            self.z_copy(distance, 1).wait_recv()
        for kind in (0, 1, 2):
            self.copy(kind).start()
        self.keep().start()

    def relay(self):
        self.copy(0).wait_recv()
        self.copy(3).start()
        self.copy(5).start()
        self.copy(1).wait_recv()
        self.copy(4).start()
        self.copy(6).start()

    def relay_last(self):
        self.copy(3).wait_recv()
        self.copy(4).wait_recv()
        self.copy(7).start()

    def finish(self):
        for kind in (2, 5, 6, 7):
            self.copy(kind).wait_recv()
        self.keep().wait()
        for kind in range(8):
            self.copy(kind).wait_send()
        for distance in range(1, self.planes):
            self.z_copy(distance, 0).wait_send()
            self.z_copy(distance, 1).wait_send()


def t_kernel(
    x_kept, gain1, taps, doc_row_ref, doc_col_ref, next_docs_ref, chosen, in_down, up_maps, out_down, out_up,
    blocks_kept, marked_kept, att_t_kept, dens, carry_kept, attended_kept, resid_grad, hidden1_kept, rank_in, rank_out, halo, term_ff, term_w,
    w_in, w_out,
    input_grad, all_ff, all_wide, all_down, all_up,
    x, blocks, marked, att_t, carry, attended, hidden1, fetch_sems, out_tile, in_tile, branch_t, grad_t, sums_grad, state, message, later, query_grad, key_grad, value_grad, proj_grad,
    conv_last, halo_send, halo_next, vg_terms, qk_terms, mask,
    ff_own, ff_slots, ff_total, wide_own, wide_slots, wide_total, down_own, down_slots, down_total, up_own, up_slots, up_total,
    chain_sems, halo_sems, load_sems, z_sends, z_lands, sends, lands, local,
):
    length, width = x.shape
    f32, bf16 = jnp.float32, jnp.bfloat16
    columns = HEAD_COUNT * PER_HEAD
    fetches = [
        pltpu.make_async_copy(kept, have, fetch_sems.at[n])
        for n, (kept, have) in enumerate(
            [
                (att_t_kept, att_t), (blocks_kept, blocks), (marked_kept, marked), (carry_kept, carry),
                (attended_kept, attended), (hidden1_kept, hidden1), (x_kept, x),
            ]
        )
    ]
    load_out = pltpu.make_async_copy(w_out, out_tile, load_sems.at[0])
    load_out.start()
    for fetch in fetches:
        fetch.start()
    place = lax.axis_index("seq")
    planes = lax.axis_size("seq")
    me = lax.axis_index("fsdp")
    sems = (z_sends, z_lands, sends, lands, local)
    ff_share = Share(0, ff_own, ff_slots, ff_total, all_ff, *sems)
    wide_share = Share(1, wide_own, wide_slots, wide_total, all_wide, *sems)
    down_share = Share(2, down_own, down_slots, down_total, all_down, *sems)
    up_share = Share(3, up_own, up_slots, up_total, all_up, *sems)

    barrier = pltpu.get_barrier_semaphore()
    others = [{"fsdp": me, "seq": (place + distance) % planes} for distance in range(1, planes)]
    for device in ff_share.near + others:
        pl.semaphore_signal(barrier, inc=1, device_id=device, device_id_type=MESH)
    pl.semaphore_wait(barrier, 3 + planes - 1)

    step = in_tile.shape[1]
    blocks_in = width // step

    def load_in(number):
        return pltpu.make_async_copy(
            w_in.at[pl.ds(number * step, step), :], in_tile.at[number % 2], load_sems.at[1 + number % 2]
        )

    load_in(0).start()
    load_in(1).start()
    to_stripes(ff_own, slice(0, 48), term_ff[...].astype(bf16))
    ff_share.z_start()
    to_stripes(wide_own, slice(0, 48), term_w[...].astype(bf16))

    doc_row = doc_row_ref[...]
    fill_mask(mask, doc_row, doc_col_ref[...])
    prev_docs = halo[:, columns:].astype(f32).T[0:1, 14:16]
    next_docs = next_docs_ref[...].T[0:1, 0:2]
    cond_before = (prev_docs[:, 1:2] == doc_row[:, 0:1]).astype(f32)
    cond_after = (next_docs[:, 0:1] == doc_row[:, length - 1 : length]).astype(f32)
    cond_whole = (doc_row[:, 0:1] == doc_row[:, length - 1 : length]).astype(f32)
    keep_first = (doc_row == doc_row[:, 0:1]).astype(f32)
    keep_first_link = keep_first * cond_before
    keep_last = (doc_row == doc_row[:, length - 1 : length]).astype(f32) * cond_after

    for start in range(0, width, 128):
        branch_t[start : start + 128, :] = resid_grad[:, start : start + 128].T.astype(bf16)
    rank_grad_t = dot_nn(out_up[...], branch_t[...]).astype(bf16)
    load_out.wait()
    for start in range(0, width, 256):
        grad_t[start : start + 256, :] = (
            dot_nn(out_tile[start : start + 256, :], branch_t[...])
            + dot_tn(out_down[:, start : start + 256], rank_grad_t)
        ).astype(bf16)
    group = HEAD_COUNT // GROUPS
    span = group * FEATS

    def head_state(h, _):
        at = pl.multiple_of(h * PER_HEAD, PER_HEAD)
        rows = pl.ds(pl.multiple_of(h * VROWS, VROWS), VROWS)
        own = pl.ds(pl.multiple_of(h * DV, 16), DV)
        grads = sum_grads(grad_t[own, :], att_t[own, :], dens[pl.ds(pl.multiple_of(h * 8, 8), 8), :][0:1])
        sums_grad[rows, :] = grads
        query_feats = features(blocks[pl.ds(at, 16), :].astype(f32), keep_first, True)
        state[pl.ds(pl.multiple_of(h * FEATS, 16), FEATS), :] = dot_nt(query_feats, grads).astype(bf16)
        return 0

    def hand_on(number):
        part = pl.ds(number * span, span)
        return pltpu.make_async_remote_copy(
            src_ref=message.at[part], dst_ref=later.at[part],
            send_sem=chain_sems.at[0, number], recv_sem=chain_sems.at[1, number],
            device_id={"fsdp": me, "seq": (place + planes - 1) % planes}, device_id_type=MESH,
        )

    @pl.when(place == planes - 1)
    def _():
        later[...] = jnp.zeros(later.shape, bf16)

    for fetch in fetches:
        fetch.wait()
    for number in range(GROUPS):
        part = pl.ds(number * span, span)
        lax.fori_loop(number * group, (number + 1) * group, head_state, 0)

        @pl.when(place == planes - 1)
        def _():
            message[part, :] = state[part, :]
            hand_on(number).start()

    def head_local(h, _):
        at = pl.multiple_of(h * PER_HEAD, PER_HEAD)
        rows = pl.ds(pl.multiple_of(h * VROWS, VROWS), VROWS)
        keys = blocks[pl.ds(at + 16, 16), :]
        queries = blocks[pl.ds(at, 16), :].astype(f32)
        scaled_q = (queries * 0.25).astype(bf16)
        ones = marked[rows, :]
        grads = sums_grad[rows, :]
        from_carry = dot_nn(carry[pl.ds(pl.multiple_of(h * FEATS, 16), FEATS), :], grads) * keep_first_link
        query_total = features_back(queries, from_carry, True)
        small = pl.multiple_of(h * 16, 16)
        for start in range(0, length, TBLOCK):
            stop = start + TBLOCK
            seen = mask[:stop, start:stop]
            shifted, weights = weights_of(keys[:, :stop], scaled_q[:, start:stop], seen)
            grad_block = grads[:, start:stop]
            score_grad = (dot_tn(ones[:, :stop], grad_block) * shifted * seen).astype(bf16)
            query_grad[pl.ds(small, 16), start:stop] = (
                query_total[:, start:stop] + dot_nn(keys[:, :stop], score_grad) * 0.25
            )
            key_part = dot_nt(scaled_q[:, start:stop], score_grad)
            value_part = dot_nt(grad_block, weights.astype(bf16))
            if start > 0:
                key_grad[pl.ds(small, 16), :start] += key_part[:, :start]
                value_grad[rows, :start] += value_part[:, :start]
            key_grad[pl.ds(small, 16), start:stop] = key_part[:, start:]
            value_grad[rows, start:stop] = value_part[:, start:]
        return 0

    def chain_slot(slot):
        for back in range(1, 4):
            number = slot - back + 1
            if 0 <= number < GROUPS:

                @pl.when(place == planes - 1 - back)
                def _():
                    part = pl.ds(number * span, span)
                    hand_on(number).wait_recv()
                    if back < 3:
                        message[part, :] = (
                            state[part, :].astype(f32) + (cond_whole * cond_after) * later[part, :].astype(f32)
                        ).astype(bf16)
                        hand_on(number).start()

    for number in range(GROUPS):
        lax.fori_loop(number * group, (number + 1) * group, head_local, 0)
        chain_slot(number)
    to_stripes(wide_own, slice(48, 64), dot_nn(rank_grad_t, attended[...]).astype(bf16))
    rank_out_t = rank_out[...].astype(f32).T.astype(bf16)
    to_stripes(wide_own, slice(64, 80), dot_nt(rank_out_t, branch_t[...]).astype(bf16))
    wide_share.z_start()
    chain_slot(GROUPS)
    ff_share.z_sum()
    chain_slot(GROUPS + 1)

    doc8 = jnp.broadcast_to(doc_row, (8, length))
    next8 = jnp.broadcast_to(next_docs, (8, 2))
    same_after = [(doc8 == sooner_by(doc8, offset, next8)).astype(f32)[0:1] for offset in (1, 2)]

    def head_finish(h, _):
        at = pl.multiple_of(h * PER_HEAD, PER_HEAD)
        rows = pl.ds(pl.multiple_of(h * VROWS, VROWS), VROWS)
        small = pl.ds(pl.multiple_of(h * 16, 16), 16)
        block = blocks[pl.ds(at, PER_HEAD), :]
        prior = halo[:, pl.ds(at, PER_HEAD)].astype(f32).T[32 : 32 + DV, 14:16]
        came = later[pl.ds(pl.multiple_of(h * FEATS, 16), FEATS), :]
        tap = taps[h]
        keys = block[16:32].astype(f32)
        key_feats = features(keys, keep_last, False)
        key_total = key_grad[small, :] + features_back(keys, dot_nn(came, marked[rows, :]) * keep_last, False)
        values = (value_grad[rows, :] + dot_tn(came, key_feats))[:DV]
        _, conv_out, gate_in, sigmoid = values_of(block, prior, tap, doc_row, prev_docs)
        conv_grad = values * gate_in * sigmoid
        proj_grad[pl.ds(at, 16), :] = query_grad[small, :].astype(bf16)
        proj_grad[pl.ds(at + 16, 16), :] = key_total.astype(bf16)
        proj_grad[pl.ds(at + 32, DV), :] = conv_backward(
            conv_grad, jnp.zeros((DV, 2), f32), tap, same_after
        ).astype(bf16)
        proj_grad[pl.ds(at + 32 + DV, DV), :] = (
            values * conv_out * sigmoid * (1.0 + gate_in * (1.0 - sigmoid))
        ).astype(bf16)
        conv_last[pl.ds(pl.multiple_of(h * DV, 16), DV), :] = conv_grad[:, length - 128 :]
        early = jnp.concatenate([conv_grad[:, :128], jnp.zeros((16, 128), f32)], axis=0).T
        halo_send[:, pl.ds(pl.multiple_of(h * 128, 128), 128)] = early[0:8]
        return 0

    for number in range(GROUPS):
        lax.fori_loop(number * group, (number + 1) * group, head_finish, 0)
        if number == 2:
            wide_share.z_sum()
    to_before = pltpu.make_async_remote_copy(
        src_ref=halo_send, dst_ref=halo_next, send_sem=halo_sems.at[0], recv_sem=halo_sems.at[1],
        device_id={"fsdp": me, "seq": (place + planes - 1) % planes}, device_id_type=MESH,
    )

    @pl.when(place > 0)
    def _():
        to_before.start()

    @pl.when(place == planes - 1)
    def _():
        halo_next[...] = jnp.zeros(halo_next.shape, f32)

    ff_share.gather_start()
    rank_in_t = rank_in[...].astype(f32).T.astype(bf16)

    @pl.when(place < planes - 1)
    def _():
        to_before.wait_recv()

    def head_end(h, total):
        at = pl.multiple_of(h * PER_HEAD, PER_HEAD)
        after = halo_next[:, pl.ds(pl.multiple_of(h * 128, 128), 128)].T[:DV, 0:2]
        last = conv_backward(
            conv_last[pl.ds(pl.multiple_of(h * DV, 16), DV), :], after, taps[h], [s[:, length - 128 :] for s in same_after]
        )
        proj_grad[pl.ds(at + 32, DV), length - 128 :] = last.astype(bf16)
        vg_terms[h, 0:16, 0:DV] = dot_nt(rank_in_t[32:48], proj_grad[pl.ds(at + 32, DV), :])
        vg_terms[h, 16:32, 0:DV] = dot_nt(rank_in_t[48:64], proj_grad[pl.ds(at + 32 + DV, DV), :])
        qk_terms[h, 0:16, 0:16] = dot_nt(rank_in_t[0:16], proj_grad[pl.ds(at, 16), :])
        qk_terms[h, 16:32, 0:16] = dot_nt(rank_in_t[16:32], proj_grad[pl.ds(at + 16, 16), :])
        return total + dot_nn(up_maps[:, pl.ds(at, PER_HEAD)], proj_grad[pl.ds(at, PER_HEAD), :])

    rank_in_grad_t = lax.fori_loop(0, HEAD_COUNT, head_end, jnp.zeros((64, length), f32)).astype(bf16)
    vg_rows = jnp.concatenate([vg_terms[h, :, 0:DV] for h in range(HEAD_COUNT)], axis=1).astype(bf16)
    up_own[0] = vg_rows[0:16]
    up_own[1] = vg_rows[16:32]
    qk_rows = jnp.concatenate(
        [qk_terms[h, 0:16, 0:16] for h in range(HEAD_COUNT)]
        + [qk_terms[h, 16:32, 0:16] for h in range(HEAD_COUNT)]
        + [chosen[...] * (1.0 / planes), jnp.zeros((16, width - 512 - 128), f32)],
        axis=1,
    )
    up_own[2] = qk_rows.astype(bf16)
    up_own[3] = jnp.zeros((16, width), bf16)
    up_share.z_start()
    in_terms = dot_nn(rank_in_grad_t, hidden1[...]).astype(bf16)
    for n in range(4):
        down_own[n] = in_terms[16 * n : 16 * n + 16]
    down_share.z_start()
    wide_share.gather_start()
    ff_share.relay()

    for number in range(blocks_in):
        load_in(number).wait()
        rows = slice(number * step, (number + 1) * step)
        part = dot_nn(in_tile[number % 2], proj_grad[...]) + dot_tn(in_down[:, rows], rank_in_grad_t)
        input_grad[:, rows] = part.T
        if number + 2 < blocks_in:
            load_in(number + 2).start()
        if number == blocks_in - 3:
            up_share.z_sum()
    down_share.z_sum()
    wide_share.relay()
    ff_share.relay_last()

    def finish_rows(rows):
        value = x[rows, :].astype(f32)
        root = row_root(value)
        normed = value * root
        scaled = input_grad[rows, :] * gain1[...]
        input_grad[rows, :] = resid_grad[rows, :] + root * (
            scaled - normed * jnp.mean(scaled * normed, -1, keepdims=True)
        )

    by_rows(length, finish_rows)
    up_share.gather_start()
    down_share.gather_start()
    wide_share.relay_last()
    up_share.relay()
    down_share.relay()
    ff_share.finish()
    wide_share.finish()
    up_share.relay_last()
    down_share.relay_last()
    up_share.finish()
    down_share.finish()

    @pl.when(place > 0)
    def _():
        to_before.wait_send()
        for number in range(GROUPS):
            hand_on(number).wait_send()


def call_t(args, weights):
    f32, bf16 = jnp.float32, jnp.bfloat16
    length, width = args[0].shape
    count, planes = lax.axis_size("fsdp"), lax.axis_size("seq")
    columns = weights[0].shape[1]
    ff = args[-2].shape[1]
    whole = pl.BlockSpec(memory_space=pltpu.VMEM)
    anyplace = pl.BlockSpec(memory_space=pl.ANY)
    shapes = [(planes, 48, stripe_width(ff)), (planes, 80, stripe_width(width)), (planes, 16, width), (planes, 16, width)]
    shares = []
    for shape in shapes:
        shares += [pltpu.VMEM(shape, bf16)] * 3
    return pl.pallas_call(
        t_kernel,
        in_specs=[anyplace if n in FETCHED else whole for n in range(len(args))] + [anyplace] * 2,
        out_specs=[whole] + [anyplace] * 4,
        out_shape=[jax.ShapeDtypeStruct((length, width), f32)]
        + [jax.ShapeDtypeStruct((count,) + shape, bf16) for shape in shapes],
        scratch_shapes=[pltpu.VMEM(args[n].shape, args[n].dtype) for n in FETCHED]
        + [
            pltpu.SemaphoreType.DMA((len(FETCHED),)),
            pltpu.VMEM((width, width), bf16),
            pltpu.VMEM((2, 256, columns), bf16),
            pltpu.VMEM((width, length), bf16),
            pltpu.VMEM((width, length), bf16),
            pltpu.VMEM((HEAD_COUNT * VROWS, length), bf16),
            pltpu.VMEM((HEAD_COUNT * FEATS, VROWS), bf16),
            pltpu.VMEM((HEAD_COUNT * FEATS, VROWS), bf16),
            pltpu.VMEM((HEAD_COUNT * FEATS, VROWS), bf16),
            pltpu.VMEM((HEAD_COUNT * 16, length), f32),
            pltpu.VMEM((HEAD_COUNT * 16, length), f32),
            pltpu.VMEM((HEAD_COUNT * VROWS, length), f32),
            pltpu.VMEM((columns, length), bf16),
            pltpu.VMEM((width, 128), f32),
            pltpu.VMEM((8, HEAD_COUNT * 128), f32),
            pltpu.VMEM((8, HEAD_COUNT * 128), f32),
            pltpu.VMEM((HEAD_COUNT, 32, 128), f32),
            pltpu.VMEM((HEAD_COUNT, 32, 128), f32),
            pltpu.VMEM((length, length), f32),
        ]
        + shares
        + [
            pltpu.SemaphoreType.DMA((2, GROUPS)),
            pltpu.SemaphoreType.DMA((2,)),
            pltpu.SemaphoreType.DMA((3,)),
            pltpu.SemaphoreType.DMA((4, 2 * (planes - 1))),
            pltpu.SemaphoreType.DMA((4, 2 * (planes - 1))),
            pltpu.SemaphoreType.DMA((4, 8)),
            pltpu.SemaphoreType.DMA((4, 8)),
            pltpu.SemaphoreType.DMA((4,)),
        ],
        compiler_params=pltpu.CompilerParams(
            collective_id=2, has_side_effects=True, vmem_limit_bytes=62 * 1024 * 1024
        ),
    )(*args, *weights)


def place_kernel(where, ff, wide, down, up, in_down, qk_up, vg_up, out_down, out_up, gu_down, gu_up, ffd_down, ffd_up):
    f32 = jnp.float32

    def unstripe(part, at, out):
        size, columns = part.shape[3], out.shape[2]
        for n in range(part.shape[1]):
            start, stop = n * size, min((n + 1) * size, columns)
            out[0, :, start:stop] = part[0, n, at : at + out.shape[1], 0 : stop - start].astype(f32)

    unstripe(ff, 0, gu_up)
    unstripe(ff, 32, ffd_down)
    unstripe(wide, 0, gu_down)
    unstripe(wide, 32, ffd_up)
    unstripe(wide, 48, out_down)
    unstripe(wide, 64, out_up)
    for n in range(4):
        in_down[0, 16 * n : 16 * n + 16] = down[0, n].astype(f32)
    vg_up[0, 0:16] = up[0, 0].astype(f32)
    vg_up[0, 16:32] = up[0, 1].astype(f32)
    qk_up[0, 0:16] = up[0, 2, :, 0:256].astype(f32)
    qk_up[0, 16:32] = up[0, 2, :, 256:512].astype(f32)


def call_place(where, parts, widths):
    rows_ff, rows_w = widths
    outs = [(64, rows_w), (32, 256), (32, rows_w), (16, rows_w), (16, rows_w), (32, rows_w), (32, rows_ff), (16, rows_ff), (16, rows_w)]

    def block(shape):
        return pl.BlockSpec((1,) + shape, lambda a, where: (a, 0, 0))

    def picked(array):
        return pl.BlockSpec((1,) + array.shape[1:], lambda a, where: (where[a], 0, 0, 0))

    return pl.pallas_call(
        place_kernel,
        grid_spec=pltpu.PrefetchScalarGridSpec(
            num_scalar_prefetch=1,
            grid=(ADAPTER_COUNT,),
            in_specs=[picked(part) for part in parts],
            out_specs=[block(shape) for shape in outs],
        ),
        out_shape=[jax.ShapeDtypeStruct((ADAPTER_COUNT,) + shape, jnp.float32) for shape in outs],
        compiler_params=pltpu.CompilerParams(vmem_limit_bytes=62 * 1024 * 1024),
    )(where, *parts)


def pick_kernel(
    chosen, in_down_all, qk_all, vg_all, out_down_all, out_up_all, gu_down_all, gu_up_all, ffd_down_all, ffd_up_all,
    taps_all, docs, gain1, gain2,
    in_down, up_maps, out_down, out_up, gu_down, gu_up, ffd_down, ffd_up, taps, doc_row, doc_col, gain1_row, gain2_row, id_block,
):
    f32, bf16 = jnp.float32, jnp.bfloat16
    in_down[...] = in_down_all[0]
    out_down[...] = out_down_all[0]
    out_up[...] = out_up_all[0]
    gu_down[...] = gu_down_all[0]
    gu_up[0:16] = gu_up_all[0, 0]
    gu_up[16:32] = gu_up_all[0, 1]
    ffd_down[...] = ffd_down_all[0]
    ffd_up[...] = ffd_up_all[0]
    up_maps[...] = jnp.zeros(up_maps.shape, bf16)
    three = jnp.concatenate([taps_all[...], jnp.zeros((5, taps_all.shape[1]), f32)], axis=0)
    for h in range(HEAD_COUNT):
        at = h * PER_HEAD
        for n in range(2):
            up_maps[16 * n : 16 * n + 16, at + 16 * n : at + 16 * n + 16] = qk_all[0, n, :, 16 * h : 16 * h + 16]
            start = at + 32 + n * DV
            up_maps[32 + 16 * n : 48 + 16 * n, start : start + DV] = vg_all[0, n, :, DV * h : DV * h + DV]
        taps[h] = three[:, DV * h : DV * h + DV].T
    row = docs[...].astype(f32)
    doc_row[...] = row
    doc_col[...] = jnp.broadcast_to(row, (8, row.shape[1])).T[:, 0:1]
    gain1_row[...] = gain1[...].reshape(1, -1)
    gain2_row[...] = gain2[...].reshape(1, -1)
    id_block[...] = jnp.full(id_block.shape, chosen[0], jnp.int32).astype(f32)


def call_pick(chosen, tables, taps, docs, gain1, gain2):
    f32, bf16 = jnp.float32, jnp.bfloat16
    in_down, qk, vg, out_down, out_up, gu_down, gu_up, ffd_down, ffd_up = tables
    length = docs.shape[1]
    width, ff = out_up.shape[2], ffd_down.shape[2]

    def picked(table):
        zeros = (0,) * (table.ndim - 1)
        return pl.BlockSpec((1,) + table.shape[1:], lambda n, chosen: (chosen[0],) + zeros)

    def whole(shape):
        return pl.BlockSpec(shape, lambda n, chosen: (0,) * len(shape))

    outs = [
        ((64, width), bf16), ((64, HEAD_COUNT * PER_HEAD), bf16), ((16, width), bf16), ((16, width), bf16), ((32, width), bf16),
        ((32, ff), bf16), ((16, ff), bf16), ((16, width), bf16), ((HEAD_COUNT, DV, 8), f32), ((1, length), f32), ((length, 1), f32),
        ((1, width), f32), ((1, width), f32), ((16, 128), f32),
    ]
    rest = (taps, docs, gain1, gain2)
    return pl.pallas_call(
        pick_kernel,
        grid_spec=pltpu.PrefetchScalarGridSpec(
            num_scalar_prefetch=1,
            grid=(1,),
            in_specs=[picked(table) for table in tables] + [whole(array.shape) for array in rest],
            out_specs=[whole(shape) for shape, _ in outs],
        ),
        out_shape=[jax.ShapeDtypeStruct(shape, kind) for shape, kind in outs],
        compiler_params=pltpu.CompilerParams(vmem_limit_bytes=62 * 1024 * 1024),
    )(chosen, *tables, *rest)


def call_heads(kernel, length, ins, outs, scratch=()):
    def spec(shape, how):
        if how == "rows":
            return pl.BlockSpec((shape[0] // HEAD_COUNT,) + shape[1:], lambda h: (h,) + (0,) * (len(shape) - 1))
        if how == "cols":
            return pl.BlockSpec((shape[0], shape[1] // HEAD_COUNT), lambda h: (0, h))
        return pl.BlockSpec(shape, lambda h: (0,) * len(shape))

    return pl.pallas_call(
        kernel,
        grid=(HEAD_COUNT,),
        in_specs=[spec(a.shape, how) for a, how in ins],
        out_specs=[spec(s.shape, how) for s, how in outs],
        out_shape=[s for s, _ in outs],
        scratch_shapes=list(scratch),
        compiler_params=pltpu.CompilerParams(vmem_limit_bytes=48 * 1024 * 1024),
    )(*[a for a, _ in ins])


def shift_pairs(count, step):
    return [(i, i + step) for i in range(count) if 0 <= i + step < count]


def chain(own, whole, link, step):
    count = lax.axis_size("seq")
    pairs = shift_pairs(count, step)
    message = own
    for _ in range(count - 2):
        got = lax.ppermute(message, "seq", pairs)
        message = (own.astype(jnp.float32) + (whole * link) * got.astype(jnp.float32)).astype(jnp.bfloat16)
    got = lax.ppermute(message, "seq", pairs)
    return (got.astype(jnp.float32) * link).astype(jnp.bfloat16)


def product(spec, left, right):
    return jnp.einsum(spec, left, right, preferred_element_type=jnp.float32)


def rms_forward(value, gain):
    inv_root = lax.rsqrt(jnp.mean(value * value, -1, keepdims=True) + epsilon)
    normed = value * inv_root
    return (normed, inv_root, (normed * gain).astype(jnp.bfloat16))


def rms_backward(grad_hidden, normed, inv_root, gain):
    scaled = grad_hidden * gain
    return inv_root * (scaled - normed * jnp.mean(scaled * normed, -1, keepdims=True))


def up_by_head(querykey, valuegate):
    parts = [
        (querykey[0], 0, FEATURE_SIZE),
        (querykey[1], FEATURE_SIZE, FEATURE_SIZE),
        (valuegate[0], 2 * FEATURE_SIZE, DV),
        (valuegate[1], 2 * FEATURE_SIZE + DV, DV),
    ]
    rows = [
        jnp.pad(
            part.reshape(ADAPTER_RANK, HEAD_COUNT, size),
            ((0, 0), (0, 0), (at, PER_HEAD - at - size)),
        )
        for part, at, size in parts
    ]
    return jnp.concatenate(rows, axis=0).reshape(4 * ADAPTER_RANK, HEAD_COUNT * PER_HEAD)


def by_collectives(
    layer_input_rows,
    segments,
    sequence_adapter_index,
    output_gradient,
    mixer_norm_gain,
    feedforward_norm_gain,
    convolution_taps,
    mixer_input_weight,
    mixer_output_weight,
    gate_up_weight,
    down_weight,
    adapter_input_down,
    adapter_querykey_up,
    adapter_valuegate_up,
    adapter_output_down,
    adapter_output_up,
    adapter_gateup_down,
    adapter_gateup_up,
    adapter_feedforward_down,
    adapter_feedforward_up,
):
    batch, length, width = layer_input_rows.shape
    assert batch == 1
    seq_count = lax.axis_size("seq")
    ff = gate_up_weight.shape[1] // 2
    bf16, f32 = jnp.bfloat16, jnp.float32
    chosen = sequence_adapter_index[0, 0]

    def select(table):
        return lax.dynamic_index_in_dim(table, chosen, 0, keepdims=False)

    in_down = select(adapter_input_down.swapaxes(1, 2))
    up_maps = up_by_head(select(adapter_querykey_up), select(adapter_valuegate_up))
    out_down = select(adapter_output_down.swapaxes(1, 2))
    out_up = select(adapter_output_up)
    gu_down = select(adapter_gateup_down.swapaxes(1, 2))
    gu_up = select(adapter_gateup_up)
    ffd_down = select(adapter_feedforward_down.swapaxes(1, 2))
    ffd_up = select(adapter_feedforward_up)
    mixer_in, mixer_out, gate_up, down_w = (
        lax.all_gather(mixer_input_weight, "fsdp", axis=0, tiled=True),
        lax.all_gather(mixer_output_weight, "fsdp", axis=0, tiled=True),
        lax.all_gather(gate_up_weight, "fsdp", axis=0, tiled=True),
        lax.all_gather(down_weight, "fsdp", axis=0, tiled=True),
    )
    docs = segments.astype(f32)
    place = lax.axis_index("seq")
    edge = jnp.concatenate([docs[:, :1], docs[:, length - 2 :], jnp.zeros((1, 125), f32)], axis=1)
    before_edge = lax.ppermute(edge, "seq", shift_pairs(seq_count, 1))
    after_edge = lax.ppermute(edge, "seq", shift_pairs(seq_count, -1))
    prev_docs = jnp.where(place == 0, -1.0, before_edge[:, 1:3])
    next_doc = jnp.where(place == seq_count - 1, -1.0, after_edge[:, 0])
    link_before = (prev_docs[0, 1] == docs[0, 0]).astype(f32)
    link_after = (next_doc[0] == docs[0, length - 1]).astype(f32)
    whole = (docs[0, 0] == docs[0, length - 1]).astype(f32)
    prev_pad = jnp.pad(prev_docs, ((0, 0), (0, 126)))
    doc_col = docs.reshape(length, 1)
    taps = jnp.pad(convolution_taps.T.reshape(HEAD_COUNT, DV, 3), ((0, 0), (0, 0), (0, 5)))

    inputs_f = layer_input_rows[0].astype(f32)
    grad_out = output_gradient[0]
    normed1, root1, hidden1 = rms_forward(inputs_f, mixer_norm_gain)
    rank_in = product("td,rd->tr", hidden1, in_down).astype(bf16)
    projected = (
        product("td,de->te", hidden1, mixer_in) + product("tr,re->te", rank_in, up_maps)
    ).astype(bf16)
    halo = lax.ppermute(projected[length - 16 :], "seq", shift_pairs(seq_count, 1))
    mask = pltpu.VMEM((length, length), f32)
    heads = HEAD_COUNT
    blocks, values, sums, state = call_heads(
        f1_kernel,
        length,
        [(projected, "cols"), (halo, "cols"), (taps, "rows"), (docs, None), (doc_col, None), (prev_pad, None)],
        [
            (jax.ShapeDtypeStruct((heads * PER_HEAD, length), bf16), "rows"),
            (jax.ShapeDtypeStruct((heads * VROWS, length), bf16), "rows"),
            (jax.ShapeDtypeStruct((heads * VROWS, length), f32), "rows"),
            (jax.ShapeDtypeStruct((heads * FEATS, VROWS), bf16), "rows"),
        ],
        [mask],
    )
    carry = chain(state, whole, link_before, 1)
    attended_t, denominator = call_heads(
        f2_kernel,
        length,
        [(blocks, "rows"), (sums, "rows"), (carry, "rows"), (docs, None)],
        [
            (jax.ShapeDtypeStruct((heads * DV, length), bf16), "rows"),
            (jax.ShapeDtypeStruct((heads * 8, length), f32), "rows"),
        ],
    )
    attended = attended_t.T
    rank_out = product("td,rd->tr", attended, out_down).astype(bf16)
    resid = (
        inputs_f
        + product("td,de->te", attended, mixer_out)
        + product("tr,re->te", rank_out, out_up)
    )
    normed2, root2, hidden2 = rms_forward(resid, feedforward_norm_gain)
    rank_mlp = product("td,rd->tr", hidden2, gu_down).astype(bf16)
    rank_ffd_grad = product("te,re->tr", grad_out, ffd_up).astype(bf16)
    inner_grad = product("te,fe->tf", grad_out, down_w) + product("tr,rf->tf", rank_ffd_grad, ffd_down)
    gate_pre = product("td,de->te", hidden2, gate_up[:, :ff]) + product(
        "tr,re->te", rank_mlp[:, :ADAPTER_RANK], gu_up[0]
    )
    up_pre = product("td,de->te", hidden2, gate_up[:, ff:]) + product(
        "tr,re->te", rank_mlp[:, ADAPTER_RANK:], gu_up[1]
    )
    sigmoid = jax.nn.sigmoid(gate_pre)
    gate_val = gate_pre * sigmoid
    inner_act = (gate_val * up_pre).astype(bf16)
    gate_grad = (inner_grad * up_pre * (sigmoid * (1.0 + gate_pre * (1.0 - sigmoid)))).astype(bf16)
    up_grad = (inner_grad * gate_val).astype(bf16)
    rank_ffd = product("tf,rf->tr", inner_act, ffd_down).astype(bf16)
    output = (
        resid + product("tf,fe->te", inner_act, down_w) + product("tr,re->te", rank_ffd, ffd_up)
    ).astype(bf16)
    rank_mlp_grad = jnp.concatenate(
        [product("tf,rf->tr", gate_grad, gu_up[0]), product("tf,rf->tr", up_grad, gu_up[1])], -1
    ).astype(bf16)
    hidden2_grad = (
        product("tf,df->td", gate_grad, gate_up[:, :ff])
        + product("tf,df->td", up_grad, gate_up[:, ff:])
        + product("tr,rd->td", rank_mlp_grad, gu_down)
    )
    resid_grad = grad_out.astype(f32) + rms_backward(hidden2_grad, normed2, root2, feedforward_norm_gain)
    branch_grad = resid_grad.astype(bf16)
    rank_out_grad = product("te,re->tr", branch_grad, out_up).astype(bf16)
    attended_grad = (
        product("te,de->td", branch_grad, mixer_out) + product("tr,rd->td", rank_out_grad, out_down)
    ).astype(bf16)
    grad_t = attended_grad.T
    later, query_grad, key_grad, value_grad = call_heads(
        b1_kernel,
        length,
        [(blocks, "rows"), (values, "rows"), (grad_t, "rows"), (attended_t, "rows"), (denominator, "rows"), (carry, "rows"), (docs, None), (doc_col, None)],
        [
            (jax.ShapeDtypeStruct((heads * FEATS, VROWS), bf16), "rows"),
            (jax.ShapeDtypeStruct((heads * 16, length), f32), "rows"),
            (jax.ShapeDtypeStruct((heads * 16, length), f32), "rows"),
            (jax.ShapeDtypeStruct((heads * VROWS, length), f32), "rows"),
        ],
        [mask],
    )
    later = chain(later, whole, link_after, -1)
    projected_grad, first_conv, tail_grad = call_heads(
        b2_kernel,
        length,
        [(blocks, "rows"), (values, "rows"), (later, "rows"), (query_grad, "rows"), (key_grad, "rows"), (value_grad, "rows"), (halo, "cols"), (taps, "rows"), (docs, None), (prev_pad, None)],
        [
            (jax.ShapeDtypeStruct((length, heads * PER_HEAD), bf16), "cols"),
            (jax.ShapeDtypeStruct((16, heads * PER_HEAD), f32), "cols"),
            (jax.ShapeDtypeStruct((16, heads * PER_HEAD), f32), "cols"),
        ],
    )
    next_conv = lax.ppermute(first_conv[:2], "seq", shift_pairs(seq_count, -1))
    taps_row = jnp.pad(
        convolution_taps.reshape(3, heads, DV),
        ((0, 0), (0, 0), (2 * FEATURE_SIZE, PER_HEAD - 2 * FEATURE_SIZE - DV)),
    ).reshape(3, heads * PER_HEAD)
    after_docs = jnp.where(place == seq_count - 1, -1.0, after_edge[0, 0])
    link_1 = (after_docs == docs[0, length - 1]).astype(f32)
    link_2 = (after_docs == docs[0, length - 2]).astype(f32)
    second = (docs[0, 1] == docs[0, 0]).astype(f32)
    second_next = lax.ppermute(second, "seq", shift_pairs(seq_count, -1))
    extra_last = taps_row[1] * next_conv[0] * link_1 + taps_row[2] * next_conv[1] * link_1 * second_next
    extra_before = taps_row[2] * next_conv[0] * link_2
    extra = jnp.concatenate(
        [jnp.zeros((14, heads * PER_HEAD), f32), extra_before[None], extra_last[None]], axis=0
    )
    projected_grad = lax.dynamic_update_slice(
        projected_grad, (tail_grad + extra).astype(bf16), (length - 16, 0)
    )
    rank_in_grad = product("te,re->tr", projected_grad, up_maps).astype(bf16)
    hidden1_grad = product("te,de->td", projected_grad, mixer_in) + product(
        "tr,rd->td", rank_in_grad, in_down
    )
    input_grad = resid_grad + rms_backward(hidden1_grad, normed1, root1, mixer_norm_gain)

    wide = product("tr,te->re", rank_in, projected_grad).reshape(4, ADAPTER_RANK, heads, PER_HEAD)
    term_qk = jnp.stack(
        [wide[0, :, :, 0:16].reshape(ADAPTER_RANK, -1), wide[1, :, :, 16:32].reshape(ADAPTER_RANK, -1)]
    )
    term_vg = jnp.concatenate(
        [
            wide[2, :, :, 32 : 32 + DV].reshape(ADAPTER_RANK, -1),
            wide[3, :, :, 32 + DV :].reshape(ADAPTER_RANK, -1),
        ]
    )
    by_width = jnp.concatenate(
        [
            product("tr,td->rd", rank_in_grad, hidden1),
            term_vg,
            product("tr,td->rd", rank_out_grad, attended),
            product("tr,td->rd", rank_out, branch_grad),
            product("tr,td->rd", rank_mlp_grad, hidden2),
            product("tr,td->rd", rank_ffd, grad_out),
        ]
    )
    by_ff = jnp.concatenate(
        [
            product("tr,tf->rf", rank_mlp[:, :ADAPTER_RANK], gate_grad),
            product("tr,tf->rf", rank_mlp[:, ADAPTER_RANK:], up_grad),
            product("tr,tf->rf", rank_ffd_grad, inner_act),
        ]
    )
    by_rank = jnp.concatenate([term_qk.reshape(32, -1), jnp.full((16, 256), chosen.astype(f32) / seq_count)])
    by_width, by_ff, by_rank = spread(by_width, by_ff, by_rank)
    sequences = by_rank.shape[0]
    onehot = (by_rank[:, 32, 0][None, :] == jnp.arange(ADAPTER_COUNT, dtype=bf16)[:, None])

    if sequences == ADAPTER_COUNT:
        where = jnp.argmax(onehot, axis=1)

        def arrange(rows):
            return jnp.take(rows, where, axis=0).astype(f32)
    else:

        def arrange(rows):
            return jnp.einsum("as,s...->a...", onehot.astype(f32), rows.astype(f32), precision="highest")

    sizes = [64, 32, 16, 16, 32, 16]
    cut = [sum(sizes[:n]) for n in range(len(sizes) + 1)]
    widths = [arrange(by_width[:, cut[n] : cut[n + 1]]) for n in range(len(sizes))]
    return (
        output[None],
        input_grad[None],
        widths[0].swapaxes(1, 2),
        arrange(by_rank[:, :32]).reshape(ADAPTER_COUNT, 2, ADAPTER_RANK, -1),
        widths[1].reshape(ADAPTER_COUNT, 2, ADAPTER_RANK, width),
        widths[2].swapaxes(1, 2),
        widths[3],
        widths[4].swapaxes(1, 2),
        arrange(by_ff[:, :32]).reshape(ADAPTER_COUNT, 2, ADAPTER_RANK, ff),
        arrange(by_ff[:, 32:]).swapaxes(1, 2),
        widths[5],
    )


def by_kernels(
    layer_input_rows,
    segments,
    sequence_adapter_index,
    output_gradient,
    mixer_norm_gain,
    feedforward_norm_gain,
    convolution_taps,
    mixer_input_weight,
    mixer_output_weight,
    gate_up_weight,
    down_weight,
    adapter_input_down,
    adapter_querykey_up,
    adapter_valuegate_up,
    adapter_output_down,
    adapter_output_up,
    adapter_gateup_down,
    adapter_gateup_up,
    adapter_feedforward_down,
    adapter_feedforward_up,
):
    x, grad_out = layer_input_rows[0], output_gradient[0]
    width, ff = x.shape[1], adapter_gateup_up.shape[-1]
    tables = (
        adapter_input_down.swapaxes(1, 2), adapter_querykey_up, adapter_valuegate_up, adapter_output_down.swapaxes(1, 2),
        adapter_output_up, adapter_gateup_down.swapaxes(1, 2), adapter_gateup_up, adapter_feedforward_down.swapaxes(1, 2),
        adapter_feedforward_up,
    )
    *maps, taps, doc_row, doc_col, gain1, gain2, id_block = call_pick(
        sequence_adapter_index[0], tables, convolution_taps, segments, mixer_norm_gain, feedforward_norm_gain
    )
    in_down, up_maps, out_down, out_up = maps[:4]
    shards = (mixer_input_weight, mixer_output_weight, gate_up_weight, down_weight)
    mixer_in, mixer_out, _, _, output, *kept = call_m(x, grad_out, gain1, gain2, taps, doc_row, doc_col, maps, shards)
    *kept, next_docs = kept
    input_grad, *parts = call_t(
        (x, gain1, taps, doc_row, doc_col, next_docs, id_block, in_down, up_maps, out_down, out_up, *kept),
        (mixer_in, mixer_out),
    )
    chosen = parts[3][:, 2, 0, 512]
    where = jnp.argmax(chosen[None, :] == jnp.arange(ADAPTER_COUNT, dtype=jnp.bfloat16)[:, None], axis=1).astype(jnp.int32)
    in_down, qk_up, vg_up, out_down, out_up, gu_down, gu_up, ffd_down, ffd_up = call_place(
        where, parts, (ff, width)
    )
    return (
        output[None],
        input_grad[None],
        in_down.swapaxes(1, 2),
        qk_up.reshape(ADAPTER_COUNT, 2, ADAPTER_RANK, -1),
        vg_up.reshape(ADAPTER_COUNT, 2, ADAPTER_RANK, width),
        out_down.swapaxes(1, 2),
        out_up,
        gu_down.swapaxes(1, 2),
        gu_up.reshape(ADAPTER_COUNT, 2, ADAPTER_RANK, ff),
        ffd_down.swapaxes(1, 2),
        ffd_up,
    )


def spread(*terms):
    summed = lax.psum(terms, "seq")
    return [lax.all_gather(term.astype(jnp.bfloat16), "fsdp") for term in summed]


def solution(mesh):
    kernels = mesh.shape["fsdp"] == ADAPTER_COUNT and mesh.shape["seq"] == 4
    return jax.shard_map(
        by_kernels if kernels else by_collectives,
        mesh=mesh,
        in_specs=(
            P("fsdp", "seq", None),
            P("fsdp", "seq"),
            P("fsdp", None),
            P("fsdp", "seq", None),
            P(),
            P(),
            P(),
            P("fsdp", None),
            P("fsdp", None),
            P("fsdp", None),
            P("fsdp", None),
        )
        + (P(),) * 9,
        out_specs=(P("fsdp", "seq", None), P("fsdp", "seq", None)) + (P(),) * 9,
        check_vma=False,
    )
```

```python
import functools

import jax
import jax.numpy as jnp
from jax import lax
from jax.experimental import pallas as pl
from jax.experimental.pallas import tpu as pltpu
from jax.sharding import PartitionSpec as P

HEAD_COUNT = 16
FEATURE_SIZE = 16
DV = 112
ADAPTER_RANK = 16
ADAPTER_COUNT = 8
PER_HEAD = 2 * FEATURE_SIZE + 2 * DV
TBLOCK = 128

epsilon = 1e-05


FEATS = 176
VROWS = 128


def dot_nn(a, b):
    return lax.dot_general(a, b, (((1,), (0,)), ((), ())), preferred_element_type=jnp.float32)


def dot_nt(a, b):
    return lax.dot_general(a, b, (((1,), (1,)), ((), ())), preferred_element_type=jnp.float32)


def dot_tn(a, b):
    return lax.dot_general(a, b, (((0,), (0,)), ((), ())), preferred_element_type=jnp.float32)


def group_scale(shift):
    return 1.0 / 32.0 if shift in (0, 8) else 1.0 / 16.0


def cycle(rows, shift):
    if shift == 0:
        return rows
    return jnp.concatenate([rows[shift:], rows[:shift]], axis=0)


def features(rows, keep, scaled):
    length = rows.shape[1]
    rows_kept = rows * keep
    parts = []
    for shift in range(9):
        item = rows_kept * cycle(rows, shift)
        parts.append(item * group_scale(shift) if scaled else item)
    parts.append(rows_kept * 0.25 if scaled else rows_kept)
    first_row = lax.broadcasted_iota(jnp.int32, (16, length), 0) == 0
    parts.append(jnp.where(first_row, jnp.broadcast_to(keep, (16, length)), 0.0))
    return jnp.concatenate(parts, axis=0).astype(jnp.bfloat16)


def features_back(rows, grad, scaled):
    total = grad[144:160] * 0.25 if scaled else grad[144:160]
    for shift in range(9):
        item = grad[16 * shift : 16 * shift + 16]
        if scaled:
            item = item * group_scale(shift)
        total = total + item * cycle(rows, shift) + cycle(item * rows, (16 - shift) % 16)
    return total


def later_by(rows, offset, before):
    lane = lax.broadcasted_iota(jnp.int32, rows.shape, 1)
    moved = pltpu.roll(rows, offset, 1)
    if offset == 1:
        return jnp.where(lane == 0, before[:, 1:2], moved)
    return jnp.where(lane == 0, before[:, 0:1], jnp.where(lane == 1, before[:, 1:2], moved))


def sooner_by(rows, offset, after):
    length = rows.shape[1]
    lane = lax.broadcasted_iota(jnp.int32, rows.shape, 1)
    moved = pltpu.roll(rows, length - offset, 1)
    if offset == 1:
        return jnp.where(lane == length - 1, after[:, 0:1], moved)
    return jnp.where(
        lane == length - 2,
        after[:, 0:1],
        jnp.where(lane == length - 1, after[:, 1:2], moved),
    )


def conv_forward(signal, before, taps, same):
    total = taps[:, 0:1] * signal
    for offset in (1, 2):
        total = total + taps[:, offset : offset + 1] * later_by(signal, offset, before) * same[offset - 1]
    return total


def conv_backward(grad, after, taps, same):
    total = taps[:, 0:1] * grad
    for offset in (1, 2):
        total = total + taps[:, offset : offset + 1] * sooner_by(grad, offset, after) * same[offset - 1]
    return total


def add_ones(values):
    length = values.shape[1]
    row = lax.broadcasted_iota(jnp.int32, (VROWS - DV, length), 0)
    return jnp.concatenate(
        [values, jnp.where(row == 0, 1.0, 0.0).astype(jnp.bfloat16)], axis=0
    )


def weights_of(keys, queries, mask):
    shifted = dot_tn(keys, queries) + 1.0
    return shifted, (0.5 * shifted * shifted + 0.5) * mask


def mix_forward(tokens, before_tokens, taps, doc_row, prev_docs, mask_ref):
    length = tokens.shape[0]
    block = tokens.astype(jnp.float32).T.astype(jnp.bfloat16)
    before = before_tokens.astype(jnp.float32).T[2 * FEATURE_SIZE : 2 * FEATURE_SIZE + DV, 14:16]
    values, _, _, _ = values_of(block, before, taps, doc_row, prev_docs)
    marked = add_ones(values)
    keep_last = (doc_row == doc_row[:, length - 1 : length]).astype(jnp.float32)
    key_feats = features(block[16:32].astype(jnp.float32), keep_last, False)
    state = dot_nt(key_feats, marked)
    scaled_q = (block[0:16].astype(jnp.float32) * 0.25).astype(jnp.bfloat16)
    sums = []
    for start in range(0, length, TBLOCK):
        stop = start + TBLOCK
        _, weights = weights_of(
            block[16:32, :stop], scaled_q[:, start:stop], mask_ref[:stop, start:stop]
        )
        sums.append(dot_nn(marked[:, :stop], weights.astype(jnp.bfloat16)))
    return block, marked, jnp.concatenate(sums, axis=1), state


def values_of(block, before, taps, doc_row, prev_docs):
    length = block.shape[1]
    doc8 = jnp.broadcast_to(doc_row, (8, length))
    prev8 = jnp.broadcast_to(prev_docs, (8, 2))
    same = [
        (doc8 == later_by(doc8, offset, prev8)).astype(jnp.float32)[0:1] for offset in (1, 2)
    ]
    conv_in = block[32 : 32 + DV].astype(jnp.float32)
    gate_in = block[32 + DV :].astype(jnp.float32)
    conv_out = conv_forward(conv_in, before, taps, same)
    sigmoid = 1.0 / (1.0 + jnp.exp(-gate_in))
    values = (gate_in * sigmoid * conv_out).astype(jnp.bfloat16)
    return values, conv_out, gate_in, sigmoid


def fill_mask(mask_ref, doc_row, doc_col):
    shape = mask_ref.shape
    causal = lax.broadcasted_iota(jnp.int32, shape, 0) <= lax.broadcasted_iota(jnp.int32, shape, 1)
    mask_ref[...] = jnp.where(causal & (doc_col == doc_row), 1.0, 0.0)


def f1_kernel(p_ref, halo_ref, taps_ref, row_ref, col_ref, prev_ref, pt_ref, v_ref, o_ref, l_ref, mask_ref):
    @pl.when(pl.program_id(0) == 0)
    def _():
        fill_mask(mask_ref, row_ref[...], col_ref[...])

    block, marked, sums, state = mix_forward(
        p_ref[...], halo_ref[...], taps_ref[0], row_ref[...], prev_ref[:, 0:2], mask_ref
    )
    pt_ref[...] = block
    v_ref[...] = marked
    o_ref[...] = sums
    l_ref[...] = state.astype(jnp.bfloat16)


def mix_finish(block, sums, carry, doc_row):
    keep_first = (doc_row == doc_row[:, 0:1]).astype(jnp.float32)
    query_feats = features(block[0:16].astype(jnp.float32), keep_first, True)
    total = sums + dot_tn(carry, query_feats)
    denominator = total[DV : DV + 1]
    return (total[:DV] / denominator).astype(jnp.bfloat16), denominator


def f2_kernel(pt_ref, o_ref, s_ref, row_ref, att_ref, den_ref):
    attended, denominator = mix_finish(pt_ref[...], o_ref[...], s_ref[...], row_ref[...])
    att_ref[...] = attended
    den_ref[...] = jnp.broadcast_to(denominator, den_ref.shape)


def sum_grads(grad, attended, denominator):
    length = grad.shape[1]
    inverse = 1.0 / denominator
    grad_f = grad.astype(jnp.float32)
    dot_term = jnp.sum(grad_f * attended.astype(jnp.float32), axis=0, keepdims=True)
    row = lax.broadcasted_iota(jnp.int32, (VROWS - DV, length), 0)
    tail = jnp.where(row == 0, jnp.broadcast_to(-dot_term * inverse, row.shape), 0.0)
    return jnp.concatenate([grad_f * inverse, tail], axis=0).astype(jnp.bfloat16)


def mix_back_local(block, marked, sums_grad, carry, doc_row, mask_ref):
    length = block.shape[1]
    keys = block[16:32]
    queries = block[0:16].astype(jnp.float32)
    scaled_q = (queries * 0.25).astype(jnp.bfloat16)
    keep_first = (doc_row == doc_row[:, 0:1]).astype(jnp.float32)
    query_grad = features_back(queries, dot_nn(carry, sums_grad) * keep_first, True)
    key_grad = jnp.zeros((16, length), jnp.float32)
    value_grad = jnp.zeros((VROWS, length), jnp.float32)
    parts = []
    for start in range(0, length, TBLOCK):
        stop = start + TBLOCK
        mask = mask_ref[:stop, start:stop]
        shifted, weights = weights_of(keys[:, :stop], scaled_q[:, start:stop], mask)
        grad_block = sums_grad[:, start:stop]
        weight_grad = dot_tn(marked[:, :stop], grad_block)
        score_grad = (weight_grad * shifted * mask).astype(jnp.bfloat16)
        parts.append(dot_nn(keys[:, :stop], score_grad) * 0.25)
        key_part = dot_nt(scaled_q[:, start:stop], score_grad)
        value_part = dot_nt(grad_block, weights.astype(jnp.bfloat16))
        if stop < length:
            key_part = jnp.concatenate(
                [key_part, jnp.zeros((16, length - stop), jnp.float32)], axis=1
            )
            value_part = jnp.concatenate(
                [value_part, jnp.zeros((VROWS, length - stop), jnp.float32)], axis=1
            )
        key_grad = key_grad + key_part
        value_grad = value_grad + value_part
    query_grad = query_grad + jnp.concatenate(parts, axis=1)
    return query_grad, key_grad, value_grad


def b1_kernel(pt_ref, v_ref, g_ref, att_ref, den_ref, s_ref, row_ref, col_ref, d_ref, dq_ref, dk_ref, dv_ref, mask_ref):
    @pl.when(pl.program_id(0) == 0)
    def _():
        fill_mask(mask_ref, row_ref[...], col_ref[...])

    doc_row = row_ref[...]
    block = pt_ref[...]
    sums_grad = sum_grads(g_ref[...], att_ref[...], den_ref[0:1])
    keep_first = (doc_row == doc_row[:, 0:1]).astype(jnp.float32)
    query_feats = features(block[0:16].astype(jnp.float32), keep_first, True)
    d_ref[...] = dot_nt(query_feats, sums_grad).astype(jnp.bfloat16)
    dq, dk, dv = mix_back_local(block, v_ref[...], sums_grad, s_ref[...], doc_row, mask_ref)
    dq_ref[...] = dq
    dk_ref[...] = dk
    dv_ref[...] = dv


def mix_back_finish(block, marked, later_state, key_grad, value_grad, doc_row, before, taps, prev_docs):
    length = block.shape[1]
    keep_last = (doc_row == doc_row[:, length - 1 : length]).astype(jnp.float32)
    keys = block[16:32].astype(jnp.float32)
    key_feats = features(keys, keep_last, False)
    key_grad = key_grad + features_back(keys, dot_nn(later_state, marked) * keep_last, False)
    value_grad = (value_grad + dot_tn(later_state, key_feats))[:DV]
    _, conv_out, gate_in, sigmoid = values_of(block, before, taps, doc_row, prev_docs)
    gate_grad = value_grad * conv_out * sigmoid * (1.0 + gate_in * (1.0 - sigmoid))
    conv_grad = value_grad * gate_in * sigmoid
    return key_grad, gate_grad, conv_grad


def b2_kernel(pt_ref, v_ref, g_ref, dq_ref, dk_ref, dv_ref, halo_ref, taps_ref, row_ref, prev_ref, dp_ref, first_ref, tail_ref):
    doc_row = row_ref[...]
    length = doc_row.shape[1]
    taps = taps_ref[0]
    before = halo_ref[...].astype(jnp.float32).T[2 * FEATURE_SIZE : 2 * FEATURE_SIZE + DV, 14:16]
    key_grad, gate_grad, conv_grad = mix_back_finish(
        pt_ref[...], v_ref[...], g_ref[...], dk_ref[...], dv_ref[...], doc_row, before, taps, prev_ref[:, 0:2]
    )
    doc8 = jnp.broadcast_to(doc_row, (8, length))
    none = jnp.full((8, 2), -1.0, jnp.float32)
    same = [(doc8 == sooner_by(doc8, offset, none)).astype(jnp.float32)[0:1] for offset in (1, 2)]
    conv_in_grad = conv_backward(conv_grad, jnp.zeros((DV, 2), jnp.float32), taps, same)
    whole = jnp.concatenate([dq_ref[...], key_grad, conv_in_grad, gate_grad], axis=0).T
    dp_ref[...] = whole.astype(jnp.bfloat16)
    tail_ref[...] = whole[length - 16 :]
    pad = jnp.zeros((16, length), jnp.float32)
    conv_tokens = jnp.concatenate([jnp.zeros((32, length), jnp.float32), conv_grad, jnp.zeros((DV, length), jnp.float32)], axis=0).T
    first_ref[...] = conv_tokens[0:16]


MESH = pl.DeviceIdType.MESH
LAG = 2
DONE = 3
FLAT = (38, 39)
AHEAD = 4
UNIT = 512
TILE = 256
KEPT = (1, 2, 3, 5, 6, 8)
GROUPS = 4


class Gather:
    kinds = 9
    flat = FLAT

    def __init__(self, shards, wholes, sends, lands):
        self.shards, self.wholes = shards, wholes
        self.sends, self.lands = sends, lands
        i = lax.axis_index("fsdp")
        z = lax.axis_index("seq")
        odd = z % 2
        self.odd = odd
        by_y = 4 - 8 * (i // 4)
        by_x = 2 - 4 * ((i // 2) % 2)
        by_core = 1 - 2 * (i % 2)
        self.slot = [i, i + by_y, i + by_x + odd * by_y, i + by_x + (1 - odd) * by_y, i + by_core]
        self.flat_slot = [i, i + by_y, i + by_x, i + by_x + by_y, i + by_core]
        self.near = [
            {"fsdp": i + by_y, "seq": z},
            {"fsdp": i + by_x, "seq": z},
            {"fsdp": i, "seq": z + 1 - 2 * odd},
            {"fsdp": i + by_core, "seq": z},
        ]

    def is_flat(self, piece):
        return isinstance(piece[0], int) and piece[0] in self.flat

    def part(self, piece, slot, half=None):
        _, which, start, size = piece
        rows = self.shards[which].shape[0]
        first, count = (0, rows) if half is None else (half * (rows // 2), rows // 2)
        return self.wholes[which].at[
            pl.ds(pl.multiple_of(slot * rows + first, 16), count), pl.ds(start, size)
        ]

    def own_part(self, piece):
        _, which, start, size = piece
        return self.shards[which].at[:, pl.ds(start, size)]

    def copy(self, kind, piece, relay=False):
        source = [0, 0, 2, 0, 1, 2, 3, 4][kind] if kind < 8 else 2
        half = None
        link = min(kind, 3)
        slots = self.slot
        if self.is_flat(piece):
            slots = self.flat_slot
            if kind == 2:
                source, half, link = 1, 0, 1
            if kind == 8:
                source, half, link = 2, 1, 0
        if relay:
            source = 1
        slot = slots[source]
        return pltpu.make_async_remote_copy(
            src_ref=self.own_part(piece) if source == 0 else self.part(piece, slot, half),
            dst_ref=self.part(piece, slot, half),
            send_sem=self.sends.at[kind, piece[0]],
            recv_sem=self.lands.at[kind, piece[0]],
            device_id=self.near[link],
            device_id_type=MESH,
        )

    def first(self, piece):
        self.copy(0, piece).start()
        if self.is_flat(piece):
            self.copy(1, piece).start()
        else:

            @pl.when(self.odd == 0)
            def _():
                self.copy(1, piece).start()

        self.copy(3, piece).start()

    def from_y(self, piece):
        self.copy(0, piece).wait_recv()

        if not self.is_flat(piece):

            @pl.when(self.odd == 1)
            def _():
                self.copy(1, piece, relay=True).start()

        self.copy(4, piece).start()
        self.copy(3, piece).wait_recv()
        self.copy(7, piece).start()

    def from_x(self, piece):
        self.copy(1, piece).wait_recv()
        self.copy(2, piece).start()
        if self.is_flat(piece):
            self.copy(8, piece).start()
        self.copy(5, piece).start()

    def from_z(self, piece):
        self.copy(2, piece).wait_recv()
        if self.is_flat(piece):
            self.copy(8, piece).wait_recv()
        self.copy(6, piece).start()

    def ready(self, piece):
        for kind in (4, 5, 6, 7):
            self.copy(kind, piece).wait_recv()

    def finish(self, piece):
        for kind in range(self.kinds if self.is_flat(piece) else 8):
            self.copy(kind, piece).wait_send()


def cuts(which, width, size):
    return [(which, at, min(size, width - at)) for at in range(0, width, size)]


def early_cuts(columns, width):
    mix = [(0, 0, 256), (0, 256, 256)] + [(0, at, 512) for at in range(512, columns, 512)]
    return mix + cuts(1, width, 512) + cuts(3, width, 256)


def by_rows(length, body, rows=64):
    def step(n, _):
        body(pl.ds(pl.multiple_of(n * rows, rows), rows))
        return 0

    lax.fori_loop(0, length // rows, step, 0)


def row_root(value):
    return lax.rsqrt(jnp.mean(value * value, -1, keepdims=True) + epsilon)


def m_kernel(
    x, g, gain1, gain2, taps, doc_row_ref, doc_col_ref, in_down, up_maps, out_down, out_up, gu_down, gu_up, ffd_down, ffd_up,
    a_in, b_in, c_in, d_in,
    a_all, b_all, c_all, d_all,
    out, blocks_out, marked_out, att_t_out, dens, carry_out, attended_out, resid_grad, hidden1_out, rank_in, rank_out, halo, term_ff, term_w, next_docs,
    blocks, marked, att_t, carry, attended, hidden1, keep_sems, first_docs,    halo_send, mask, sums, state, message, resid, hidden2, out_acc, grad_acc, a_tile, b_tile, g_tile, u_tile, d_tile, rank_acc,
    sends, lands, halo_sems, chain_sems, load_sems,
):
    length, width = x.shape
    ff = d_all.shape[0]
    units = -(-ff // UNIT)
    last_size = ff - (units - 1) * UNIT
    f32, bf16 = jnp.float32, jnp.bfloat16
    place = lax.axis_index("seq")
    planes = lax.axis_size("seq")
    me = lax.axis_index("fsdp")
    job = Gather([a_in, b_in, c_in, d_in], [a_all, b_all, c_all, d_all], sends, lands)

    early = early_cuts(a_in.shape[1], b_in.shape[1])
    early = [(number,) + piece for number, piece in enumerate(early)]
    base = len(early)
    mix_pieces = [p for p in early if p[1] == 0]
    out_pieces = [p for p in early if p[1] == 1]
    down_pieces = [p for p in early if p[1] == 3]
    total = base + 2 * units

    def late(number, size=UNIT):
        at = number - base
        start = (at // 2) * UNIT + (at % 2) * ff
        if not isinstance(start, int):
            start = pl.multiple_of(start, TILE)
        return (number, 2, start, size)

    def piece_at(number):
        if number < base:
            return early[number]
        return late(number, UNIT if number < total - 2 else last_size)

    def each_late(number, action):
        @pl.when(number < total - 2)
        def _():
            action(late(number))

        for end in (total - 2, total - 1):

            @pl.when(number == end)
            def _():
                action(piece_at(end))

    def pump(number):
        job.from_y(piece_at(number))
        if number + AHEAD < total:
            job.first(piece_at(number + AHEAD))
        if number >= LAG:
            job.from_x(piece_at(number - LAG))
        if number >= 2 * LAG:
            job.from_z(piece_at(number - 2 * LAG))

    barrier = pltpu.get_barrier_semaphore()
    for device in (job.near[0], job.near[1], job.near[3]):
        pl.semaphore_signal(barrier, inc=1, device_id=device, device_id_type=MESH)
    before = {"fsdp": me, "seq": (place + planes - 1) % planes}
    after = {"fsdp": me, "seq": (place + 1) % planes}

    @pl.when(place > 0)
    def _():
        pl.semaphore_signal(barrier, inc=1, device_id=before, device_id_type=MESH)

    @pl.when(place < planes - 1)
    def _():
        pl.semaphore_signal(barrier, inc=1, device_id=after, device_id_type=MESH)

    inner = (place > 0) & (place < planes - 1)

    @pl.when(inner)
    def _():
        pl.semaphore_wait(barrier, 5)

    @pl.when(jnp.logical_not(inner))
    def _():
        pl.semaphore_wait(barrier, 4)

    for piece in early[:AHEAD]:
        job.first(piece)
    first_docs[...] = jnp.broadcast_to(doc_col_ref[0:8, :], (8, 128))
    docs_back = pltpu.make_async_remote_copy(
        src_ref=first_docs, dst_ref=next_docs, send_sem=halo_sems.at[2], recv_sem=halo_sems.at[3], device_id=before, device_id_type=MESH
    )

    @pl.when(place > 0)
    def _():
        docs_back.start()

    @pl.when(place == planes - 1)
    def _():
        next_docs[...] = jnp.full(next_docs.shape, -1.0, f32)

    def norm1(rows):
        value = x[rows, :].astype(f32)
        hidden1[rows, :] = (value * row_root(value) * gain1[...]).astype(bf16)

    by_rows(length, norm1)
    rank_in[...] = dot_nt(hidden1[...], in_down[...]).astype(bf16)
    doc_row = doc_row_ref[...]
    fill_mask(mask, doc_row, doc_col_ref[...])
    cond_whole = (doc_row[:, 0:1] == doc_row[:, length - 1 : length]).astype(f32)

    def load_mix(number):
        _, _, start, size = mix_pieces[number]
        return pltpu.make_async_copy(
            a_all.at[:, pl.ds(start, size)], a_tile.at[number % 2, :, :size], load_sems.at[number % 2]
        )

    def project(number):
        _, _, start, size = mix_pieces[number]
        load_mix(number).wait()
        projected = dot_nn(hidden1[...], a_tile[number % 2, :, :size]) + dot_nn(rank_in[...], up_maps[:, start : start + size])
        halo_send[:, start : start + size] = projected[length - 16 :].astype(bf16)
        for at in range(0, size, PER_HEAD):
            blocks[start + at : start + at + PER_HEAD, :] = projected[:, at : at + PER_HEAD].T.astype(bf16)

    for number in range(2 * LAG):
        job.from_y(piece_at(number))
        job.first(piece_at(number + AHEAD))
        if 1 <= number <= LAG:
            job.from_x(piece_at(number - 1))
    for number, piece in enumerate(mix_pieces):
        pump(number + 2 * LAG)
        job.ready(piece)
        load_mix(number).start()
        if number > 0:
            project(number - 1)
    project(len(mix_pieces) - 1)
    columns = HEAD_COUNT * PER_HEAD
    halo_send[:, columns:] = jnp.broadcast_to(
        doc_col_ref[length - 16 :, :], (16, 128)
    ).astype(bf16)
    to_next = pltpu.make_async_remote_copy(
        src_ref=halo_send, dst_ref=halo, send_sem=halo_sems.at[0], recv_sem=halo_sems.at[1], device_id=after, device_id_type=MESH
    )

    @pl.when(place < planes - 1)
    def _():
        to_next.start()

    @pl.when(place == 0)
    def _():
        halo[:, :columns] = jnp.zeros((16, columns), bf16)
        halo[:, columns:] = jnp.full((16, 128), -1.0, bf16)

    next_piece = len(mix_pieces) + 2 * LAG

    def pump_next():
        nonlocal next_piece
        pump(next_piece)
        next_piece += 1

    pump_next()

    @pl.when(place > 0)
    def _():
        to_next.wait_recv()

    prev_docs = halo[:, columns:].astype(f32).T[0:1, 14:16]
    cond_before = (prev_docs[:, 1:2] == doc_row[:, 0:1]).astype(f32)
    keep_last = (doc_row == doc_row[:, length - 1 : length]).astype(f32)

    def head_state(h, _):
        at = pl.multiple_of(h * PER_HEAD, PER_HEAD)
        block = blocks[pl.ds(at, PER_HEAD), :]
        prior = halo[:, pl.ds(at, PER_HEAD)].astype(f32).T[32 : 32 + DV, 14:16]
        values, _, _, _ = values_of(block, prior, taps[h], doc_row, prev_docs)
        ones = add_ones(values)
        marked[pl.ds(pl.multiple_of(h * VROWS, VROWS), VROWS), :] = ones
        key_feats = features(block[16:32].astype(f32), keep_last, False)
        state[pl.ds(pl.multiple_of(h * FEATS, 16), FEATS), :] = dot_nt(key_feats, ones).astype(bf16)
        return 0

    group = HEAD_COUNT // GROUPS
    half = HEAD_COUNT // 2
    lax.fori_loop(0, half, head_state, 0)
    pump_next()
    lax.fori_loop(half, HEAD_COUNT, head_state, 0)
    pump_next()
    span = group * FEATS

    def hand_on(number):
        part = pl.ds(number * span, span)
        return pltpu.make_async_remote_copy(
            src_ref=message.at[part], dst_ref=carry.at[part],
            send_sem=chain_sems.at[0, number], recv_sem=chain_sems.at[1, number], device_id=after, device_id_type=MESH,
        )

    @pl.when(place == 0)
    def _():
        carry[...] = jnp.zeros(carry.shape, bf16)
        message[...] = state[...]
        for number in range(GROUPS):
            hand_on(number).start()

    def chain_slot(slot):
        for plane in range(1, 4):
            number = slot - plane + 1
            if 0 <= number < GROUPS:

                @pl.when(place == plane)
                def _():
                    part = pl.ds(number * span, span)
                    hand_on(number).wait_recv()
                    if plane < 3:
                        message[part, :] = (
                            state[part, :].astype(f32) + (cond_whole * cond_before) * carry[part, :].astype(f32)
                        ).astype(bf16)
                        hand_on(number).start()

    def head_local(h, _):
        at = pl.multiple_of(h * PER_HEAD, PER_HEAD)
        keys = blocks[pl.ds(at + 16, 16), :]
        scaled_q = (blocks[pl.ds(at, 16), :].astype(f32) * 0.25).astype(bf16)
        rows = pl.multiple_of(h * VROWS, VROWS)
        ones = marked[pl.ds(rows, VROWS), :]
        for start in range(0, length, TBLOCK):
            stop = start + TBLOCK
            _, weights = weights_of(keys[:, :stop], scaled_q[:, start:stop], mask[:stop, start:stop])
            sums[pl.ds(rows, VROWS), start:stop] = dot_nn(ones[:, :stop], weights.astype(bf16))
        return 0

    for number in range(GROUPS):
        lax.fori_loop(number * group, (number + 1) * group, head_local, 0)
        chain_slot(number)
        pump_next()

    keep_first = (doc_row == doc_row[:, 0:1]).astype(f32) * cond_before

    def head_finish(h, _):
        at = pl.multiple_of(h * PER_HEAD, PER_HEAD)
        rows = pl.multiple_of(h * VROWS, VROWS)
        query_feats = features(blocks[pl.ds(at, 16), :].astype(f32), keep_first, True)
        both = sums[pl.ds(rows, VROWS), :] + dot_tn(carry[pl.ds(pl.multiple_of(h * FEATS, 16), FEATS), :], query_feats)
        denominator = both[DV : DV + 1]
        att_t[pl.ds(pl.multiple_of(h * DV, 16), DV), :] = (both[:DV] / denominator).astype(bf16)
        dens[pl.ds(pl.multiple_of(h * 8, 8), 8), :] = jnp.broadcast_to(denominator, (8, length))
        return 0

    chain_slot(GROUPS)
    lax.fori_loop(0, half, head_finish, 0)
    pump_next()
    chain_slot(GROUPS + 1)
    lax.fori_loop(half, HEAD_COUNT, head_finish, 0)

    def turn(n, _):
        rows = pl.ds(pl.multiple_of(n * 128, 128), 128)
        attended[:, rows] = att_t[rows, :].astype(f32).T.astype(bf16)
        return 0

    lax.fori_loop(0, width // 128, turn, 0)
    keeps = [
        pltpu.make_async_copy(have, kept, keep_sems.at[n])
        for n, (have, kept) in enumerate(
            [
                (blocks, blocks_out), (marked, marked_out), (att_t, att_t_out),
                (carry, carry_out), (attended, attended_out), (hidden1, hidden1_out),
            ]
        )
    ]
    for keep in keeps:
        keep.start()
    pump_next()

    rank_out[...] = dot_nt(attended[...], out_down[...]).astype(bf16)
    for piece in out_pieces:
        job.ready(piece)
        _, _, start, size = piece
        load = pltpu.make_async_copy(b_all.at[:, pl.ds(start, size)], b_tile.at[:, :size], load_sems.at[0])
        load.start()
        load.wait()
        resid[:, start : start + size] = (
            x[:, start : start + size].astype(f32)
            + dot_nn(attended[...], b_tile[:, :size])
            + dot_nn(rank_out[...], out_up[:, start : start + size])
        )
    pump_next()

    def norm2(rows):
        value = resid[rows, :]
        hidden2[rows, :] = (value * row_root(value) * gain2[...]).astype(bf16)
        out_acc[rows, :] = value
        grad_acc[rows, :] = jnp.zeros(value.shape, f32)

    by_rows(length, norm2)
    rank_gate = dot_nt(hidden2[...], gu_down[0:16, :]).astype(bf16)
    rank_up = dot_nt(hidden2[...], gu_down[16:32, :]).astype(bf16)
    rank_ffd_grad = dot_nt(g[...], ffd_up[...]).astype(bf16)
    rank_gate_t = rank_gate.astype(f32).T.astype(bf16)
    rank_up_t = rank_up.astype(f32).T.astype(bf16)
    rank_ffd_grad_t = rank_ffd_grad.astype(f32).T.astype(bf16)
    rank_acc[...] = jnp.zeros(rank_acc.shape, f32)
    while next_piece < base + 2 * LAG:
        pump_next()
    for piece in down_pieces:
        job.ready(piece)

    def loads(unit, slot, size):
        start = unit * UNIT
        if not isinstance(start, int):
            start = pl.multiple_of(start, TILE)
        return [
            pltpu.make_async_copy(c_all.at[:, pl.ds(start, size)], g_tile.at[slot, :, :size], load_sems.at[slot]),
            pltpu.make_async_copy(c_all.at[:, pl.ds(ff + start, size)], u_tile.at[slot, :, :size], load_sems.at[2 + slot]),
            pltpu.make_async_copy(d_all.at[pl.ds(start, size), :], d_tile.at[slot, :size, :], load_sems.at[4 + slot]),
        ]

    def hidden_tile(unit, slot, part):
        inside = slice(part * TILE, (part + 1) * TILE)
        start = unit * UNIT + part * TILE
        cols = pl.ds(start if isinstance(start, int) else pl.multiple_of(start, TILE), TILE)
        gate_w, up_w, down_w = g_tile[slot, :, inside], u_tile[slot, :, inside], d_tile[slot, inside, :]
        gate_map, up_map, down_map = gu_up[0:16, cols], gu_up[16:32, cols], ffd_down[:, cols]
        gate_pre = dot_nn(hidden2[...], gate_w) + dot_nn(rank_gate, gate_map)
        up_pre = dot_nn(hidden2[...], up_w) + dot_nn(rank_up, up_map)
        inner_grad = dot_nt(g[...], down_w) + dot_nn(rank_ffd_grad, down_map)
        sigmoid = 1.0 / (1.0 + jnp.exp(-gate_pre))
        gate_val = gate_pre * sigmoid
        inner = (gate_val * up_pre).astype(bf16)
        gate_grad = (inner_grad * up_pre * (sigmoid * (1.0 + gate_pre * (1.0 - sigmoid)))).astype(bf16)
        up_grad = (inner_grad * gate_val).astype(bf16)
        out_acc[...] += dot_nn(inner, down_w)
        grad_acc[...] += dot_nt(gate_grad, gate_w) + dot_nt(up_grad, up_w)
        rank_acc[0] += dot_nt(inner, down_map)
        rank_acc[1] += dot_nt(gate_grad, gate_map)
        rank_acc[2] += dot_nt(up_grad, up_map)
        term_ff[0:16, cols] = dot_nn(rank_gate_t, gate_grad)
        term_ff[16:32, cols] = dot_nn(rank_up_t, up_grad)
        term_ff[32:48, cols] = dot_nn(rank_ffd_grad_t, inner)

    def ff_pump(number):
        each_late(number, job.from_y)
        each_late(number + AHEAD, job.first)
        each_late(number - LAG, job.from_x)
        each_late(number - 2 * LAG, job.from_z)

    def ff_ready(unit, slot, size, pieces):
        for piece in pieces:
            job.ready(piece)
        for load in loads(unit, slot, size):
            load.start()

    def ff_load_wait(unit, slot, size):
        for load in loads(unit, slot, size):
            load.wait()

    def ff_step(unit, _):
        slot = unit % 2
        ahead = base + 2 * unit + 2 * LAG
        ff_pump(ahead)

        @pl.when(unit >= 1)
        def _():
            ff_load_wait(unit - 1, 1 - slot, UNIT)
            hidden_tile(unit - 1, 1 - slot, 0)

        ff_pump(ahead + 1)
        ff_ready(unit, slot, UNIT, [late(base + 2 * unit), late(base + 2 * unit + 1)])

        for number in range(0, len(early), 2):

            @pl.when(unit == 1 + number // 4)
            def _():
                for piece in early[number : number + 2]:
                    job.finish(piece)

        @pl.when(unit >= DONE)
        def _():
            job.finish(late(base + 2 * (unit - DONE)))
            job.finish(late(base + 2 * (unit - DONE) + 1))

        @pl.when(unit >= 1)
        def _():
            hidden_tile(unit - 1, 1 - slot, 1)

        return 0

    lax.fori_loop(0, units - 1, ff_step, 0)
    final = units - 1
    job.from_z(piece_at(total - 2))
    job.from_z(piece_at(total - 1))
    ff_load_wait(final - 1, (final - 1) % 2, UNIT)
    hidden_tile(final - 1, (final - 1) % 2, 0)
    ff_ready(final, final % 2, last_size, [piece_at(total - 2), piece_at(total - 1)])
    hidden_tile(final - 1, (final - 1) % 2, 1)
    ff_load_wait(final, final % 2, last_size)
    for part in range(last_size // TILE):
        hidden_tile(final, final % 2, part)

    rank_ffd = rank_acc[0].astype(bf16)
    rank_gate_grad = rank_acc[1].astype(bf16)
    rank_up_grad = rank_acc[2].astype(bf16)
    out_acc[...] += dot_nn(rank_ffd, ffd_up[...])
    grad_acc[...] += dot_nn(rank_gate_grad, gu_down[0:16, :]) + dot_nn(rank_up_grad, gu_down[16:32, :])
    term_w[0:16, :] = dot_tn(rank_gate_grad, hidden2[...])
    term_w[16:32, :] = dot_tn(rank_up_grad, hidden2[...])
    term_w[32:48, :] = dot_tn(rank_ffd, g[...])

    def finish_rows(rows):
        out[rows, :] = out_acc[rows, :].astype(bf16)
        value = resid[rows, :]
        root = row_root(value)
        normed = value * root
        scaled = grad_acc[rows, :] * gain2[...]
        resid_grad[rows, :] = g[rows, :].astype(f32) + root * (
            scaled - normed * jnp.mean(scaled * normed, -1, keepdims=True)
        )

    by_rows(length, finish_rows)

    for keep in keeps:
        keep.wait()

    def finish_late(number, _):
        job.finish(late(number))
        return 0

    lax.fori_loop(base + 2 * (units - 1 - DONE), total - 2, finish_late, 0)
    job.finish(piece_at(total - 2))
    job.finish(piece_at(total - 1))

    @pl.when(place > 0)
    def _():
        docs_back.wait_send()

    @pl.when(place < planes - 1)
    def _():
        docs_back.wait_recv()
        to_next.wait_send()
        for number in range(GROUPS):
            hand_on(number).wait_send()


def call_m(x, g, gain1, gain2, taps, doc_row, doc_col, maps, shards):
    length, width = x.shape
    f32, bf16 = jnp.float32, jnp.bfloat16
    count = lax.axis_size("fsdp")
    a, b, c, d = shards
    ff = d.shape[0] * count
    columns = a.shape[1]
    pieces = len(early_cuts(columns, width)) + 2 * -(-ff // UNIT)
    whole = pl.BlockSpec(memory_space=pltpu.VMEM)
    anyplace = pl.BlockSpec(memory_space=pl.ANY)
    vmem_out = [
        ((length, width), bf16),
        ((columns, length), bf16),
        ((HEAD_COUNT * VROWS, length), bf16),
        ((width, length), bf16),
        ((HEAD_COUNT * 8, length), f32),
        ((HEAD_COUNT * FEATS, VROWS), bf16),
        ((length, width), bf16),
        ((length, width), f32),
        ((length, width), bf16),
        ((length, 64), bf16),
        ((length, 16), bf16),
        ((16, columns + 128), bf16),
        ((48, ff), f32),
        ((48, width), f32),
        ((8, 128), f32),
    ]
    args = (x, g, gain1, gain2, taps, doc_row, doc_col) + tuple(maps)
    return pl.pallas_call(
        m_kernel,
        in_specs=[whole] * len(args) + [anyplace] * 4,
        out_specs=[anyplace] * 4 + [anyplace if n in KEPT else whole for n in range(len(vmem_out))],
        out_shape=[jax.ShapeDtypeStruct((t.shape[0] * count, t.shape[1]), t.dtype) for t in shards]
        + [jax.ShapeDtypeStruct(s, t) for s, t in vmem_out],
        scratch_shapes=[pltpu.VMEM(*vmem_out[n]) for n in KEPT]
        + [
            pltpu.SemaphoreType.DMA((len(KEPT),)),
            pltpu.VMEM((8, 128), f32),
            pltpu.VMEM((16, columns + 128), bf16),
            pltpu.VMEM((length, length), f32),
            pltpu.VMEM((HEAD_COUNT * VROWS, length), f32),
            pltpu.VMEM((HEAD_COUNT * FEATS, VROWS), bf16),
            pltpu.VMEM((HEAD_COUNT * FEATS, VROWS), bf16),
            pltpu.VMEM((length, width), f32),
            pltpu.VMEM((length, width), bf16),
            pltpu.VMEM((length, width), f32),
            pltpu.VMEM((length, width), f32),
            pltpu.VMEM((2, width, 512), bf16),
            pltpu.VMEM((width, 512), bf16),
            pltpu.VMEM((2, width, UNIT), bf16),
            pltpu.VMEM((2, width, UNIT), bf16),
            pltpu.VMEM((2, UNIT, width), bf16),
            pltpu.VMEM((3, length, 16), f32),
            pltpu.SemaphoreType.DMA((9, pieces)),
            pltpu.SemaphoreType.DMA((9, pieces)),
            pltpu.SemaphoreType.DMA((4,)),
            pltpu.SemaphoreType.DMA((2, GROUPS)),
            pltpu.SemaphoreType.DMA((6,)),
        ],
        compiler_params=pltpu.CompilerParams(
            collective_id=1, has_side_effects=True, vmem_limit_bytes=62 * 1024 * 1024
        ),
    )(*args, *shards)


def stripe_width(columns):
    return -(-columns // (4 * 128)) * 128


FETCHED = (0, 11, 12, 13, 15, 16, 18)


def to_stripes(own, rows, value):
    size = own.shape[2]
    columns = value.shape[1]
    for n in range(own.shape[0]):
        piece = value[:, n * size : min((n + 1) * size, columns)]
        if piece.shape[1] < size:
            piece = jnp.concatenate(
                [piece, jnp.zeros((piece.shape[0], size - piece.shape[1]), piece.dtype)], axis=1
            )
        own[n, rows, :] = piece


class Share:
    def __init__(self, number, own, slots, total, everyone, z_sends, z_lands, sends, lands, local):
        self.number, self.own, self.slots, self.total, self.everyone = number, own, slots, total, everyone
        self.z_sends, self.z_lands, self.sends, self.lands, self.local = z_sends, z_lands, sends, lands, local
        i = lax.axis_index("fsdp")
        self.place = lax.axis_index("seq")
        self.planes = lax.axis_size("seq")
        by_y = 4 - 8 * (i // 4)
        by_x = 2 - 4 * ((i // 2) % 2)
        by_core = 1 - 2 * (i % 2)
        self.slot = [i, i + by_y, i + by_x, i + by_x + by_y]
        self.near = [
            {"fsdp": i + by_y, "seq": self.place},
            {"fsdp": i + by_x, "seq": self.place},
            {"fsdp": i + by_core, "seq": self.place},
        ]
        self.me = i

    def z_copy(self, distance, summed):
        plane = (self.place + distance) % self.planes
        kind = 3 * summed + distance - 1
        return pltpu.make_async_remote_copy(
            src_ref=self.total.at[self.place] if summed else self.own.at[plane],
            dst_ref=(self.total if summed else self.slots).at[self.place],
            send_sem=self.z_sends.at[self.number, kind],
            recv_sem=self.z_lands.at[self.number, kind],
            device_id={"fsdp": self.me, "seq": plane},
            device_id_type=MESH,
        )

    def z_start(self):
        for distance in range(1, self.planes):
            self.z_copy(distance, 0).start()
        self.slots[self.place] = self.own[self.place]

    def z_sum(self):
        for distance in range(1, self.planes):
            self.z_copy(distance, 0).wait_recv()
        total = self.slots[0].astype(jnp.float32)
        for plane in range(1, self.planes):
            total = total + self.slots[plane].astype(jnp.float32)
        self.total[self.place] = total.astype(jnp.bfloat16)
        for distance in range(1, self.planes):
            self.z_copy(distance, 1).start()

    def copy(self, kind):
        half = self.planes // 2
        first, second, every = pl.ds(0, half), pl.ds(half, half), pl.ds(0, self.planes)
        where, slot, part = [
            (0, 0, every), (1, 0, every), (2, 0, every),
            (1, 1, first), (0, 2, second),
            (2, 1, every), (2, 2, every), (2, 3, every),
        ][kind]
        there = self.everyone.at[self.slot[slot], part]
        return pltpu.make_async_remote_copy(
            src_ref=self.total if slot == 0 else there,
            dst_ref=there,
            send_sem=self.sends.at[self.number, kind],
            recv_sem=self.lands.at[self.number, kind],
            device_id=self.near[where],
            device_id_type=MESH,
        )

    def keep(self):
        return pltpu.make_async_copy(self.total, self.everyone.at[self.slot[0]], self.local.at[self.number])

    def gather_start(self):
        for distance in range(1, self.planes):
            self.z_copy(distance, 1).wait_recv()
        for kind in (0, 1, 2):
            self.copy(kind).start()
        self.keep().start()

    def relay(self):
        self.copy(0).wait_recv()
        self.copy(3).start()
        self.copy(5).start()
        self.copy(1).wait_recv()
        self.copy(4).start()
        self.copy(6).start()

    def relay_last(self):
        self.copy(3).wait_recv()
        self.copy(4).wait_recv()
        self.copy(7).start()

    def finish(self):
        for kind in (2, 5, 6, 7):
            self.copy(kind).wait_recv()
        self.keep().wait()
        for kind in range(8):
            self.copy(kind).wait_send()
        for distance in range(1, self.planes):
            self.z_copy(distance, 0).wait_send()
            self.z_copy(distance, 1).wait_send()


def t_kernel(
    x_kept, gain1, taps, doc_row_ref, doc_col_ref, next_docs_ref, chosen, in_down, up_maps, out_down, out_up,
    blocks_kept, marked_kept, att_t_kept, dens, carry_kept, attended_kept, resid_grad, hidden1_kept, rank_in, rank_out, halo, term_ff, term_w,
    w_in, w_out,
    input_grad, all_ff, all_wide, all_down, all_up,
    x, blocks, marked, att_t, carry, attended, hidden1, fetch_sems, out_tile, in_tile, branch_t, grad_t, sums_grad, state, message, later, query_grad, key_grad, value_grad, proj_grad,
    conv_last, halo_send, halo_next, vg_terms, qk_terms, mask,
    ff_own, ff_slots, ff_total, wide_own, wide_slots, wide_total, down_own, down_slots, down_total, up_own, up_slots, up_total,
    chain_sems, halo_sems, load_sems, z_sends, z_lands, sends, lands, local,
):
    length, width = x.shape
    f32, bf16 = jnp.float32, jnp.bfloat16
    columns = HEAD_COUNT * PER_HEAD
    fetches = [
        pltpu.make_async_copy(kept, have, fetch_sems.at[n])
        for n, (kept, have) in enumerate(
            [
                (att_t_kept, att_t), (blocks_kept, blocks), (marked_kept, marked), (carry_kept, carry),
                (attended_kept, attended), (hidden1_kept, hidden1), (x_kept, x),
            ]
        )
    ]
    load_out = pltpu.make_async_copy(w_out, out_tile, load_sems.at[0])
    load_out.start()
    for fetch in fetches:
        fetch.start()
    place = lax.axis_index("seq")
    planes = lax.axis_size("seq")
    me = lax.axis_index("fsdp")
    sems = (z_sends, z_lands, sends, lands, local)
    ff_share = Share(0, ff_own, ff_slots, ff_total, all_ff, *sems)
    wide_share = Share(1, wide_own, wide_slots, wide_total, all_wide, *sems)
    down_share = Share(2, down_own, down_slots, down_total, all_down, *sems)
    up_share = Share(3, up_own, up_slots, up_total, all_up, *sems)

    barrier = pltpu.get_barrier_semaphore()
    others = [{"fsdp": me, "seq": (place + distance) % planes} for distance in range(1, planes)]
    for device in ff_share.near + others:
        pl.semaphore_signal(barrier, inc=1, device_id=device, device_id_type=MESH)
    pl.semaphore_wait(barrier, 3 + planes - 1)

    step = in_tile.shape[1]
    blocks_in = width // step

    def load_in(number):
        return pltpu.make_async_copy(
            w_in.at[pl.ds(number * step, step), :], in_tile.at[number % 2], load_sems.at[1 + number % 2]
        )

    load_in(0).start()
    load_in(1).start()
    to_stripes(ff_own, slice(0, 48), term_ff[...].astype(bf16))
    ff_share.z_start()
    to_stripes(wide_own, slice(0, 48), term_w[...].astype(bf16))

    doc_row = doc_row_ref[...]
    fill_mask(mask, doc_row, doc_col_ref[...])
    prev_docs = halo[:, columns:].astype(f32).T[0:1, 14:16]
    next_docs = next_docs_ref[...].T[0:1, 0:2]
    cond_before = (prev_docs[:, 1:2] == doc_row[:, 0:1]).astype(f32)
    cond_after = (next_docs[:, 0:1] == doc_row[:, length - 1 : length]).astype(f32)
    cond_whole = (doc_row[:, 0:1] == doc_row[:, length - 1 : length]).astype(f32)
    keep_first = (doc_row == doc_row[:, 0:1]).astype(f32)
    keep_first_link = keep_first * cond_before
    keep_last = (doc_row == doc_row[:, length - 1 : length]).astype(f32) * cond_after

    for start in range(0, width, 128):
        branch_t[start : start + 128, :] = resid_grad[:, start : start + 128].T.astype(bf16)
    rank_grad_t = dot_nn(out_up[...], branch_t[...]).astype(bf16)
    load_out.wait()
    for start in range(0, width, 256):
        grad_t[start : start + 256, :] = (
            dot_nn(out_tile[start : start + 256, :], branch_t[...])
            + dot_tn(out_down[:, start : start + 256], rank_grad_t)
        ).astype(bf16)
    group = HEAD_COUNT // GROUPS
    span = group * FEATS

    def head_state(h, _):
        at = pl.multiple_of(h * PER_HEAD, PER_HEAD)
        rows = pl.ds(pl.multiple_of(h * VROWS, VROWS), VROWS)
        own = pl.ds(pl.multiple_of(h * DV, 16), DV)
        grads = sum_grads(grad_t[own, :], att_t[own, :], dens[pl.ds(pl.multiple_of(h * 8, 8), 8), :][0:1])
        sums_grad[rows, :] = grads
        query_feats = features(blocks[pl.ds(at, 16), :].astype(f32), keep_first, True)
        state[pl.ds(pl.multiple_of(h * FEATS, 16), FEATS), :] = dot_nt(query_feats, grads).astype(bf16)
        return 0

    def hand_on(number):
        part = pl.ds(number * span, span)
        return pltpu.make_async_remote_copy(
            src_ref=message.at[part], dst_ref=later.at[part],
            send_sem=chain_sems.at[0, number], recv_sem=chain_sems.at[1, number],
            device_id={"fsdp": me, "seq": (place + planes - 1) % planes}, device_id_type=MESH,
        )

    @pl.when(place == planes - 1)
    def _():
        later[...] = jnp.zeros(later.shape, bf16)

    for fetch in fetches:
        fetch.wait()
    for number in range(GROUPS):
        part = pl.ds(number * span, span)
        lax.fori_loop(number * group, (number + 1) * group, head_state, 0)

        @pl.when(place == planes - 1)
        def _():
            message[part, :] = state[part, :]
            hand_on(number).start()

    def head_local(h, _):
        at = pl.multiple_of(h * PER_HEAD, PER_HEAD)
        rows = pl.ds(pl.multiple_of(h * VROWS, VROWS), VROWS)
        keys = blocks[pl.ds(at + 16, 16), :]
        queries = blocks[pl.ds(at, 16), :].astype(f32)
        scaled_q = (queries * 0.25).astype(bf16)
        ones = marked[rows, :]
        grads = sums_grad[rows, :]
        from_carry = dot_nn(carry[pl.ds(pl.multiple_of(h * FEATS, 16), FEATS), :], grads) * keep_first_link
        query_total = features_back(queries, from_carry, True)
        small = pl.multiple_of(h * 16, 16)
        for start in range(0, length, TBLOCK):
            stop = start + TBLOCK
            seen = mask[:stop, start:stop]
            shifted, weights = weights_of(keys[:, :stop], scaled_q[:, start:stop], seen)
            grad_block = grads[:, start:stop]
            score_grad = (dot_tn(ones[:, :stop], grad_block) * shifted * seen).astype(bf16)
            query_grad[pl.ds(small, 16), start:stop] = (
                query_total[:, start:stop] + dot_nn(keys[:, :stop], score_grad) * 0.25
            )
            key_part = dot_nt(scaled_q[:, start:stop], score_grad)
            value_part = dot_nt(grad_block, weights.astype(bf16))
            if start > 0:
                key_grad[pl.ds(small, 16), :start] += key_part[:, :start]
                value_grad[rows, :start] += value_part[:, :start]
            key_grad[pl.ds(small, 16), start:stop] = key_part[:, start:]
            value_grad[rows, start:stop] = value_part[:, start:]
        return 0

    def chain_slot(slot):
        for back in range(1, 4):
            number = slot - back + 1
            if 0 <= number < GROUPS:

                @pl.when(place == planes - 1 - back)
                def _():
                    part = pl.ds(number * span, span)
                    hand_on(number).wait_recv()
                    if back < 3:
                        message[part, :] = (
                            state[part, :].astype(f32) + (cond_whole * cond_after) * later[part, :].astype(f32)
                        ).astype(bf16)
                        hand_on(number).start()

    for number in range(GROUPS):
        lax.fori_loop(number * group, (number + 1) * group, head_local, 0)
        chain_slot(number)
    to_stripes(wide_own, slice(48, 64), dot_nn(rank_grad_t, attended[...]).astype(bf16))
    rank_out_t = rank_out[...].astype(f32).T.astype(bf16)
    to_stripes(wide_own, slice(64, 80), dot_nt(rank_out_t, branch_t[...]).astype(bf16))
    wide_share.z_start()
    chain_slot(GROUPS)
    ff_share.z_sum()
    chain_slot(GROUPS + 1)

    doc8 = jnp.broadcast_to(doc_row, (8, length))
    next8 = jnp.broadcast_to(next_docs, (8, 2))
    same_after = [(doc8 == sooner_by(doc8, offset, next8)).astype(f32)[0:1] for offset in (1, 2)]

    def head_finish(h, _):
        at = pl.multiple_of(h * PER_HEAD, PER_HEAD)
        rows = pl.ds(pl.multiple_of(h * VROWS, VROWS), VROWS)
        small = pl.ds(pl.multiple_of(h * 16, 16), 16)
        block = blocks[pl.ds(at, PER_HEAD), :]
        prior = halo[:, pl.ds(at, PER_HEAD)].astype(f32).T[32 : 32 + DV, 14:16]
        came = later[pl.ds(pl.multiple_of(h * FEATS, 16), FEATS), :]
        tap = taps[h]
        keys = block[16:32].astype(f32)
        key_feats = features(keys, keep_last, False)
        key_total = key_grad[small, :] + features_back(keys, dot_nn(came, marked[rows, :]) * keep_last, False)
        values = (value_grad[rows, :] + dot_tn(came, key_feats))[:DV]
        _, conv_out, gate_in, sigmoid = values_of(block, prior, tap, doc_row, prev_docs)
        conv_grad = values * gate_in * sigmoid
        proj_grad[pl.ds(at, 16), :] = query_grad[small, :].astype(bf16)
        proj_grad[pl.ds(at + 16, 16), :] = key_total.astype(bf16)
        proj_grad[pl.ds(at + 32, DV), :] = conv_backward(
            conv_grad, jnp.zeros((DV, 2), f32), tap, same_after
        ).astype(bf16)
        proj_grad[pl.ds(at + 32 + DV, DV), :] = (
            values * conv_out * sigmoid * (1.0 + gate_in * (1.0 - sigmoid))
        ).astype(bf16)
        conv_last[pl.ds(pl.multiple_of(h * DV, 16), DV), :] = conv_grad[:, length - 128 :]
        early = jnp.concatenate([conv_grad[:, :128], jnp.zeros((16, 128), f32)], axis=0).T
        halo_send[:, pl.ds(pl.multiple_of(h * 128, 128), 128)] = early[0:8]
        return 0

    for number in range(GROUPS):
        lax.fori_loop(number * group, (number + 1) * group, head_finish, 0)
        if number == 2:
            wide_share.z_sum()
    to_before = pltpu.make_async_remote_copy(
        src_ref=halo_send, dst_ref=halo_next, send_sem=halo_sems.at[0], recv_sem=halo_sems.at[1],
        device_id={"fsdp": me, "seq": (place + planes - 1) % planes}, device_id_type=MESH,
    )

    @pl.when(place > 0)
    def _():
        to_before.start()

    @pl.when(place == planes - 1)
    def _():
        halo_next[...] = jnp.zeros(halo_next.shape, f32)

    ff_share.gather_start()
    rank_in_t = rank_in[...].astype(f32).T.astype(bf16)

    @pl.when(place < planes - 1)
    def _():
        to_before.wait_recv()

    def head_end(h, total):
        at = pl.multiple_of(h * PER_HEAD, PER_HEAD)
        after = halo_next[:, pl.ds(pl.multiple_of(h * 128, 128), 128)].T[:DV, 0:2]
        last = conv_backward(
            conv_last[pl.ds(pl.multiple_of(h * DV, 16), DV), :], after, taps[h], [s[:, length - 128 :] for s in same_after]
        )
        proj_grad[pl.ds(at + 32, DV), length - 128 :] = last.astype(bf16)
        vg_terms[h, 0:16, 0:DV] = dot_nt(rank_in_t[32:48], proj_grad[pl.ds(at + 32, DV), :])
        vg_terms[h, 16:32, 0:DV] = dot_nt(rank_in_t[48:64], proj_grad[pl.ds(at + 32 + DV, DV), :])
        qk_terms[h, 0:16, 0:16] = dot_nt(rank_in_t[0:16], proj_grad[pl.ds(at, 16), :])
        qk_terms[h, 16:32, 0:16] = dot_nt(rank_in_t[16:32], proj_grad[pl.ds(at + 16, 16), :])
        return total + dot_nn(up_maps[:, pl.ds(at, PER_HEAD)], proj_grad[pl.ds(at, PER_HEAD), :])

    rank_in_grad_t = lax.fori_loop(0, HEAD_COUNT, head_end, jnp.zeros((64, length), f32)).astype(bf16)
    vg_rows = jnp.concatenate([vg_terms[h, :, 0:DV] for h in range(HEAD_COUNT)], axis=1).astype(bf16)
    up_own[0] = vg_rows[0:16]
    up_own[1] = vg_rows[16:32]
    qk_rows = jnp.concatenate(
        [qk_terms[h, 0:16, 0:16] for h in range(HEAD_COUNT)]
        + [qk_terms[h, 16:32, 0:16] for h in range(HEAD_COUNT)]
        + [chosen[...] * (1.0 / planes), jnp.zeros((16, width - 512 - 128), f32)],
        axis=1,
    )
    up_own[2] = qk_rows.astype(bf16)
    up_own[3] = jnp.zeros((16, width), bf16)
    up_share.z_start()
    in_terms = dot_nn(rank_in_grad_t, hidden1[...]).astype(bf16)
    for n in range(4):
        down_own[n] = in_terms[16 * n : 16 * n + 16]
    down_share.z_start()
    wide_share.gather_start()
    ff_share.relay()

    for number in range(blocks_in):
        load_in(number).wait()
        rows = slice(number * step, (number + 1) * step)
        part = dot_nn(in_tile[number % 2], proj_grad[...]) + dot_tn(in_down[:, rows], rank_in_grad_t)
        input_grad[:, rows] = part.T
        if number + 2 < blocks_in:
            load_in(number + 2).start()
        if number == blocks_in - 3:
            up_share.z_sum()
    down_share.z_sum()
    wide_share.relay()
    ff_share.relay_last()

    def finish_rows(rows):
        value = x[rows, :].astype(f32)
        root = row_root(value)
        normed = value * root
        scaled = input_grad[rows, :] * gain1[...]
        input_grad[rows, :] = resid_grad[rows, :] + root * (
            scaled - normed * jnp.mean(scaled * normed, -1, keepdims=True)
        )

    by_rows(length, finish_rows)
    up_share.gather_start()
    down_share.gather_start()
    wide_share.relay_last()
    up_share.relay()
    down_share.relay()
    ff_share.finish()
    wide_share.finish()
    up_share.relay_last()
    down_share.relay_last()
    up_share.finish()
    down_share.finish()

    @pl.when(place > 0)
    def _():
        to_before.wait_send()
        for number in range(GROUPS):
            hand_on(number).wait_send()


def call_t(args, weights):
    f32, bf16 = jnp.float32, jnp.bfloat16
    length, width = args[0].shape
    count, planes = lax.axis_size("fsdp"), lax.axis_size("seq")
    columns = weights[0].shape[1]
    ff = args[-2].shape[1]
    whole = pl.BlockSpec(memory_space=pltpu.VMEM)
    anyplace = pl.BlockSpec(memory_space=pl.ANY)
    shapes = [(planes, 48, stripe_width(ff)), (planes, 80, stripe_width(width)), (planes, 16, width), (planes, 16, width)]
    shares = []
    for shape in shapes:
        shares += [pltpu.VMEM(shape, bf16)] * 3
    return pl.pallas_call(
        t_kernel,
        in_specs=[anyplace if n in FETCHED else whole for n in range(len(args))] + [anyplace] * 2,
        out_specs=[whole] + [anyplace] * 4,
        out_shape=[jax.ShapeDtypeStruct((length, width), f32)]
        + [jax.ShapeDtypeStruct((count,) + shape, bf16) for shape in shapes],
        scratch_shapes=[pltpu.VMEM(args[n].shape, args[n].dtype) for n in FETCHED]
        + [
            pltpu.SemaphoreType.DMA((len(FETCHED),)),
            pltpu.VMEM((width, width), bf16),
            pltpu.VMEM((2, 256, columns), bf16),
            pltpu.VMEM((width, length), bf16),
            pltpu.VMEM((width, length), bf16),
            pltpu.VMEM((HEAD_COUNT * VROWS, length), bf16),
            pltpu.VMEM((HEAD_COUNT * FEATS, VROWS), bf16),
            pltpu.VMEM((HEAD_COUNT * FEATS, VROWS), bf16),
            pltpu.VMEM((HEAD_COUNT * FEATS, VROWS), bf16),
            pltpu.VMEM((HEAD_COUNT * 16, length), f32),
            pltpu.VMEM((HEAD_COUNT * 16, length), f32),
            pltpu.VMEM((HEAD_COUNT * VROWS, length), f32),
            pltpu.VMEM((columns, length), bf16),
            pltpu.VMEM((width, 128), f32),
            pltpu.VMEM((8, HEAD_COUNT * 128), f32),
            pltpu.VMEM((8, HEAD_COUNT * 128), f32),
            pltpu.VMEM((HEAD_COUNT, 32, 128), f32),
            pltpu.VMEM((HEAD_COUNT, 32, 128), f32),
            pltpu.VMEM((length, length), f32),
        ]
        + shares
        + [
            pltpu.SemaphoreType.DMA((2, GROUPS)),
            pltpu.SemaphoreType.DMA((2,)),
            pltpu.SemaphoreType.DMA((3,)),
            pltpu.SemaphoreType.DMA((4, 2 * (planes - 1))),
            pltpu.SemaphoreType.DMA((4, 2 * (planes - 1))),
            pltpu.SemaphoreType.DMA((4, 8)),
            pltpu.SemaphoreType.DMA((4, 8)),
            pltpu.SemaphoreType.DMA((4,)),
        ],
        compiler_params=pltpu.CompilerParams(
            collective_id=2, has_side_effects=True, vmem_limit_bytes=62 * 1024 * 1024
        ),
    )(*args, *weights)


def place_kernel(where, ff, wide, down, up, in_down, qk_up, vg_up, out_down, out_up, gu_down, gu_up, ffd_down, ffd_up):
    f32 = jnp.float32

    def unstripe(part, at, out):
        size, columns = part.shape[3], out.shape[2]
        for n in range(part.shape[1]):
            start, stop = n * size, min((n + 1) * size, columns)
            out[0, :, start:stop] = part[0, n, at : at + out.shape[1], 0 : stop - start].astype(f32)

    unstripe(ff, 0, gu_up)
    unstripe(ff, 32, ffd_down)
    unstripe(wide, 0, gu_down)
    unstripe(wide, 32, ffd_up)
    unstripe(wide, 48, out_down)
    unstripe(wide, 64, out_up)
    for n in range(4):
        in_down[0, 16 * n : 16 * n + 16] = down[0, n].astype(f32)
    vg_up[0, 0:16] = up[0, 0].astype(f32)
    vg_up[0, 16:32] = up[0, 1].astype(f32)
    qk_up[0, 0:16] = up[0, 2, :, 0:256].astype(f32)
    qk_up[0, 16:32] = up[0, 2, :, 256:512].astype(f32)


def call_place(where, parts, widths):
    rows_ff, rows_w = widths
    outs = [(64, rows_w), (32, 256), (32, rows_w), (16, rows_w), (16, rows_w), (32, rows_w), (32, rows_ff), (16, rows_ff), (16, rows_w)]

    def block(shape):
        return pl.BlockSpec((1,) + shape, lambda a, where: (a, 0, 0))

    def picked(array):
        return pl.BlockSpec((1,) + array.shape[1:], lambda a, where: (where[a], 0, 0, 0))

    return pl.pallas_call(
        place_kernel,
        grid_spec=pltpu.PrefetchScalarGridSpec(
            num_scalar_prefetch=1,
            grid=(ADAPTER_COUNT,),
            in_specs=[picked(part) for part in parts],
            out_specs=[block(shape) for shape in outs],
        ),
        out_shape=[jax.ShapeDtypeStruct((ADAPTER_COUNT,) + shape, jnp.float32) for shape in outs],
        compiler_params=pltpu.CompilerParams(vmem_limit_bytes=62 * 1024 * 1024),
    )(where, *parts)


def pick_kernel(
    chosen, in_down_all, qk_all, vg_all, out_down_all, out_up_all, gu_down_all, gu_up_all, ffd_down_all, ffd_up_all,
    taps_all, docs, gain1, gain2,
    in_down, up_maps, out_down, out_up, gu_down, gu_up, ffd_down, ffd_up, taps, doc_row, doc_col, gain1_row, gain2_row, id_block,
):
    f32, bf16 = jnp.float32, jnp.bfloat16
    in_down[...] = in_down_all[0]
    out_down[...] = out_down_all[0]
    out_up[...] = out_up_all[0]
    gu_down[...] = gu_down_all[0]
    gu_up[0:16] = gu_up_all[0, 0]
    gu_up[16:32] = gu_up_all[0, 1]
    ffd_down[...] = ffd_down_all[0]
    ffd_up[...] = ffd_up_all[0]
    up_maps[...] = jnp.zeros(up_maps.shape, bf16)
    three = jnp.concatenate([taps_all[...], jnp.zeros((5, taps_all.shape[1]), f32)], axis=0)
    for h in range(HEAD_COUNT):
        at = h * PER_HEAD
        for n in range(2):
            up_maps[16 * n : 16 * n + 16, at + 16 * n : at + 16 * n + 16] = qk_all[0, n, :, 16 * h : 16 * h + 16]
            start = at + 32 + n * DV
            up_maps[32 + 16 * n : 48 + 16 * n, start : start + DV] = vg_all[0, n, :, DV * h : DV * h + DV]
        taps[h] = three[:, DV * h : DV * h + DV].T
    row = docs[...].astype(f32)
    doc_row[...] = row
    doc_col[...] = jnp.broadcast_to(row, (8, row.shape[1])).T[:, 0:1]
    gain1_row[...] = gain1[...].reshape(1, -1)
    gain2_row[...] = gain2[...].reshape(1, -1)
    id_block[...] = jnp.full(id_block.shape, chosen[0], jnp.int32).astype(f32)


def call_pick(chosen, tables, taps, docs, gain1, gain2):
    f32, bf16 = jnp.float32, jnp.bfloat16
    in_down, qk, vg, out_down, out_up, gu_down, gu_up, ffd_down, ffd_up = tables
    length = docs.shape[1]
    width, ff = out_up.shape[2], ffd_down.shape[2]

    def picked(table):
        zeros = (0,) * (table.ndim - 1)
        return pl.BlockSpec((1,) + table.shape[1:], lambda n, chosen: (chosen[0],) + zeros)

    def whole(shape):
        return pl.BlockSpec(shape, lambda n, chosen: (0,) * len(shape))

    outs = [
        ((64, width), bf16), ((64, HEAD_COUNT * PER_HEAD), bf16), ((16, width), bf16), ((16, width), bf16), ((32, width), bf16),
        ((32, ff), bf16), ((16, ff), bf16), ((16, width), bf16), ((HEAD_COUNT, DV, 8), f32), ((1, length), f32), ((length, 1), f32),
        ((1, width), f32), ((1, width), f32), ((16, 128), f32),
    ]
    rest = (taps, docs, gain1, gain2)
    return pl.pallas_call(
        pick_kernel,
        grid_spec=pltpu.PrefetchScalarGridSpec(
            num_scalar_prefetch=1,
            grid=(1,),
            in_specs=[picked(table) for table in tables] + [whole(array.shape) for array in rest],
            out_specs=[whole(shape) for shape, _ in outs],
        ),
        out_shape=[jax.ShapeDtypeStruct(shape, kind) for shape, kind in outs],
        compiler_params=pltpu.CompilerParams(vmem_limit_bytes=62 * 1024 * 1024),
    )(chosen, *tables, *rest)


def call_heads(kernel, length, ins, outs, scratch=()):
    def spec(shape, how):
        if how == "rows":
            return pl.BlockSpec((shape[0] // HEAD_COUNT,) + shape[1:], lambda h: (h,) + (0,) * (len(shape) - 1))
        if how == "cols":
            return pl.BlockSpec((shape[0], shape[1] // HEAD_COUNT), lambda h: (0, h))
        return pl.BlockSpec(shape, lambda h: (0,) * len(shape))

    return pl.pallas_call(
        kernel,
        grid=(HEAD_COUNT,),
        in_specs=[spec(a.shape, how) for a, how in ins],
        out_specs=[spec(s.shape, how) for s, how in outs],
        out_shape=[s for s, _ in outs],
        scratch_shapes=list(scratch),
        compiler_params=pltpu.CompilerParams(vmem_limit_bytes=48 * 1024 * 1024),
    )(*[a for a, _ in ins])


def shift_pairs(count, step):
    return [(i, i + step) for i in range(count) if 0 <= i + step < count]


def chain(own, whole, link, step):
    count = lax.axis_size("seq")
    pairs = shift_pairs(count, step)
    message = own
    for _ in range(count - 2):
        got = lax.ppermute(message, "seq", pairs)
        message = (own.astype(jnp.float32) + (whole * link) * got.astype(jnp.float32)).astype(jnp.bfloat16)
    got = lax.ppermute(message, "seq", pairs)
    return (got.astype(jnp.float32) * link).astype(jnp.bfloat16)


def product(spec, left, right):
    return jnp.einsum(spec, left, right, preferred_element_type=jnp.float32)


def rms_forward(value, gain):
    inv_root = lax.rsqrt(jnp.mean(value * value, -1, keepdims=True) + epsilon)
    normed = value * inv_root
    return (normed, inv_root, (normed * gain).astype(jnp.bfloat16))


def rms_backward(grad_hidden, normed, inv_root, gain):
    scaled = grad_hidden * gain
    return inv_root * (scaled - normed * jnp.mean(scaled * normed, -1, keepdims=True))


def up_by_head(querykey, valuegate):
    parts = [
        (querykey[0], 0, FEATURE_SIZE),
        (querykey[1], FEATURE_SIZE, FEATURE_SIZE),
        (valuegate[0], 2 * FEATURE_SIZE, DV),
        (valuegate[1], 2 * FEATURE_SIZE + DV, DV),
    ]
    rows = [
        jnp.pad(
            part.reshape(ADAPTER_RANK, HEAD_COUNT, size),
            ((0, 0), (0, 0), (at, PER_HEAD - at - size)),
        )
        for part, at, size in parts
    ]
    return jnp.concatenate(rows, axis=0).reshape(4 * ADAPTER_RANK, HEAD_COUNT * PER_HEAD)


def by_collectives(
    layer_input_rows,
    segments,
    sequence_adapter_index,
    output_gradient,
    mixer_norm_gain,
    feedforward_norm_gain,
    convolution_taps,
    mixer_input_weight,
    mixer_output_weight,
    gate_up_weight,
    down_weight,
    adapter_input_down,
    adapter_querykey_up,
    adapter_valuegate_up,
    adapter_output_down,
    adapter_output_up,
    adapter_gateup_down,
    adapter_gateup_up,
    adapter_feedforward_down,
    adapter_feedforward_up,
):
    batch, length, width = layer_input_rows.shape
    assert batch == 1
    seq_count = lax.axis_size("seq")
    ff = gate_up_weight.shape[1] // 2
    bf16, f32 = jnp.bfloat16, jnp.float32
    chosen = sequence_adapter_index[0, 0]

    def select(table):
        return lax.dynamic_index_in_dim(table, chosen, 0, keepdims=False)

    in_down = select(adapter_input_down.swapaxes(1, 2))
    up_maps = up_by_head(select(adapter_querykey_up), select(adapter_valuegate_up))
    out_down = select(adapter_output_down.swapaxes(1, 2))
    out_up = select(adapter_output_up)
    gu_down = select(adapter_gateup_down.swapaxes(1, 2))
    gu_up = select(adapter_gateup_up)
    ffd_down = select(adapter_feedforward_down.swapaxes(1, 2))
    ffd_up = select(adapter_feedforward_up)
    mixer_in, mixer_out, gate_up, down_w = (
        lax.all_gather(mixer_input_weight, "fsdp", axis=0, tiled=True),
        lax.all_gather(mixer_output_weight, "fsdp", axis=0, tiled=True),
        lax.all_gather(gate_up_weight, "fsdp", axis=0, tiled=True),
        lax.all_gather(down_weight, "fsdp", axis=0, tiled=True),
    )
    docs = segments.astype(f32)
    place = lax.axis_index("seq")
    edge = jnp.concatenate([docs[:, :1], docs[:, length - 2 :], jnp.zeros((1, 125), f32)], axis=1)
    before_edge = lax.ppermute(edge, "seq", shift_pairs(seq_count, 1))
    after_edge = lax.ppermute(edge, "seq", shift_pairs(seq_count, -1))
    prev_docs = jnp.where(place == 0, -1.0, before_edge[:, 1:3])
    next_doc = jnp.where(place == seq_count - 1, -1.0, after_edge[:, 0])
    link_before = (prev_docs[0, 1] == docs[0, 0]).astype(f32)
    link_after = (next_doc[0] == docs[0, length - 1]).astype(f32)
    whole = (docs[0, 0] == docs[0, length - 1]).astype(f32)
    prev_pad = jnp.pad(prev_docs, ((0, 0), (0, 126)))
    doc_col = docs.reshape(length, 1)
    taps = jnp.pad(convolution_taps.T.reshape(HEAD_COUNT, DV, 3), ((0, 0), (0, 0), (0, 5)))

    inputs_f = layer_input_rows[0].astype(f32)
    grad_out = output_gradient[0]
    normed1, root1, hidden1 = rms_forward(inputs_f, mixer_norm_gain)
    rank_in = product("td,rd->tr", hidden1, in_down).astype(bf16)
    projected = (
        product("td,de->te", hidden1, mixer_in) + product("tr,re->te", rank_in, up_maps)
    ).astype(bf16)
    halo = lax.ppermute(projected[length - 16 :], "seq", shift_pairs(seq_count, 1))
    mask = pltpu.VMEM((length, length), f32)
    heads = HEAD_COUNT
    blocks, values, sums, state = call_heads(
        f1_kernel,
        length,
        [(projected, "cols"), (halo, "cols"), (taps, "rows"), (docs, None), (doc_col, None), (prev_pad, None)],
        [
            (jax.ShapeDtypeStruct((heads * PER_HEAD, length), bf16), "rows"),
            (jax.ShapeDtypeStruct((heads * VROWS, length), bf16), "rows"),
            (jax.ShapeDtypeStruct((heads * VROWS, length), f32), "rows"),
            (jax.ShapeDtypeStruct((heads * FEATS, VROWS), bf16), "rows"),
        ],
        [mask],
    )
    carry = chain(state, whole, link_before, 1)
    attended_t, denominator = call_heads(
        f2_kernel,
        length,
        [(blocks, "rows"), (sums, "rows"), (carry, "rows"), (docs, None)],
        [
            (jax.ShapeDtypeStruct((heads * DV, length), bf16), "rows"),
            (jax.ShapeDtypeStruct((heads * 8, length), f32), "rows"),
        ],
    )
    attended = attended_t.T
    rank_out = product("td,rd->tr", attended, out_down).astype(bf16)
    resid = (
        inputs_f
        + product("td,de->te", attended, mixer_out)
        + product("tr,re->te", rank_out, out_up)
    )
    normed2, root2, hidden2 = rms_forward(resid, feedforward_norm_gain)
    rank_mlp = product("td,rd->tr", hidden2, gu_down).astype(bf16)
    rank_ffd_grad = product("te,re->tr", grad_out, ffd_up).astype(bf16)
    inner_grad = product("te,fe->tf", grad_out, down_w) + product("tr,rf->tf", rank_ffd_grad, ffd_down)
    gate_pre = product("td,de->te", hidden2, gate_up[:, :ff]) + product(
        "tr,re->te", rank_mlp[:, :ADAPTER_RANK], gu_up[0]
    )
    up_pre = product("td,de->te", hidden2, gate_up[:, ff:]) + product(
        "tr,re->te", rank_mlp[:, ADAPTER_RANK:], gu_up[1]
    )
    sigmoid = jax.nn.sigmoid(gate_pre)
    gate_val = gate_pre * sigmoid
    inner_act = (gate_val * up_pre).astype(bf16)
    gate_grad = (inner_grad * up_pre * (sigmoid * (1.0 + gate_pre * (1.0 - sigmoid)))).astype(bf16)
    up_grad = (inner_grad * gate_val).astype(bf16)
    rank_ffd = product("tf,rf->tr", inner_act, ffd_down).astype(bf16)
    output = (
        resid + product("tf,fe->te", inner_act, down_w) + product("tr,re->te", rank_ffd, ffd_up)
    ).astype(bf16)
    rank_mlp_grad = jnp.concatenate(
        [product("tf,rf->tr", gate_grad, gu_up[0]), product("tf,rf->tr", up_grad, gu_up[1])], -1
    ).astype(bf16)
    hidden2_grad = (
        product("tf,df->td", gate_grad, gate_up[:, :ff])
        + product("tf,df->td", up_grad, gate_up[:, ff:])
        + product("tr,rd->td", rank_mlp_grad, gu_down)
    )
    resid_grad = grad_out.astype(f32) + rms_backward(hidden2_grad, normed2, root2, feedforward_norm_gain)
    branch_grad = resid_grad.astype(bf16)
    rank_out_grad = product("te,re->tr", branch_grad, out_up).astype(bf16)
    attended_grad = (
        product("te,de->td", branch_grad, mixer_out) + product("tr,rd->td", rank_out_grad, out_down)
    ).astype(bf16)
    grad_t = attended_grad.T
    later, query_grad, key_grad, value_grad = call_heads(
        b1_kernel,
        length,
        [(blocks, "rows"), (values, "rows"), (grad_t, "rows"), (attended_t, "rows"), (denominator, "rows"), (carry, "rows"), (docs, None), (doc_col, None)],
        [
            (jax.ShapeDtypeStruct((heads * FEATS, VROWS), bf16), "rows"),
            (jax.ShapeDtypeStruct((heads * 16, length), f32), "rows"),
            (jax.ShapeDtypeStruct((heads * 16, length), f32), "rows"),
            (jax.ShapeDtypeStruct((heads * VROWS, length), f32), "rows"),
        ],
        [mask],
    )
    later = chain(later, whole, link_after, -1)
    projected_grad, first_conv, tail_grad = call_heads(
        b2_kernel,
        length,
        [(blocks, "rows"), (values, "rows"), (later, "rows"), (query_grad, "rows"), (key_grad, "rows"), (value_grad, "rows"), (halo, "cols"), (taps, "rows"), (docs, None), (prev_pad, None)],
        [
            (jax.ShapeDtypeStruct((length, heads * PER_HEAD), bf16), "cols"),
            (jax.ShapeDtypeStruct((16, heads * PER_HEAD), f32), "cols"),
            (jax.ShapeDtypeStruct((16, heads * PER_HEAD), f32), "cols"),
        ],
    )
    next_conv = lax.ppermute(first_conv[:2], "seq", shift_pairs(seq_count, -1))
    taps_row = jnp.pad(
        convolution_taps.reshape(3, heads, DV),
        ((0, 0), (0, 0), (2 * FEATURE_SIZE, PER_HEAD - 2 * FEATURE_SIZE - DV)),
    ).reshape(3, heads * PER_HEAD)
    after_docs = jnp.where(place == seq_count - 1, -1.0, after_edge[0, 0])
    link_1 = (after_docs == docs[0, length - 1]).astype(f32)
    link_2 = (after_docs == docs[0, length - 2]).astype(f32)
    second = (docs[0, 1] == docs[0, 0]).astype(f32)
    second_next = lax.ppermute(second, "seq", shift_pairs(seq_count, -1))
    extra_last = taps_row[1] * next_conv[0] * link_1 + taps_row[2] * next_conv[1] * link_1 * second_next
    extra_before = taps_row[2] * next_conv[0] * link_2
    extra = jnp.concatenate(
        [jnp.zeros((14, heads * PER_HEAD), f32), extra_before[None], extra_last[None]], axis=0
    )
    projected_grad = lax.dynamic_update_slice(
        projected_grad, (tail_grad + extra).astype(bf16), (length - 16, 0)
    )
    rank_in_grad = product("te,re->tr", projected_grad, up_maps).astype(bf16)
    hidden1_grad = product("te,de->td", projected_grad, mixer_in) + product(
        "tr,rd->td", rank_in_grad, in_down
    )
    input_grad = resid_grad + rms_backward(hidden1_grad, normed1, root1, mixer_norm_gain)

    wide = product("tr,te->re", rank_in, projected_grad).reshape(4, ADAPTER_RANK, heads, PER_HEAD)
    term_qk = jnp.stack(
        [wide[0, :, :, 0:16].reshape(ADAPTER_RANK, -1), wide[1, :, :, 16:32].reshape(ADAPTER_RANK, -1)]
    )
    term_vg = jnp.concatenate(
        [
            wide[2, :, :, 32 : 32 + DV].reshape(ADAPTER_RANK, -1),
            wide[3, :, :, 32 + DV :].reshape(ADAPTER_RANK, -1),
        ]
    )
    by_width = jnp.concatenate(
        [
            product("tr,td->rd", rank_in_grad, hidden1),
            term_vg,
            product("tr,td->rd", rank_out_grad, attended),
            product("tr,td->rd", rank_out, branch_grad),
            product("tr,td->rd", rank_mlp_grad, hidden2),
            product("tr,td->rd", rank_ffd, grad_out),
        ]
    )
    by_ff = jnp.concatenate(
        [
            product("tr,tf->rf", rank_mlp[:, :ADAPTER_RANK], gate_grad),
            product("tr,tf->rf", rank_mlp[:, ADAPTER_RANK:], up_grad),
            product("tr,tf->rf", rank_ffd_grad, inner_act),
        ]
    )
    by_rank = jnp.concatenate([term_qk.reshape(32, -1), jnp.full((16, 256), chosen.astype(f32) / seq_count)])
    by_width, by_ff, by_rank = spread(by_width, by_ff, by_rank)
    sequences = by_rank.shape[0]
    onehot = (by_rank[:, 32, 0][None, :] == jnp.arange(ADAPTER_COUNT, dtype=bf16)[:, None])

    if sequences == ADAPTER_COUNT:
        where = jnp.argmax(onehot, axis=1)

        def arrange(rows):
            return jnp.take(rows, where, axis=0).astype(f32)
    else:

        def arrange(rows):
            return jnp.einsum("as,s...->a...", onehot.astype(f32), rows.astype(f32), precision="highest")

    sizes = [64, 32, 16, 16, 32, 16]
    cut = [sum(sizes[:n]) for n in range(len(sizes) + 1)]
    widths = [arrange(by_width[:, cut[n] : cut[n + 1]]) for n in range(len(sizes))]
    return (
        output[None],
        input_grad[None],
        widths[0].swapaxes(1, 2),
        arrange(by_rank[:, :32]).reshape(ADAPTER_COUNT, 2, ADAPTER_RANK, -1),
        widths[1].reshape(ADAPTER_COUNT, 2, ADAPTER_RANK, width),
        widths[2].swapaxes(1, 2),
        widths[3],
        widths[4].swapaxes(1, 2),
        arrange(by_ff[:, :32]).reshape(ADAPTER_COUNT, 2, ADAPTER_RANK, ff),
        arrange(by_ff[:, 32:]).swapaxes(1, 2),
        widths[5],
    )


def by_kernels(
    layer_input_rows,
    segments,
    sequence_adapter_index,
    output_gradient,
    mixer_norm_gain,
    feedforward_norm_gain,
    convolution_taps,
    mixer_input_weight,
    mixer_output_weight,
    gate_up_weight,
    down_weight,
    adapter_input_down,
    adapter_querykey_up,
    adapter_valuegate_up,
    adapter_output_down,
    adapter_output_up,
    adapter_gateup_down,
    adapter_gateup_up,
    adapter_feedforward_down,
    adapter_feedforward_up,
):
    x, grad_out = layer_input_rows[0], output_gradient[0]
    width, ff = x.shape[1], adapter_gateup_up.shape[-1]
    tables = (
        adapter_input_down.swapaxes(1, 2), adapter_querykey_up, adapter_valuegate_up, adapter_output_down.swapaxes(1, 2),
        adapter_output_up, adapter_gateup_down.swapaxes(1, 2), adapter_gateup_up, adapter_feedforward_down.swapaxes(1, 2),
        adapter_feedforward_up,
    )
    *maps, taps, doc_row, doc_col, gain1, gain2, id_block = call_pick(
        sequence_adapter_index[0], tables, convolution_taps, segments, mixer_norm_gain, feedforward_norm_gain
    )
    in_down, up_maps, out_down, out_up = maps[:4]
    shards = (mixer_input_weight, mixer_output_weight, gate_up_weight, down_weight)
    mixer_in, mixer_out, _, _, output, *kept = call_m(x, grad_out, gain1, gain2, taps, doc_row, doc_col, maps, shards)
    *kept, next_docs = kept
    input_grad, *parts = call_t(
        (x, gain1, taps, doc_row, doc_col, next_docs, id_block, in_down, up_maps, out_down, out_up, *kept),
        (mixer_in, mixer_out),
    )
    chosen = parts[3][:, 2, 0, 512]
    where = jnp.argmax(chosen[None, :] == jnp.arange(ADAPTER_COUNT, dtype=jnp.bfloat16)[:, None], axis=1).astype(jnp.int32)
    in_down, qk_up, vg_up, out_down, out_up, gu_down, gu_up, ffd_down, ffd_up = call_place(
        where, parts, (ff, width)
    )
    return (
        output[None],
        input_grad[None],
        in_down.swapaxes(1, 2),
        qk_up.reshape(ADAPTER_COUNT, 2, ADAPTER_RANK, -1),
        vg_up.reshape(ADAPTER_COUNT, 2, ADAPTER_RANK, width),
        out_down.swapaxes(1, 2),
        out_up,
        gu_down.swapaxes(1, 2),
        gu_up.reshape(ADAPTER_COUNT, 2, ADAPTER_RANK, ff),
        ffd_down.swapaxes(1, 2),
        ffd_up,
    )


def spread(*terms):
    summed = lax.psum(terms, "seq")
    return [lax.all_gather(term.astype(jnp.bfloat16), "fsdp") for term in summed]


def solution(mesh):
    kernels = mesh.shape["fsdp"] == ADAPTER_COUNT and mesh.shape["seq"] == 4
    return jax.shard_map(
        by_kernels if kernels else by_collectives,
        mesh=mesh,
        in_specs=(
            P("fsdp", "seq", None),
            P("fsdp", "seq"),
            P("fsdp", None),
            P("fsdp", "seq", None),
            P(),
            P(),
            P(),
            P("fsdp", None),
            P("fsdp", None),
            P("fsdp", None),
            P("fsdp", None),
        )
        + (P(),) * 9,
        out_specs=(P("fsdp", "seq", None), P("fsdp", "seq", None)) + (P(),) * 9,
        check_vma=False,
    )
```

```python
import functools

import jax
import jax.numpy as jnp
from jax import lax
from jax.experimental import pallas as pl
from jax.experimental.pallas import tpu as pltpu
from jax.sharding import PartitionSpec as P

HEAD_COUNT = 16
FEATURE_SIZE = 16
DV = 112
ADAPTER_RANK = 16
ADAPTER_COUNT = 8
PER_HEAD = 2 * FEATURE_SIZE + 2 * DV
TBLOCK = 128

epsilon = 1e-05


FEATS = 176
VROWS = 128


def dot_nn(a, b):
    return lax.dot_general(a, b, (((1,), (0,)), ((), ())), preferred_element_type=jnp.float32)


def dot_nt(a, b):
    return lax.dot_general(a, b, (((1,), (1,)), ((), ())), preferred_element_type=jnp.float32)


def dot_tn(a, b):
    return lax.dot_general(a, b, (((0,), (0,)), ((), ())), preferred_element_type=jnp.float32)


def group_scale(shift):
    return 1.0 / 32.0 if shift in (0, 8) else 1.0 / 16.0


def cycle(rows, shift):
    if shift == 0:
        return rows
    return jnp.concatenate([rows[shift:], rows[:shift]], axis=0)


def features(rows, keep, scaled):
    length = rows.shape[1]
    rows_kept = rows * keep
    parts = []
    for shift in range(9):
        item = rows_kept * cycle(rows, shift)
        parts.append(item * group_scale(shift) if scaled else item)
    parts.append(rows_kept * 0.25 if scaled else rows_kept)
    first_row = lax.broadcasted_iota(jnp.int32, (16, length), 0) == 0
    parts.append(jnp.where(first_row, jnp.broadcast_to(keep, (16, length)), 0.0))
    return jnp.concatenate(parts, axis=0).astype(jnp.bfloat16)


def features_back(rows, grad, scaled):
    total = grad[144:160] * 0.25 if scaled else grad[144:160]
    for shift in range(9):
        item = grad[16 * shift : 16 * shift + 16]
        if scaled:
            item = item * group_scale(shift)
        total = total + item * cycle(rows, shift) + cycle(item * rows, (16 - shift) % 16)
    return total


def later_by(rows, offset, before):
    lane = lax.broadcasted_iota(jnp.int32, rows.shape, 1)
    moved = pltpu.roll(rows, offset, 1)
    if offset == 1:
        return jnp.where(lane == 0, before[:, 1:2], moved)
    return jnp.where(lane == 0, before[:, 0:1], jnp.where(lane == 1, before[:, 1:2], moved))


def sooner_by(rows, offset, after):
    length = rows.shape[1]
    lane = lax.broadcasted_iota(jnp.int32, rows.shape, 1)
    moved = pltpu.roll(rows, length - offset, 1)
    if offset == 1:
        return jnp.where(lane == length - 1, after[:, 0:1], moved)
    return jnp.where(
        lane == length - 2,
        after[:, 0:1],
        jnp.where(lane == length - 1, after[:, 1:2], moved),
    )


def conv_forward(signal, before, taps, same):
    total = taps[:, 0:1] * signal
    for offset in (1, 2):
        total = total + taps[:, offset : offset + 1] * later_by(signal, offset, before) * same[offset - 1]
    return total


def conv_backward(grad, after, taps, same):
    total = taps[:, 0:1] * grad
    for offset in (1, 2):
        total = total + taps[:, offset : offset + 1] * sooner_by(grad, offset, after) * same[offset - 1]
    return total


def add_ones(values):
    length = values.shape[1]
    row = lax.broadcasted_iota(jnp.int32, (VROWS - DV, length), 0)
    return jnp.concatenate(
        [values, jnp.where(row == 0, 1.0, 0.0).astype(jnp.bfloat16)], axis=0
    )


def weights_of(keys, queries, mask):
    shifted = dot_tn(keys, queries) + 1.0
    return shifted, (0.5 * shifted * shifted + 0.5) * mask


def mix_forward(tokens, before_tokens, taps, doc_row, prev_docs, mask_ref):
    length = tokens.shape[0]
    block = tokens.astype(jnp.float32).T.astype(jnp.bfloat16)
    before = before_tokens.astype(jnp.float32).T[2 * FEATURE_SIZE : 2 * FEATURE_SIZE + DV, 14:16]
    values, _, _, _ = values_of(block, before, taps, doc_row, prev_docs)
    marked = add_ones(values)
    keep_last = (doc_row == doc_row[:, length - 1 : length]).astype(jnp.float32)
    key_feats = features(block[16:32].astype(jnp.float32), keep_last, False)
    state = dot_nt(key_feats, marked)
    scaled_q = (block[0:16].astype(jnp.float32) * 0.25).astype(jnp.bfloat16)
    sums = []
    for start in range(0, length, TBLOCK):
        stop = start + TBLOCK
        _, weights = weights_of(
            block[16:32, :stop], scaled_q[:, start:stop], mask_ref[:stop, start:stop]
        )
        sums.append(dot_nn(marked[:, :stop], weights.astype(jnp.bfloat16)))
    return block, marked, jnp.concatenate(sums, axis=1), state


def values_of(block, before, taps, doc_row, prev_docs):
    length = block.shape[1]
    doc8 = jnp.broadcast_to(doc_row, (8, length))
    prev8 = jnp.broadcast_to(prev_docs, (8, 2))
    same = [
        (doc8 == later_by(doc8, offset, prev8)).astype(jnp.float32)[0:1] for offset in (1, 2)
    ]
    conv_in = block[32 : 32 + DV].astype(jnp.float32)
    gate_in = block[32 + DV :].astype(jnp.float32)
    conv_out = conv_forward(conv_in, before, taps, same)
    sigmoid = 1.0 / (1.0 + jnp.exp(-gate_in))
    values = (gate_in * sigmoid * conv_out).astype(jnp.bfloat16)
    return values, conv_out, gate_in, sigmoid


def fill_mask(mask_ref, doc_row, doc_col):
    shape = mask_ref.shape
    causal = lax.broadcasted_iota(jnp.int32, shape, 0) <= lax.broadcasted_iota(jnp.int32, shape, 1)
    mask_ref[...] = jnp.where(causal & (doc_col == doc_row), 1.0, 0.0)


def f1_kernel(p_ref, halo_ref, taps_ref, row_ref, col_ref, prev_ref, pt_ref, v_ref, o_ref, l_ref, mask_ref):
    @pl.when(pl.program_id(0) == 0)
    def _():
        fill_mask(mask_ref, row_ref[...], col_ref[...])

    block, marked, sums, state = mix_forward(
        p_ref[...], halo_ref[...], taps_ref[0], row_ref[...], prev_ref[:, 0:2], mask_ref
    )
    pt_ref[...] = block
    v_ref[...] = marked
    o_ref[...] = sums
    l_ref[...] = state.astype(jnp.bfloat16)


def mix_finish(block, sums, carry, doc_row):
    keep_first = (doc_row == doc_row[:, 0:1]).astype(jnp.float32)
    query_feats = features(block[0:16].astype(jnp.float32), keep_first, True)
    total = sums + dot_tn(carry, query_feats)
    denominator = total[DV : DV + 1]
    return (total[:DV] / denominator).astype(jnp.bfloat16), denominator


def f2_kernel(pt_ref, o_ref, s_ref, row_ref, att_ref, den_ref):
    attended, denominator = mix_finish(pt_ref[...], o_ref[...], s_ref[...], row_ref[...])
    att_ref[...] = attended
    den_ref[...] = jnp.broadcast_to(denominator, den_ref.shape)


def sum_grads(grad, attended, denominator):
    length = grad.shape[1]
    inverse = 1.0 / denominator
    grad_f = grad.astype(jnp.float32)
    dot_term = jnp.sum(grad_f * attended.astype(jnp.float32), axis=0, keepdims=True)
    row = lax.broadcasted_iota(jnp.int32, (VROWS - DV, length), 0)
    tail = jnp.where(row == 0, jnp.broadcast_to(-dot_term * inverse, row.shape), 0.0)
    return jnp.concatenate([grad_f * inverse, tail], axis=0).astype(jnp.bfloat16)


def mix_back_local(block, marked, sums_grad, carry, doc_row, mask_ref):
    length = block.shape[1]
    keys = block[16:32]
    queries = block[0:16].astype(jnp.float32)
    scaled_q = (queries * 0.25).astype(jnp.bfloat16)
    keep_first = (doc_row == doc_row[:, 0:1]).astype(jnp.float32)
    query_grad = features_back(queries, dot_nn(carry, sums_grad) * keep_first, True)
    key_grad = jnp.zeros((16, length), jnp.float32)
    value_grad = jnp.zeros((VROWS, length), jnp.float32)
    parts = []
    for start in range(0, length, TBLOCK):
        stop = start + TBLOCK
        mask = mask_ref[:stop, start:stop]
        shifted, weights = weights_of(keys[:, :stop], scaled_q[:, start:stop], mask)
        grad_block = sums_grad[:, start:stop]
        weight_grad = dot_tn(marked[:, :stop], grad_block)
        score_grad = (weight_grad * shifted * mask).astype(jnp.bfloat16)
        parts.append(dot_nn(keys[:, :stop], score_grad) * 0.25)
        key_part = dot_nt(scaled_q[:, start:stop], score_grad)
        value_part = dot_nt(grad_block, weights.astype(jnp.bfloat16))
        if stop < length:
            key_part = jnp.concatenate(
                [key_part, jnp.zeros((16, length - stop), jnp.float32)], axis=1
            )
            value_part = jnp.concatenate(
                [value_part, jnp.zeros((VROWS, length - stop), jnp.float32)], axis=1
            )
        key_grad = key_grad + key_part
        value_grad = value_grad + value_part
    query_grad = query_grad + jnp.concatenate(parts, axis=1)
    return query_grad, key_grad, value_grad


def b1_kernel(pt_ref, v_ref, g_ref, att_ref, den_ref, s_ref, row_ref, col_ref, d_ref, dq_ref, dk_ref, dv_ref, mask_ref):
    @pl.when(pl.program_id(0) == 0)
    def _():
        fill_mask(mask_ref, row_ref[...], col_ref[...])

    doc_row = row_ref[...]
    block = pt_ref[...]
    sums_grad = sum_grads(g_ref[...], att_ref[...], den_ref[0:1])
    keep_first = (doc_row == doc_row[:, 0:1]).astype(jnp.float32)
    query_feats = features(block[0:16].astype(jnp.float32), keep_first, True)
    d_ref[...] = dot_nt(query_feats, sums_grad).astype(jnp.bfloat16)
    dq, dk, dv = mix_back_local(block, v_ref[...], sums_grad, s_ref[...], doc_row, mask_ref)
    dq_ref[...] = dq
    dk_ref[...] = dk
    dv_ref[...] = dv


def mix_back_finish(block, marked, later_state, key_grad, value_grad, doc_row, before, taps, prev_docs):
    length = block.shape[1]
    keep_last = (doc_row == doc_row[:, length - 1 : length]).astype(jnp.float32)
    keys = block[16:32].astype(jnp.float32)
    key_feats = features(keys, keep_last, False)
    key_grad = key_grad + features_back(keys, dot_nn(later_state, marked) * keep_last, False)
    value_grad = (value_grad + dot_tn(later_state, key_feats))[:DV]
    _, conv_out, gate_in, sigmoid = values_of(block, before, taps, doc_row, prev_docs)
    gate_grad = value_grad * conv_out * sigmoid * (1.0 + gate_in * (1.0 - sigmoid))
    conv_grad = value_grad * gate_in * sigmoid
    return key_grad, gate_grad, conv_grad


def b2_kernel(pt_ref, v_ref, g_ref, dq_ref, dk_ref, dv_ref, halo_ref, taps_ref, row_ref, prev_ref, dp_ref, first_ref, tail_ref):
    doc_row = row_ref[...]
    length = doc_row.shape[1]
    taps = taps_ref[0]
    before = halo_ref[...].astype(jnp.float32).T[2 * FEATURE_SIZE : 2 * FEATURE_SIZE + DV, 14:16]
    key_grad, gate_grad, conv_grad = mix_back_finish(
        pt_ref[...], v_ref[...], g_ref[...], dk_ref[...], dv_ref[...], doc_row, before, taps, prev_ref[:, 0:2]
    )
    doc8 = jnp.broadcast_to(doc_row, (8, length))
    none = jnp.full((8, 2), -1.0, jnp.float32)
    same = [(doc8 == sooner_by(doc8, offset, none)).astype(jnp.float32)[0:1] for offset in (1, 2)]
    conv_in_grad = conv_backward(conv_grad, jnp.zeros((DV, 2), jnp.float32), taps, same)
    whole = jnp.concatenate([dq_ref[...], key_grad, conv_in_grad, gate_grad], axis=0).T
    dp_ref[...] = whole.astype(jnp.bfloat16)
    tail_ref[...] = whole[length - 16 :]
    pad = jnp.zeros((16, length), jnp.float32)
    conv_tokens = jnp.concatenate([jnp.zeros((32, length), jnp.float32), conv_grad, jnp.zeros((DV, length), jnp.float32)], axis=0).T
    first_ref[...] = conv_tokens[0:16]


MESH = pl.DeviceIdType.MESH
LAG = 2
DONE = 3
FLAT = (38, 39)
AHEAD = 4
UNIT = 512
TILE = 256
KEPT = (1, 2, 3, 5, 6, 8)
GROUPS = 4


class Gather:
    kinds = 9
    flat = FLAT

    def __init__(self, shards, wholes, sends, lands):
        self.shards, self.wholes = shards, wholes
        self.sends, self.lands = sends, lands
        i = lax.axis_index("fsdp")
        z = lax.axis_index("seq")
        odd = z % 2
        self.odd = odd
        by_y = 4 - 8 * (i // 4)
        by_x = 2 - 4 * ((i // 2) % 2)
        by_core = 1 - 2 * (i % 2)
        self.slot = [i, i + by_y, i + by_x + odd * by_y, i + by_x + (1 - odd) * by_y, i + by_core]
        self.flat_slot = [i, i + by_y, i + by_x, i + by_x + by_y, i + by_core]
        self.near = [
            {"fsdp": i + by_y, "seq": z},
            {"fsdp": i + by_x, "seq": z},
            {"fsdp": i, "seq": z + 1 - 2 * odd},
            {"fsdp": i + by_core, "seq": z},
        ]

    def is_flat(self, piece):
        return isinstance(piece[0], int) and piece[0] in self.flat

    def part(self, piece, slot, half=None):
        _, which, start, size = piece
        rows = self.shards[which].shape[0]
        first, count = (0, rows) if half is None else (half * (rows // 2), rows // 2)
        return self.wholes[which].at[
            pl.ds(pl.multiple_of(slot * rows + first, 16), count), pl.ds(start, size)
        ]

    def own_part(self, piece):
        _, which, start, size = piece
        return self.shards[which].at[:, pl.ds(start, size)]

    def copy(self, kind, piece, relay=False):
        source = [0, 0, 2, 0, 1, 2, 3, 4][kind] if kind < 8 else 2
        half = None
        link = min(kind, 3)
        slots = self.slot
        if self.is_flat(piece):
            slots = self.flat_slot
            if kind == 2:
                source, half, link = 1, 0, 1
            if kind == 8:
                source, half, link = 2, 1, 0
        if relay:
            source = 1
        slot = slots[source]
        return pltpu.make_async_remote_copy(
            src_ref=self.own_part(piece) if source == 0 else self.part(piece, slot, half),
            dst_ref=self.part(piece, slot, half),
            send_sem=self.sends.at[kind, piece[0]],
            recv_sem=self.lands.at[kind, piece[0]],
            device_id=self.near[link],
            device_id_type=MESH,
        )

    def first(self, piece):
        self.copy(0, piece).start()
        if self.is_flat(piece):
            self.copy(1, piece).start()
        else:

            @pl.when(self.odd == 0)
            def _():
                self.copy(1, piece).start()

        self.copy(3, piece).start()

    def from_y(self, piece):
        self.copy(0, piece).wait_recv()

        if not self.is_flat(piece):

            @pl.when(self.odd == 1)
            def _():
                self.copy(1, piece, relay=True).start()

        self.copy(4, piece).start()
        self.copy(3, piece).wait_recv()
        self.copy(7, piece).start()

    def from_x(self, piece):
        self.copy(1, piece).wait_recv()
        self.copy(2, piece).start()
        if self.is_flat(piece):
            self.copy(8, piece).start()
        self.copy(5, piece).start()

    def from_z(self, piece):
        self.copy(2, piece).wait_recv()
        if self.is_flat(piece):
            self.copy(8, piece).wait_recv()
        self.copy(6, piece).start()

    def ready(self, piece):
        for kind in (4, 5, 6, 7):
            self.copy(kind, piece).wait_recv()

    def finish(self, piece):
        for kind in range(self.kinds if self.is_flat(piece) else 8):
            self.copy(kind, piece).wait_send()


def cuts(which, width, size):
    return [(which, at, min(size, width - at)) for at in range(0, width, size)]


def early_cuts(columns, width):
    mix = [(0, 0, 256), (0, 256, 256)] + [(0, at, 512) for at in range(512, columns, 512)]
    return mix + cuts(1, width, 512) + cuts(3, width, 256)


def by_rows(length, body, rows=64):
    def step(n, _):
        body(pl.ds(pl.multiple_of(n * rows, rows), rows))
        return 0

    lax.fori_loop(0, length // rows, step, 0)


def row_root(value):
    return lax.rsqrt(jnp.mean(value * value, -1, keepdims=True) + epsilon)


def m_kernel(
    x, g, gain1, gain2, taps, doc_row_ref, doc_col_ref, in_down, up_maps, out_down, out_up, gu_down, gu_up, ffd_down, ffd_up,
    a_in, b_in, c_in, d_in,
    a_all, b_all, c_all, d_all,
    out, blocks_out, marked_out, att_t_out, dens, carry_out, attended_out, resid_grad, hidden1_out, rank_in, rank_out, halo, term_ff, term_w, next_docs,
    blocks, marked, att_t, carry, attended, hidden1, keep_sems, first_docs,    halo_send, mask, sums, state, message, resid, hidden2, out_acc, grad_acc, a_tile, b_tile, g_tile, u_tile, d_tile, rank_acc,
    sends, lands, halo_sems, chain_sems, load_sems,
):
    length, width = x.shape
    ff = d_all.shape[0]
    units = -(-ff // UNIT)
    last_size = ff - (units - 1) * UNIT
    f32, bf16 = jnp.float32, jnp.bfloat16
    place = lax.axis_index("seq")
    planes = lax.axis_size("seq")
    me = lax.axis_index("fsdp")
    job = Gather([a_in, b_in, c_in, d_in], [a_all, b_all, c_all, d_all], sends, lands)

    early = early_cuts(a_in.shape[1], b_in.shape[1])
    early = [(number,) + piece for number, piece in enumerate(early)]
    base = len(early)
    mix_pieces = [p for p in early if p[1] == 0]
    out_pieces = [p for p in early if p[1] == 1]
    down_pieces = [p for p in early if p[1] == 3]
    total = base + 2 * units

    def late(number, size=UNIT):
        at = number - base
        start = (at // 2) * UNIT + (at % 2) * ff
        if not isinstance(start, int):
            start = pl.multiple_of(start, TILE)
        return (number, 2, start, size)

    def piece_at(number):
        if number < base:
            return early[number]
        return late(number, UNIT if number < total - 2 else last_size)

    def each_late(number, action):
        @pl.when(number < total - 2)
        def _():
            action(late(number))

        for end in (total - 2, total - 1):

            @pl.when(number == end)
            def _():
                action(piece_at(end))

    def pump(number):
        job.from_y(piece_at(number))
        if number + AHEAD < total:
            job.first(piece_at(number + AHEAD))
        if number >= LAG:
            job.from_x(piece_at(number - LAG))
        if number >= 2 * LAG:
            job.from_z(piece_at(number - 2 * LAG))

    barrier = pltpu.get_barrier_semaphore()
    for device in (job.near[0], job.near[1], job.near[3]):
        pl.semaphore_signal(barrier, inc=1, device_id=device, device_id_type=MESH)
    before = {"fsdp": me, "seq": (place + planes - 1) % planes}
    after = {"fsdp": me, "seq": (place + 1) % planes}

    @pl.when(place > 0)
    def _():
        pl.semaphore_signal(barrier, inc=1, device_id=before, device_id_type=MESH)

    @pl.when(place < planes - 1)
    def _():
        pl.semaphore_signal(barrier, inc=1, device_id=after, device_id_type=MESH)

    inner = (place > 0) & (place < planes - 1)

    @pl.when(inner)
    def _():
        pl.semaphore_wait(barrier, 5)

    @pl.when(jnp.logical_not(inner))
    def _():
        pl.semaphore_wait(barrier, 4)

    for piece in early[:AHEAD]:
        job.first(piece)
    first_docs[...] = jnp.broadcast_to(doc_col_ref[0:8, :], (8, 128))
    docs_back = pltpu.make_async_remote_copy(
        src_ref=first_docs, dst_ref=next_docs, send_sem=halo_sems.at[2], recv_sem=halo_sems.at[3], device_id=before, device_id_type=MESH
    )

    @pl.when(place > 0)
    def _():
        docs_back.start()

    @pl.when(place == planes - 1)
    def _():
        next_docs[...] = jnp.full(next_docs.shape, -1.0, f32)

    def norm1(rows):
        value = x[rows, :].astype(f32)
        hidden1[rows, :] = (value * row_root(value) * gain1[...]).astype(bf16)

    by_rows(length, norm1)
    rank_in[...] = dot_nt(hidden1[...], in_down[...]).astype(bf16)
    doc_row = doc_row_ref[...]
    fill_mask(mask, doc_row, doc_col_ref[...])
    cond_whole = (doc_row[:, 0:1] == doc_row[:, length - 1 : length]).astype(f32)

    def load_mix(number):
        _, _, start, size = mix_pieces[number]
        return pltpu.make_async_copy(
            a_all.at[:, pl.ds(start, size)], a_tile.at[number % 2, :, :size], load_sems.at[number % 2]
        )

    def project(number):
        _, _, start, size = mix_pieces[number]
        load_mix(number).wait()
        projected = dot_nn(hidden1[...], a_tile[number % 2, :, :size]) + dot_nn(rank_in[...], up_maps[:, start : start + size])
        halo_send[:, start : start + size] = projected[length - 16 :].astype(bf16)
        for at in range(0, size, PER_HEAD):
            blocks[start + at : start + at + PER_HEAD, :] = projected[:, at : at + PER_HEAD].T.astype(bf16)

    for number in range(2 * LAG):
        job.from_y(piece_at(number))
        job.first(piece_at(number + AHEAD))
        if 1 <= number <= LAG:
            job.from_x(piece_at(number - 1))
    for number, piece in enumerate(mix_pieces):
        pump(number + 2 * LAG)
        job.ready(piece)
        load_mix(number).start()
        if number > 0:
            project(number - 1)
    project(len(mix_pieces) - 1)
    columns = HEAD_COUNT * PER_HEAD
    halo_send[:, columns:] = jnp.broadcast_to(
        doc_col_ref[length - 16 :, :], (16, 128)
    ).astype(bf16)
    to_next = pltpu.make_async_remote_copy(
        src_ref=halo_send, dst_ref=halo, send_sem=halo_sems.at[0], recv_sem=halo_sems.at[1], device_id=after, device_id_type=MESH
    )

    @pl.when(place < planes - 1)
    def _():
        to_next.start()

    @pl.when(place == 0)
    def _():
        halo[:, :columns] = jnp.zeros((16, columns), bf16)
        halo[:, columns:] = jnp.full((16, 128), -1.0, bf16)

    next_piece = len(mix_pieces) + 2 * LAG

    def pump_next():
        nonlocal next_piece
        pump(next_piece)
        next_piece += 1

    pump_next()

    @pl.when(place > 0)
    def _():
        to_next.wait_recv()

    prev_docs = halo[:, columns:].astype(f32).T[0:1, 14:16]
    cond_before = (prev_docs[:, 1:2] == doc_row[:, 0:1]).astype(f32)
    keep_last = (doc_row == doc_row[:, length - 1 : length]).astype(f32)

    def head_state(h, _):
        at = pl.multiple_of(h * PER_HEAD, PER_HEAD)
        block = blocks[pl.ds(at, PER_HEAD), :]
        prior = halo[:, pl.ds(at, PER_HEAD)].astype(f32).T[32 : 32 + DV, 14:16]
        values, _, _, _ = values_of(block, prior, taps[h], doc_row, prev_docs)
        ones = add_ones(values)
        marked[pl.ds(pl.multiple_of(h * VROWS, VROWS), VROWS), :] = ones
        key_feats = features(block[16:32].astype(f32), keep_last, False)
        state[pl.ds(pl.multiple_of(h * FEATS, 16), FEATS), :] = dot_nt(key_feats, ones).astype(bf16)
        return 0

    group = HEAD_COUNT // GROUPS
    half = HEAD_COUNT // 2
    lax.fori_loop(0, half, head_state, 0)
    pump_next()
    lax.fori_loop(half, HEAD_COUNT, head_state, 0)
    pump_next()
    span = group * FEATS

    def hand_on(number):
        part = pl.ds(number * span, span)
        return pltpu.make_async_remote_copy(
            src_ref=message.at[part], dst_ref=carry.at[part],
            send_sem=chain_sems.at[0, number], recv_sem=chain_sems.at[1, number], device_id=after, device_id_type=MESH,
        )

    @pl.when(place == 0)
    def _():
        carry[...] = jnp.zeros(carry.shape, bf16)
        message[...] = state[...]
        for number in range(GROUPS):
            hand_on(number).start()

    def chain_slot(slot):
        for plane in range(1, 4):
            number = slot - plane + 1
            if 0 <= number < GROUPS:

                @pl.when(place == plane)
                def _():
                    part = pl.ds(number * span, span)
                    hand_on(number).wait_recv()
                    if plane < 3:
                        message[part, :] = (
                            state[part, :].astype(f32) + (cond_whole * cond_before) * carry[part, :].astype(f32)
                        ).astype(bf16)
                        hand_on(number).start()

    def head_local(h, _):
        at = pl.multiple_of(h * PER_HEAD, PER_HEAD)
        keys = blocks[pl.ds(at + 16, 16), :]
        scaled_q = (blocks[pl.ds(at, 16), :].astype(f32) * 0.25).astype(bf16)
        rows = pl.multiple_of(h * VROWS, VROWS)
        ones = marked[pl.ds(rows, VROWS), :]
        for start in range(0, length, TBLOCK):
            stop = start + TBLOCK
            _, weights = weights_of(keys[:, :stop], scaled_q[:, start:stop], mask[:stop, start:stop])
            sums[pl.ds(rows, VROWS), start:stop] = dot_nn(ones[:, :stop], weights.astype(bf16))
        return 0

    for number in range(GROUPS):
        lax.fori_loop(number * group, (number + 1) * group, head_local, 0)
        chain_slot(number)
        pump_next()

    keep_first = (doc_row == doc_row[:, 0:1]).astype(f32) * cond_before

    def head_finish(h, _):
        at = pl.multiple_of(h * PER_HEAD, PER_HEAD)
        rows = pl.multiple_of(h * VROWS, VROWS)
        query_feats = features(blocks[pl.ds(at, 16), :].astype(f32), keep_first, True)
        both = sums[pl.ds(rows, VROWS), :] + dot_tn(carry[pl.ds(pl.multiple_of(h * FEATS, 16), FEATS), :], query_feats)
        denominator = both[DV : DV + 1]
        att_t[pl.ds(pl.multiple_of(h * DV, 16), DV), :] = (both[:DV] / denominator).astype(bf16)
        dens[pl.ds(pl.multiple_of(h * 8, 8), 8), :] = jnp.broadcast_to(denominator, (8, length))
        return 0

    chain_slot(GROUPS)
    lax.fori_loop(0, half, head_finish, 0)
    pump_next()
    chain_slot(GROUPS + 1)
    lax.fori_loop(half, HEAD_COUNT, head_finish, 0)

    def turn(n, _):
        rows = pl.ds(pl.multiple_of(n * 128, 128), 128)
        attended[:, rows] = att_t[rows, :].astype(f32).T.astype(bf16)
        return 0

    lax.fori_loop(0, width // 128, turn, 0)
    keeps = [
        pltpu.make_async_copy(have, kept, keep_sems.at[n])
        for n, (have, kept) in enumerate(
            [
                (blocks, blocks_out), (marked, marked_out), (att_t, att_t_out),
                (carry, carry_out), (attended, attended_out), (hidden1, hidden1_out),
            ]
        )
    ]
    for keep in keeps:
        keep.start()
    pump_next()

    rank_out[...] = dot_nt(attended[...], out_down[...]).astype(bf16)
    for piece in out_pieces:
        job.ready(piece)
        _, _, start, size = piece
        load = pltpu.make_async_copy(b_all.at[:, pl.ds(start, size)], b_tile.at[:, :size], load_sems.at[0])
        load.start()
        load.wait()
        resid[:, start : start + size] = (
            x[:, start : start + size].astype(f32)
            + dot_nn(attended[...], b_tile[:, :size])
            + dot_nn(rank_out[...], out_up[:, start : start + size])
        )
    pump_next()

    def norm2(rows):
        value = resid[rows, :]
        hidden2[rows, :] = (value * row_root(value) * gain2[...]).astype(bf16)
        out_acc[rows, :] = value
        grad_acc[rows, :] = jnp.zeros(value.shape, f32)

    by_rows(length, norm2)
    rank_gate = dot_nt(hidden2[...], gu_down[0:16, :]).astype(bf16)
    rank_up = dot_nt(hidden2[...], gu_down[16:32, :]).astype(bf16)
    rank_ffd_grad = dot_nt(g[...], ffd_up[...]).astype(bf16)
    rank_gate_t = rank_gate.astype(f32).T.astype(bf16)
    rank_up_t = rank_up.astype(f32).T.astype(bf16)
    rank_ffd_grad_t = rank_ffd_grad.astype(f32).T.astype(bf16)
    rank_acc[...] = jnp.zeros(rank_acc.shape, f32)
    while next_piece < base + 2 * LAG:
        pump_next()
    for piece in down_pieces:
        job.ready(piece)

    def loads(unit, slot, size):
        start = unit * UNIT
        if not isinstance(start, int):
            start = pl.multiple_of(start, TILE)
        return [
            pltpu.make_async_copy(c_all.at[:, pl.ds(start, size)], g_tile.at[slot, :, :size], load_sems.at[slot]),
            pltpu.make_async_copy(c_all.at[:, pl.ds(ff + start, size)], u_tile.at[slot, :, :size], load_sems.at[2 + slot]),
            pltpu.make_async_copy(d_all.at[pl.ds(start, size), :], d_tile.at[slot, :size, :], load_sems.at[4 + slot]),
        ]

    def hidden_tile(unit, slot, part):
        inside = slice(part * TILE, (part + 1) * TILE)
        start = unit * UNIT + part * TILE
        cols = pl.ds(start if isinstance(start, int) else pl.multiple_of(start, TILE), TILE)
        gate_w, up_w, down_w = g_tile[slot, :, inside], u_tile[slot, :, inside], d_tile[slot, inside, :]
        gate_map, up_map, down_map = gu_up[0:16, cols], gu_up[16:32, cols], ffd_down[:, cols]
        gate_pre = dot_nn(hidden2[...], gate_w) + dot_nn(rank_gate, gate_map)
        up_pre = dot_nn(hidden2[...], up_w) + dot_nn(rank_up, up_map)
        inner_grad = dot_nt(g[...], down_w) + dot_nn(rank_ffd_grad, down_map)
        sigmoid = 1.0 / (1.0 + jnp.exp(-gate_pre))
        gate_val = gate_pre * sigmoid
        inner = (gate_val * up_pre).astype(bf16)
        gate_grad = (inner_grad * up_pre * (sigmoid * (1.0 + gate_pre * (1.0 - sigmoid)))).astype(bf16)
        up_grad = (inner_grad * gate_val).astype(bf16)
        out_acc[...] += dot_nn(inner, down_w)
        grad_acc[...] += dot_nt(gate_grad, gate_w) + dot_nt(up_grad, up_w)
        rank_acc[0] += dot_nt(inner, down_map)
        rank_acc[1] += dot_nt(gate_grad, gate_map)
        rank_acc[2] += dot_nt(up_grad, up_map)
        term_ff[0:16, cols] = dot_nn(rank_gate_t, gate_grad)
        term_ff[16:32, cols] = dot_nn(rank_up_t, up_grad)
        term_ff[32:48, cols] = dot_nn(rank_ffd_grad_t, inner)

    def ff_pump(number):
        each_late(number, job.from_y)
        each_late(number + AHEAD, job.first)
        each_late(number - LAG, job.from_x)
        each_late(number - 2 * LAG, job.from_z)

    def ff_ready(unit, slot, size, pieces):
        for piece in pieces:
            job.ready(piece)
        for load in loads(unit, slot, size):
            load.start()

    def ff_load_wait(unit, slot, size):
        for load in loads(unit, slot, size):
            load.wait()

    def ff_step(unit, _):
        slot = unit % 2
        ahead = base + 2 * unit + 2 * LAG
        ff_pump(ahead)

        @pl.when(unit >= 1)
        def _():
            ff_load_wait(unit - 1, 1 - slot, UNIT)
            hidden_tile(unit - 1, 1 - slot, 0)

        ff_pump(ahead + 1)
        ff_ready(unit, slot, UNIT, [late(base + 2 * unit), late(base + 2 * unit + 1)])

        for number in range(0, len(early), 2):

            @pl.when(unit == 1 + number // 4)
            def _():
                for piece in early[number : number + 2]:
                    job.finish(piece)

        @pl.when(unit >= DONE)
        def _():
            job.finish(late(base + 2 * (unit - DONE)))
            job.finish(late(base + 2 * (unit - DONE) + 1))

        @pl.when(unit >= 1)
        def _():
            hidden_tile(unit - 1, 1 - slot, 1)

        return 0

    lax.fori_loop(0, units - 1, ff_step, 0)
    final = units - 1
    job.from_z(piece_at(total - 2))
    job.from_z(piece_at(total - 1))
    ff_load_wait(final - 1, (final - 1) % 2, UNIT)
    hidden_tile(final - 1, (final - 1) % 2, 0)
    ff_ready(final, final % 2, last_size, [piece_at(total - 2), piece_at(total - 1)])
    hidden_tile(final - 1, (final - 1) % 2, 1)
    ff_load_wait(final, final % 2, last_size)
    for part in range(last_size // TILE):
        hidden_tile(final, final % 2, part)

    rank_ffd = rank_acc[0].astype(bf16)
    rank_gate_grad = rank_acc[1].astype(bf16)
    rank_up_grad = rank_acc[2].astype(bf16)
    out_acc[...] += dot_nn(rank_ffd, ffd_up[...])
    grad_acc[...] += dot_nn(rank_gate_grad, gu_down[0:16, :]) + dot_nn(rank_up_grad, gu_down[16:32, :])
    term_w[0:16, :] = dot_tn(rank_gate_grad, hidden2[...])
    term_w[16:32, :] = dot_tn(rank_up_grad, hidden2[...])
    term_w[32:48, :] = dot_tn(rank_ffd, g[...])

    def finish_rows(rows):
        out[rows, :] = out_acc[rows, :].astype(bf16)
        value = resid[rows, :]
        root = row_root(value)
        normed = value * root
        scaled = grad_acc[rows, :] * gain2[...]
        resid_grad[rows, :] = g[rows, :].astype(f32) + root * (
            scaled - normed * jnp.mean(scaled * normed, -1, keepdims=True)
        )

    by_rows(length, finish_rows)

    for keep in keeps:
        keep.wait()

    def finish_late(number, _):
        job.finish(late(number))
        return 0

    lax.fori_loop(base + 2 * (units - 1 - DONE), total - 2, finish_late, 0)
    job.finish(piece_at(total - 2))
    job.finish(piece_at(total - 1))

    @pl.when(place > 0)
    def _():
        docs_back.wait_send()

    @pl.when(place < planes - 1)
    def _():
        docs_back.wait_recv()
        to_next.wait_send()
        for number in range(GROUPS):
            hand_on(number).wait_send()


def call_m(x, g, gain1, gain2, taps, doc_row, doc_col, maps, shards):
    length, width = x.shape
    f32, bf16 = jnp.float32, jnp.bfloat16
    count = lax.axis_size("fsdp")
    a, b, c, d = shards
    ff = d.shape[0] * count
    columns = a.shape[1]
    pieces = len(early_cuts(columns, width)) + 2 * -(-ff // UNIT)
    whole = pl.BlockSpec(memory_space=pltpu.VMEM)
    anyplace = pl.BlockSpec(memory_space=pl.ANY)
    vmem_out = [
        ((length, width), bf16),
        ((columns, length), bf16),
        ((HEAD_COUNT * VROWS, length), bf16),
        ((width, length), bf16),
        ((HEAD_COUNT * 8, length), f32),
        ((HEAD_COUNT * FEATS, VROWS), bf16),
        ((length, width), bf16),
        ((length, width), f32),
        ((length, width), bf16),
        ((length, 64), bf16),
        ((length, 16), bf16),
        ((16, columns + 128), bf16),
        ((48, ff), f32),
        ((48, width), f32),
        ((8, 128), f32),
    ]
    args = (x, g, gain1, gain2, taps, doc_row, doc_col) + tuple(maps)
    return pl.pallas_call(
        m_kernel,
        in_specs=[whole] * len(args) + [anyplace] * 4,
        out_specs=[anyplace] * 4 + [anyplace if n in KEPT else whole for n in range(len(vmem_out))],
        out_shape=[jax.ShapeDtypeStruct((t.shape[0] * count, t.shape[1]), t.dtype) for t in shards]
        + [jax.ShapeDtypeStruct(s, t) for s, t in vmem_out],
        scratch_shapes=[pltpu.VMEM(*vmem_out[n]) for n in KEPT]
        + [
            pltpu.SemaphoreType.DMA((len(KEPT),)),
            pltpu.VMEM((8, 128), f32),
            pltpu.VMEM((16, columns + 128), bf16),
            pltpu.VMEM((length, length), f32),
            pltpu.VMEM((HEAD_COUNT * VROWS, length), f32),
            pltpu.VMEM((HEAD_COUNT * FEATS, VROWS), bf16),
            pltpu.VMEM((HEAD_COUNT * FEATS, VROWS), bf16),
            pltpu.VMEM((length, width), f32),
            pltpu.VMEM((length, width), bf16),
            pltpu.VMEM((length, width), f32),
            pltpu.VMEM((length, width), f32),
            pltpu.VMEM((2, width, 512), bf16),
            pltpu.VMEM((width, 512), bf16),
            pltpu.VMEM((2, width, UNIT), bf16),
            pltpu.VMEM((2, width, UNIT), bf16),
            pltpu.VMEM((2, UNIT, width), bf16),
            pltpu.VMEM((3, length, 16), f32),
            pltpu.SemaphoreType.DMA((9, pieces)),
            pltpu.SemaphoreType.DMA((9, pieces)),
            pltpu.SemaphoreType.DMA((4,)),
            pltpu.SemaphoreType.DMA((2, GROUPS)),
            pltpu.SemaphoreType.DMA((6,)),
        ],
        compiler_params=pltpu.CompilerParams(
            collective_id=1, has_side_effects=True, vmem_limit_bytes=62 * 1024 * 1024
        ),
    )(*args, *shards)


def stripe_width(columns):
    return -(-columns // (4 * 128)) * 128


FETCHED = (0, 11, 12, 13, 15, 16, 18)


def to_stripes(own, rows, value):
    size = own.shape[2]
    columns = value.shape[1]
    for n in range(own.shape[0]):
        piece = value[:, n * size : min((n + 1) * size, columns)]
        if piece.shape[1] < size:
            piece = jnp.concatenate(
                [piece, jnp.zeros((piece.shape[0], size - piece.shape[1]), piece.dtype)], axis=1
            )
        own[n, rows, :] = piece


class Share:
    def __init__(self, number, own, slots, total, everyone, z_sends, z_lands, sends, lands, local):
        self.number, self.own, self.slots, self.total, self.everyone = number, own, slots, total, everyone
        self.z_sends, self.z_lands, self.sends, self.lands, self.local = z_sends, z_lands, sends, lands, local
        i = lax.axis_index("fsdp")
        self.place = lax.axis_index("seq")
        self.planes = lax.axis_size("seq")
        by_y = 4 - 8 * (i // 4)
        by_x = 2 - 4 * ((i // 2) % 2)
        by_core = 1 - 2 * (i % 2)
        self.slot = [i, i + by_y, i + by_x, i + by_x + by_y]
        self.near = [
            {"fsdp": i + by_y, "seq": self.place},
            {"fsdp": i + by_x, "seq": self.place},
            {"fsdp": i + by_core, "seq": self.place},
        ]
        self.me = i

    def z_copy(self, distance, summed):
        plane = (self.place + distance) % self.planes
        kind = 3 * summed + distance - 1
        return pltpu.make_async_remote_copy(
            src_ref=self.total.at[self.place] if summed else self.own.at[plane],
            dst_ref=(self.total if summed else self.slots).at[self.place],
            send_sem=self.z_sends.at[self.number, kind],
            recv_sem=self.z_lands.at[self.number, kind],
            device_id={"fsdp": self.me, "seq": plane},
            device_id_type=MESH,
        )

    def z_start(self):
        for distance in range(1, self.planes):
            self.z_copy(distance, 0).start()
        self.slots[self.place] = self.own[self.place]

    def z_sum(self):
        for distance in range(1, self.planes):
            self.z_copy(distance, 0).wait_recv()
        total = self.slots[0].astype(jnp.float32)
        for plane in range(1, self.planes):
            total = total + self.slots[plane].astype(jnp.float32)
        self.total[self.place] = total.astype(jnp.bfloat16)
        for distance in range(1, self.planes):
            self.z_copy(distance, 1).start()

    def copy(self, kind):
        half = self.planes // 2
        first, second, every = pl.ds(0, half), pl.ds(half, half), pl.ds(0, self.planes)
        where, slot, part = [
            (0, 0, every), (1, 0, every), (2, 0, every),
            (1, 1, first), (0, 2, second),
            (2, 1, every), (2, 2, every), (2, 3, every),
        ][kind]
        there = self.everyone.at[self.slot[slot], part]
        return pltpu.make_async_remote_copy(
            src_ref=self.total if slot == 0 else there,
            dst_ref=there,
            send_sem=self.sends.at[self.number, kind],
            recv_sem=self.lands.at[self.number, kind],
            device_id=self.near[where],
            device_id_type=MESH,
        )

    def keep(self):
        return pltpu.make_async_copy(self.total, self.everyone.at[self.slot[0]], self.local.at[self.number])

    def gather_start(self):
        for distance in range(1, self.planes):
            self.z_copy(distance, 1).wait_recv()
        for kind in (0, 1, 2):
            self.copy(kind).start()
        self.keep().start()

    def relay(self):
        self.copy(0).wait_recv()
        self.copy(3).start()
        self.copy(5).start()
        self.copy(1).wait_recv()
        self.copy(4).start()
        self.copy(6).start()

    def relay_last(self):
        self.copy(3).wait_recv()
        self.copy(4).wait_recv()
        self.copy(7).start()

    def finish(self):
        for kind in (2, 5, 6, 7):
            self.copy(kind).wait_recv()
        self.keep().wait()
        for kind in range(8):
            self.copy(kind).wait_send()
        for distance in range(1, self.planes):
            self.z_copy(distance, 0).wait_send()
            self.z_copy(distance, 1).wait_send()


def t_kernel(
    x_kept, gain1, taps, doc_row_ref, doc_col_ref, next_docs_ref, chosen, in_down, up_maps, out_down, out_up,
    blocks_kept, marked_kept, att_t_kept, dens, carry_kept, attended_kept, resid_grad, hidden1_kept, rank_in, rank_out, halo, term_ff, term_w,
    w_in, w_out,
    input_grad, all_ff, all_wide, all_down, all_up,
    x, blocks, marked, att_t, carry, attended, hidden1, fetch_sems, out_tile, in_tile, branch_t, grad_t, sums_grad, state, message, later, query_grad, key_grad, value_grad, proj_grad,
    conv_last, halo_send, halo_next, vg_terms, qk_terms, mask,
    ff_own, ff_slots, ff_total, wide_own, wide_slots, wide_total, down_own, down_slots, down_total, up_own, up_slots, up_total,
    chain_sems, halo_sems, load_sems, z_sends, z_lands, sends, lands, local,
):
    length, width = x.shape
    f32, bf16 = jnp.float32, jnp.bfloat16
    columns = HEAD_COUNT * PER_HEAD
    fetches = [
        pltpu.make_async_copy(kept, have, fetch_sems.at[n])
        for n, (kept, have) in enumerate(
            [
                (att_t_kept, att_t), (blocks_kept, blocks), (marked_kept, marked), (carry_kept, carry),
                (attended_kept, attended), (hidden1_kept, hidden1), (x_kept, x),
            ]
        )
    ]
    load_out = pltpu.make_async_copy(w_out, out_tile, load_sems.at[0])
    load_out.start()
    for fetch in fetches:
        fetch.start()
    place = lax.axis_index("seq")
    planes = lax.axis_size("seq")
    me = lax.axis_index("fsdp")
    sems = (z_sends, z_lands, sends, lands, local)
    ff_share = Share(0, ff_own, ff_slots, ff_total, all_ff, *sems)
    wide_share = Share(1, wide_own, wide_slots, wide_total, all_wide, *sems)
    down_share = Share(2, down_own, down_slots, down_total, all_down, *sems)
    up_share = Share(3, up_own, up_slots, up_total, all_up, *sems)

    barrier = pltpu.get_barrier_semaphore()
    others = [{"fsdp": me, "seq": (place + distance) % planes} for distance in range(1, planes)]
    for device in ff_share.near + others:
        pl.semaphore_signal(barrier, inc=1, device_id=device, device_id_type=MESH)
    pl.semaphore_wait(barrier, 3 + planes - 1)

    step = in_tile.shape[1]
    blocks_in = width // step

    def load_in(number):
        return pltpu.make_async_copy(
            w_in.at[pl.ds(number * step, step), :], in_tile.at[number % 2], load_sems.at[1 + number % 2]
        )

    load_in(0).start()
    load_in(1).start()
    to_stripes(ff_own, slice(0, 48), term_ff[...].astype(bf16))
    ff_share.z_start()
    to_stripes(wide_own, slice(0, 48), term_w[...].astype(bf16))

    doc_row = doc_row_ref[...]
    fill_mask(mask, doc_row, doc_col_ref[...])
    prev_docs = halo[:, columns:].astype(f32).T[0:1, 14:16]
    next_docs = next_docs_ref[...].T[0:1, 0:2]
    cond_before = (prev_docs[:, 1:2] == doc_row[:, 0:1]).astype(f32)
    cond_after = (next_docs[:, 0:1] == doc_row[:, length - 1 : length]).astype(f32)
    cond_whole = (doc_row[:, 0:1] == doc_row[:, length - 1 : length]).astype(f32)
    keep_first = (doc_row == doc_row[:, 0:1]).astype(f32)
    keep_first_link = keep_first * cond_before
    keep_last = (doc_row == doc_row[:, length - 1 : length]).astype(f32) * cond_after

    for start in range(0, width, 128):
        branch_t[start : start + 128, :] = resid_grad[:, start : start + 128].T.astype(bf16)
    rank_grad_t = dot_nn(out_up[...], branch_t[...]).astype(bf16)
    load_out.wait()
    for start in range(0, width, 256):
        grad_t[start : start + 256, :] = (
            dot_nn(out_tile[start : start + 256, :], branch_t[...])
            + dot_tn(out_down[:, start : start + 256], rank_grad_t)
        ).astype(bf16)
    group = HEAD_COUNT // GROUPS
    span = group * FEATS

    def head_state(h, _):
        at = pl.multiple_of(h * PER_HEAD, PER_HEAD)
        rows = pl.ds(pl.multiple_of(h * VROWS, VROWS), VROWS)
        own = pl.ds(pl.multiple_of(h * DV, 16), DV)
        grads = sum_grads(grad_t[own, :], att_t[own, :], dens[pl.ds(pl.multiple_of(h * 8, 8), 8), :][0:1])
        sums_grad[rows, :] = grads
        query_feats = features(blocks[pl.ds(at, 16), :].astype(f32), keep_first, True)
        state[pl.ds(pl.multiple_of(h * FEATS, 16), FEATS), :] = dot_nt(query_feats, grads).astype(bf16)
        return 0

    def hand_on(number):
        part = pl.ds(number * span, span)
        return pltpu.make_async_remote_copy(
            src_ref=message.at[part], dst_ref=later.at[part],
            send_sem=chain_sems.at[0, number], recv_sem=chain_sems.at[1, number],
            device_id={"fsdp": me, "seq": (place + planes - 1) % planes}, device_id_type=MESH,
        )

    @pl.when(place == planes - 1)
    def _():
        later[...] = jnp.zeros(later.shape, bf16)

    for fetch in fetches:
        fetch.wait()
    for number in range(GROUPS):
        part = pl.ds(number * span, span)
        lax.fori_loop(number * group, (number + 1) * group, head_state, 0)

        @pl.when(place == planes - 1)
        def _():
            message[part, :] = state[part, :]
            hand_on(number).start()

    def head_local(h, _):
        at = pl.multiple_of(h * PER_HEAD, PER_HEAD)
        rows = pl.ds(pl.multiple_of(h * VROWS, VROWS), VROWS)
        keys = blocks[pl.ds(at + 16, 16), :]
        queries = blocks[pl.ds(at, 16), :].astype(f32)
        scaled_q = (queries * 0.25).astype(bf16)
        ones = marked[rows, :]
        grads = sums_grad[rows, :]
        from_carry = dot_nn(carry[pl.ds(pl.multiple_of(h * FEATS, 16), FEATS), :], grads) * keep_first_link
        query_total = features_back(queries, from_carry, True)
        small = pl.multiple_of(h * 16, 16)
        for start in range(0, length, TBLOCK):
            stop = start + TBLOCK
            seen = mask[:stop, start:stop]
            shifted, weights = weights_of(keys[:, :stop], scaled_q[:, start:stop], seen)
            grad_block = grads[:, start:stop]
            score_grad = (dot_tn(ones[:, :stop], grad_block) * shifted * seen).astype(bf16)
            query_grad[pl.ds(small, 16), start:stop] = (
                query_total[:, start:stop] + dot_nn(keys[:, :stop], score_grad) * 0.25
            )
            key_part = dot_nt(scaled_q[:, start:stop], score_grad)
            value_part = dot_nt(grad_block, weights.astype(bf16))
            if start > 0:
                key_grad[pl.ds(small, 16), :start] += key_part[:, :start]
                value_grad[rows, :start] += value_part[:, :start]
            key_grad[pl.ds(small, 16), start:stop] = key_part[:, start:]
            value_grad[rows, start:stop] = value_part[:, start:]
        return 0

    def chain_slot(slot):
        for back in range(1, 4):
            number = slot - back + 1
            if 0 <= number < GROUPS:

                @pl.when(place == planes - 1 - back)
                def _():
                    part = pl.ds(number * span, span)
                    hand_on(number).wait_recv()
                    if back < 3:
                        message[part, :] = (
                            state[part, :].astype(f32) + (cond_whole * cond_after) * later[part, :].astype(f32)
                        ).astype(bf16)
                        hand_on(number).start()

    for number in range(GROUPS):
        lax.fori_loop(number * group, (number + 1) * group, head_local, 0)
        chain_slot(number)
    to_stripes(wide_own, slice(48, 64), dot_nn(rank_grad_t, attended[...]).astype(bf16))
    rank_out_t = rank_out[...].astype(f32).T.astype(bf16)
    to_stripes(wide_own, slice(64, 80), dot_nt(rank_out_t, branch_t[...]).astype(bf16))
    chain_slot(GROUPS)
    chain_slot(GROUPS + 1)
    wide_share.z_start()
    ff_share.z_sum()

    doc8 = jnp.broadcast_to(doc_row, (8, length))
    next8 = jnp.broadcast_to(next_docs, (8, 2))
    same_after = [(doc8 == sooner_by(doc8, offset, next8)).astype(f32)[0:1] for offset in (1, 2)]

    def head_finish(h, _):
        at = pl.multiple_of(h * PER_HEAD, PER_HEAD)
        rows = pl.ds(pl.multiple_of(h * VROWS, VROWS), VROWS)
        small = pl.ds(pl.multiple_of(h * 16, 16), 16)
        block = blocks[pl.ds(at, PER_HEAD), :]
        prior = halo[:, pl.ds(at, PER_HEAD)].astype(f32).T[32 : 32 + DV, 14:16]
        came = later[pl.ds(pl.multiple_of(h * FEATS, 16), FEATS), :]
        tap = taps[h]
        keys = block[16:32].astype(f32)
        key_feats = features(keys, keep_last, False)
        key_total = key_grad[small, :] + features_back(keys, dot_nn(came, marked[rows, :]) * keep_last, False)
        values = (value_grad[rows, :] + dot_tn(came, key_feats))[:DV]
        _, conv_out, gate_in, sigmoid = values_of(block, prior, tap, doc_row, prev_docs)
        conv_grad = values * gate_in * sigmoid
        proj_grad[pl.ds(at, 16), :] = query_grad[small, :].astype(bf16)
        proj_grad[pl.ds(at + 16, 16), :] = key_total.astype(bf16)
        proj_grad[pl.ds(at + 32, DV), :] = conv_backward(
            conv_grad, jnp.zeros((DV, 2), f32), tap, same_after
        ).astype(bf16)
        proj_grad[pl.ds(at + 32 + DV, DV), :] = (
            values * conv_out * sigmoid * (1.0 + gate_in * (1.0 - sigmoid))
        ).astype(bf16)
        conv_last[pl.ds(pl.multiple_of(h * DV, 16), DV), :] = conv_grad[:, length - 128 :]
        early = jnp.concatenate([conv_grad[:, :128], jnp.zeros((16, 128), f32)], axis=0).T
        halo_send[:, pl.ds(pl.multiple_of(h * 128, 128), 128)] = early[0:8]
        return 0

    for number in range(GROUPS):
        lax.fori_loop(number * group, (number + 1) * group, head_finish, 0)
        if number == 2:
            wide_share.z_sum()
    to_before = pltpu.make_async_remote_copy(
        src_ref=halo_send, dst_ref=halo_next, send_sem=halo_sems.at[0], recv_sem=halo_sems.at[1],
        device_id={"fsdp": me, "seq": (place + planes - 1) % planes}, device_id_type=MESH,
    )

    @pl.when(place > 0)
    def _():
        to_before.start()

    @pl.when(place == planes - 1)
    def _():
        halo_next[...] = jnp.zeros(halo_next.shape, f32)

    ff_share.gather_start()
    rank_in_t = rank_in[...].astype(f32).T.astype(bf16)

    @pl.when(place < planes - 1)
    def _():
        to_before.wait_recv()

    def head_end(h, total):
        at = pl.multiple_of(h * PER_HEAD, PER_HEAD)
        after = halo_next[:, pl.ds(pl.multiple_of(h * 128, 128), 128)].T[:DV, 0:2]
        last = conv_backward(
            conv_last[pl.ds(pl.multiple_of(h * DV, 16), DV), :], after, taps[h], [s[:, length - 128 :] for s in same_after]
        )
        proj_grad[pl.ds(at + 32, DV), length - 128 :] = last.astype(bf16)
        vg_terms[h, 0:16, 0:DV] = dot_nt(rank_in_t[32:48], proj_grad[pl.ds(at + 32, DV), :])
        vg_terms[h, 16:32, 0:DV] = dot_nt(rank_in_t[48:64], proj_grad[pl.ds(at + 32 + DV, DV), :])
        qk_terms[h, 0:16, 0:16] = dot_nt(rank_in_t[0:16], proj_grad[pl.ds(at, 16), :])
        qk_terms[h, 16:32, 0:16] = dot_nt(rank_in_t[16:32], proj_grad[pl.ds(at + 16, 16), :])
        return total + dot_nn(up_maps[:, pl.ds(at, PER_HEAD)], proj_grad[pl.ds(at, PER_HEAD), :])

    rank_in_grad_t = lax.fori_loop(0, HEAD_COUNT, head_end, jnp.zeros((64, length), f32)).astype(bf16)
    vg_rows = jnp.concatenate([vg_terms[h, :, 0:DV] for h in range(HEAD_COUNT)], axis=1).astype(bf16)
    up_own[0] = vg_rows[0:16]
    up_own[1] = vg_rows[16:32]
    qk_rows = jnp.concatenate(
        [qk_terms[h, 0:16, 0:16] for h in range(HEAD_COUNT)]
        + [qk_terms[h, 16:32, 0:16] for h in range(HEAD_COUNT)]
        + [chosen[...] * (1.0 / planes), jnp.zeros((16, width - 512 - 128), f32)],
        axis=1,
    )
    up_own[2] = qk_rows.astype(bf16)
    up_own[3] = jnp.zeros((16, width), bf16)
    up_share.z_start()
    in_terms = dot_nn(rank_in_grad_t, hidden1[...]).astype(bf16)
    for n in range(4):
        down_own[n] = in_terms[16 * n : 16 * n + 16]
    down_share.z_start()
    wide_share.gather_start()
    ff_share.relay()

    for number in range(blocks_in):
        load_in(number).wait()
        rows = slice(number * step, (number + 1) * step)
        part = dot_nn(in_tile[number % 2], proj_grad[...]) + dot_tn(in_down[:, rows], rank_in_grad_t)
        input_grad[:, rows] = part.T
        if number + 2 < blocks_in:
            load_in(number + 2).start()
        if number == blocks_in - 3:
            up_share.z_sum()
    down_share.z_sum()
    wide_share.relay()
    ff_share.relay_last()

    def finish_rows(rows):
        value = x[rows, :].astype(f32)
        root = row_root(value)
        normed = value * root
        scaled = input_grad[rows, :] * gain1[...]
        input_grad[rows, :] = resid_grad[rows, :] + root * (
            scaled - normed * jnp.mean(scaled * normed, -1, keepdims=True)
        )

    by_rows(length, finish_rows)
    up_share.gather_start()
    down_share.gather_start()
    wide_share.relay_last()
    up_share.relay()
    down_share.relay()
    ff_share.finish()
    wide_share.finish()
    up_share.relay_last()
    down_share.relay_last()
    up_share.finish()
    down_share.finish()

    @pl.when(place > 0)
    def _():
        to_before.wait_send()
        for number in range(GROUPS):
            hand_on(number).wait_send()


def call_t(args, weights):
    f32, bf16 = jnp.float32, jnp.bfloat16
    length, width = args[0].shape
    count, planes = lax.axis_size("fsdp"), lax.axis_size("seq")
    columns = weights[0].shape[1]
    ff = args[-2].shape[1]
    whole = pl.BlockSpec(memory_space=pltpu.VMEM)
    anyplace = pl.BlockSpec(memory_space=pl.ANY)
    shapes = [(planes, 48, stripe_width(ff)), (planes, 80, stripe_width(width)), (planes, 16, width), (planes, 16, width)]
    shares = []
    for shape in shapes:
        shares += [pltpu.VMEM(shape, bf16)] * 3
    return pl.pallas_call(
        t_kernel,
        in_specs=[anyplace if n in FETCHED else whole for n in range(len(args))] + [anyplace] * 2,
        out_specs=[whole] + [anyplace] * 4,
        out_shape=[jax.ShapeDtypeStruct((length, width), f32)]
        + [jax.ShapeDtypeStruct((count,) + shape, bf16) for shape in shapes],
        scratch_shapes=[pltpu.VMEM(args[n].shape, args[n].dtype) for n in FETCHED]
        + [
            pltpu.SemaphoreType.DMA((len(FETCHED),)),
            pltpu.VMEM((width, width), bf16),
            pltpu.VMEM((2, 256, columns), bf16),
            pltpu.VMEM((width, length), bf16),
            pltpu.VMEM((width, length), bf16),
            pltpu.VMEM((HEAD_COUNT * VROWS, length), bf16),
            pltpu.VMEM((HEAD_COUNT * FEATS, VROWS), bf16),
            pltpu.VMEM((HEAD_COUNT * FEATS, VROWS), bf16),
            pltpu.VMEM((HEAD_COUNT * FEATS, VROWS), bf16),
            pltpu.VMEM((HEAD_COUNT * 16, length), f32),
            pltpu.VMEM((HEAD_COUNT * 16, length), f32),
            pltpu.VMEM((HEAD_COUNT * VROWS, length), f32),
            pltpu.VMEM((columns, length), bf16),
            pltpu.VMEM((width, 128), f32),
            pltpu.VMEM((8, HEAD_COUNT * 128), f32),
            pltpu.VMEM((8, HEAD_COUNT * 128), f32),
            pltpu.VMEM((HEAD_COUNT, 32, 128), f32),
            pltpu.VMEM((HEAD_COUNT, 32, 128), f32),
            pltpu.VMEM((length, length), f32),
        ]
        + shares
        + [
            pltpu.SemaphoreType.DMA((2, GROUPS)),
            pltpu.SemaphoreType.DMA((2,)),
            pltpu.SemaphoreType.DMA((3,)),
            pltpu.SemaphoreType.DMA((4, 2 * (planes - 1))),
            pltpu.SemaphoreType.DMA((4, 2 * (planes - 1))),
            pltpu.SemaphoreType.DMA((4, 8)),
            pltpu.SemaphoreType.DMA((4, 8)),
            pltpu.SemaphoreType.DMA((4,)),
        ],
        compiler_params=pltpu.CompilerParams(
            collective_id=2, has_side_effects=True, vmem_limit_bytes=62 * 1024 * 1024
        ),
    )(*args, *weights)


def place_kernel(where, ff, wide, down, up, in_down, qk_up, vg_up, out_down, out_up, gu_down, gu_up, ffd_down, ffd_up):
    f32 = jnp.float32

    def unstripe(part, at, out):
        size, columns = part.shape[3], out.shape[2]
        for n in range(part.shape[1]):
            start, stop = n * size, min((n + 1) * size, columns)
            out[0, :, start:stop] = part[0, n, at : at + out.shape[1], 0 : stop - start].astype(f32)

    unstripe(ff, 0, gu_up)
    unstripe(ff, 32, ffd_down)
    unstripe(wide, 0, gu_down)
    unstripe(wide, 32, ffd_up)
    unstripe(wide, 48, out_down)
    unstripe(wide, 64, out_up)
    for n in range(4):
        in_down[0, 16 * n : 16 * n + 16] = down[0, n].astype(f32)
    vg_up[0, 0:16] = up[0, 0].astype(f32)
    vg_up[0, 16:32] = up[0, 1].astype(f32)
    qk_up[0, 0:16] = up[0, 2, :, 0:256].astype(f32)
    qk_up[0, 16:32] = up[0, 2, :, 256:512].astype(f32)


def call_place(where, parts, widths):
    rows_ff, rows_w = widths
    outs = [(64, rows_w), (32, 256), (32, rows_w), (16, rows_w), (16, rows_w), (32, rows_w), (32, rows_ff), (16, rows_ff), (16, rows_w)]

    def block(shape):
        return pl.BlockSpec((1,) + shape, lambda a, where: (a, 0, 0))

    def picked(array):
        return pl.BlockSpec((1,) + array.shape[1:], lambda a, where: (where[a], 0, 0, 0))

    return pl.pallas_call(
        place_kernel,
        grid_spec=pltpu.PrefetchScalarGridSpec(
            num_scalar_prefetch=1,
            grid=(ADAPTER_COUNT,),
            in_specs=[picked(part) for part in parts],
            out_specs=[block(shape) for shape in outs],
        ),
        out_shape=[jax.ShapeDtypeStruct((ADAPTER_COUNT,) + shape, jnp.float32) for shape in outs],
        compiler_params=pltpu.CompilerParams(vmem_limit_bytes=62 * 1024 * 1024),
    )(where, *parts)


def pick_kernel(
    chosen, in_down_all, qk_all, vg_all, out_down_all, out_up_all, gu_down_all, gu_up_all, ffd_down_all, ffd_up_all,
    taps_all, docs, gain1, gain2,
    in_down, up_maps, out_down, out_up, gu_down, gu_up, ffd_down, ffd_up, taps, doc_row, doc_col, gain1_row, gain2_row, id_block,
):
    f32, bf16 = jnp.float32, jnp.bfloat16
    in_down[...] = in_down_all[0]
    out_down[...] = out_down_all[0]
    out_up[...] = out_up_all[0]
    gu_down[...] = gu_down_all[0]
    gu_up[0:16] = gu_up_all[0, 0]
    gu_up[16:32] = gu_up_all[0, 1]
    ffd_down[...] = ffd_down_all[0]
    ffd_up[...] = ffd_up_all[0]
    up_maps[...] = jnp.zeros(up_maps.shape, bf16)
    three = jnp.concatenate([taps_all[...], jnp.zeros((5, taps_all.shape[1]), f32)], axis=0)
    for h in range(HEAD_COUNT):
        at = h * PER_HEAD
        for n in range(2):
            up_maps[16 * n : 16 * n + 16, at + 16 * n : at + 16 * n + 16] = qk_all[0, n, :, 16 * h : 16 * h + 16]
            start = at + 32 + n * DV
            up_maps[32 + 16 * n : 48 + 16 * n, start : start + DV] = vg_all[0, n, :, DV * h : DV * h + DV]
        taps[h] = three[:, DV * h : DV * h + DV].T
    row = docs[...].astype(f32)
    doc_row[...] = row
    doc_col[...] = jnp.broadcast_to(row, (8, row.shape[1])).T[:, 0:1]
    gain1_row[...] = gain1[...].reshape(1, -1)
    gain2_row[...] = gain2[...].reshape(1, -1)
    id_block[...] = jnp.full(id_block.shape, chosen[0], jnp.int32).astype(f32)


def call_pick(chosen, tables, taps, docs, gain1, gain2):
    f32, bf16 = jnp.float32, jnp.bfloat16
    in_down, qk, vg, out_down, out_up, gu_down, gu_up, ffd_down, ffd_up = tables
    length = docs.shape[1]
    width, ff = out_up.shape[2], ffd_down.shape[2]

    def picked(table):
        zeros = (0,) * (table.ndim - 1)
        return pl.BlockSpec((1,) + table.shape[1:], lambda n, chosen: (chosen[0],) + zeros)

    def whole(shape):
        return pl.BlockSpec(shape, lambda n, chosen: (0,) * len(shape))

    outs = [
        ((64, width), bf16), ((64, HEAD_COUNT * PER_HEAD), bf16), ((16, width), bf16), ((16, width), bf16), ((32, width), bf16),
        ((32, ff), bf16), ((16, ff), bf16), ((16, width), bf16), ((HEAD_COUNT, DV, 8), f32), ((1, length), f32), ((length, 1), f32),
        ((1, width), f32), ((1, width), f32), ((16, 128), f32),
    ]
    rest = (taps, docs, gain1, gain2)
    return pl.pallas_call(
        pick_kernel,
        grid_spec=pltpu.PrefetchScalarGridSpec(
            num_scalar_prefetch=1,
            grid=(1,),
            in_specs=[picked(table) for table in tables] + [whole(array.shape) for array in rest],
            out_specs=[whole(shape) for shape, _ in outs],
        ),
        out_shape=[jax.ShapeDtypeStruct(shape, kind) for shape, kind in outs],
        compiler_params=pltpu.CompilerParams(vmem_limit_bytes=62 * 1024 * 1024),
    )(chosen, *tables, *rest)


def call_heads(kernel, length, ins, outs, scratch=()):
    def spec(shape, how):
        if how == "rows":
            return pl.BlockSpec((shape[0] // HEAD_COUNT,) + shape[1:], lambda h: (h,) + (0,) * (len(shape) - 1))
        if how == "cols":
            return pl.BlockSpec((shape[0], shape[1] // HEAD_COUNT), lambda h: (0, h))
        return pl.BlockSpec(shape, lambda h: (0,) * len(shape))

    return pl.pallas_call(
        kernel,
        grid=(HEAD_COUNT,),
        in_specs=[spec(a.shape, how) for a, how in ins],
        out_specs=[spec(s.shape, how) for s, how in outs],
        out_shape=[s for s, _ in outs],
        scratch_shapes=list(scratch),
        compiler_params=pltpu.CompilerParams(vmem_limit_bytes=48 * 1024 * 1024),
    )(*[a for a, _ in ins])


def shift_pairs(count, step):
    return [(i, i + step) for i in range(count) if 0 <= i + step < count]


def chain(own, whole, link, step):
    count = lax.axis_size("seq")
    pairs = shift_pairs(count, step)
    message = own
    for _ in range(count - 2):
        got = lax.ppermute(message, "seq", pairs)
        message = (own.astype(jnp.float32) + (whole * link) * got.astype(jnp.float32)).astype(jnp.bfloat16)
    got = lax.ppermute(message, "seq", pairs)
    return (got.astype(jnp.float32) * link).astype(jnp.bfloat16)


def product(spec, left, right):
    return jnp.einsum(spec, left, right, preferred_element_type=jnp.float32)


def rms_forward(value, gain):
    inv_root = lax.rsqrt(jnp.mean(value * value, -1, keepdims=True) + epsilon)
    normed = value * inv_root
    return (normed, inv_root, (normed * gain).astype(jnp.bfloat16))


def rms_backward(grad_hidden, normed, inv_root, gain):
    scaled = grad_hidden * gain
    return inv_root * (scaled - normed * jnp.mean(scaled * normed, -1, keepdims=True))


def up_by_head(querykey, valuegate):
    parts = [
        (querykey[0], 0, FEATURE_SIZE),
        (querykey[1], FEATURE_SIZE, FEATURE_SIZE),
        (valuegate[0], 2 * FEATURE_SIZE, DV),
        (valuegate[1], 2 * FEATURE_SIZE + DV, DV),
    ]
    rows = [
        jnp.pad(
            part.reshape(ADAPTER_RANK, HEAD_COUNT, size),
            ((0, 0), (0, 0), (at, PER_HEAD - at - size)),
        )
        for part, at, size in parts
    ]
    return jnp.concatenate(rows, axis=0).reshape(4 * ADAPTER_RANK, HEAD_COUNT * PER_HEAD)


def by_collectives(
    layer_input_rows,
    segments,
    sequence_adapter_index,
    output_gradient,
    mixer_norm_gain,
    feedforward_norm_gain,
    convolution_taps,
    mixer_input_weight,
    mixer_output_weight,
    gate_up_weight,
    down_weight,
    adapter_input_down,
    adapter_querykey_up,
    adapter_valuegate_up,
    adapter_output_down,
    adapter_output_up,
    adapter_gateup_down,
    adapter_gateup_up,
    adapter_feedforward_down,
    adapter_feedforward_up,
):
    batch, length, width = layer_input_rows.shape
    assert batch == 1
    seq_count = lax.axis_size("seq")
    ff = gate_up_weight.shape[1] // 2
    bf16, f32 = jnp.bfloat16, jnp.float32
    chosen = sequence_adapter_index[0, 0]

    def select(table):
        return lax.dynamic_index_in_dim(table, chosen, 0, keepdims=False)

    in_down = select(adapter_input_down.swapaxes(1, 2))
    up_maps = up_by_head(select(adapter_querykey_up), select(adapter_valuegate_up))
    out_down = select(adapter_output_down.swapaxes(1, 2))
    out_up = select(adapter_output_up)
    gu_down = select(adapter_gateup_down.swapaxes(1, 2))
    gu_up = select(adapter_gateup_up)
    ffd_down = select(adapter_feedforward_down.swapaxes(1, 2))
    ffd_up = select(adapter_feedforward_up)
    mixer_in, mixer_out, gate_up, down_w = (
        lax.all_gather(mixer_input_weight, "fsdp", axis=0, tiled=True),
        lax.all_gather(mixer_output_weight, "fsdp", axis=0, tiled=True),
        lax.all_gather(gate_up_weight, "fsdp", axis=0, tiled=True),
        lax.all_gather(down_weight, "fsdp", axis=0, tiled=True),
    )
    docs = segments.astype(f32)
    place = lax.axis_index("seq")
    edge = jnp.concatenate([docs[:, :1], docs[:, length - 2 :], jnp.zeros((1, 125), f32)], axis=1)
    before_edge = lax.ppermute(edge, "seq", shift_pairs(seq_count, 1))
    after_edge = lax.ppermute(edge, "seq", shift_pairs(seq_count, -1))
    prev_docs = jnp.where(place == 0, -1.0, before_edge[:, 1:3])
    next_doc = jnp.where(place == seq_count - 1, -1.0, after_edge[:, 0])
    link_before = (prev_docs[0, 1] == docs[0, 0]).astype(f32)
    link_after = (next_doc[0] == docs[0, length - 1]).astype(f32)
    whole = (docs[0, 0] == docs[0, length - 1]).astype(f32)
    prev_pad = jnp.pad(prev_docs, ((0, 0), (0, 126)))
    doc_col = docs.reshape(length, 1)
    taps = jnp.pad(convolution_taps.T.reshape(HEAD_COUNT, DV, 3), ((0, 0), (0, 0), (0, 5)))

    inputs_f = layer_input_rows[0].astype(f32)
    grad_out = output_gradient[0]
    normed1, root1, hidden1 = rms_forward(inputs_f, mixer_norm_gain)
    rank_in = product("td,rd->tr", hidden1, in_down).astype(bf16)
    projected = (
        product("td,de->te", hidden1, mixer_in) + product("tr,re->te", rank_in, up_maps)
    ).astype(bf16)
    halo = lax.ppermute(projected[length - 16 :], "seq", shift_pairs(seq_count, 1))
    mask = pltpu.VMEM((length, length), f32)
    heads = HEAD_COUNT
    blocks, values, sums, state = call_heads(
        f1_kernel,
        length,
        [(projected, "cols"), (halo, "cols"), (taps, "rows"), (docs, None), (doc_col, None), (prev_pad, None)],
        [
            (jax.ShapeDtypeStruct((heads * PER_HEAD, length), bf16), "rows"),
            (jax.ShapeDtypeStruct((heads * VROWS, length), bf16), "rows"),
            (jax.ShapeDtypeStruct((heads * VROWS, length), f32), "rows"),
            (jax.ShapeDtypeStruct((heads * FEATS, VROWS), bf16), "rows"),
        ],
        [mask],
    )
    carry = chain(state, whole, link_before, 1)
    attended_t, denominator = call_heads(
        f2_kernel,
        length,
        [(blocks, "rows"), (sums, "rows"), (carry, "rows"), (docs, None)],
        [
            (jax.ShapeDtypeStruct((heads * DV, length), bf16), "rows"),
            (jax.ShapeDtypeStruct((heads * 8, length), f32), "rows"),
        ],
    )
    attended = attended_t.T
    rank_out = product("td,rd->tr", attended, out_down).astype(bf16)
    resid = (
        inputs_f
        + product("td,de->te", attended, mixer_out)
        + product("tr,re->te", rank_out, out_up)
    )
    normed2, root2, hidden2 = rms_forward(resid, feedforward_norm_gain)
    rank_mlp = product("td,rd->tr", hidden2, gu_down).astype(bf16)
    rank_ffd_grad = product("te,re->tr", grad_out, ffd_up).astype(bf16)
    inner_grad = product("te,fe->tf", grad_out, down_w) + product("tr,rf->tf", rank_ffd_grad, ffd_down)
    gate_pre = product("td,de->te", hidden2, gate_up[:, :ff]) + product(
        "tr,re->te", rank_mlp[:, :ADAPTER_RANK], gu_up[0]
    )
    up_pre = product("td,de->te", hidden2, gate_up[:, ff:]) + product(
        "tr,re->te", rank_mlp[:, ADAPTER_RANK:], gu_up[1]
    )
    sigmoid = jax.nn.sigmoid(gate_pre)
    gate_val = gate_pre * sigmoid
    inner_act = (gate_val * up_pre).astype(bf16)
    gate_grad = (inner_grad * up_pre * (sigmoid * (1.0 + gate_pre * (1.0 - sigmoid)))).astype(bf16)
    up_grad = (inner_grad * gate_val).astype(bf16)
    rank_ffd = product("tf,rf->tr", inner_act, ffd_down).astype(bf16)
    output = (
        resid + product("tf,fe->te", inner_act, down_w) + product("tr,re->te", rank_ffd, ffd_up)
    ).astype(bf16)
    rank_mlp_grad = jnp.concatenate(
        [product("tf,rf->tr", gate_grad, gu_up[0]), product("tf,rf->tr", up_grad, gu_up[1])], -1
    ).astype(bf16)
    hidden2_grad = (
        product("tf,df->td", gate_grad, gate_up[:, :ff])
        + product("tf,df->td", up_grad, gate_up[:, ff:])
        + product("tr,rd->td", rank_mlp_grad, gu_down)
    )
    resid_grad = grad_out.astype(f32) + rms_backward(hidden2_grad, normed2, root2, feedforward_norm_gain)
    branch_grad = resid_grad.astype(bf16)
    rank_out_grad = product("te,re->tr", branch_grad, out_up).astype(bf16)
    attended_grad = (
        product("te,de->td", branch_grad, mixer_out) + product("tr,rd->td", rank_out_grad, out_down)
    ).astype(bf16)
    grad_t = attended_grad.T
    later, query_grad, key_grad, value_grad = call_heads(
        b1_kernel,
        length,
        [(blocks, "rows"), (values, "rows"), (grad_t, "rows"), (attended_t, "rows"), (denominator, "rows"), (carry, "rows"), (docs, None), (doc_col, None)],
        [
            (jax.ShapeDtypeStruct((heads * FEATS, VROWS), bf16), "rows"),
            (jax.ShapeDtypeStruct((heads * 16, length), f32), "rows"),
            (jax.ShapeDtypeStruct((heads * 16, length), f32), "rows"),
            (jax.ShapeDtypeStruct((heads * VROWS, length), f32), "rows"),
        ],
        [mask],
    )
    later = chain(later, whole, link_after, -1)
    projected_grad, first_conv, tail_grad = call_heads(
        b2_kernel,
        length,
        [(blocks, "rows"), (values, "rows"), (later, "rows"), (query_grad, "rows"), (key_grad, "rows"), (value_grad, "rows"), (halo, "cols"), (taps, "rows"), (docs, None), (prev_pad, None)],
        [
            (jax.ShapeDtypeStruct((length, heads * PER_HEAD), bf16), "cols"),
            (jax.ShapeDtypeStruct((16, heads * PER_HEAD), f32), "cols"),
            (jax.ShapeDtypeStruct((16, heads * PER_HEAD), f32), "cols"),
        ],
    )
    next_conv = lax.ppermute(first_conv[:2], "seq", shift_pairs(seq_count, -1))
    taps_row = jnp.pad(
        convolution_taps.reshape(3, heads, DV),
        ((0, 0), (0, 0), (2 * FEATURE_SIZE, PER_HEAD - 2 * FEATURE_SIZE - DV)),
    ).reshape(3, heads * PER_HEAD)
    after_docs = jnp.where(place == seq_count - 1, -1.0, after_edge[0, 0])
    link_1 = (after_docs == docs[0, length - 1]).astype(f32)
    link_2 = (after_docs == docs[0, length - 2]).astype(f32)
    second = (docs[0, 1] == docs[0, 0]).astype(f32)
    second_next = lax.ppermute(second, "seq", shift_pairs(seq_count, -1))
    extra_last = taps_row[1] * next_conv[0] * link_1 + taps_row[2] * next_conv[1] * link_1 * second_next
    extra_before = taps_row[2] * next_conv[0] * link_2
    extra = jnp.concatenate(
        [jnp.zeros((14, heads * PER_HEAD), f32), extra_before[None], extra_last[None]], axis=0
    )
    projected_grad = lax.dynamic_update_slice(
        projected_grad, (tail_grad + extra).astype(bf16), (length - 16, 0)
    )
    rank_in_grad = product("te,re->tr", projected_grad, up_maps).astype(bf16)
    hidden1_grad = product("te,de->td", projected_grad, mixer_in) + product(
        "tr,rd->td", rank_in_grad, in_down
    )
    input_grad = resid_grad + rms_backward(hidden1_grad, normed1, root1, mixer_norm_gain)

    wide = product("tr,te->re", rank_in, projected_grad).reshape(4, ADAPTER_RANK, heads, PER_HEAD)
    term_qk = jnp.stack(
        [wide[0, :, :, 0:16].reshape(ADAPTER_RANK, -1), wide[1, :, :, 16:32].reshape(ADAPTER_RANK, -1)]
    )
    term_vg = jnp.concatenate(
        [
            wide[2, :, :, 32 : 32 + DV].reshape(ADAPTER_RANK, -1),
            wide[3, :, :, 32 + DV :].reshape(ADAPTER_RANK, -1),
        ]
    )
    by_width = jnp.concatenate(
        [
            product("tr,td->rd", rank_in_grad, hidden1),
            term_vg,
            product("tr,td->rd", rank_out_grad, attended),
            product("tr,td->rd", rank_out, branch_grad),
            product("tr,td->rd", rank_mlp_grad, hidden2),
            product("tr,td->rd", rank_ffd, grad_out),
        ]
    )
    by_ff = jnp.concatenate(
        [
            product("tr,tf->rf", rank_mlp[:, :ADAPTER_RANK], gate_grad),
            product("tr,tf->rf", rank_mlp[:, ADAPTER_RANK:], up_grad),
            product("tr,tf->rf", rank_ffd_grad, inner_act),
        ]
    )
    by_rank = jnp.concatenate([term_qk.reshape(32, -1), jnp.full((16, 256), chosen.astype(f32) / seq_count)])
    by_width, by_ff, by_rank = spread(by_width, by_ff, by_rank)
    sequences = by_rank.shape[0]
    onehot = (by_rank[:, 32, 0][None, :] == jnp.arange(ADAPTER_COUNT, dtype=bf16)[:, None])

    if sequences == ADAPTER_COUNT:
        where = jnp.argmax(onehot, axis=1)

        def arrange(rows):
            return jnp.take(rows, where, axis=0).astype(f32)
    else:

        def arrange(rows):
            return jnp.einsum("as,s...->a...", onehot.astype(f32), rows.astype(f32), precision="highest")

    sizes = [64, 32, 16, 16, 32, 16]
    cut = [sum(sizes[:n]) for n in range(len(sizes) + 1)]
    widths = [arrange(by_width[:, cut[n] : cut[n + 1]]) for n in range(len(sizes))]
    return (
        output[None],
        input_grad[None],
        widths[0].swapaxes(1, 2),
        arrange(by_rank[:, :32]).reshape(ADAPTER_COUNT, 2, ADAPTER_RANK, -1),
        widths[1].reshape(ADAPTER_COUNT, 2, ADAPTER_RANK, width),
        widths[2].swapaxes(1, 2),
        widths[3],
        widths[4].swapaxes(1, 2),
        arrange(by_ff[:, :32]).reshape(ADAPTER_COUNT, 2, ADAPTER_RANK, ff),
        arrange(by_ff[:, 32:]).swapaxes(1, 2),
        widths[5],
    )


def by_kernels(
    layer_input_rows,
    segments,
    sequence_adapter_index,
    output_gradient,
    mixer_norm_gain,
    feedforward_norm_gain,
    convolution_taps,
    mixer_input_weight,
    mixer_output_weight,
    gate_up_weight,
    down_weight,
    adapter_input_down,
    adapter_querykey_up,
    adapter_valuegate_up,
    adapter_output_down,
    adapter_output_up,
    adapter_gateup_down,
    adapter_gateup_up,
    adapter_feedforward_down,
    adapter_feedforward_up,
):
    x, grad_out = layer_input_rows[0], output_gradient[0]
    width, ff = x.shape[1], adapter_gateup_up.shape[-1]
    tables = (
        adapter_input_down.swapaxes(1, 2), adapter_querykey_up, adapter_valuegate_up, adapter_output_down.swapaxes(1, 2),
        adapter_output_up, adapter_gateup_down.swapaxes(1, 2), adapter_gateup_up, adapter_feedforward_down.swapaxes(1, 2),
        adapter_feedforward_up,
    )
    *maps, taps, doc_row, doc_col, gain1, gain2, id_block = call_pick(
        sequence_adapter_index[0], tables, convolution_taps, segments, mixer_norm_gain, feedforward_norm_gain
    )
    in_down, up_maps, out_down, out_up = maps[:4]
    shards = (mixer_input_weight, mixer_output_weight, gate_up_weight, down_weight)
    mixer_in, mixer_out, _, _, output, *kept = call_m(x, grad_out, gain1, gain2, taps, doc_row, doc_col, maps, shards)
    *kept, next_docs = kept
    input_grad, *parts = call_t(
        (x, gain1, taps, doc_row, doc_col, next_docs, id_block, in_down, up_maps, out_down, out_up, *kept),
        (mixer_in, mixer_out),
    )
    chosen = parts[3][:, 2, 0, 512]
    where = jnp.argmax(chosen[None, :] == jnp.arange(ADAPTER_COUNT, dtype=jnp.bfloat16)[:, None], axis=1).astype(jnp.int32)
    in_down, qk_up, vg_up, out_down, out_up, gu_down, gu_up, ffd_down, ffd_up = call_place(
        where, parts, (ff, width)
    )
    return (
        output[None],
        input_grad[None],
        in_down.swapaxes(1, 2),
        qk_up.reshape(ADAPTER_COUNT, 2, ADAPTER_RANK, -1),
        vg_up.reshape(ADAPTER_COUNT, 2, ADAPTER_RANK, width),
        out_down.swapaxes(1, 2),
        out_up,
        gu_down.swapaxes(1, 2),
        gu_up.reshape(ADAPTER_COUNT, 2, ADAPTER_RANK, ff),
        ffd_down.swapaxes(1, 2),
        ffd_up,
    )


def spread(*terms):
    summed = lax.psum(terms, "seq")
    return [lax.all_gather(term.astype(jnp.bfloat16), "fsdp") for term in summed]


def solution(mesh):
    kernels = mesh.shape["fsdp"] == ADAPTER_COUNT and mesh.shape["seq"] == 4
    return jax.shard_map(
        by_kernels if kernels else by_collectives,
        mesh=mesh,
        in_specs=(
            P("fsdp", "seq", None),
            P("fsdp", "seq"),
            P("fsdp", None),
            P("fsdp", "seq", None),
            P(),
            P(),
            P(),
            P("fsdp", None),
            P("fsdp", None),
            P("fsdp", None),
            P("fsdp", None),
        )
        + (P(),) * 9,
        out_specs=(P("fsdp", "seq", None), P("fsdp", "seq", None)) + (P(),) * 9,
        check_vma=False,
    )
```
